32 devices in a mesh: batch: 4 (over x, core), mp: 8 (over z, y).
Axes of the slice: x: 2, y: 2, z: 4, core: 2. Of those that a mesh axis runs over, the one named last changes fastest.
Arguments:
- features: bfloat16 [2, 6144, 9216], P(None, 'batch', 'mp'), may hold values from -6 to 6
- weights: bfloat16 [2, 9216, 4096], P(None, None, 'mp'), may hold values from -0.0625 to 0.0625
- bias: float32 [2, 4096], P(None, 'mp'), may hold values from -3 to 3
- stitch: float32 [2, 2, 4096], P(None, None, 'mp'), may hold values from 0.1 to 1
- cotangent: bfloat16 [2, 6144, 4096], P(None, 'batch', 'mp'), may hold values from -84 to 84
- crop_counts: int32 [256], P('batch'), may hold values from 1 to 47
- row_mask: int32 [6144], P('batch'), may hold values 0 or 1
- flags: int32 [2, 2, 8], replicated, may hold values from 0 to 1
Outputs:
- mixed: bfloat16 [2, 6144, 4096], P(None, 'batch', 'mp')
- grad_features: bfloat16 [2, 6144, 9216], P(None, 'batch', 'mp')
- grad_weights: float32 [2, 9216, 4096], P(None, None, 'mp')
- grad_bias: float32 [2, 4096], P(None, 'mp')
- grad_stitch: float32 [2, 2, 4096], P(None, None, 'mp')
The draws below stay inside these ranges and needn't reach their ends.
All inputs are finite; a program needn't handle non-finite values. No bound on the sum of `row_mask` on one device may be relied on, other than what follows from the above.
Results may differ from the reference program's by a relative error of at most 0.0049.
Values may be sent and summed in bfloat16 or wider, within the bound.
A program may use at most 448 MiB of HBM per device.

```python
import jax
import jax.numpy as jnp
from jax import lax

IN_CH = 9216
OUT_CH = 4096
ROWS_DEV = 1536
IMG_DEV = 64
FLAG_GROUPS = 8
CROP_MOST = 48
ROWS = 6144
IMAGES = 256
N_BATCH = 4


def draw_cotangent(key, part):
    key = jax.random.fold_in(key, 11)
    first, second = jax.random.split(key)
    common = jnp.clip(jax.random.normal(first, (1, ROWS, OUT_CH), jnp.float32), -5.0, 5.0)
    own = jnp.clip(jax.random.normal(second, (2, ROWS, OUT_CH), jnp.float32), -5.0, 5.0)
    return (12.0 * (0.6 * common + 0.8 * own)).astype(jnp.bfloat16)


def plant(values, own_key, least, largest):
    shape = values.shape
    place = [jax.random.randint(jax.random.fold_in(own_key, axis), (), 0, shape[axis]) for axis in range(len(shape))]
    values = values.at[tuple(place)].set(least)
    longest = shape.index(max(shape))
    place[longest] = (place[longest] + 1) % shape[longest]
    return values.at[tuple(place)].set(largest)


def level_of(stream_key, dims, pieces, smallest, top_value):
    def one(position, shards_of):
        draws = jax.random.uniform(jax.random.fold_in(jax.random.fold_in(stream_key, 6), position), (shards_of,), jnp.float32, smallest / len(pieces), top_value / len(pieces))
        return jnp.repeat(jnp.exp(draws), dims[position] // shards_of).reshape((-1,) + (1,) * (len(dims) - position - 1))

    loudness = one(*pieces[0])
    for cut in pieces[1:]:
        loudness = loudness * one(*cut)
    return loudness


def scatter_about(own_key, extent, scale, most, cuts=(), kind=jnp.bfloat16):
    loudness = level_of(own_key, extent, cuts, -0.22, 0.18) if cuts else 1.0
    values = jax.random.normal(own_key, extent, jnp.float32) * scale * loudness
    return jnp.minimum(jnp.maximum(values, -most), most).astype(kind)


def setup_inputs(seed: int = 0) -> dict:
    splits = jax.random.split(jax.random.key(seed), 9)
    features = scatter_about(splits[0], (2, ROWS, IN_CH), 1.0, 6.0, ((1, 4), (2, 8)))
    weights = scatter_about(splits[1], (2, IN_CH, OUT_CH), IN_CH ** -0.5, 0.0625, ((2, 8),))
    bias = scatter_about(splits[2], (2, OUT_CH), 0.5, 3.0, ((1, 8),), jnp.float32)
    stitch = jnp.clip(0.1 + 0.9 * jax.random.uniform(splits[3], (2, 2, OUT_CH), jnp.float32) ** level_of(splits[3], (2, 2, OUT_CH), ((2, 8),), -0.2, 0.2), 0.1, 1.0)
    cotangent = draw_cotangent(jax.random.fold_in(splits[8], 71), 0)
    crop_counts = plant(jax.random.randint(splits[5], (IMAGES,), 1, CROP_MOST), jax.random.fold_in(splits[5], 1), 1, CROP_MOST - 1).astype(jnp.int32)
    row_mask = plant((jax.random.randint(splits[6], (ROWS,), 0, 8) < 7).astype(jnp.int32), jax.random.fold_in(splits[6], 1), 0, 1)
    flags = plant(jax.random.randint(splits[7], (2, 2, FLAG_GROUPS), 0, 2), jax.random.fold_in(splits[7], 1), 0, 1).astype(jnp.int32)
    return dict(features=features, weights=weights, bias=bias, stitch=stitch, cotangent=cotangent, crop_counts=crop_counts, row_mask=row_mask, flags=flags)


@jax.custom_vjp
def low(v):
    return lax.optimization_barrier(v.astype(jnp.bfloat16)).astype(jnp.float32)

@jax.custom_vjp
def low_back(v):
    return v

def low_keep(v):
    return (low(v), None)

def low_pass(kept, grad):
    return (grad,)

def back_keep(v):
    return (v, None)

def back_low(kept, grad):
    return (low(grad),)
low.defvjp(low_keep, low_pass)
low_back.defvjp(back_keep, back_low)

def row_weights(counts, mask):
    ends = jnp.cumsum(counts)
    starts = ends - counts
    index = lax.broadcasted_iota(jnp.int32, (mask.shape[0], counts.shape[0]), 0)
    inside = (index >= starts[None, :]) & (index < ends[None, :])
    count_row = lax.optimization_barrier(jnp.sum(jnp.where(inside, counts[None, :], 0), axis=1))
    live = (count_row > 0) & (mask == 1)
    return jnp.where(live, 1.0 / jnp.maximum(count_row, 1).astype(jnp.float32), 0.0).astype(jnp.float32)

def head(features, weights):
    return low_back(jnp.einsum('trk,tkc->trc', features, weights, precision=lax.Precision.HIGHEST))

def tail(linear, bias, stitch):
    hidden = jax.nn.gelu(linear + bias[:, None, :], approximate=False)
    return stitch[:, 0, None, :] * hidden[0][None] + stitch[:, 1, None, :] * hidden[1][None]

def reference(features, weights, bias, stitch, cotangent, crop_counts, row_mask, flags):
    feat = features.astype(jnp.float32)
    wts = weights.astype(jnp.float32)
    weight_rows = jax.vmap(row_weights)(crop_counts.reshape(N_BATCH, IMG_DEV), row_mask.reshape(N_BATCH, ROWS_DEV)).reshape(-1)
    grad_out = cotangent.astype(jnp.float32) * weight_rows[None, :, None]
    linear, head_back = jax.vjp(head, feat, wts)
    mixed, tail_back = jax.vjp(tail, linear, bias, stitch)
    grad_linear, unused_bias, grad_stitch = tail_back(grad_out)
    grad_feat, grad_wts = head_back(grad_linear)
    task_list = []
    for task in range(2):
        select = (jnp.arange(2) == task).astype(jnp.float32)[:, None, None]
        task_list.append(tail_back(grad_out * select)[1])
    task_bias = jnp.stack(task_list)
    channel = jnp.arange(OUT_CH, dtype=jnp.int32)
    member = ((channel % FLAG_GROUPS)[:, None] == jnp.arange(FLAG_GROUPS, dtype=jnp.int32)[None, :]).astype(jnp.float32)
    dots = jnp.dot(task_bias[0] * task_bias[1], member, precision=lax.Precision.HIGHEST)
    norms = jnp.einsum('stc,cg->stg', task_bias * task_bias, member, precision=lax.Precision.HIGHEST)
    flag = flags.astype(jnp.float32)
    coef_first = jnp.dot(flag[0] * dots / (norms[1] + 1e-06), member.T, precision=lax.Precision.HIGHEST)
    coef_second = jnp.dot(flag[1] * dots / (norms[0] + 1e-06), member.T, precision=lax.Precision.HIGHEST)
    first = task_bias[0] - coef_first * task_bias[1]
    second = task_bias[1] - coef_second * task_bias[0]
    grad_bias = first + second
    return (mixed.astype(jnp.bfloat16), grad_feat.astype(jnp.bfloat16), grad_wts, grad_bias, grad_stitch)
```

```python
import jax
import jax.numpy as jnp
from jax import lax
from jax.sharding import PartitionSpec as P

FLAG_GROUPS = 8
OUTER = 4


def row_weights(counts, mask):
    ends = jnp.cumsum(counts)
    starts = ends - counts
    index = lax.broadcasted_iota(jnp.int32, (mask.shape[0], counts.shape[0]), 0)
    inside = (index >= starts[None, :]) & (index < ends[None, :])
    count_row = jnp.sum(jnp.where(inside, counts[None, :], 0), axis=1)
    live = (count_row > 0) & (mask == 1)
    return jnp.where(live, 1.0 / jnp.maximum(count_row, 1).astype(jnp.float32), 0.0)


def project_bias(task_bias, flags):
    local_width = task_bias.shape[2]
    channel = lax.axis_index("mp") * local_width + lax.broadcasted_iota(
        jnp.int32, (local_width, FLAG_GROUPS), 0
    )
    member = (
        channel % FLAG_GROUPS == lax.broadcasted_iota(jnp.int32, (local_width, FLAG_GROUPS), 1)
    ).astype(jnp.float32)
    dots = jnp.dot(task_bias[0] * task_bias[1], member, precision=lax.Precision.HIGHEST)
    norms = jnp.einsum(
        "stc,cg->stg", task_bias * task_bias, member, precision=lax.Precision.HIGHEST
    )
    dots, norms = lax.psum((dots, norms), "mp")
    flag = flags.astype(jnp.float32)
    coef_first = jnp.dot(
        flag[0] * dots / (norms[1] + 1e-06), member.T, precision=lax.Precision.HIGHEST
    )
    coef_second = jnp.dot(
        flag[1] * dots / (norms[0] + 1e-06), member.T, precision=lax.Precision.HIGHEST
    )
    first = task_bias[0] - coef_first * task_bias[1]
    second = task_bias[1] - coef_second * task_bias[0]
    return first + second


def generic_plan(mesh):
    n_mp = mesh.shape["mp"]
    n_batch = mesh.shape["batch"]
    inner = n_mp // OUTER
    inner_groups = [[o * inner + i for i in range(inner)] for o in range(OUTER)]
    outer_groups = [[o * inner + i for o in range(OUTER)] for i in range(inner)]

    def per_device(features, weights, bias, stitch, cotangent, crop_counts, row_mask, flags):
        rows = features.shape[1]
        width = weights.shape[2]
        depth = features.shape[2] * inner
        held = lax.all_gather(
            features, "mp", axis=2, tiled=True, axis_index_groups=inner_groups
        )
        split = weights.reshape(2, OUTER, depth, width)
        block = lax.all_to_all(
            split, "mp", split_axis=1, concat_axis=1, axis_index_groups=outer_groups
        )
        block = block.reshape(2, OUTER, depth, width)
        part = jnp.einsum("trk,tokc->otrc", held, block, preferred_element_type=jnp.float32)
        linear = lax.psum_scatter(
            part.astype(jnp.bfloat16),
            "mp",
            scatter_dimension=0,
            axis_index_groups=outer_groups,
        ).astype(jnp.float32)
        pre = linear + bias[:, None, :]
        hidden, gelu_back = jax.vjp(lambda v: jax.nn.gelu(v, approximate=False), pre)
        mixed = stitch[:, 0, None, :] * hidden[0][None] + stitch[:, 1, None, :] * hidden[1][None]
        scale_rows = row_weights(crop_counts, row_mask)
        grad_out = cotangent.astype(jnp.float32) * scale_rows[None, :, None]
        first_task = gelu_back(stitch[0][:, None, :] * grad_out[0][None])[0]
        second_task = gelu_back(stitch[1][:, None, :] * grad_out[1][None])[0]
        task_bias = jnp.stack([jnp.sum(first_task, axis=1), jnp.sum(second_task, axis=1)])
        grad_linear = (first_task + second_task).astype(jnp.bfloat16)
        grad_stitch = jnp.sum(grad_out[:, None] * hidden[None], axis=2)
        every = lax.all_gather(grad_linear, "mp", axis_index_groups=outer_groups)
        grad_part = jnp.einsum(
            "otrc,tokc->trk", every, block, preferred_element_type=jnp.float32
        )
        grad_part = grad_part.astype(jnp.bfloat16).reshape(2, rows, inner, depth // inner)
        grad_features = lax.psum_scatter(
            grad_part.transpose(2, 0, 1, 3),
            "mp",
            scatter_dimension=0,
            axis_index_groups=inner_groups,
        )
        weight_part = jnp.einsum(
            "trk,otrc->otkc", held, every, preferred_element_type=jnp.float32
        )
        weight_part = weight_part.astype(jnp.bfloat16).reshape(
            OUTER, 2, n_batch, depth // n_batch, width
        )
        share = lax.psum_scatter(
            weight_part.transpose(2, 0, 1, 3, 4), "batch", scatter_dimension=0
        )
        share = lax.all_to_all(
            share, "mp", split_axis=0, concat_axis=0, axis_index_groups=outer_groups
        )
        share = share.reshape(OUTER, 2, depth // n_batch, width)
        whole = lax.all_gather(share, "batch")
        grad_weights = whole.transpose(2, 1, 0, 3, 4).reshape(2, OUTER * depth, width)
        task_bias, grad_stitch = lax.psum((task_bias, grad_stitch), "batch")
        grad_bias = project_bias(task_bias, flags)
        return (
            mixed.astype(jnp.bfloat16),
            grad_features.astype(jnp.bfloat16),
            grad_weights.astype(jnp.float32),
            grad_bias,
            grad_stitch,
        )

    return per_device


def solution(mesh):
    in_specs = (
        P(None, "batch", "mp"),
        P(None, None, "mp"),
        P(None, "mp"),
        P(None, None, "mp"),
        P(None, "batch", "mp"),
        P("batch"),
        P("batch"),
        P(),
    )
    out_specs = (
        P(None, "batch", "mp"),
        P(None, "batch", "mp"),
        P(None, None, "mp"),
        P(None, "mp"),
        P(None, None, "mp"),
    )
    return jax.shard_map(
        generic_plan(mesh), mesh=mesh, in_specs=in_specs, out_specs=out_specs, check_vma=False
    )
```

```python
import functools

import jax
import jax.numpy as jnp
from jax import lax
from jax.experimental import pallas as pl
from jax.experimental.pallas import tpu as pltpu
from jax.sharding import PartitionSpec as P

FLAG_GROUPS = 8
OUTER = 4


def row_weights(counts, mask):
    ends = jnp.cumsum(counts)
    starts = ends - counts
    index = lax.broadcasted_iota(jnp.int32, (mask.shape[0], counts.shape[0]), 0)
    inside = (index >= starts[None, :]) & (index < ends[None, :])
    count_row = jnp.sum(jnp.where(inside, counts[None, :], 0), axis=1)
    live = (count_row > 0) & (mask == 1)
    return jnp.where(live, 1.0 / jnp.maximum(count_row, 1).astype(jnp.float32), 0.0)


def project_bias(task_bias, flags):
    local_width = task_bias.shape[2]
    channel = lax.axis_index("mp") * local_width + lax.broadcasted_iota(
        jnp.int32, (local_width, FLAG_GROUPS), 0
    )
    member = (
        channel % FLAG_GROUPS == lax.broadcasted_iota(jnp.int32, (local_width, FLAG_GROUPS), 1)
    ).astype(jnp.float32)
    dots = jnp.dot(task_bias[0] * task_bias[1], member, precision=lax.Precision.HIGHEST)
    norms = jnp.einsum(
        "stc,cg->stg", task_bias * task_bias, member, precision=lax.Precision.HIGHEST
    )
    dots, norms = lax.psum((dots, norms), "mp")
    flag = flags.astype(jnp.float32)
    coef_first = jnp.dot(
        flag[0] * dots / (norms[1] + 1e-06), member.T, precision=lax.Precision.HIGHEST
    )
    coef_second = jnp.dot(
        flag[1] * dots / (norms[0] + 1e-06), member.T, precision=lax.Precision.HIGHEST
    )
    first = task_bias[0] - coef_first * task_bias[1]
    second = task_bias[1] - coef_second * task_bias[0]
    return first + second


def generic_plan(mesh):
    n_mp = mesh.shape["mp"]
    n_batch = mesh.shape["batch"]
    inner = n_mp // OUTER
    inner_groups = [[o * inner + i for i in range(inner)] for o in range(OUTER)]
    outer_groups = [[o * inner + i for o in range(OUTER)] for i in range(inner)]

    def per_device(features, weights, bias, stitch, cotangent, crop_counts, row_mask, flags):
        rows = features.shape[1]
        width = weights.shape[2]
        depth = features.shape[2] * inner
        held = lax.all_gather(
            features, "mp", axis=2, tiled=True, axis_index_groups=inner_groups
        )
        split = weights.reshape(2, OUTER, depth, width)
        block = lax.all_to_all(
            split, "mp", split_axis=1, concat_axis=1, axis_index_groups=outer_groups
        )
        block = block.reshape(2, OUTER, depth, width)
        part = jnp.einsum("trk,tokc->otrc", held, block, preferred_element_type=jnp.float32)
        linear = lax.psum_scatter(
            part.astype(jnp.bfloat16),
            "mp",
            scatter_dimension=0,
            axis_index_groups=outer_groups,
        ).astype(jnp.float32)
        pre = linear + bias[:, None, :]
        hidden, gelu_back = jax.vjp(lambda v: jax.nn.gelu(v, approximate=False), pre)
        mixed = stitch[:, 0, None, :] * hidden[0][None] + stitch[:, 1, None, :] * hidden[1][None]
        scale_rows = row_weights(crop_counts, row_mask)
        grad_out = cotangent.astype(jnp.float32) * scale_rows[None, :, None]
        first_task = gelu_back(stitch[0][:, None, :] * grad_out[0][None])[0]
        second_task = gelu_back(stitch[1][:, None, :] * grad_out[1][None])[0]
        task_bias = jnp.stack([jnp.sum(first_task, axis=1), jnp.sum(second_task, axis=1)])
        grad_linear = (first_task + second_task).astype(jnp.bfloat16)
        grad_stitch = jnp.sum(grad_out[:, None] * hidden[None], axis=2)
        every = lax.all_gather(grad_linear, "mp", axis_index_groups=outer_groups)
        grad_part = jnp.einsum(
            "otrc,tokc->trk", every, block, preferred_element_type=jnp.float32
        )
        grad_part = grad_part.astype(jnp.bfloat16).reshape(2, rows, inner, depth // inner)
        grad_features = lax.psum_scatter(
            grad_part.transpose(2, 0, 1, 3),
            "mp",
            scatter_dimension=0,
            axis_index_groups=inner_groups,
        )
        weight_part = jnp.einsum(
            "trk,otrc->otkc", held, every, preferred_element_type=jnp.float32
        )
        weight_part = weight_part.astype(jnp.bfloat16).reshape(
            OUTER, 2, n_batch, depth // n_batch, width
        )
        share = lax.psum_scatter(
            weight_part.transpose(2, 0, 1, 3, 4), "batch", scatter_dimension=0
        )
        share = lax.all_to_all(
            share, "mp", split_axis=0, concat_axis=0, axis_index_groups=outer_groups
        )
        share = share.reshape(OUTER, 2, depth // n_batch, width)
        whole = lax.all_gather(share, "batch")
        grad_weights = whole.transpose(2, 1, 0, 3, 4).reshape(2, OUTER * depth, width)
        task_bias, grad_stitch = lax.psum((task_bias, grad_stitch), "batch")
        grad_bias = project_bias(task_bias, flags)
        return (
            mixed.astype(jnp.bfloat16),
            grad_features.astype(jnp.bfloat16),
            grad_weights.astype(jnp.float32),
            grad_bias,
            grad_stitch,
        )

    return per_device


MESH = pl.DeviceIdType.MESH
BF16 = jnp.bfloat16
F32 = jnp.float32
ZED = 4
HALVES = 2
PHASES = 4
RING = 8
BAND = 32


def half(value):
    return value.astype(BF16)


def wide(value):
    return value.astype(F32)


def fused_kernel(
    rows, deep, width, chunk,
    feat, wts, cot, bias, stitch, scale, flag_lanes,
    mixed, gfeat, gwt, gbias, gstitch, xn, dxn,
    wv, gl, rs, h0, xc, pf, cc, mx, own, dsend, dfetch, dout,
    xsrc, xt, cstage, cland, xstage, xland, kept, zstage,
    stat, sums, sums_land, prods, prods_land,
    rs_send, rs_recv, ag_send, ag_recv, xs_send, xs_recv,
    wz_send, wz_recv, wx_send, wx_recv, wc_send, wc_recv, wl,
    xf, cf, mxs, dx_send, dx_recv, df, dod,
    tile_in, c_send, c_recv, x_send, x_recv, z_send, z_recv, zl,
    ax_send, ax_recv, ac_send, ac_recv, t_send, t_recv,
):
    batch, mp = lax.axis_index("batch"), lax.axis_index("mp")
    z, y = mp // 2, mp % 2
    x, c = batch // 2, batch % 2
    up = {"mp": mp + 2}
    down = {"mp": mp - 2}
    across_y = {"mp": 2 * z + 1 - y}
    across_x = {"batch": 2 * (1 - x) + c}
    across_c = {"batch": 2 * x + 1 - c}

    def at_z(other):
        return {"mp": 2 * other + y}

    others = (3 - z, (z + 2) % 4, z + 1 - 2 * (z % 2))

    n_chunk = rows // chunk
    total = PHASES * n_chunk
    hw = width // HALVES
    kz = 2 * deep
    quarter = deep // 2
    tile = deep // 3
    xw = hw // 2
    cat = ZED * hw

    def mult(value, unit):
        return pl.multiple_of(value, unit)

    def remote(src, dst, send, recv, device):
        return pltpu.make_async_remote_copy(
            src_ref=src, dst_ref=dst, send_sem=send, recv_sem=recv,
            device_id=device, device_id_type=MESH,
        )

    def cols(b):
        return pl.ds(mult(b * hw, hw), hw)

    def chunk_rows(i):
        return pl.ds(mult(i * chunk, chunk), chunk)

    def x_copy(e):
        t, i = e // n_chunk, e % n_chunk
        return remote(
            feat.at[t, chunk_rows(i)], xn.at[t, chunk_rows(i)],
            xs_send.at[e], xs_recv.at[e], across_y,
        )

    def x_fetch(k):
        p, i = k // n_chunk, k % n_chunk
        t, buf = p // HALVES, k % 2
        return (
            pltpu.make_async_copy(
                feat.at[t, chunk_rows(i)],
                xc.at[buf, :, pl.ds(mult(deep * y, deep), deep)], xf.at[buf, 0],
            ),
            pltpu.make_async_copy(
                xn.at[t, chunk_rows(i)],
                xc.at[buf, :, pl.ds(mult(deep * (1 - y), deep), deep)], xf.at[buf, 1],
            ),
        )

    def cot_fetch(k):
        p, i = k // n_chunk, k % n_chunk
        return pltpu.make_async_copy(
            cot.at[:, chunk_rows(i), cols(p % HALVES)], cc.at[k % 2], cf.at[k % 2]
        )

    def w_own(p):
        return pltpu.make_async_copy(
            wts.at[p // HALVES, pl.ds(mult(kz * z, kz), kz), cols(p % HALVES)],
            wv.at[p, :, cols(z)], wl.at[p],
        )

    def w_rows():
        return pl.ds(mult(deep * c + quarter * x, quarter), quarter)

    def w_z(p, to):
        return remote(
            wts.at[
                p // HALVES,
                pl.ds(mult(kz * to + deep * c + quarter * x, quarter), quarter),
                cols(p % HALVES),
            ],
            wv.at[p, w_rows(), cols(z)],
            wz_send.at[p, to], wz_recv.at[p, z], at_z(to),
        )

    def w_z_in(p, frm):
        here = wv.at[p, w_rows(), cols(frm)]
        return remote(here, here, wz_send.at[p, frm], wz_recv.at[p, frm], at_z(frm))

    def w_x(p, b):
        here = wv.at[p, w_rows(), cols(b)]
        return remote(here, here, wx_send.at[p, b], wx_recv.at[p, b], across_x)

    def w_x_in(p, b):
        here = wv.at[
            p, pl.ds(mult(deep * c + quarter * (1 - x), quarter), quarter), cols(b)
        ]
        return remote(here, here, wx_send.at[p, b], wx_recv.at[p, b], across_x)

    def w_c(p, b):
        here = wv.at[p, pl.ds(mult(deep * c, deep), deep), cols(b)]
        return remote(here, here, wc_send.at[p, b], wc_recv.at[p, b], across_c)

    def w_c_in(p, b):
        here = wv.at[p, pl.ds(mult(deep * (1 - c), deep), deep), cols(b)]
        return remote(here, here, wc_send.at[p, b], wc_recv.at[p, b], across_c)

    def rs_up(k, b):
        slot = k % RING
        return remote(
            rs.at[slot, b], rs.at[slot, b], rs_send.at[slot, b], rs_recv.at[slot, b], up
        )

    def rs_down(k, b):
        slot = k % RING
        to = jnp.where(b == z - 1, ZED, b)
        return remote(
            rs.at[slot, b], rs.at[slot, to], rs_send.at[slot, b], rs_recv.at[slot, to], down
        )

    def rs_in(k, place, device):
        slot = k % RING
        return remote(
            rs.at[slot, place], rs.at[slot, place],
            rs_send.at[slot, place % ZED], rs_recv.at[slot, place], device,
        )

    def ag(k, b, going, device):
        p, i, slot = k // n_chunk, k % n_chunk, k % RING
        here = gl.at[p, chunk_rows(i), cols(b)]
        return remote(
            here, here, ag_send.at[slot, going * ZED + b], ag_recv.at[slot, b], device
        )

    def dx_copy(e):
        t, i = e // n_chunk, e % n_chunk
        return remote(
            dsend.at[e % 2], dxn.at[t, chunk_rows(i)],
            dx_send.at[e % 2], dx_recv.at[e], across_y,
        )

    def dx_fetch(e):
        return pltpu.make_async_copy(
            dxn.at[e // n_chunk, chunk_rows(e % n_chunk)], dfetch, df.at[0]
        )

    def dx_out(e):
        return pltpu.make_async_copy(
            dout, gfeat.at[e // n_chunk, chunk_rows(e % n_chunk)], dod.at[0]
        )

    def mixed_out(e):
        return pltpu.make_async_copy(
            mx.at[e % 2],
            mixed.at[:, chunk_rows(e % n_chunk), cols(e // n_chunk)], mxs.at[e % 2],
        )

    def tile_fetch(g, hk, start):
        t, j = g // (3 * HALVES), g % 3
        lanes = pl.ds(mult(tile * j, tile), tile)
        near = pltpu.make_async_copy(feat.at[t, :, lanes], xsrc, tile_in.at[0])
        if not start:
            near.wait()
            return

        @pl.when(hk == y)
        def _():
            near.start()

        @pl.when(hk != y)
        def _():
            pltpu.make_async_copy(xn.at[t, :, lanes], xsrc, tile_in.at[0]).start()

    def core_copy(g):
        return remote(cstage, cland.at[g % 2], c_send.at[0], c_recv.at[g % 2], across_c)

    def across_copy(g):
        return remote(xstage, xland.at[g % 2], x_send.at[0], x_recv.at[g % 2], across_x)

    def piece(g, source, lanes, n_lanes):
        p, j = g // 3, g % 3
        return gwt.at[
            p // HALVES, source,
            pl.ds(mult(deep * c + tile * j, tile), tile),
            pl.ds(mult(hw * (p % HALVES) + lanes, xw), n_lanes),
        ]

    def z_copy(g, to):
        return remote(
            zstage.at[g % 2, to], piece(g, z, xw * x, xw),
            z_send.at[g % 2, to], z_recv.at[g, z], at_z(to),
        )

    def z_in(g, frm):
        here = piece(g, frm, xw * x, xw)
        return remote(here, here, z_send.at[g % 2, frm], z_recv.at[g, frm], at_z(frm))

    def z_own(g):
        return pltpu.make_async_copy(
            zstage.at[g % 2, z], piece(g, z, xw * x, xw), zl.at[g % 2]
        )

    def spread(g, cc_, lanes, n_lanes):
        p, j = g // 3, g % 3
        return gwt.at[
            p // HALVES, :,
            pl.ds(mult(deep * cc_ + tile * j, tile), tile),
            pl.ds(mult(hw * (p % HALVES) + lanes, xw), n_lanes),
        ]

    def ax_copy(g):
        here = spread(g, c, xw * x, xw)
        return remote(here, here, ax_send.at[g], ax_recv.at[g], across_x)

    def ax_in(g):
        here = spread(g, c, xw * (1 - x), xw)
        return remote(here, here, ax_send.at[g], ax_recv.at[g], across_x)

    def ac_copy(g):
        here = spread(g, c, 0, hw)
        return remote(here, here, ac_send.at[g], ac_recv.at[g], across_c)

    def ac_in(g):
        here = spread(g, 1 - c, 0, hw)
        return remote(here, here, ac_send.at[g], ac_recv.at[g], across_c)

    def sum_copy(stage, device):
        return remote(
            sums.at[stage], sums_land.at[stage], t_send.at[stage], t_recv.at[stage], device
        )

    def prod_y():
        return remote(prods.at[0], prods_land.at[ZED], t_send.at[2], t_recv.at[2], across_y)

    def prod_z(to):
        return remote(
            prods.at[1], prods_land.at[z], t_send.at[3 + to], t_recv.at[3 + z], at_z(to)
        )

    def prod_z_in(frm):
        here = prods_land.at[frm]
        return remote(here, here, t_send.at[3 + frm], t_recv.at[3 + frm], at_z(frm))

    barrier = pltpu.get_barrier_semaphore()
    for device in [at_z(o) for o in others] + [across_y, across_x, across_c]:
        pl.semaphore_signal(barrier, inc=1, device_id=device, device_id_type=MESH)
    pl.semaphore_wait(barrier, 6)

    for to in others:
        w_z(0, to).start()
    x_copy(0).start()
    x_copy(1).start()
    w_own(0).start()
    cot_fetch(0).start()
    for frm in others:
        w_z_in(0, frm).wait_recv()
        w_x(0, frm).start()
    for to in others:
        w_z(1, to).start()
    w_own(1).start()
    for frm in others:
        w_x_in(0, frm).wait_recv()
        w_c(0, frm).start()
    x_copy(0).wait_recv()
    for copy in x_fetch(0):
        copy.start()

    def multiply_tile(into):
        pass

    def final(k):
        p, i, slot = k // n_chunk, k % n_chunk, k % RING
        t, h = p // HALVES, p % HALVES
        cot_fetch(k).wait()

        @pl.when(z > 0)
        def _():
            rs_in(k, z, down).wait_recv()

        @pl.when(z < ZED - 1)
        def _():
            rs_in(k, ZED, up).wait_recv()

        @pl.when((t == 1) & (k >= 2 * n_chunk + 2))
        def _():
            mixed_out(k - 2 * n_chunk - 2).wait()

        @pl.when(i == 0)
        def _():
            stat[p] = jnp.zeros(stat.shape[1:], F32)

        lanes = cols(h)
        shift = bias[pl.ds(t, 1), lanes]
        st = [stitch[pl.ds(s * 2 + t, 1), lanes] for s in range(2)]
        low = jnp.where(z > 0, 1.0, 0.0).astype(F32)
        high = jnp.where(z < ZED - 1, 1.0, 0.0).astype(F32)
        band = min(BAND, chunk)

        def step(r, carry):
            here = pl.ds(mult(r * band, band), band)
            there = pl.ds(mult(i * chunk + r * band, band), band)
            value = pf[k % 4, z, here, :]
            below = wide(rs[slot, z, here, :])
            above = wide(rs[slot, ZED, here, :])
            value = value + jnp.where(low > 0, below, 0.0) + jnp.where(high > 0, above, 0.0)
            pre = value + shift
            phi = 0.5 * (1.0 + lax.erf(pre * 0.7071067811865476))
            hidden = pre * phi
            slope = phi + pre * (jnp.exp(-0.5 * pre * pre) * 0.3989422804014327)
            weight = scale[there, 0:1]
            first = wide(cc[k % 2, 0, here, :]) * weight
            second = wide(cc[k % 2, 1, here, :]) * weight
            back0 = st[0] * first * slope
            back1 = st[1] * second * slope
            gl[p, there, cols(z)] = half(back0 + back1)

            def fold(v):
                return jnp.sum(v.reshape(band // 8, 8, hw), axis=0)

            stat[p, 0] += fold(back0)
            stat[p, 1] += fold(back1)
            stat[p, 2] += fold(first * hidden)
            stat[p, 3] += fold(second * hidden)

            @pl.when(t == 0)
            def _():
                h0[h, there, :] = hidden

            @pl.when(t == 1)
            def _():
                before = h0[h, there, :]
                for s in range(2):
                    mx[k % 2, s, here, :] = half(
                        stitch[pl.ds(s * 2, 1), lanes] * before + st[s] * hidden
                    )

            return carry

        lax.fori_loop(0, chunk // band, step, 0)

        @pl.when(z < ZED - 1)
        def _():
            ag(k, z, 0, up).start()

        @pl.when(z > 0)
        def _():
            ag(k, z, 1, down).start()

        @pl.when(t == 1)
        def _():
            mixed_out(k - 2 * n_chunk).start()

        @pl.when(k + 1 < total)
        def _():
            cot_fetch(k + 1).start()

    def forward_ag(k, far):
        @pl.when((k >= 0) & (k < total))
        def _():
            @pl.when(z - far >= 0)
            def _():
                ag(k, z - far, 0, up).wait_recv()

                @pl.when(z < ZED - 1)
                def _():
                    ag(k, z - far, 0, up).start()

            @pl.when(z + far < ZED)
            def _():
                ag(k, z + far, 1, down).wait_recv()

                @pl.when(z > 0)
                def _():
                    ag(k, z + far, 1, down).start()

    def dx_part(e, j, hk):
        t, i = e // n_chunk, e % n_chunk
        there = chunk_rows(i)
        krows = pl.ds(mult(deep * hk + tile * j, tile), tile)
        acc = None
        for h in range(HALVES):
            part = lax.dot_general(
                gl[2 * t + h, there, :], wv[2 * t + h, krows, :],
                (((1,), (1,)), ((), ())), preferred_element_type=F32,
            )
            acc = part if acc is None else acc + part
        return acc

    def dx_step(e):
        @pl.when(e >= 2)
        def _():
            dx_copy(e - 2).wait_send()

        def far(j, carry):
            dsend[e % 2, :, pl.ds(mult(tile * j, tile), tile)] = half(dx_part(e, j, 1 - y))
            return carry

        lax.fori_loop(0, 3, far, 0)
        dx_copy(e).start()

        def near(j, carry):
            own[e % 2, :, pl.ds(mult(tile * j, tile), tile)] = dx_part(e, j, y)
            return carry

        lax.fori_loop(0, 3, near, 0)

    def turn(hk_unused):
        wide_lane = min(128, tile)

        def step(q, carry):
            lanes = pl.ds(mult(q * wide_lane, wide_lane), wide_lane)
            xt[lanes, :] = xsrc[:, lanes].T
            return carry

        lax.fori_loop(0, tile // wide_lane, step, 0)

    def tile_dot(g, b):
        return jnp.dot(xt[...], gl[g // 3, :, cols(b)], preferred_element_type=F32)

    def stage_one(g):
        tile_fetch(g, 1 - c, False)
        turn(0)
        tile_fetch(g, c, True)

        def step(b, carry):
            cstage[:, cols(b)] = half(tile_dot(g, b))
            return carry

        lax.fori_loop(0, ZED, step, 0)
        core_copy(g).start()

    def stage_two(g):
        tile_fetch(g, c, False)
        turn(0)

        @pl.when(g % 3 < 2)
        def _():
            tile_fetch(g + 1, 1 - c, True)

        core_copy(g).wait()

        def step(b, carry):
            block = tile_dot(g, b) + wide(cland[g % 2, :, cols(b)])
            left, right = block[:, :xw], block[:, xw:]
            kept[b] = jnp.where(x == 0, left, right)
            xstage[b] = half(jnp.where(x == 0, right, left))
            return carry

        lax.fori_loop(0, ZED, step, 0)
        across_copy(g).start()

    def stage_three(g):
        across_copy(g).wait()

        @pl.when(g >= 2)
        def _():
            for to in others:
                z_copy(g - 2, to).wait_send()

        def step(b, carry):
            zstage[g % 2, b] = half(kept[b] + wide(xland[g % 2, b]))
            return carry

        lax.fori_loop(0, ZED, step, 0)
        for to in others:
            z_copy(g, to).start()
        z_own(g).start()

    def stage_four(g):
        z_own(g).wait()
        for frm in others:
            z_in(g, frm).wait_recv()
        ax_copy(g).start()

    def stage_five(g):
        ax_in(g).wait_recv()
        ac_copy(g).start()

    def stage_six(g):
        ac_in(g).wait_recv()

    def tiles_at(k, late, do):
        s = k - late - 2 * n_chunk
        p, j = (s + n_chunk) // n_chunk - 1, (s + n_chunk) % n_chunk

        @pl.when((s >= 0) & (p < PHASES) & (j < 3))
        def _():
            do(3 * p + j)

    def body(k, carry):
        @pl.when((k >= 5) & (k < total + 5))
        def _():
            def step(b, inner):
                @pl.when(b < z)
                def _():
                    rs_down(k - 5, b).wait_send()

                @pl.when(b > z)
                def _():
                    rs_up(k - 5, b).wait_send()

                return inner

            lax.fori_loop(0, ZED, step, 0)

        @pl.when((k >= 8) & (k < total + 8))
        def _():
            def step(b, inner):
                @pl.when((z < ZED - 1) & (b <= z))
                def _():
                    ag(k - 8, b, 0, up).wait_send()

                @pl.when((z > 0) & (b >= z))
                def _():
                    ag(k - 8, b, 1, down).wait_send()

                return inner

            lax.fori_loop(0, ZED, step, 0)

        @pl.when(k < total)
        def _():
            p, i = k // n_chunk, k % n_chunk

            @pl.when(i == 0)
            def _():
                w_own(p).wait()
                for frm in others:
                    w_c_in(p, frm).wait_recv()

            for copy in x_fetch(k):
                copy.wait()

            def step(b, inner):
                pf[k % 4, b] = jnp.dot(
                    xc[k % 2], wv[p, :, cols(b)], preferred_element_type=F32
                )
                return inner

            lax.fori_loop(0, ZED, step, 0)

        ku = k - z

        @pl.when((ku >= 0) & (ku < total) & (z < ZED - 1))
        def _():
            slot = ku % RING

            def step(b, inner):
                @pl.when(z > 0)
                def _():
                    rs_in(ku, b, down).wait_recv()
                    rs[slot, b] = half(wide(rs[slot, b]) + pf[ku % 4, b])

                @pl.when(z == 0)
                def _():
                    rs[slot, b] = half(pf[ku % 4, b])

                rs_up(ku, b).start()
                return inner

            lax.fori_loop(z + 1, ZED, step, 0)

        kd = k - (ZED - 1 - z)

        @pl.when((kd >= 0) & (kd < total) & (z > 0))
        def _():
            slot = kd % RING

            def step(b, inner):
                @pl.when(z < ZED - 1)
                def _():
                    rs_in(kd, b, up).wait_recv()
                    rs[slot, b] = half(wide(rs[slot, b]) + pf[kd % 4, b])

                @pl.when(z == ZED - 1)
                def _():
                    rs[slot, b] = half(pf[kd % 4, b])

                rs_down(kd, b).start()
                return inner

            lax.fori_loop(0, z, step, 0)

        @pl.when(k + 2 < 2 * n_chunk)
        def _():
            x_copy(k + 2).start()

        @pl.when(k + 1 < total)
        def _():
            nxt = k + 1

            @pl.when((nxt // n_chunk) % HALVES == 0)
            def _():
                x_copy((nxt // n_chunk // HALVES) * n_chunk + nxt % n_chunk).wait_recv()

            for copy in x_fetch(nxt):
                copy.start()

        @pl.when((k >= 3) & (k < total + 3))
        def _():
            final(k - 3)

        forward_ag(k - 4, 1)
        forward_ag(k - 5, 2)
        forward_ag(k - 6, 3)

        for late, what in ((8, 0), (6, 1), (8, 2)):
            s = k - late
            t = s // (2 * n_chunk)
            i = s % (2 * n_chunk) - n_chunk

            @pl.when((s >= 0) & (s < total) & (i >= 0))
            def _(what=what, t=t, i=i):
                e = t * n_chunk + i
                if what == 0:
                    dx_copy(e).wait_recv()
                    dx_fetch(e).start()

                    @pl.when(e >= 1)
                    def _():
                        dx_out(e - 1).wait()

                    dx_fetch(e).wait()

                    def step(j, inner):
                        lanes = pl.ds(mult(tile * j, tile), tile)
                        dout[:, lanes] = half(own[e % 2, :, lanes] + wide(dfetch[:, lanes]))
                        return inner

                    lax.fori_loop(0, 3, step, 0)
                    dx_out(e).start()
                elif what == 1:
                    dx_step(e)

        tiles_at(k, 2, stage_three)
        tiles_at(k, 1, stage_two)
        tiles_at(k, 0, stage_one)
        tiles_at(k, 3, stage_four)
        tiles_at(k, 4, stage_five)
        tiles_at(k, 5, stage_six)

        @pl.when((k % n_chunk == n_chunk - 1) & (k >= 2 * n_chunk - 1) & (k < 6 * n_chunk - 1))
        def _():
            p = (k + 1) // n_chunk - 2
            tile_fetch(3 * p, 1 - c, True)

        p_next = k // n_chunk + 1

        @pl.when(p_next < PHASES)
        def _():
            @pl.when((k % n_chunk == 0) & (k > 0))
            def _():
                for to in others:
                    w_z(p_next, to).start()
                w_own(p_next).start()

            @pl.when(k % n_chunk == n_chunk // 3)
            def _():
                for frm in others:
                    w_z_in(p_next, frm).wait_recv()
                    w_x(p_next, frm).start()

            @pl.when(k % n_chunk == (2 * n_chunk) // 3)
            def _():
                for frm in others:
                    w_x_in(p_next, frm).wait_recv()
                    w_c(p_next, frm).start()

        @pl.when(k == total + 3)
        def _():
            for p in range(PHASES):
                t, h = p // HALVES, p % HALVES
                for s in range(2):
                    for what in range(2):
                        sums[0, pl.ds(4 * what + 2 * s + t, 1), h * hw : (h + 1) * hw] = jnp.sum(
                            stat[p, 2 * what + s], axis=0, keepdims=True
                        )
            sum_copy(0, across_c).start()

        @pl.when(k == total + 4)
        def _():
            sum_copy(0, across_c).wait()
            sums[1] = sums[0] + sums_land[0]
            sum_copy(1, across_x).start()

        lane = min(128, width)

        @pl.when(k == total + 5)
        def _():
            sum_copy(1, across_x).wait()
            both = sums[1] + sums_land[1]
            sums[2] = both
            member = (
                lax.broadcasted_iota(jnp.int32, (width, lane), 0) % FLAG_GROUPS
                == lax.broadcasted_iota(jnp.int32, (width, lane), 1) % FLAG_GROUPS
            ).astype(F32)
            bias_rows = both[0:4]
            inner = both[0:2] * both[2:4]
            stack = jnp.concatenate([inner, bias_rows * bias_rows, inner], axis=0)
            prods[0] = jnp.dot(
                stack, member, precision=lax.Precision.HIGHEST, preferred_element_type=F32
            )
            prod_y().start()

        @pl.when(k == total + 6)
        def _():
            prod_y().wait()
            prods[1] = prods[0] + prods_land[ZED]
            for to in others:
                prod_z(to).start()

        @pl.when(k == total + 7)
        def _():
            for frm in others:
                prod_z_in(frm).wait_recv()
            prods_land[z] = prods[1]
            whole = prods_land[0] + prods_land[1] + prods_land[2] + prods_land[3]
            both = sums[2]
            spread_out = [
                jnp.concatenate([whole[r : r + 1]] * (width // lane), axis=1) for r in range(6)
            ]
            flags_out = [
                jnp.concatenate([flag_lanes[r : r + 1]] * (width // lane), axis=1)
                for r in range(4)
            ]
            for t in range(2):
                task0, task1 = both[t : t + 1], both[2 + t : 3 + t]
                coef0 = flags_out[t] * spread_out[t] / (spread_out[4 + t] + 1e-06)
                coef1 = flags_out[2 + t] * spread_out[t] / (spread_out[2 + t] + 1e-06)
                gbias[t : t + 1] = (task0 - coef0 * task1) + (task1 - coef1 * task0)
            gstitch[...] = both[4:8]

        return carry

    lax.fori_loop(0, total + 2 * n_chunk + 2, body, 0)

    last = 3 * PHASES - 1
    for g in (last - 1, last):
        for to in others:
            z_copy(g, to).wait_send()
    for e in (2 * n_chunk - 2, 2 * n_chunk - 1):
        dx_copy(e).wait_send()
        mixed_out(e).wait()
    dx_out(2 * n_chunk - 1).wait()

    def drain_tiles(g, carry):
        ax_copy(g).wait_send()
        ac_copy(g).wait_send()
        return carry

    lax.fori_loop(0, last + 1, drain_tiles, 0)

    def drain_x(e, carry):
        x_copy(e).wait_send()
        return carry

    lax.fori_loop(0, 2 * n_chunk, drain_x, 0)

    def drain_w(p, carry):
        for to in others:
            w_z(p, to).wait_send()
            w_x(p, to).wait_send()
            w_c(p, to).wait_send()
        return carry

    lax.fori_loop(0, PHASES, drain_w, 0)
    for to in others:
        prod_z(to).wait_send()


def fused_call(feat, wts, cot, bias, stitch, scale, flag_lanes):
    rows, deep, width = feat.shape[1], feat.shape[2], wts.shape[2]
    chunk = rows // 6
    hw, kz, tile = width // 2, 2 * deep, deep // 3
    cat, xw = 4 * hw, width // 4
    lane = min(128, width)
    dma = pltpu.SemaphoreType.DMA
    anywhere = pl.BlockSpec(memory_space=pl.ANY)
    inside = pl.BlockSpec(memory_space=pltpu.VMEM)

    def v(shape, kind=BF16):
        return pltpu.VMEM(shape, kind)

    out_shape = [
        jax.ShapeDtypeStruct((2, rows, width), BF16),
        jax.ShapeDtypeStruct((2, rows, deep), BF16),
        jax.ShapeDtypeStruct((2, ZED, kz, width), BF16),
        jax.ShapeDtypeStruct((2, width), F32),
        jax.ShapeDtypeStruct((4, width), F32),
        jax.ShapeDtypeStruct((2, rows, deep), BF16),
        jax.ShapeDtypeStruct((2, rows, deep), BF16),
    ]
    scratch = [
        v((PHASES, kz, cat)),
        v((PHASES, rows, cat)),
        v((RING, 5, chunk, hw)),
        v((2, rows, hw), F32),
        v((2, chunk, kz)),
        v((4, ZED, chunk, hw), F32),
        v((2, 2, chunk, hw)),
        v((2, 2, chunk, hw)),
        v((2, chunk, deep), F32),
        v((2, chunk, deep)),
        v((chunk, deep)),
        v((chunk, deep)),
        v((rows, tile)),
        v((tile, rows)),
        v((tile, cat)),
        v((2, tile, cat)),
        v((ZED, tile, xw)),
        v((2, ZED, tile, xw)),
        v((ZED, tile, xw), F32),
        v((2, ZED, tile, xw)),
        v((PHASES, 4, 8, hw), F32),
        v((3, 8, width), F32),
        v((2, 8, width), F32),
        v((2, 8, lane), F32),
        v((5, 8, lane), F32),
        dma((RING, 4)), dma((RING, 5)), dma((RING, 8)), dma((RING, 4)),
        dma((12,)), dma((12,)),
        dma((4, 4)), dma((4, 4)), dma((4, 4)), dma((4, 4)), dma((4, 4)), dma((4, 4)), dma((4,)),
        dma((2, 2)), dma((2,)), dma((2,)), dma((2,)), dma((12,)), dma((1,)), dma((1,)),
        dma((1,)), dma((1,)), dma((2,)), dma((1,)), dma((2,)), dma((2, 4)), dma((12, 4)), dma((2,)),
        dma((12,)), dma((12,)), dma((12,)), dma((12,)), dma((8,)), dma((8,)),
    ]
    flops = 3 * 2 * 2 * rows * kz * cat * 2
    return pl.pallas_call(
        functools.partial(fused_kernel, rows, deep, width, chunk),
        out_shape=out_shape,
        in_specs=[anywhere] * 3 + [inside] * 4,
        out_specs=[anywhere] * 3 + [inside] * 2 + [anywhere] * 2,
        scratch_shapes=scratch,
        compiler_params=pltpu.CompilerParams(
            collective_id=0, has_side_effects=True, vmem_limit_bytes=64 * 1024 * 1024
        ),
        cost_estimate=pl.CostEstimate(
            flops=flops, bytes_accessed=200_000_000, transcendentals=2 * rows * width * 2
        ),
        name="cross_stitch_step",
    )(feat, wts, cot, bias, stitch, scale, flag_lanes)


def fused_plan(mesh):
    def per_device(features, weights, bias, stitch, cotangent, crop_counts, row_mask, flags):
        rows, deep = features.shape[1:]
        width = weights.shape[2]
        lane = min(128, width)
        scale = jnp.broadcast_to(row_weights(crop_counts, row_mask)[:, None], (rows, lane))
        flag_lanes = jnp.tile(flags.astype(F32).reshape(4, FLAG_GROUPS), (1, lane // FLAG_GROUPS))
        mixed, gfeat, gwt, gbias, gstitch, _, _ = fused_call(
            features, weights, cotangent, bias, stitch.reshape(4, width), scale, flag_lanes
        )
        return (
            mixed,
            gfeat,
            gwt.reshape(2, ZED * 2 * deep, width).astype(F32),
            gbias,
            gstitch.reshape(2, 2, width),
        )

    return per_device


def plan_for(mesh):
    if mesh.shape["batch"] == 4 and mesh.shape["mp"] == 2 * ZED:
        return fused_plan(mesh)
    return generic_plan(mesh)


def solution(mesh):
    in_specs = (
        P(None, "batch", "mp"),
        P(None, None, "mp"),
        P(None, "mp"),
        P(None, None, "mp"),
        P(None, "batch", "mp"),
        P("batch"),
        P("batch"),
        P(),
    )
    out_specs = (
        P(None, "batch", "mp"),
        P(None, "batch", "mp"),
        P(None, None, "mp"),
        P(None, "mp"),
        P(None, None, "mp"),
    )
    return jax.shard_map(
        plan_for(mesh), mesh=mesh, in_specs=in_specs, out_specs=out_specs, check_vma=False
    )
```

```python
import functools

import jax
import jax.numpy as jnp
from jax import lax
from jax.experimental import pallas as pl
from jax.experimental.pallas import tpu as pltpu
from jax.sharding import PartitionSpec as P

FLAG_GROUPS = 8
OUTER = 4


def row_weights(counts, mask):
    ends = jnp.cumsum(counts)
    starts = ends - counts
    index = lax.broadcasted_iota(jnp.int32, (mask.shape[0], counts.shape[0]), 0)
    inside = (index >= starts[None, :]) & (index < ends[None, :])
    count_row = jnp.sum(jnp.where(inside, counts[None, :], 0), axis=1)
    live = (count_row > 0) & (mask == 1)
    return jnp.where(live, 1.0 / jnp.maximum(count_row, 1).astype(jnp.float32), 0.0)


def project_bias(task_bias, flags):
    local_width = task_bias.shape[2]
    channel = lax.axis_index("mp") * local_width + lax.broadcasted_iota(
        jnp.int32, (local_width, FLAG_GROUPS), 0
    )
    member = (
        channel % FLAG_GROUPS == lax.broadcasted_iota(jnp.int32, (local_width, FLAG_GROUPS), 1)
    ).astype(jnp.float32)
    dots = jnp.dot(task_bias[0] * task_bias[1], member, precision=lax.Precision.HIGHEST)
    norms = jnp.einsum(
        "stc,cg->stg", task_bias * task_bias, member, precision=lax.Precision.HIGHEST
    )
    dots, norms = lax.psum((dots, norms), "mp")
    flag = flags.astype(jnp.float32)
    coef_first = jnp.dot(
        flag[0] * dots / (norms[1] + 1e-06), member.T, precision=lax.Precision.HIGHEST
    )
    coef_second = jnp.dot(
        flag[1] * dots / (norms[0] + 1e-06), member.T, precision=lax.Precision.HIGHEST
    )
    first = task_bias[0] - coef_first * task_bias[1]
    second = task_bias[1] - coef_second * task_bias[0]
    return first + second


def generic_plan(mesh):
    n_mp = mesh.shape["mp"]
    n_batch = mesh.shape["batch"]
    inner = n_mp // OUTER
    inner_groups = [[o * inner + i for i in range(inner)] for o in range(OUTER)]
    outer_groups = [[o * inner + i for o in range(OUTER)] for i in range(inner)]

    def per_device(features, weights, bias, stitch, cotangent, crop_counts, row_mask, flags):
        rows = features.shape[1]
        width = weights.shape[2]
        depth = features.shape[2] * inner
        held = lax.all_gather(
            features, "mp", axis=2, tiled=True, axis_index_groups=inner_groups
        )
        split = weights.reshape(2, OUTER, depth, width)
        block = lax.all_to_all(
            split, "mp", split_axis=1, concat_axis=1, axis_index_groups=outer_groups
        )
        block = block.reshape(2, OUTER, depth, width)
        part = jnp.einsum("trk,tokc->otrc", held, block, preferred_element_type=jnp.float32)
        linear = lax.psum_scatter(
            part.astype(jnp.bfloat16),
            "mp",
            scatter_dimension=0,
            axis_index_groups=outer_groups,
        ).astype(jnp.float32)
        pre = linear + bias[:, None, :]
        hidden, gelu_back = jax.vjp(lambda v: jax.nn.gelu(v, approximate=False), pre)
        mixed = stitch[:, 0, None, :] * hidden[0][None] + stitch[:, 1, None, :] * hidden[1][None]
        scale_rows = row_weights(crop_counts, row_mask)
        grad_out = cotangent.astype(jnp.float32) * scale_rows[None, :, None]
        first_task = gelu_back(stitch[0][:, None, :] * grad_out[0][None])[0]
        second_task = gelu_back(stitch[1][:, None, :] * grad_out[1][None])[0]
        task_bias = jnp.stack([jnp.sum(first_task, axis=1), jnp.sum(second_task, axis=1)])
        grad_linear = (first_task + second_task).astype(jnp.bfloat16)
        grad_stitch = jnp.sum(grad_out[:, None] * hidden[None], axis=2)
        every = lax.all_gather(grad_linear, "mp", axis_index_groups=outer_groups)
        grad_part = jnp.einsum(
            "otrc,tokc->trk", every, block, preferred_element_type=jnp.float32
        )
        grad_part = grad_part.astype(jnp.bfloat16).reshape(2, rows, inner, depth // inner)
        grad_features = lax.psum_scatter(
            grad_part.transpose(2, 0, 1, 3),
            "mp",
            scatter_dimension=0,
            axis_index_groups=inner_groups,
        )
        weight_part = jnp.einsum(
            "trk,otrc->otkc", held, every, preferred_element_type=jnp.float32
        )
        weight_part = weight_part.astype(jnp.bfloat16).reshape(
            OUTER, 2, n_batch, depth // n_batch, width
        )
        share = lax.psum_scatter(
            weight_part.transpose(2, 0, 1, 3, 4), "batch", scatter_dimension=0
        )
        share = lax.all_to_all(
            share, "mp", split_axis=0, concat_axis=0, axis_index_groups=outer_groups
        )
        share = share.reshape(OUTER, 2, depth // n_batch, width)
        whole = lax.all_gather(share, "batch")
        grad_weights = whole.transpose(2, 1, 0, 3, 4).reshape(2, OUTER * depth, width)
        task_bias, grad_stitch = lax.psum((task_bias, grad_stitch), "batch")
        grad_bias = project_bias(task_bias, flags)
        return (
            mixed.astype(jnp.bfloat16),
            grad_features.astype(jnp.bfloat16),
            grad_weights.astype(jnp.float32),
            grad_bias,
            grad_stitch,
        )

    return per_device


MESH = pl.DeviceIdType.MESH
BF16 = jnp.bfloat16
F32 = jnp.float32
ZED = 4
HALVES = 2
PHASES = 4
RING = 8
BAND = 32
SUB = 2
PRODUCTS = 6


def half(value):
    return value.astype(BF16)


def wide(value):
    return value.astype(F32)


def fused_kernel(
    rows, deep, width, chunk,
    feat, wts, cot, bias, stitch, counts, mask, flags,
    mixed, gfeat, gwt, gbias, gstitch, xn, dxn,
    wv, gl, rs, h0, xc, pf, cc, mx, own, dsend, dfetch, dout,
    xsrc, xt, cstage, cland, xstage, xland, kept, zstage,
    scale, stat, sums, sums_land, prods, prods_land,
    rs_send, rs_recv, ag_send, ag_recv, xs_send, xs_recv,
    wz_send, wz_recv, wx_send, wx_recv, wc_send, wc_recv, wl,
    xf, cf, mxs, dx_send, dx_recv, df, dod,
    tile_in, c_send, c_recv, x_send, x_recv, z_send, z_recv, zl,
    ax_send, ax_recv, ac_send, ac_recv, t_send, t_recv,
):
    batch, mp = lax.axis_index("batch"), lax.axis_index("mp")
    z, y = mp // 2, mp % 2
    x, c = batch // 2, batch % 2
    up = {"mp": mp + 2}
    down = {"mp": mp - 2}
    across_y = {"mp": 2 * z + 1 - y}
    across_x = {"batch": 2 * (1 - x) + c}
    across_c = {"batch": 2 * x + 1 - c}

    def at_z(other):
        return {"mp": 2 * other + y}

    others = (3 - z, (z + 2) % 4, z + 1 - 2 * (z % 2))

    n_chunk = rows // chunk
    total = PHASES * n_chunk
    part = chunk // SUB
    n_part = rows // part
    parts = PHASES * n_part
    images = counts.shape[1]
    hw = width // HALVES
    kz = 2 * deep
    quarter = deep // 2
    tile = deep // 3
    xw = hw // 2

    def mult(value, unit):
        return pl.multiple_of(value, unit)

    def remote(src, dst, send, recv, device):
        return pltpu.make_async_remote_copy(
            src_ref=src, dst_ref=dst, send_sem=send, recv_sem=recv,
            device_id=device, device_id_type=MESH,
        )

    def cols(b):
        return pl.ds(mult(b * hw, hw), hw)

    def chunk_rows(i):
        return pl.ds(mult(i * chunk, chunk), chunk)

    def part_rows(i):
        return pl.ds(mult(i * part, part), part)

    def x_copy(e):
        t, i = e // n_chunk, e % n_chunk
        return remote(
            feat.at[t, chunk_rows(i)], xn.at[t, chunk_rows(i)],
            xs_send.at[e], xs_recv.at[e], across_y,
        )

    def x_fetch(k):
        p, i = k // n_chunk, k % n_chunk
        t, buf = p // HALVES, k % 2
        return (
            pltpu.make_async_copy(
                feat.at[t, chunk_rows(i)],
                xc.at[buf, :, pl.ds(mult(deep * y, deep), deep)], xf.at[buf, 0],
            ),
            pltpu.make_async_copy(
                xn.at[t, chunk_rows(i)],
                xc.at[buf, :, pl.ds(mult(deep * (1 - y), deep), deep)], xf.at[buf, 1],
            ),
        )

    def cot_fetch(u):
        p, i = u // n_part, u % n_part
        return pltpu.make_async_copy(
            cot.at[:, part_rows(i), cols(p % HALVES)], cc.at[u % 2], cf.at[u % 2]
        )

    def w_own(p):
        return pltpu.make_async_copy(
            wts.at[p // HALVES, pl.ds(mult(kz * z, kz), kz), cols(p % HALVES)],
            wv.at[p, :, cols(z)], wl.at[p],
        )

    def w_rows():
        return pl.ds(mult(deep * c + quarter * x, quarter), quarter)

    def w_z(p, to):
        return remote(
            wts.at[
                p // HALVES,
                pl.ds(mult(kz * to + deep * c + quarter * x, quarter), quarter),
                cols(p % HALVES),
            ],
            wv.at[p, w_rows(), cols(z)],
            wz_send.at[p, to], wz_recv.at[p, z], at_z(to),
        )

    def w_z_in(p, frm):
        here = wv.at[p, w_rows(), cols(frm)]
        return remote(here, here, wz_send.at[p, frm], wz_recv.at[p, frm], at_z(frm))

    def w_x(p, b):
        here = wv.at[p, w_rows(), cols(b)]
        return remote(here, here, wx_send.at[p, b], wx_recv.at[p, b], across_x)

    def w_x_in(p, b):
        here = wv.at[
            p, pl.ds(mult(deep * c + quarter * (1 - x), quarter), quarter), cols(b)
        ]
        return remote(here, here, wx_send.at[p, b], wx_recv.at[p, b], across_x)

    def w_c(p, b):
        here = wv.at[p, pl.ds(mult(deep * c, deep), deep), cols(b)]
        return remote(here, here, wc_send.at[p, b], wc_recv.at[p, b], across_c)

    def w_c_in(p, b):
        here = wv.at[p, pl.ds(mult(deep * (1 - c), deep), deep), cols(b)]
        return remote(here, here, wc_send.at[p, b], wc_recv.at[p, b], across_c)

    def rs_up(u, b):
        slot = u % RING
        return remote(
            rs.at[slot, b], rs.at[slot, b], rs_send.at[slot, b], rs_recv.at[slot, b], up
        )

    def rs_down(u, b):
        slot = u % RING
        to = jnp.where(b == z - 1, ZED, b)
        return remote(
            rs.at[slot, b], rs.at[slot, to], rs_send.at[slot, b], rs_recv.at[slot, to], down
        )

    def rs_in(u, place, device):
        slot = u % RING
        return remote(
            rs.at[slot, place], rs.at[slot, place],
            rs_send.at[slot, place % ZED], rs_recv.at[slot, place], device,
        )

    def ag(u, b, going, device):
        p, i, slot = u // n_part, u % n_part, u % RING
        here = gl.at[p, part_rows(i), cols(b)]
        return remote(
            here, here, ag_send.at[slot, going * ZED + b], ag_recv.at[slot, b], device
        )

    def dx_copy(e):
        t, i = e // n_chunk, e % n_chunk
        return remote(
            dsend.at[e % 2], dxn.at[t, chunk_rows(i)],
            dx_send.at[e % 2], dx_recv.at[e], across_y,
        )

    def dx_fetch(e):
        return pltpu.make_async_copy(
            dxn.at[e // n_chunk, chunk_rows(e % n_chunk)], dfetch, df.at[0]
        )

    def dx_out(e):
        return pltpu.make_async_copy(
            dout, gfeat.at[e // n_chunk, chunk_rows(e % n_chunk)], dod.at[0]
        )

    def mixed_out(e):
        return pltpu.make_async_copy(
            mx.at[e % 2],
            mixed.at[:, part_rows(e % n_part), cols(e // n_part)], mxs.at[e % 2],
        )

    def tile_fetch(g, hk, start):
        t, j = g // (3 * HALVES), g % 3
        lanes = pl.ds(mult(tile * j, tile), tile)
        near = pltpu.make_async_copy(feat.at[t, :, lanes], xsrc, tile_in.at[0])
        if not start:
            near.wait()
            return

        @pl.when(hk == y)
        def _():
            near.start()

        @pl.when(hk != y)
        def _():
            pltpu.make_async_copy(xn.at[t, :, lanes], xsrc, tile_in.at[0]).start()

    def core_copy(g):
        return remote(cstage, cland.at[g % 2], c_send.at[0], c_recv.at[g % 2], across_c)

    def across_copy(g, b):
        return remote(
            xstage.at[b], xland.at[g % 2, b], x_send.at[b], x_recv.at[g % 2, b], across_x
        )

    def piece(g, source, core, lanes, n_lanes):
        p, j = g // 3, g % 3
        return gwt.at[
            p // HALVES, source,
            pl.ds(mult(deep * core + tile * j, tile), tile),
            pl.ds(mult(hw * (p % HALVES) + lanes, xw), n_lanes),
        ]

    def z_copy(g, to):
        return remote(
            zstage.at[g % 2, to], piece(g, z, c, xw * x, xw),
            z_send.at[g % 2, to], z_recv.at[g, z], at_z(to),
        )

    def z_in(g, frm):
        here = piece(g, frm, c, xw * x, xw)
        return remote(here, here, z_send.at[g % 2, frm], z_recv.at[g, frm], at_z(frm))

    def z_own(g):
        return pltpu.make_async_copy(
            zstage.at[g % 2, z], piece(g, z, c, xw * x, xw), zl.at[g % 2]
        )

    def ax_own(g):
        return remote(
            zstage.at[g % 2, z], piece(g, z, c, xw * x, xw),
            ax_send.at[g, z], ax_recv.at[g, z], across_x,
        )

    def ax_copy(g, b):
        here = piece(g, b, c, xw * x, xw)
        return remote(here, here, ax_send.at[g, b], ax_recv.at[g, b], across_x)

    def ax_in(g, b):
        here = piece(g, b, c, xw * (1 - x), xw)
        return remote(here, here, ax_send.at[g, b], ax_recv.at[g, b], across_x)

    def ac_copy(g, b):
        here = piece(g, b, c, 0, hw)
        return remote(here, here, ac_send.at[g, b], ac_recv.at[g, b], across_c)

    def ac_in(g, b):
        here = piece(g, b, 1 - c, 0, hw)
        return remote(here, here, ac_send.at[g, b], ac_recv.at[g, b], across_c)

    def sum_copy(stage, device):
        return remote(
            sums.at[stage], sums_land.at[stage], t_send.at[stage], t_recv.at[stage], device
        )

    def prod_y():
        return remote(prods.at[0], prods_land.at[ZED], t_send.at[2], t_recv.at[2], across_y)

    def prod_z(to):
        return remote(
            prods.at[1], prods_land.at[z], t_send.at[3 + to], t_recv.at[3 + z], at_z(to)
        )

    def prod_z_in(frm):
        here = prods_land.at[frm]
        return remote(here, here, t_send.at[3 + frm], t_recv.at[3 + frm], at_z(frm))

    barrier = pltpu.get_barrier_semaphore()
    for device in [at_z(o) for o in others] + [across_y, across_x, across_c]:
        pl.semaphore_signal(barrier, inc=1, device_id=device, device_id_type=MESH)
    pl.semaphore_wait(barrier, 6)

    for to in others:
        w_z(0, to).start()
    x_copy(0).start()
    x_copy(1).start()
    w_own(0).start()
    cot_fetch(0).start()

    image_row = lax.broadcasted_iota(jnp.int32, (images, images), 0)
    image_col = lax.broadcasted_iota(jnp.int32, (images, images), 1)
    crops = counts[...].astype(F32)
    ends = jnp.dot(
        jnp.broadcast_to(crops, (8, images)), (image_row <= image_col).astype(F32),
        precision=lax.Precision.HIGHEST, preferred_element_type=F32,
    )[0:1]
    starts = ends - crops
    block = min(128, chunk)
    lane = scale.shape[1]

    for r in range(rows // block):
        index = (
            lax.broadcasted_iota(jnp.int32, (block, images), 0) + r * block
        ).astype(F32)
        inside = (index >= starts) & (index < ends)
        count_row = jnp.sum(jnp.where(inside, crops, 0.0), axis=1, keepdims=True)
        diagonal = lax.broadcasted_iota(jnp.int32, (block, block), 0) == (
            lax.broadcasted_iota(jnp.int32, (block, block), 1)
        )
        usable = jnp.sum(
            jnp.where(diagonal, mask[:, r * block : (r + 1) * block].astype(F32), 0.0),
            axis=1, keepdims=True,
        )
        live = (count_row > 0.0) & (usable == 1.0)
        share = jnp.where(live, 1.0 / jnp.maximum(count_row, 1.0), 0.0)
        scale[r * block : (r + 1) * block, :] = jnp.broadcast_to(share, (block, lane))

    for frm in others:
        w_z_in(0, frm).wait_recv()
        w_x(0, frm).start()
    for to in others:
        w_z(1, to).start()
    w_own(1).start()
    for frm in others:
        w_x_in(0, frm).wait_recv()
        w_c(0, frm).start()
    x_copy(0).wait_recv()
    for copy in x_fetch(0):
        copy.start()

    def final(u):
        p, i, slot = u // n_part, u % n_part, u % RING
        t, h = p // HALVES, p % HALVES
        cot_fetch(u).wait()

        @pl.when(z > 0)
        def _():
            rs_in(u, z, down).wait_recv()

        @pl.when(z < ZED - 1)
        def _():
            rs_in(u, ZED, up).wait_recv()

        @pl.when(u >= 2 * n_part + 2)
        def _():
            mixed_out(u - 2 * n_part - 2).wait()

        @pl.when(i == 0)
        def _():
            stat[p] = jnp.zeros(stat.shape[1:], F32)

        lanes = cols(h)
        shift = bias[pl.ds(t, 1), lanes]
        st = [stitch[s, pl.ds(t, 1), lanes] for s in range(2)]
        band = min(BAND, part)

        def step(r, carry):
            here = part_rows_of(r, band)
            there = pl.ds(mult(i * part + r * band, band), band)
            value = pf[u % PRODUCTS, z, here, :]
            below = wide(rs[slot, z, here, :])
            above = wide(rs[slot, ZED, here, :])
            value = value + jnp.where(z > 0, below, 0.0) + jnp.where(z < ZED - 1, above, 0.0)
            pre = value + shift
            phi = 0.5 * (1.0 + lax.erf(pre * 0.7071067811865476))
            hidden = pre * phi
            slope = phi + pre * (jnp.exp(-0.5 * pre * pre) * 0.3989422804014327)
            weight = scale[there, 0:1]
            first = wide(cc[u % 2, 0, here, :]) * weight
            second = wide(cc[u % 2, 1, here, :]) * weight
            back0 = st[0] * first * slope
            back1 = st[1] * second * slope
            gl[p, there, cols(z)] = half(back0 + back1)

            def fold(v):
                return jnp.sum(v.reshape(band // 8, 8, hw), axis=0)

            stat[p, 0] += fold(back0)
            stat[p, 1] += fold(back1)
            stat[p, 2] += fold(first * hidden)
            stat[p, 3] += fold(second * hidden)

            @pl.when(t == 0)
            def _():
                h0[h, there, :] = hidden

            @pl.when(t == 1)
            def _():
                before = h0[h, there, :]
                for s in range(2):
                    mx[u % 2, s, here, :] = half(
                        stitch[s, 0:1, lanes] * before + st[s] * hidden
                    )

            return carry

        lax.fori_loop(0, part // band, step, 0)

        @pl.when(z < ZED - 1)
        def _():
            ag(u, z, 0, up).start()

        @pl.when(z > 0)
        def _():
            ag(u, z, 1, down).start()

        @pl.when(t == 1)
        def _():
            mixed_out(u - 2 * n_part).start()

        @pl.when(u + 1 < parts)
        def _():
            cot_fetch(u + 1).start()

    def part_rows_of(r, band):
        return pl.ds(mult(r * band, band), band)

    def forward_ag(u, far):
        @pl.when((u >= 0) & (u < parts))
        def _():
            @pl.when(z - far >= 0)
            def _():
                ag(u, z - far, 0, up).wait_recv()

                @pl.when(z < ZED - 1)
                def _():
                    ag(u, z - far, 0, up).start()

            @pl.when(z + far < ZED)
            def _():
                ag(u, z + far, 1, down).wait_recv()

                @pl.when(z > 0)
                def _():
                    ag(u, z + far, 1, down).start()

    def dx_part(e, j, hk):
        t, i = e // n_chunk, e % n_chunk
        there = chunk_rows(i)
        krows = pl.ds(mult(deep * hk + tile * j, tile), tile)
        acc = None
        for h in range(HALVES):
            term = lax.dot_general(
                gl[2 * t + h, there, :], wv[2 * t + h, krows, :],
                (((1,), (1,)), ((), ())), preferred_element_type=F32,
            )
            acc = term if acc is None else acc + term
        return acc

    def dx_step(e):
        @pl.when(e >= 2)
        def _():
            dx_copy(e - 2).wait_send()

        def far(j, carry):
            dsend[e % 2, :, pl.ds(mult(tile * j, tile), tile)] = half(dx_part(e, j, 1 - y))
            return carry

        lax.fori_loop(0, 3, far, 0)
        dx_copy(e).start()

        def near(j, carry):
            own[e % 2, :, pl.ds(mult(tile * j, tile), tile)] = dx_part(e, j, y)
            return carry

        lax.fori_loop(0, 3, near, 0)

    def dx_final(e):
        dx_copy(e).wait_recv()
        dx_fetch(e).start()

        @pl.when(e >= 1)
        def _():
            dx_out(e - 1).wait()

        dx_fetch(e).wait()

        def step(j, inner):
            lanes = pl.ds(mult(tile * j, tile), tile)
            dout[:, lanes] = half(own[e % 2, :, lanes] + wide(dfetch[:, lanes]))
            return inner

        lax.fori_loop(0, 3, step, 0)
        dx_out(e).start()

    def features_at(u, late, do):
        s = u - late
        k = s // SUB
        t, i = k // (2 * n_chunk), k % (2 * n_chunk) - n_chunk

        @pl.when((s >= 0) & (s % SUB == 0) & (k < total) & (i >= 0))
        def _():
            do(t * n_chunk + i)

    def turn():
        lanes_at_once = min(128, tile)

        def step(q, carry):
            lanes = pl.ds(mult(q * lanes_at_once, lanes_at_once), lanes_at_once)
            xt[lanes, :] = xsrc[:, lanes].T
            return carry

        lax.fori_loop(0, tile // lanes_at_once, step, 0)

    def tile_dot(g, b):
        return jnp.dot(xt[...], gl[g // 3, :, cols(b)], preferred_element_type=F32)

    def stage_one(g):
        tile_fetch(g, 1 - c, False)
        turn()
        tile_fetch(g, c, True)

        def step(b, carry):
            cstage[:, cols(b)] = half(tile_dot(g, b))
            return carry

        lax.fori_loop(0, ZED, step, 0)
        core_copy(g).start()

    def stage_two(g):
        tile_fetch(g, c, False)
        turn()

        @pl.when(g % 3 < 2)
        def _():
            tile_fetch(g + 1, 1 - c, True)

        core_copy(g).wait()

        def step(q, carry):
            b = (z + 3 + 3 * q) % ZED
            block = tile_dot(g, b) + wide(cland[g % 2, :, cols(b)])
            left, right = block[:, :xw], block[:, xw:]
            kept[b] = jnp.where(x == 0, left, right)
            xstage[b] = half(jnp.where(x == 0, right, left))
            across_copy(g, b).start()
            return carry

        lax.fori_loop(0, ZED, step, 0)

    def stage_three(g):
        @pl.when(g >= 2)
        def _():
            for to in others:
                z_copy(g - 2, to).wait_send()
            ax_own(g - 2).wait_send()

        def add(b):
            across_copy(g, b).wait()
            zstage[g % 2, b] = half(kept[b] + wide(xland[g % 2, b]))

        def step(q, carry):
            b = (z + 3 + 3 * q) % ZED
            add(b)
            z_copy(g, b).start()
            return carry

        lax.fori_loop(0, ZED - 1, step, 0)
        add(z)
        z_own(g).start()
        ax_own(g).start()

    def stage_four(g):
        def step(q, carry):
            b = (z + 1 + q) % ZED
            z_in(g, b).wait_recv()
            ax_copy(g, b).start()
            return carry

        lax.fori_loop(0, ZED - 1, step, 0)
        z_own(g).wait()

    def stage_five(g):
        def step(q, carry):
            b = (z + q) % ZED
            ax_in(g, b).wait_recv()
            ac_copy(g, b).start()
            return carry

        lax.fori_loop(0, ZED, step, 0)

    def stage_six(g):
        def step(b, carry):
            ac_in(g, b).wait_recv()
            return carry

        lax.fori_loop(0, ZED, step, 0)

    first_tile = n_part + 6

    def tiles_at(u, late, do):
        s = u - late - first_tile
        v = s // 2
        p, j = v // n_chunk, v % n_chunk

        @pl.when((s >= 0) & (s % 2 == 0) & (p < PHASES) & (j < 3))
        def _():
            do(3 * p + j)

    def body(u, carry):
        @pl.when((u >= 5) & (u < parts + 5))
        def _():
            def step(b, inner):
                @pl.when(b < z)
                def _():
                    rs_down(u - 5, b).wait_send()

                @pl.when(b > z)
                def _():
                    rs_up(u - 5, b).wait_send()

                return inner

            lax.fori_loop(0, ZED, step, 0)

        @pl.when((u >= 8) & (u < parts + 8))
        def _():
            def step(b, inner):
                @pl.when((z < ZED - 1) & (b <= z))
                def _():
                    ag(u - 8, b, 0, up).wait_send()

                @pl.when((z > 0) & (b >= z))
                def _():
                    ag(u - 8, b, 1, down).wait_send()

                return inner

            lax.fori_loop(0, ZED, step, 0)

        k = u // SUB

        @pl.when((u < parts) & (u % SUB == 0))
        def _():
            p, i = k // n_chunk, k % n_chunk

            @pl.when(i == 0)
            def _():
                w_own(p).wait()
                for frm in others:
                    w_c_in(p, frm).wait_recv()

            for copy in x_fetch(k):
                copy.wait()

            def step(b, inner):
                product = jnp.dot(
                    xc[k % 2], wv[p, :, cols(b)], preferred_element_type=F32
                )
                for s in range(SUB):
                    pf[(u + s) % PRODUCTS, b] = product[s * part : (s + 1) * part]
                return inner

            lax.fori_loop(0, ZED, step, 0)

        uu = u - z

        @pl.when((uu >= 0) & (uu < parts) & (z < ZED - 1))
        def _():
            slot = uu % RING

            def step(b, inner):
                @pl.when(z > 0)
                def _():
                    rs_in(uu, b, down).wait_recv()
                    rs[slot, b] = half(wide(rs[slot, b]) + pf[uu % PRODUCTS, b])

                @pl.when(z == 0)
                def _():
                    rs[slot, b] = half(pf[uu % PRODUCTS, b])

                rs_up(uu, b).start()
                return inner

            lax.fori_loop(z + 1, ZED, step, 0)

        ud = u - (ZED - 1 - z)

        @pl.when((ud >= 0) & (ud < parts) & (z > 0))
        def _():
            slot = ud % RING

            def step(b, inner):
                @pl.when(z < ZED - 1)
                def _():
                    rs_in(ud, b, up).wait_recv()
                    rs[slot, b] = half(wide(rs[slot, b]) + pf[ud % PRODUCTS, b])

                @pl.when(z == ZED - 1)
                def _():
                    rs[slot, b] = half(pf[ud % PRODUCTS, b])

                rs_down(ud, b).start()
                return inner

            lax.fori_loop(0, z, step, 0)

        @pl.when(u % SUB == 0)
        def _():
            @pl.when(k + 2 < 2 * n_chunk)
            def _():
                x_copy(k + 2).start()

            @pl.when(k + 1 < total)
            def _():
                nxt = k + 1

                @pl.when((nxt // n_chunk) % HALVES == 0)
                def _():
                    x_copy((nxt // n_chunk // HALVES) * n_chunk + nxt % n_chunk).wait_recv()

                for copy in x_fetch(nxt):
                    copy.start()

        @pl.when((u >= 3) & (u < parts + 3))
        def _():
            final(u - 3)

        forward_ag(u - 4, 1)
        forward_ag(u - 5, 2)
        forward_ag(u - 6, 3)

        features_at(u, 7 + 2 * SUB, dx_final)
        features_at(u, 7, dx_step)

        tiles_at(u, 3, stage_three)
        tiles_at(u, 1, stage_two)
        tiles_at(u, 0, stage_one)
        tiles_at(u, 6, stage_four)
        tiles_at(u, 8, stage_five)
        tiles_at(u, 10, stage_six)

        @pl.when((u % n_part == 5) & (u > n_part) & (u < (PHASES + 1) * n_part))
        def _():
            tile_fetch(3 * (u // n_part - 1), 1 - c, True)

        p_next = u // n_part + 1
        v = u % n_part

        @pl.when(p_next < PHASES)
        def _():
            for q in range(3):
                @pl.when((v == 2 * q) & (p_next > 1))
                def _(q=q):
                    w_z(p_next, others[q]).start()

                @pl.when(v == 2 * q + 5)
                def _(q=q):
                    w_z_in(p_next, others[q]).wait_recv()
                    w_x(p_next, others[q]).start()

                @pl.when(v == 2 * q + 7)
                def _(q=q):
                    w_x_in(p_next, others[q]).wait_recv()
                    w_c(p_next, others[q]).start()

            @pl.when((v == 1) & (p_next > 1))
            def _():
                w_own(p_next).start()

        @pl.when(u == parts + 3)
        def _():
            for p in range(PHASES):
                t, h = p // HALVES, p % HALVES
                for s in range(2):
                    for what in range(2):
                        sums[0, pl.ds(4 * what + 2 * s + t, 1), h * hw : (h + 1) * hw] = jnp.sum(
                            stat[p, 2 * what + s], axis=0, keepdims=True
                        )
            sum_copy(0, across_c).start()

        @pl.when(u == parts + 4)
        def _():
            sum_copy(0, across_c).wait()
            sums[1] = sums[0] + sums_land[0]
            sum_copy(1, across_x).start()

        @pl.when(u == parts + 5)
        def _():
            sum_copy(1, across_x).wait()
            both = sums[1] + sums_land[1]
            sums[2] = both
            member = (
                lax.broadcasted_iota(jnp.int32, (width, lane), 0) % FLAG_GROUPS
                == lax.broadcasted_iota(jnp.int32, (width, lane), 1) % FLAG_GROUPS
            ).astype(F32)
            bias_rows = both[0:4]
            inner = both[0:2] * both[2:4]
            stack = jnp.concatenate([inner, bias_rows * bias_rows, inner], axis=0)
            prods[0] = jnp.dot(
                stack, member, precision=lax.Precision.HIGHEST, preferred_element_type=F32
            )
            prod_y().start()

        @pl.when(u == parts + 6)
        def _():
            prod_y().wait()
            prods[1] = prods[0] + prods_land[ZED]
            for to in others:
                prod_z(to).start()

        @pl.when(u == parts + 7)
        def _():
            for frm in others:
                prod_z_in(frm).wait_recv()
            prods_land[z] = prods[1]
            whole = prods_land[0] + prods_land[1] + prods_land[2] + prods_land[3]
            both = sums[2]
            group = lax.broadcasted_iota(jnp.int32, (1, lane), 1) % FLAG_GROUPS

            def over(row):
                return jnp.concatenate([row] * (width // lane), axis=1)

            def flag_row(s, t):
                row = jnp.zeros((1, lane), F32)
                for g in range(FLAG_GROUPS):
                    row = jnp.where(group == g, flags[s, t, g].astype(F32), row)
                return row

            for t in range(2):
                task0, task1 = both[t : t + 1], both[2 + t : 3 + t]
                dots = whole[t : t + 1]
                coef0 = over(flag_row(0, t) * dots / (whole[4 + t : 5 + t] + 1e-06))
                coef1 = over(flag_row(1, t) * dots / (whole[2 + t : 3 + t] + 1e-06))
                gbias[t : t + 1] = (task0 - coef0 * task1) + (task1 - coef1 * task0)
            for s in range(2):
                gstitch[s] = both[4 + 2 * s : 6 + 2 * s]

        return carry

    lax.fori_loop(0, first_tile + 2 * (n_chunk * (PHASES - 1) + 2) + 11, body, 0)

    last = 3 * PHASES - 1
    for g in (last - 1, last):
        for to in others:
            z_copy(g, to).wait_send()
        ax_own(g).wait_send()
    for e in (2 * n_chunk - 2, 2 * n_chunk - 1):
        dx_copy(e).wait_send()
    for e in (2 * n_part - 2, 2 * n_part - 1):
        mixed_out(e).wait()
    dx_out(2 * n_chunk - 1).wait()

    def drain_tiles(g, carry):
        for b in others:
            ax_copy(g, b).wait_send()
        for b in range(ZED):
            ac_copy(g, b).wait_send()
        return carry

    lax.fori_loop(0, last + 1, drain_tiles, 0)

    def drain_x(e, carry):
        x_copy(e).wait_send()
        return carry

    lax.fori_loop(0, 2 * n_chunk, drain_x, 0)

    def drain_w(p, carry):
        for to in others:
            w_z(p, to).wait_send()
            w_x(p, to).wait_send()
            w_c(p, to).wait_send()
        return carry

    lax.fori_loop(0, PHASES, drain_w, 0)
    for to in others:
        prod_z(to).wait_send()


def fused_call(feat, wts, cot, bias, stitch, counts, mask, flags):
    rows, deep, width = feat.shape[1], feat.shape[2], wts.shape[2]
    chunk = rows // 6
    part = chunk // SUB
    hw, kz, tile = width // 2, 2 * deep, deep // 3
    cat, xw = 4 * hw, width // 4
    lane = min(128, width)
    dma = pltpu.SemaphoreType.DMA
    anywhere = pl.BlockSpec(memory_space=pl.ANY)
    inside = pl.BlockSpec(memory_space=pltpu.VMEM)
    scalars = pl.BlockSpec(memory_space=pltpu.SMEM)

    def v(shape, kind=BF16):
        return pltpu.VMEM(shape, kind)

    out_shape = [
        jax.ShapeDtypeStruct((2, rows, width), BF16),
        jax.ShapeDtypeStruct((2, rows, deep), BF16),
        jax.ShapeDtypeStruct((2, ZED, kz, width), BF16),
        jax.ShapeDtypeStruct((2, width), F32),
        jax.ShapeDtypeStruct((2, 2, width), F32),
        jax.ShapeDtypeStruct((2, rows, deep), BF16),
        jax.ShapeDtypeStruct((2, rows, deep), BF16),
    ]
    scratch = [
        v((PHASES, kz, cat)),
        v((PHASES, rows, cat)),
        v((RING, 5, part, hw)),
        v((2, rows, hw), F32),
        v((2, chunk, kz)),
        v((PRODUCTS, ZED, part, hw), F32),
        v((2, 2, part, hw)),
        v((2, 2, part, hw)),
        v((2, chunk, deep), F32),
        v((2, chunk, deep)),
        v((chunk, deep)),
        v((chunk, deep)),
        v((rows, tile)),
        v((tile, rows)),
        v((tile, cat)),
        v((2, tile, cat)),
        v((ZED, tile, xw)),
        v((2, ZED, tile, xw)),
        v((ZED, tile, xw), F32),
        v((2, ZED, tile, xw)),
        v((rows, lane), F32),
        v((PHASES, 4, 8, hw), F32),
        v((3, 8, width), F32),
        v((2, 8, width), F32),
        v((2, 8, lane), F32),
        v((5, 8, lane), F32),
        dma((RING, 4)), dma((RING, 5)), dma((RING, 8)), dma((RING, 4)),
        dma((12,)), dma((12,)),
        dma((4, 4)), dma((4, 4)), dma((4, 4)), dma((4, 4)), dma((4, 4)), dma((4, 4)), dma((4,)),
        dma((2, 2)), dma((2,)), dma((2,)), dma((2,)), dma((12,)), dma((1,)), dma((1,)),
        dma((1,)), dma((1,)), dma((2,)), dma((4,)), dma((2, 4)), dma((2, 4)), dma((12, 4)),
        dma((2,)),
        dma((12, 4)), dma((12, 4)), dma((12, 4)), dma((12, 4)), dma((8,)), dma((8,)),
    ]
    flops = 3 * 2 * 2 * rows * kz * cat * 2
    return pl.pallas_call(
        functools.partial(fused_kernel, rows, deep, width, chunk),
        out_shape=out_shape,
        in_specs=[anywhere] * 3 + [inside] * 4 + [scalars],
        out_specs=[anywhere] * 3 + [inside] * 2 + [anywhere] * 2,
        scratch_shapes=scratch,
        compiler_params=pltpu.CompilerParams(
            collective_id=0, has_side_effects=True, vmem_limit_bytes=64 * 1024 * 1024
        ),
        cost_estimate=pl.CostEstimate(
            flops=flops, bytes_accessed=200_000_000, transcendentals=2 * rows * width * 2
        ),
        name="cross_stitch_step",
    )(feat, wts, cot, bias, stitch, counts, mask, flags)


def widen_kernel(low, out):
    out[...] = wide(low[...])


def widen(low):
    tall, width = low.shape
    block = tall // 12
    spec = pl.BlockSpec((block, width), lambda i: (i, 0))
    return pl.pallas_call(
        widen_kernel,
        grid=(12,),
        in_specs=[spec],
        out_specs=spec,
        out_shape=jax.ShapeDtypeStruct(low.shape, F32),
        compiler_params=pltpu.CompilerParams(vmem_limit_bytes=60 * 1024 * 1024),
        cost_estimate=pl.CostEstimate(
            flops=tall * width, bytes_accessed=6 * tall * width, transcendentals=0
        ),
        name="widen",
    )(low)


def fused_plan(mesh):
    def per_device(features, weights, bias, stitch, cotangent, crop_counts, row_mask, flags):
        rows, deep = features.shape[1:]
        width = weights.shape[2]
        mixed, gfeat, gwt, gbias, gstitch, _, _ = fused_call(
            features, weights, cotangent, bias, stitch,
            crop_counts.reshape(1, -1), row_mask.reshape(1, -1), flags,
        )
        grad_weights = widen(gwt.reshape(-1, width)).reshape(2, ZED * 2 * deep, width)
        return mixed, gfeat, grad_weights, gbias, gstitch

    return per_device


def plan_for(mesh):
    if mesh.shape["batch"] == 4 and mesh.shape["mp"] == 2 * ZED:
        return fused_plan(mesh)
    return generic_plan(mesh)


def solution(mesh):
    in_specs = (
        P(None, "batch", "mp"),
        P(None, None, "mp"),
        P(None, "mp"),
        P(None, None, "mp"),
        P(None, "batch", "mp"),
        P("batch"),
        P("batch"),
        P(),
    )
    out_specs = (
        P(None, "batch", "mp"),
        P(None, "batch", "mp"),
        P(None, None, "mp"),
        P(None, "mp"),
        P(None, None, "mp"),
    )
    return jax.shard_map(
        plan_for(mesh), mesh=mesh, in_specs=in_specs, out_specs=out_specs, check_vma=False
    )
```

```python
import collections
import functools

import jax
import jax.numpy as jnp
from jax import lax
from jax.experimental import pallas as pl
from jax.experimental.pallas import tpu as pltpu
from jax.sharding import PartitionSpec as P

FLAG_GROUPS = 8
OUTER = 4


def row_weights(counts, mask):
    ends = jnp.cumsum(counts)
    starts = ends - counts
    index = lax.broadcasted_iota(jnp.int32, (mask.shape[0], counts.shape[0]), 0)
    inside = (index >= starts[None, :]) & (index < ends[None, :])
    count_row = jnp.sum(jnp.where(inside, counts[None, :], 0), axis=1)
    live = (count_row > 0) & (mask == 1)
    return jnp.where(live, 1.0 / jnp.maximum(count_row, 1).astype(jnp.float32), 0.0)


def project_bias(task_bias, flags):
    local_width = task_bias.shape[2]
    channel = lax.axis_index("mp") * local_width + lax.broadcasted_iota(
        jnp.int32, (local_width, FLAG_GROUPS), 0
    )
    member = (
        channel % FLAG_GROUPS == lax.broadcasted_iota(jnp.int32, (local_width, FLAG_GROUPS), 1)
    ).astype(jnp.float32)
    dots = jnp.dot(task_bias[0] * task_bias[1], member, precision=lax.Precision.HIGHEST)
    norms = jnp.einsum(
        "stc,cg->stg", task_bias * task_bias, member, precision=lax.Precision.HIGHEST
    )
    dots, norms = lax.psum((dots, norms), "mp")
    flag = flags.astype(jnp.float32)
    coef_first = jnp.dot(
        flag[0] * dots / (norms[1] + 1e-06), member.T, precision=lax.Precision.HIGHEST
    )
    coef_second = jnp.dot(
        flag[1] * dots / (norms[0] + 1e-06), member.T, precision=lax.Precision.HIGHEST
    )
    first = task_bias[0] - coef_first * task_bias[1]
    second = task_bias[1] - coef_second * task_bias[0]
    return first + second


def generic_plan(mesh):
    n_mp = mesh.shape["mp"]
    n_batch = mesh.shape["batch"]
    inner = n_mp // OUTER
    inner_groups = [[o * inner + i for i in range(inner)] for o in range(OUTER)]
    outer_groups = [[o * inner + i for o in range(OUTER)] for i in range(inner)]

    def per_device(features, weights, bias, stitch, cotangent, crop_counts, row_mask, flags):
        rows = features.shape[1]
        width = weights.shape[2]
        depth = features.shape[2] * inner
        held = lax.all_gather(
            features, "mp", axis=2, tiled=True, axis_index_groups=inner_groups
        )
        split = weights.reshape(2, OUTER, depth, width)
        block = lax.all_to_all(
            split, "mp", split_axis=1, concat_axis=1, axis_index_groups=outer_groups
        )
        block = block.reshape(2, OUTER, depth, width)
        part = jnp.einsum("trk,tokc->otrc", held, block, preferred_element_type=jnp.float32)
        linear = lax.psum_scatter(
            part.astype(jnp.bfloat16),
            "mp",
            scatter_dimension=0,
            axis_index_groups=outer_groups,
        ).astype(jnp.float32)
        pre = linear + bias[:, None, :]
        hidden, gelu_back = jax.vjp(lambda v: jax.nn.gelu(v, approximate=False), pre)
        mixed = stitch[:, 0, None, :] * hidden[0][None] + stitch[:, 1, None, :] * hidden[1][None]
        scale_rows = row_weights(crop_counts, row_mask)
        grad_out = cotangent.astype(jnp.float32) * scale_rows[None, :, None]
        first_task = gelu_back(stitch[0][:, None, :] * grad_out[0][None])[0]
        second_task = gelu_back(stitch[1][:, None, :] * grad_out[1][None])[0]
        task_bias = jnp.stack([jnp.sum(first_task, axis=1), jnp.sum(second_task, axis=1)])
        grad_linear = (first_task + second_task).astype(jnp.bfloat16)
        grad_stitch = jnp.sum(grad_out[:, None] * hidden[None], axis=2)
        every = lax.all_gather(grad_linear, "mp", axis_index_groups=outer_groups)
        grad_part = jnp.einsum(
            "otrc,tokc->trk", every, block, preferred_element_type=jnp.float32
        )
        grad_part = grad_part.astype(jnp.bfloat16).reshape(2, rows, inner, depth // inner)
        grad_features = lax.psum_scatter(
            grad_part.transpose(2, 0, 1, 3),
            "mp",
            scatter_dimension=0,
            axis_index_groups=inner_groups,
        )
        weight_part = jnp.einsum(
            "trk,otrc->otkc", held, every, preferred_element_type=jnp.float32
        )
        weight_part = weight_part.astype(jnp.bfloat16).reshape(
            OUTER, 2, n_batch, depth // n_batch, width
        )
        share = lax.psum_scatter(
            weight_part.transpose(2, 0, 1, 3, 4), "batch", scatter_dimension=0
        )
        share = lax.all_to_all(
            share, "mp", split_axis=0, concat_axis=0, axis_index_groups=outer_groups
        )
        share = share.reshape(OUTER, 2, depth // n_batch, width)
        whole = lax.all_gather(share, "batch")
        grad_weights = whole.transpose(2, 1, 0, 3, 4).reshape(2, OUTER * depth, width)
        task_bias, grad_stitch = lax.psum((task_bias, grad_stitch), "batch")
        grad_bias = project_bias(task_bias, flags)
        return (
            mixed.astype(jnp.bfloat16),
            grad_features.astype(jnp.bfloat16),
            grad_weights.astype(jnp.float32),
            grad_bias,
            grad_stitch,
        )

    return per_device


MESH = pl.DeviceIdType.MESH
BF16 = jnp.bfloat16
F32 = jnp.float32
ZED = 4
HALVES = 2
PHASES = 4
RING = 8
BAND = 32
SUB = 2
PRODUCTS = 6


Part = collections.namedtuple("Part", ("u", "p", "i", "t", "h", "slot", "prod", "buf"))
Tile = collections.namedtuple("Tile", ("g", "p", "t", "h", "j", "buf"))


def half(value):
    return value.astype(BF16)


def wide(value):
    return value.astype(F32)


def fused_kernel(
    rows, deep, width, chunk,
    feat, wts, cot, bias, stitch, counts, mask, flags,
    mixed, gfeat, gwt, gbias, gstitch, xn, dxn,
    wv, gl, rs, h0, xc, pf, cc, mx, own, dsend, dfetch, dout,
    xsrc, xt, cstage, cland, xstage, xland, kept, zstage,
    scale, stat, sums, sums_land, prods, prods_land,
    rs_send, rs_recv, ag_send, ag_recv, xs_send, xs_recv,
    wz_send, wz_recv, wx_send, wx_recv, wc_send, wc_recv, wl,
    xf, cf, mxs, dx_send, dx_recv, df, dod,
    tile_in, c_send, c_recv, x_send, x_recv, z_send, z_recv, zl, zx_send,
    ax_send, ax_recv, ac_send, ac_recv, t_send, t_recv,
):
    batch, mp = lax.axis_index("batch"), lax.axis_index("mp")
    z, y = mp // 2, mp % 2
    x, c = batch // 2, batch % 2
    up = {"mp": mp + 2}
    down = {"mp": mp - 2}
    across_y = {"mp": 2 * z + 1 - y}
    across_x = {"batch": 2 * (1 - x) + c}
    across_c = {"batch": 2 * x + 1 - c}

    def at_z(other):
        return {"mp": 2 * other + y}

    others = (3 - z, (z + 2) % 4, z + 1 - 2 * (z % 2))

    n_chunk = rows // chunk
    total = PHASES * n_chunk
    part = chunk // SUB
    n_part = rows // part
    parts = PHASES * n_part
    images = counts.shape[1]
    hw = width // HALVES
    kz = 2 * deep
    quarter = deep // 2
    tile = deep // 3
    strip = quarter // 6
    xw = hw // 2

    def mult(value, unit):
        return pl.multiple_of(value, unit)

    def remote(src, dst, send, recv, device):
        return pltpu.make_async_remote_copy(
            src_ref=src, dst_ref=dst, send_sem=send, recv_sem=recv,
            device_id=device, device_id_type=MESH,
        )

    def cols(b):
        return pl.ds(mult(b * hw, hw), hw)

    def chunk_rows(i):
        return pl.ds(mult(i * chunk, chunk), chunk)

    def part_rows(i):
        return pl.ds(mult(i * part, part), part)

    def tower(p):
        t = jnp.where(p >= HALVES, 1, 0)
        return t, p - HALVES * t

    def x_copy(t, i):
        e = t * n_chunk + i
        return remote(
            feat.at[t, chunk_rows(i)], xn.at[t, chunk_rows(i)],
            xs_send.at[e], xs_recv.at[e], across_y,
        )

    def x_fetch(t, i, buf):
        return (
            pltpu.make_async_copy(
                feat.at[t, chunk_rows(i)],
                xc.at[buf, :, pl.ds(mult(deep * y, deep), deep)], xf.at[buf, 0],
            ),
            pltpu.make_async_copy(
                xn.at[t, chunk_rows(i)],
                xc.at[buf, :, pl.ds(mult(deep * (1 - y), deep), deep)], xf.at[buf, 1],
            ),
        )

    def cot_fetch(h, i, buf):
        return pltpu.make_async_copy(
            cot.at[:, part_rows(i), cols(h)], cc.at[buf], cf.at[buf]
        )

    def w_own(p):
        t, h = tower(p)
        return pltpu.make_async_copy(
            wts.at[t, pl.ds(mult(kz * z, kz), kz), cols(h)], wv.at[p, :, cols(z)], wl.at[p],
        )

    def w_rows():
        return pl.ds(mult(deep * c + quarter * x, quarter), quarter)

    def w_z(p, to):
        t, h = tower(p)
        return remote(
            wts.at[
                t, pl.ds(mult(kz * to + deep * c + quarter * x, quarter), quarter), cols(h)
            ],
            wv.at[p, w_rows(), cols(z)],
            wz_send.at[p, to], wz_recv.at[p, z], at_z(to),
        )

    def w_z_strip(p, to, r):
        t, h = tower(p)
        at = deep * c + quarter * x + strip * r
        return remote(
            wts.at[t, pl.ds(mult(kz * to + at, strip), strip), cols(h)],
            wv.at[p, pl.ds(mult(at, strip), strip), cols(z)],
            wz_send.at[p, to], wz_recv.at[p, z], at_z(to),
        )

    def w_z_in(p, frm):
        here = wv.at[p, w_rows(), cols(frm)]
        return remote(here, here, wz_send.at[p, frm], wz_recv.at[p, frm], at_z(frm))

    def w_x(p, b):
        here = wv.at[p, w_rows(), cols(b)]
        return remote(here, here, wx_send.at[p, b], wx_recv.at[p, b], across_x)

    def w_x_in(p, b):
        here = wv.at[
            p, pl.ds(mult(deep * c + quarter * (1 - x), quarter), quarter), cols(b)
        ]
        return remote(here, here, wx_send.at[p, b], wx_recv.at[p, b], across_x)

    def w_c(p, b):
        here = wv.at[p, pl.ds(mult(deep * c, deep), deep), cols(b)]
        return remote(here, here, wc_send.at[p, b], wc_recv.at[p, b], across_c)

    def w_c_in(p, b):
        here = wv.at[p, pl.ds(mult(deep * (1 - c), deep), deep), cols(b)]
        return remote(here, here, wc_send.at[p, b], wc_recv.at[p, b], across_c)

    def rs_up(slot, zz):
        run = rs.at[slot, zz + 2 : ZED + 1]
        return remote(run, run, rs_send.at[slot, 0], rs_recv.at[slot, 0], up)

    def rs_down(slot, zz):
        run = rs.at[slot, 0:zz]
        return remote(run, run, rs_send.at[slot, 1], rs_recv.at[slot, 1], down)

    def rs_from_below(slot, zz):
        run = rs.at[slot, zz + 1 : ZED + 1]
        return remote(run, run, rs_send.at[slot, 0], rs_recv.at[slot, 0], down)

    def rs_from_above(slot, zz):
        run = rs.at[slot, 0 : zz + 1]
        return remote(run, run, rs_send.at[slot, 1], rs_recv.at[slot, 1], up)

    def at_place(first, last, do):
        for zz in range(first, last + 1):
            @pl.when(z == zz)
            def _(zz=zz):
                do(zz)

    def ag(at, b, going, device):
        here = gl.at[at.p, part_rows(at.i), cols(b)]
        return remote(
            here, here, ag_send.at[at.slot, going * ZED + b], ag_recv.at[at.slot, b], device
        )

    def dx_copy(t, i, buf):
        return remote(
            dsend.at[buf], dxn.at[t, chunk_rows(i)],
            dx_send.at[buf], dx_recv.at[t * n_chunk + i], across_y,
        )

    def dx_fetch(t, i):
        return pltpu.make_async_copy(dxn.at[t, chunk_rows(i)], dfetch, df.at[0])

    def dx_out(t, i):
        return pltpu.make_async_copy(dout, gfeat.at[t, chunk_rows(i)], dod.at[0])

    def mixed_out(h, i, buf):
        return pltpu.make_async_copy(
            mx.at[buf], mixed.at[:, part_rows(i), cols(h)], mxs.at[buf]
        )

    def tile_fetch(t, j, hk, start):
        lanes = pl.ds(mult(tile * j, tile), tile)
        near = pltpu.make_async_copy(feat.at[t, :, lanes], xsrc, tile_in.at[0])
        if not start:
            near.wait()
            return

        @pl.when(hk == y)
        def _():
            near.start()

        @pl.when(hk != y)
        def _():
            pltpu.make_async_copy(xn.at[t, :, lanes], xsrc, tile_in.at[0]).start()

    def core_copy(g):
        return remote(cstage, cland.at[g.buf], c_send.at[0], c_recv.at[g.buf], across_c)

    def across_copy(g, b):
        return remote(
            xstage.at[b], xland.at[g.buf, b], x_send.at[b], x_recv.at[g.buf, b], across_x
        )

    def piece(g, source, core, lanes, n_lanes):
        return gwt.at[
            g.t, source,
            pl.ds(mult(deep * core + tile * g.j, tile), tile),
            pl.ds(mult(hw * g.h + lanes, xw), n_lanes),
        ]

    def z_copy(g, to):
        return remote(
            zstage.at[g.buf, to], piece(g, z, c, xw * x, xw),
            z_send.at[g.buf, to], z_recv.at[g.g, z], at_z(to),
        )

    def z_in(g, frm):
        here = piece(g, frm, c, xw * x, xw)
        return remote(here, here, z_send.at[g.buf, frm], z_recv.at[g.g, frm], at_z(frm))

    def z_own(g):
        return pltpu.make_async_copy(
            zstage.at[g.buf, z], piece(g, z, c, xw * x, xw), zl.at[g.buf]
        )

    def ax_own(g):
        return remote(
            zstage.at[g.buf, z], piece(g, z, c, xw * x, xw),
            zx_send.at[g.buf], ax_recv.at[g.g, z], across_x,
        )

    def ax_copy(g, b):
        here = piece(g, b, c, xw * x, xw)
        return remote(here, here, ax_send.at[g.g, b], ax_recv.at[g.g, b], across_x)

    def ax_in(g, b):
        here = piece(g, b, c, xw * (1 - x), xw)
        return remote(here, here, ax_send.at[g.g, b], ax_recv.at[g.g, b], across_x)

    def ac_copy(g, b):
        here = piece(g, b, c, 0, hw)
        return remote(here, here, ac_send.at[g.g, b], ac_recv.at[g.g, b], across_c)

    def ac_in(g, b):
        here = piece(g, b, 1 - c, 0, hw)
        return remote(here, here, ac_send.at[g.g, b], ac_recv.at[g.g, b], across_c)

    def sum_copy(stage, device):
        return remote(
            sums.at[stage], sums_land.at[stage], t_send.at[stage], t_recv.at[stage], device
        )

    def prod_y():
        return remote(prods.at[0], prods_land.at[ZED], t_send.at[2], t_recv.at[2], across_y)

    def prod_z(to):
        return remote(
            prods.at[1], prods_land.at[z], t_send.at[3 + to], t_recv.at[3 + z], at_z(to)
        )

    def prod_z_in(frm):
        here = prods_land.at[frm]
        return remote(here, here, t_send.at[3 + frm], t_recv.at[3 + frm], at_z(frm))

    barrier = pltpu.get_barrier_semaphore()
    for device in [at_z(o) for o in others] + [across_y, across_x, across_c]:
        pl.semaphore_signal(barrier, inc=1, device_id=device, device_id_type=MESH)
    pl.semaphore_wait(barrier, 6)

    for to in others:
        w_z(0, to).start()
    x_copy(0, 0).start()
    x_copy(0, 1).start()
    w_own(0).start()
    cot_fetch(0, 0, 0).start()

    image_row = lax.broadcasted_iota(jnp.int32, (images, images), 0)
    image_col = lax.broadcasted_iota(jnp.int32, (images, images), 1)
    crops = counts[...].astype(F32)
    ends = jnp.dot(
        jnp.broadcast_to(crops, (8, images)), (image_row <= image_col).astype(F32),
        precision=lax.Precision.HIGHEST, preferred_element_type=F32,
    )[0:1]
    starts = ends - crops
    block = min(128, chunk)
    lane = scale.shape[1]

    for r in range(rows // block):
        index = (
            lax.broadcasted_iota(jnp.int32, (block, images), 0) + r * block
        ).astype(F32)
        inside = (index >= starts) & (index < ends)
        count_row = jnp.sum(jnp.where(inside, crops, 0.0), axis=1, keepdims=True)
        diagonal = lax.broadcasted_iota(jnp.int32, (block, block), 0) == (
            lax.broadcasted_iota(jnp.int32, (block, block), 1)
        )
        usable = jnp.sum(
            jnp.where(diagonal, mask[:, r * block : (r + 1) * block].astype(F32), 0.0),
            axis=1, keepdims=True,
        )
        live = (count_row > 0.0) & (usable == 1.0)
        share = jnp.where(live, 1.0 / jnp.maximum(count_row, 1.0), 0.0)
        scale[r * block : (r + 1) * block, :] = jnp.broadcast_to(share, (block, lane))

    for frm in others:
        w_z_in(0, frm).wait_recv()
        w_x(0, frm).start()
    for to in others:
        w_z(1, to).start()
    w_own(1).start()
    for frm in others:
        w_x_in(0, frm).wait_recv()
        w_c(0, frm).start()
    x_copy(0, 0).wait_recv()
    for copy in x_fetch(0, 0, 0):
        copy.start()

    def final(at, later):
        p, i, slot, t, h, buf = at.p, at.i, at.slot, at.t, at.h, at.buf
        cot_fetch(h, i, buf).wait()

        @pl.when(at.u >= 2 * n_part + 2)
        def _():
            mixed_out(h, i, buf).wait()

        @pl.when(i == 0)
        def _():
            stat[p] = jnp.zeros(stat.shape[1:], F32)

        lanes = cols(h)
        shift = bias[pl.ds(t, 1), lanes]
        st = [stitch[s, pl.ds(t, 1), lanes] for s in range(2)]
        band = min(BAND, part)

        def step(r, carry):
            here = part_rows_of(r, band)
            there = pl.ds(mult(i * part + r * band, band), band)
            value = pf[at.prod, z, here, :]
            below = wide(rs[slot, z + 1, here, :])
            above = wide(rs[slot, z, here, :])
            value = value + jnp.where(z > 0, below, 0.0) + jnp.where(z < ZED - 1, above, 0.0)
            pre = value + shift
            phi = 0.5 * (1.0 + lax.erf(pre * 0.7071067811865476))
            hidden = pre * phi
            slope = phi + pre * (jnp.exp(-0.5 * pre * pre) * 0.3989422804014327)
            weight = scale[there, 0:1]
            first = wide(cc[buf, 0, here, :]) * weight
            second = wide(cc[buf, 1, here, :]) * weight
            back0 = st[0] * first * slope
            back1 = st[1] * second * slope
            gl[p, there, cols(z)] = half(back0 + back1)

            def fold(v):
                return jnp.sum(v.reshape(band // 8, 8, hw), axis=0)

            stat[p, 0] += fold(back0)
            stat[p, 1] += fold(back1)
            stat[p, 2] += fold(first * hidden)
            stat[p, 3] += fold(second * hidden)

            @pl.when(t == 0)
            def _():
                h0[h, there, :] = hidden

            @pl.when(t == 1)
            def _():
                before = h0[h, there, :]
                for s in range(2):
                    mx[buf, s, here, :] = half(
                        stitch[s, 0:1, lanes] * before + st[s] * hidden
                    )

            return carry

        lax.fori_loop(0, part // band, step, 0)

        @pl.when(z < ZED - 1)
        def _():
            ag(at, z, 0, up).start()

        @pl.when(z > 0)
        def _():
            ag(at, z, 1, down).start()

        @pl.when(t == 1)
        def _():
            mixed_out(h, i, buf).start()

        @pl.when(at.u + 1 < parts)
        def _():
            cot_fetch(later.h, later.i, later.buf).start()

    def part_rows_of(r, band):
        return pl.ds(mult(r * band, band), band)

    def forward_ag(at, far):
        @pl.when((at.u >= 0) & (at.u < parts))
        def _():
            @pl.when(z - far >= 0)
            def _():
                ag(at, z - far, 0, up).wait_recv()

                @pl.when(z < ZED - 1)
                def _():
                    ag(at, z - far, 0, up).start()

            @pl.when(z + far < ZED)
            def _():
                ag(at, z + far, 1, down).wait_recv()

                @pl.when(z > 0)
                def _():
                    ag(at, z + far, 1, down).start()

    def dx_part(t, i, hk):
        there = chunk_rows(i)
        krows = pl.ds(mult(deep * hk, deep), deep)
        acc = None
        for h in range(HALVES):
            term = lax.dot_general(
                gl[2 * t + h, there, :], wv[2 * t + h, krows, :],
                (((1,), (1,)), ((), ())), preferred_element_type=F32,
            )
            acc = term if acc is None else acc + term
        return acc

    def dx_step(t, i, buf):
        @pl.when((i >= 2) | (t > 0))
        def _():
            dx_copy(t, i, buf).wait_send()

        dsend[buf] = half(dx_part(t, i, 1 - y))
        dx_copy(t, i, buf).start()
        own[buf] = dx_part(t, i, y)

    def dx_begin(t, i, buf):
        dx_copy(t, i, buf).wait_recv()
        dx_fetch(t, i).start()

    def dx_final(t, i, buf):
        @pl.when((i >= 1) | (t > 0))
        def _():
            dx_out(t, i).wait()

        dx_fetch(t, i).wait()

        def step(j, inner):
            lanes = pl.ds(mult(tile * j, tile), tile)
            dout[:, lanes] = half(own[buf, :, lanes] + wide(dfetch[:, lanes]))
            return inner

        lax.fori_loop(0, 3, step, 0)
        dx_out(t, i).start()

    def features_at(at, do):
        i = lax.div(at.i, SUB)

        @pl.when((at.u >= 0) & (at.u < parts) & (i * SUB == at.i) & (at.h == 1))
        def _():
            do(at.t, i, lax.rem(i, 2))

    def turn():
        lanes_at_once = min(128, tile)

        def step(q, carry):
            lanes = pl.ds(mult(q * lanes_at_once, lanes_at_once), lanes_at_once)
            xt[lanes, :] = xsrc[:, lanes].T
            return carry

        lax.fori_loop(0, tile // lanes_at_once, step, 0)

    def tile_dot(g):
        return jnp.dot(xt[...], gl[g.p], preferred_element_type=F32)

    def stage_one(g):
        tile_fetch(g.t, g.j, 1 - c, False)
        turn()
        tile_fetch(g.t, g.j, c, True)
        cstage[...] = half(tile_dot(g))
        core_copy(g).start()

    def stage_two(g):
        tile_fetch(g.t, g.j, c, False)
        turn()

        @pl.when(g.j < 2)
        def _():
            tile_fetch(g.t, g.j + 1, 1 - c, True)

        core_copy(g).wait()
        product = tile_dot(g)
        for b in range(ZED):
            block = product[:, b * hw : (b + 1) * hw] + wide(
                cland[g.buf, :, b * hw : (b + 1) * hw]
            )
            left, right = block[:, :xw], block[:, xw:]
            kept[b] = jnp.where(x == 0, left, right)
            xstage[b] = half(jnp.where(x == 0, right, left))

        def send(q, carry):
            across_copy(g, lax.rem(z + 3 + 3 * q, ZED)).start()
            return carry

        lax.fori_loop(0, ZED, send, 0)

    def stage_three(g):
        @pl.when(g.g >= 2)
        def _():
            for to in others:
                z_copy(g, to).wait_send()
            ax_own(g).wait_send()

        def add(b):
            across_copy(g, b).wait()
            zstage[g.buf, b] = half(kept[b] + wide(xland[g.buf, b]))

        def step(q, carry):
            b = lax.rem(z + 3 + 3 * q, ZED)
            add(b)
            z_copy(g, b).start()
            return carry

        lax.fori_loop(0, ZED - 1, step, 0)
        add(z)
        z_own(g).start()
        ax_own(g).start()

    def stage_four(g):
        def step(q, carry):
            b = lax.rem(z + 1 + q, ZED)
            z_in(g, b).wait_recv()
            ax_copy(g, b).start()
            return carry

        lax.fori_loop(0, ZED - 1, step, 0)
        z_own(g).wait()

    def stage_five(g):
        def step(q, carry):
            b = lax.rem(z + q, ZED)
            ax_in(g, b).wait_recv()
            ac_copy(g, b).start()
            return carry

        lax.fori_loop(0, ZED, step, 0)

    def stage_six(g):
        def step(b, carry):
            ac_in(g, b).wait_recv()
            return carry

        lax.fori_loop(0, ZED, step, 0)

    first_tile = n_part + 6

    def tiles_at(at, do):
        j = lax.div(at.i, 4)
        p = at.p - 1

        @pl.when((p >= 0) & (p < PHASES) & (4 * j == at.i))
        def _():
            t, h = tower(p)
            g = 3 * p + j
            do(Tile(g=g, p=p, t=t, h=h, j=j, buf=lax.rem(g, 2)))

    def body(u, carry):
        p0 = lax.div(u, n_part)
        i0 = u - p0 * n_part
        slot0, prod0 = lax.rem(u, RING), lax.rem(u, PRODUCTS)
        buf0 = lax.rem(u, 2)

        def before(lag):
            if isinstance(lag, int):
                whole, left = divmod(lag, n_part)
            else:
                whole, left = 0, lag
            under = i0 < left
            p = p0 - whole - jnp.where(under, 1, 0)
            i = i0 - left + jnp.where(under, n_part, 0)
            in_ring = lag % RING if isinstance(lag, int) else lag
            in_prods = lag % PRODUCTS if isinstance(lag, int) else lag
            slot = slot0 - in_ring + jnp.where(slot0 < in_ring, RING, 0)
            prod = prod0 - in_prods + jnp.where(prod0 < in_prods, PRODUCTS, 0)
            t, h = tower(p)
            return Part(u=u - lag, p=p, i=i, t=t, h=h, slot=slot, prod=prod, buf=lax.rem(i, 2))

        @pl.when((u >= 5) & (u < parts + 5))
        def _():
            slot = before(5).slot
            at_place(0, ZED - 2, lambda zz: rs_up(slot, zz).wait_send())
            at_place(1, ZED - 1, lambda zz: rs_down(slot, zz).wait_send())

        @pl.when((u >= 8) & (u < parts + 8))
        def _():
            at = before(8)

            def step(b, inner):
                @pl.when((z < ZED - 1) & (b <= z))
                def _():
                    ag(at, b, 0, up).wait_send()

                @pl.when((z > 0) & (b >= z))
                def _():
                    ag(at, b, 1, down).wait_send()

                return inner

            lax.fori_loop(0, ZED, step, 0)

        ck = lax.div(i0, SUB)
        fresh = ck * SUB == i0
        t0, h0_ = tower(p0)
        xbuf = lax.rem(ck, 2)

        @pl.when((u < parts) & fresh)
        def _():
            @pl.when(i0 == 0)
            def _():
                w_own(p0).wait()
                for frm in others:
                    w_c_in(p0, frm).wait_recv()

            for copy in x_fetch(t0, ck, xbuf):
                copy.wait()

            product = jnp.dot(xc[xbuf], wv[p0], preferred_element_type=F32)
            for b in range(ZED):
                for s in range(SUB):
                    pf[prod0 + s, b] = product[
                        s * part : (s + 1) * part, b * hw : (b + 1) * hw
                    ]

        going_up = before(z)

        @pl.when((going_up.u >= 0) & (going_up.u < parts))
        def _():
            slot, prod = going_up.slot, going_up.prod
            at_place(1, ZED - 1, lambda zz: rs_from_below(slot, zz).wait_recv())

            @pl.when(z == 0)
            def _():
                for b in range(1, ZED):
                    rs[slot, b + 1] = half(pf[prod, b])

            @pl.when(z > 0)
            def _():
                def step(b, inner):
                    rs[slot, b + 1] = half(wide(rs[slot, b + 1]) + pf[prod, b])
                    return inner

                lax.fori_loop(z + 1, ZED, step, 0)

            at_place(0, ZED - 2, lambda zz: rs_up(slot, zz).start())

        going_down = before(ZED - 1 - z)

        @pl.when((going_down.u >= 0) & (going_down.u < parts))
        def _():
            slot, prod = going_down.slot, going_down.prod
            at_place(0, ZED - 2, lambda zz: rs_from_above(slot, zz).wait_recv())

            @pl.when(z == ZED - 1)
            def _():
                for b in range(ZED - 1):
                    rs[slot, b] = half(pf[prod, b])

            @pl.when(z < ZED - 1)
            def _():
                def step(b, inner):
                    rs[slot, b] = half(wide(rs[slot, b]) + pf[prod, b])
                    return inner

                lax.fori_loop(0, z, step, 0)

            at_place(1, ZED - 1, lambda zz: rs_down(slot, zz).start())

        @pl.when(fresh & (u + 2 * SUB < 2 * n_part))
        def _():
            k = p0 * n_chunk + ck + 2
            over = jnp.where(k >= n_chunk, 1, 0)
            x_copy(over, k - over * n_chunk).start()

        @pl.when(fresh & (u + SUB < parts))
        def _():
            wrap = jnp.where(ck + 1 == n_chunk, 1, 0)
            i = ck + 1 - wrap * n_chunk
            t, h = tower(p0 + wrap)

            @pl.when(h == 0)
            def _():
                x_copy(t, i).wait_recv()

            for copy in x_fetch(t, i, lax.rem(i, 2)):
                copy.start()

        @pl.when((u >= 3) & (u < parts + 3))
        def _():
            final(before(3), before(2))

        forward_ag(before(4), 1)
        forward_ag(before(5), 2)
        forward_ag(before(6), 3)

        features_at(before(6 + 2 * SUB), dx_begin)
        features_at(before(7 + 2 * SUB), dx_final)
        features_at(before(7), dx_step)

        tiles_at(before(11), stage_three)
        tiles_at(before(8), stage_two)
        tiles_at(before(6), stage_one)
        tiles_at(before(14), stage_four)
        tiles_at(before(16), stage_five)
        tiles_at(before(18), stage_six)

        @pl.when((i0 == 5) & (p0 > 0) & (p0 < PHASES + 1))
        def _():
            t, _h = tower(p0 - 1)
            tile_fetch(t, 0, 1 - c, True)

        @pl.when(p0 + 1 < PHASES)
        def _():
            @pl.when((i0 < 6) & (p0 > 0))
            def _():
                for to in others:
                    w_z_strip(p0 + 1, to, i0).start()

            for q in range(3):
                @pl.when(i0 == q + 7)
                def _(q=q):
                    w_z_in(p0 + 1, others[q]).wait_recv()
                    w_x(p0 + 1, others[q]).start()

                @pl.when(i0 == q + 9)
                def _(q=q):
                    w_x_in(p0 + 1, others[q]).wait_recv()
                    w_c(p0 + 1, others[q]).start()

            @pl.when((i0 == 1) & (p0 > 0))
            def _():
                w_own(p0 + 1).start()

        @pl.when(u == parts + 3)
        def _():
            for p in range(PHASES):
                t, h = p // HALVES, p % HALVES
                for s in range(2):
                    for what in range(2):
                        sums[0, pl.ds(4 * what + 2 * s + t, 1), h * hw : (h + 1) * hw] = jnp.sum(
                            stat[p, 2 * what + s], axis=0, keepdims=True
                        )
            sum_copy(0, across_c).start()

        @pl.when(u == parts + 4)
        def _():
            sum_copy(0, across_c).wait()
            sums[1] = sums[0] + sums_land[0]
            sum_copy(1, across_x).start()

        @pl.when(u == parts + 5)
        def _():
            sum_copy(1, across_x).wait()
            both = sums[1] + sums_land[1]
            sums[2] = both
            member = (
                lax.broadcasted_iota(jnp.int32, (width, lane), 0) % FLAG_GROUPS
                == lax.broadcasted_iota(jnp.int32, (width, lane), 1) % FLAG_GROUPS
            ).astype(F32)
            bias_rows = both[0:4]
            inner = both[0:2] * both[2:4]
            stack = jnp.concatenate([inner, bias_rows * bias_rows, inner], axis=0)
            prods[0] = jnp.dot(
                stack, member, precision=lax.Precision.HIGHEST, preferred_element_type=F32
            )
            prod_y().start()

        @pl.when(u == parts + 6)
        def _():
            prod_y().wait()
            prods[1] = prods[0] + prods_land[ZED]
            for to in others:
                prod_z(to).start()

        @pl.when(u == parts + 7)
        def _():
            for frm in others:
                prod_z_in(frm).wait_recv()
            prods_land[z] = prods[1]
            whole = prods_land[0] + prods_land[1] + prods_land[2] + prods_land[3]
            both = sums[2]
            group = lax.broadcasted_iota(jnp.int32, (1, lane), 1) % FLAG_GROUPS

            def over(row):
                return jnp.concatenate([row] * (width // lane), axis=1)

            def flag_row(s, t):
                row = jnp.zeros((1, lane), F32)
                for g in range(FLAG_GROUPS):
                    row = jnp.where(group == g, flags[s, t, g].astype(F32), row)
                return row

            for t in range(2):
                task0, task1 = both[t : t + 1], both[2 + t : 3 + t]
                dots = whole[t : t + 1]
                coef0 = over(flag_row(0, t) * dots / (whole[4 + t : 5 + t] + 1e-06))
                coef1 = over(flag_row(1, t) * dots / (whole[2 + t : 3 + t] + 1e-06))
                gbias[t : t + 1] = (task0 - coef0 * task1) + (task1 - coef1 * task0)
            for s in range(2):
                gstitch[s] = both[4 + 2 * s : 6 + 2 * s]

        return carry

    lax.fori_loop(0, first_tile + n_part * (PHASES - 1) + 21, body, 0)

    last = 3 * PHASES - 1

    def tile_of(g):
        p, j = divmod(g, 3)
        return Tile(g=g, p=p, t=p // HALVES, h=p % HALVES, j=j, buf=g % 2)

    for g in (last - 1, last):
        for to in others:
            z_copy(tile_of(g), to).wait_send()
        ax_own(tile_of(g)).wait_send()
    for i in (n_chunk - 2, n_chunk - 1):
        dx_copy(1, i, i % 2).wait_send()
    for i in (n_part - 2, n_part - 1):
        mixed_out(1, i, i % 2).wait()
    dx_out(1, n_chunk - 1).wait()

    def drain_tiles(g, carry):
        p = lax.div(g, 3)
        t, h = tower(p)
        at = Tile(g=g, p=p, t=t, h=h, j=g - 3 * p, buf=lax.rem(g, 2))
        for b in others:
            ax_copy(at, b).wait_send()
        for b in range(ZED):
            ac_copy(at, b).wait_send()
        return carry

    lax.fori_loop(0, last + 1, drain_tiles, 0)

    def drain_x(i, carry):
        x_copy(0, i).wait_send()
        x_copy(1, i).wait_send()
        return carry

    lax.fori_loop(0, n_chunk, drain_x, 0)

    def drain_w(p, carry):
        for to in others:
            w_z(p, to).wait_send()
            w_x(p, to).wait_send()
            w_c(p, to).wait_send()
        return carry

    lax.fori_loop(0, PHASES, drain_w, 0)
    for to in others:
        prod_z(to).wait_send()


def fused_call(feat, wts, cot, bias, stitch, counts, mask, flags):
    rows, deep, width = feat.shape[1], feat.shape[2], wts.shape[2]
    chunk = rows // 6
    part = chunk // SUB
    hw, kz, tile = width // 2, 2 * deep, deep // 3
    cat, xw = 4 * hw, width // 4
    lane = min(128, width)
    dma = pltpu.SemaphoreType.DMA
    anywhere = pl.BlockSpec(memory_space=pl.ANY)
    inside = pl.BlockSpec(memory_space=pltpu.VMEM)
    scalars = pl.BlockSpec(memory_space=pltpu.SMEM)

    def v(shape, kind=BF16):
        return pltpu.VMEM(shape, kind)

    out_shape = [
        jax.ShapeDtypeStruct((2, rows, width), BF16),
        jax.ShapeDtypeStruct((2, rows, deep), BF16),
        jax.ShapeDtypeStruct((2, ZED, kz, width), BF16),
        jax.ShapeDtypeStruct((2, width), F32),
        jax.ShapeDtypeStruct((2, 2, width), F32),
        jax.ShapeDtypeStruct((2, rows, deep), BF16),
        jax.ShapeDtypeStruct((2, rows, deep), BF16),
    ]
    scratch = [
        v((PHASES, kz, cat)),
        v((PHASES, rows, cat)),
        v((RING, 5, part, hw)),
        v((2, rows, hw), F32),
        v((2, chunk, kz)),
        v((PRODUCTS, ZED, part, hw), F32),
        v((2, 2, part, hw)),
        v((2, 2, part, hw)),
        v((2, chunk, deep), F32),
        v((2, chunk, deep)),
        v((chunk, deep)),
        v((chunk, deep)),
        v((rows, tile)),
        v((tile, rows)),
        v((tile, cat)),
        v((2, tile, cat)),
        v((ZED, tile, xw)),
        v((2, ZED, tile, xw)),
        v((ZED, tile, xw), F32),
        v((2, ZED, tile, xw)),
        v((rows, lane), F32),
        v((PHASES, 4, 8, hw), F32),
        v((3, 8, width), F32),
        v((2, 8, width), F32),
        v((2, 8, lane), F32),
        v((5, 8, lane), F32),
        dma((RING, 2)), dma((RING, 2)), dma((RING, 8)), dma((RING, 4)),
        dma((12,)), dma((12,)),
        dma((4, 4)), dma((4, 4)), dma((4, 4)), dma((4, 4)), dma((4, 4)), dma((4, 4)), dma((4,)),
        dma((2, 2)), dma((2,)), dma((2,)), dma((2,)), dma((12,)), dma((1,)), dma((1,)),
        dma((1,)), dma((1,)), dma((2,)), dma((4,)), dma((2, 4)), dma((2, 4)), dma((12, 4)),
        dma((2,)), dma((2,)),
        dma((12, 4)), dma((12, 4)), dma((12, 4)), dma((12, 4)), dma((8,)), dma((8,)),
    ]
    flops = 3 * 2 * 2 * rows * kz * cat * 2
    return pl.pallas_call(
        functools.partial(fused_kernel, rows, deep, width, chunk),
        out_shape=out_shape,
        in_specs=[anywhere] * 3 + [inside] * 4 + [scalars],
        out_specs=[anywhere] * 3 + [inside] * 2 + [anywhere] * 2,
        scratch_shapes=scratch,
        compiler_params=pltpu.CompilerParams(
            collective_id=0, has_side_effects=True, vmem_limit_bytes=64 * 1024 * 1024
        ),
        cost_estimate=pl.CostEstimate(
            flops=flops, bytes_accessed=200_000_000, transcendentals=2 * rows * width * 2
        ),
        name="cross_stitch_step",
    )(feat, wts, cot, bias, stitch, counts, mask, flags)


def widen_kernel(low, out):
    out[...] = wide(low[...])


def widen(low):
    tall, width = low.shape
    block = tall // 36
    spec = pl.BlockSpec((block, width), lambda i: (i, 0))
    return pl.pallas_call(
        widen_kernel,
        grid=(36,),
        in_specs=[spec],
        out_specs=spec,
        out_shape=jax.ShapeDtypeStruct(low.shape, F32),
        compiler_params=pltpu.CompilerParams(vmem_limit_bytes=48 * 1024 * 1024),
        cost_estimate=pl.CostEstimate(
            flops=tall * width, bytes_accessed=6 * tall * width, transcendentals=0
        ),
        name="widen",
    )(low)


def fused_plan(mesh):
    def per_device(features, weights, bias, stitch, cotangent, crop_counts, row_mask, flags):
        rows, deep = features.shape[1:]
        width = weights.shape[2]
        mixed, gfeat, gwt, gbias, gstitch, _, _ = fused_call(
            features, weights, cotangent, bias, stitch,
            crop_counts.reshape(1, -1), row_mask.reshape(1, -1), flags,
        )
        grad_weights = widen(gwt.reshape(-1, width)).reshape(2, ZED * 2 * deep, width)
        return mixed, gfeat, grad_weights, gbias, gstitch

    return per_device


def plan_for(mesh):
    if mesh.shape["batch"] == 4 and mesh.shape["mp"] == 2 * ZED:
        return fused_plan(mesh)
    return generic_plan(mesh)


def solution(mesh):
    in_specs = (
        P(None, "batch", "mp"),
        P(None, None, "mp"),
        P(None, "mp"),
        P(None, None, "mp"),
        P(None, "batch", "mp"),
        P("batch"),
        P("batch"),
        P(),
    )
    out_specs = (
        P(None, "batch", "mp"),
        P(None, "batch", "mp"),
        P(None, None, "mp"),
        P(None, "mp"),
        P(None, None, "mp"),
    )
    return jax.shard_map(
        plan_for(mesh), mesh=mesh, in_specs=in_specs, out_specs=out_specs, check_vma=False
    )
```

```python
import collections
import functools

import jax
import jax.numpy as jnp
from jax import lax
from jax.experimental import pallas as pl
from jax.experimental.pallas import tpu as pltpu
from jax.sharding import PartitionSpec as P

FLAG_GROUPS = 8
OUTER = 4


def row_weights(counts, mask):
    ends = jnp.cumsum(counts)
    starts = ends - counts
    index = lax.broadcasted_iota(jnp.int32, (mask.shape[0], counts.shape[0]), 0)
    inside = (index >= starts[None, :]) & (index < ends[None, :])
    count_row = jnp.sum(jnp.where(inside, counts[None, :], 0), axis=1)
    live = (count_row > 0) & (mask == 1)
    return jnp.where(live, 1.0 / jnp.maximum(count_row, 1).astype(jnp.float32), 0.0)


def project_bias(task_bias, flags):
    local_width = task_bias.shape[2]
    channel = lax.axis_index("mp") * local_width + lax.broadcasted_iota(
        jnp.int32, (local_width, FLAG_GROUPS), 0
    )
    member = (
        channel % FLAG_GROUPS == lax.broadcasted_iota(jnp.int32, (local_width, FLAG_GROUPS), 1)
    ).astype(jnp.float32)
    dots = jnp.dot(task_bias[0] * task_bias[1], member, precision=lax.Precision.HIGHEST)
    norms = jnp.einsum(
        "stc,cg->stg", task_bias * task_bias, member, precision=lax.Precision.HIGHEST
    )
    dots, norms = lax.psum((dots, norms), "mp")
    flag = flags.astype(jnp.float32)
    coef_first = jnp.dot(
        flag[0] * dots / (norms[1] + 1e-06), member.T, precision=lax.Precision.HIGHEST
    )
    coef_second = jnp.dot(
        flag[1] * dots / (norms[0] + 1e-06), member.T, precision=lax.Precision.HIGHEST
    )
    first = task_bias[0] - coef_first * task_bias[1]
    second = task_bias[1] - coef_second * task_bias[0]
    return first + second


def generic_plan(mesh):
    n_mp = mesh.shape["mp"]
    n_batch = mesh.shape["batch"]
    inner = n_mp // OUTER
    inner_groups = [[o * inner + i for i in range(inner)] for o in range(OUTER)]
    outer_groups = [[o * inner + i for o in range(OUTER)] for i in range(inner)]

    def per_device(features, weights, bias, stitch, cotangent, crop_counts, row_mask, flags):
        rows = features.shape[1]
        width = weights.shape[2]
        depth = features.shape[2] * inner
        held = lax.all_gather(
            features, "mp", axis=2, tiled=True, axis_index_groups=inner_groups
        )
        split = weights.reshape(2, OUTER, depth, width)
        block = lax.all_to_all(
            split, "mp", split_axis=1, concat_axis=1, axis_index_groups=outer_groups
        )
        block = block.reshape(2, OUTER, depth, width)
        part = jnp.einsum("trk,tokc->otrc", held, block, preferred_element_type=jnp.float32)
        linear = lax.psum_scatter(
            part.astype(jnp.bfloat16),
            "mp",
            scatter_dimension=0,
            axis_index_groups=outer_groups,
        ).astype(jnp.float32)
        pre = linear + bias[:, None, :]
        hidden, gelu_back = jax.vjp(lambda v: jax.nn.gelu(v, approximate=False), pre)
        mixed = stitch[:, 0, None, :] * hidden[0][None] + stitch[:, 1, None, :] * hidden[1][None]
        scale_rows = row_weights(crop_counts, row_mask)
        grad_out = cotangent.astype(jnp.float32) * scale_rows[None, :, None]
        first_task = gelu_back(stitch[0][:, None, :] * grad_out[0][None])[0]
        second_task = gelu_back(stitch[1][:, None, :] * grad_out[1][None])[0]
        task_bias = jnp.stack([jnp.sum(first_task, axis=1), jnp.sum(second_task, axis=1)])
        grad_linear = (first_task + second_task).astype(jnp.bfloat16)
        grad_stitch = jnp.sum(grad_out[:, None] * hidden[None], axis=2)
        every = lax.all_gather(grad_linear, "mp", axis_index_groups=outer_groups)
        grad_part = jnp.einsum(
            "otrc,tokc->trk", every, block, preferred_element_type=jnp.float32
        )
        grad_part = grad_part.astype(jnp.bfloat16).reshape(2, rows, inner, depth // inner)
        grad_features = lax.psum_scatter(
            grad_part.transpose(2, 0, 1, 3),
            "mp",
            scatter_dimension=0,
            axis_index_groups=inner_groups,
        )
        weight_part = jnp.einsum(
            "trk,otrc->otkc", held, every, preferred_element_type=jnp.float32
        )
        weight_part = weight_part.astype(jnp.bfloat16).reshape(
            OUTER, 2, n_batch, depth // n_batch, width
        )
        share = lax.psum_scatter(
            weight_part.transpose(2, 0, 1, 3, 4), "batch", scatter_dimension=0
        )
        share = lax.all_to_all(
            share, "mp", split_axis=0, concat_axis=0, axis_index_groups=outer_groups
        )
        share = share.reshape(OUTER, 2, depth // n_batch, width)
        whole = lax.all_gather(share, "batch")
        grad_weights = whole.transpose(2, 1, 0, 3, 4).reshape(2, OUTER * depth, width)
        task_bias, grad_stitch = lax.psum((task_bias, grad_stitch), "batch")
        grad_bias = project_bias(task_bias, flags)
        return (
            mixed.astype(jnp.bfloat16),
            grad_features.astype(jnp.bfloat16),
            grad_weights.astype(jnp.float32),
            grad_bias,
            grad_stitch,
        )

    return per_device


MESH = pl.DeviceIdType.MESH
BF16 = jnp.bfloat16
F32 = jnp.float32
ZED = 4
HALVES = 2
PHASES = 4
RING = 8
BAND = 32
SUB = 2
PRODUCTS = 6
WIDEN_BLOCKS = 12
WIDEN_SLOTS = 4


Part = collections.namedtuple("Part", ("u", "p", "i", "t", "h", "slot", "prod", "buf"))
Tile = collections.namedtuple("Tile", ("g", "p", "t", "h", "j", "buf"))


def half(value):
    return value.astype(BF16)


def wide(value):
    return value.astype(F32)


def fused_kernel(
    rows, deep, width, chunk,
    feat, wts, cot, bias, stitch, counts, mask, flags,
    mixed, gfeat, gwt, gbias, gstitch, xn, dxn,
    wv, gl, rs, h0, xc, pf, cc, mx, own, dsend, dfetch, dout,
    xsrc, xt, cstage, cland, xstage, xland, kept, zstage,
    scale, stat, sums, sums_land, prods, prods_land,
    rs_send, rs_recv, ag_send, ag_recv, xs_send, xs_recv,
    wz_send, wz_recv, wx_send, wx_recv, wc_send, wc_recv, wl,
    xf, cf, mxs, dx_send, dx_recv, df, dod,
    tile_in, c_send, c_recv, x_send, x_recv, z_send, z_recv, zl, zx_send,
    ax_send, ax_recv, ac_send, ac_recv, t_send, t_recv,
):
    batch, mp = lax.axis_index("batch"), lax.axis_index("mp")
    z, y = mp // 2, mp % 2
    x, c = batch // 2, batch % 2
    up = {"mp": mp + 2}
    down = {"mp": mp - 2}
    across_y = {"mp": 2 * z + 1 - y}
    across_x = {"batch": 2 * (1 - x) + c}
    across_c = {"batch": 2 * x + 1 - c}

    def at_z(other):
        return {"mp": 2 * other + y}

    others = (3 - z, (z + 2) % 4, z + 1 - 2 * (z % 2))

    n_chunk = rows // chunk
    total = PHASES * n_chunk
    part = chunk // SUB
    n_part = rows // part
    parts = PHASES * n_part
    images = counts.shape[1]
    hw = width // HALVES
    kz = 2 * deep
    quarter = deep // 2
    tile = deep // 3
    strip = quarter // 6
    xw = hw // 2

    def mult(value, unit):
        return pl.multiple_of(value, unit)

    def remote(src, dst, send, recv, device):
        return pltpu.make_async_remote_copy(
            src_ref=src, dst_ref=dst, send_sem=send, recv_sem=recv,
            device_id=device, device_id_type=MESH,
        )

    def cols(b):
        return pl.ds(mult(b * hw, hw), hw)

    def chunk_rows(i):
        return pl.ds(mult(i * chunk, chunk), chunk)

    def part_rows(i):
        return pl.ds(mult(i * part, part), part)

    def tower(p):
        t = jnp.where(p >= HALVES, 1, 0)
        return t, p - HALVES * t

    def x_copy(t, i):
        e = t * n_chunk + i
        return remote(
            feat.at[t, chunk_rows(i)], xn.at[t, chunk_rows(i)],
            xs_send.at[e], xs_recv.at[e], across_y,
        )

    def x_fetch(t, i, buf):
        return (
            pltpu.make_async_copy(
                feat.at[t, chunk_rows(i)],
                xc.at[buf, :, pl.ds(mult(deep * y, deep), deep)], xf.at[buf, 0],
            ),
            pltpu.make_async_copy(
                xn.at[t, chunk_rows(i)],
                xc.at[buf, :, pl.ds(mult(deep * (1 - y), deep), deep)], xf.at[buf, 1],
            ),
        )

    def cot_fetch(h, i, buf):
        return pltpu.make_async_copy(
            cot.at[:, part_rows(i), cols(h)], cc.at[buf], cf.at[buf]
        )

    def w_own(p):
        t, h = tower(p)
        return pltpu.make_async_copy(
            wts.at[t, pl.ds(mult(kz * z, kz), kz), cols(h)], wv.at[p, :, cols(z)], wl.at[p],
        )

    def w_rows():
        return pl.ds(mult(deep * c + quarter * x, quarter), quarter)

    def w_z(p, to):
        t, h = tower(p)
        return remote(
            wts.at[
                t, pl.ds(mult(kz * to + deep * c + quarter * x, quarter), quarter), cols(h)
            ],
            wv.at[p, w_rows(), cols(z)],
            wz_send.at[p, to], wz_recv.at[p, z], at_z(to),
        )

    def w_z_strip(p, to, r):
        t, h = tower(p)
        at = deep * c + quarter * x + strip * r
        return remote(
            wts.at[t, pl.ds(mult(kz * to + at, strip), strip), cols(h)],
            wv.at[p, pl.ds(mult(at, strip), strip), cols(z)],
            wz_send.at[p, to], wz_recv.at[p, z], at_z(to),
        )

    def w_z_in(p, frm):
        here = wv.at[p, w_rows(), cols(frm)]
        return remote(here, here, wz_send.at[p, frm], wz_recv.at[p, frm], at_z(frm))

    def w_x(p, b):
        here = wv.at[p, w_rows(), cols(b)]
        return remote(here, here, wx_send.at[p, b], wx_recv.at[p, b], across_x)

    def w_x_in(p, b):
        here = wv.at[
            p, pl.ds(mult(deep * c + quarter * (1 - x), quarter), quarter), cols(b)
        ]
        return remote(here, here, wx_send.at[p, b], wx_recv.at[p, b], across_x)

    def w_c(p, b):
        here = wv.at[p, pl.ds(mult(deep * c, deep), deep), cols(b)]
        return remote(here, here, wc_send.at[p, b], wc_recv.at[p, b], across_c)

    def w_c_in(p, b):
        here = wv.at[p, pl.ds(mult(deep * (1 - c), deep), deep), cols(b)]
        return remote(here, here, wc_send.at[p, b], wc_recv.at[p, b], across_c)

    def rs_up(slot, zz):
        run = rs.at[slot, zz + 2 : ZED + 1]
        return remote(run, run, rs_send.at[slot, 0], rs_recv.at[slot, 0], up)

    def rs_down(slot, zz):
        run = rs.at[slot, 0:zz]
        return remote(run, run, rs_send.at[slot, 1], rs_recv.at[slot, 1], down)

    def rs_from_below(slot, zz):
        run = rs.at[slot, zz + 1 : ZED + 1]
        return remote(run, run, rs_send.at[slot, 0], rs_recv.at[slot, 0], down)

    def rs_from_above(slot, zz):
        run = rs.at[slot, 0 : zz + 1]
        return remote(run, run, rs_send.at[slot, 1], rs_recv.at[slot, 1], up)

    def at_place(first, last, do):
        for zz in range(first, last + 1):
            @pl.when(z == zz)
            def _(zz=zz):
                do(zz)

    def ag(at, b, going, device):
        here = gl.at[at.p, part_rows(at.i), cols(b)]
        return remote(
            here, here, ag_send.at[at.slot, going * ZED + b], ag_recv.at[at.slot, b], device
        )

    def dx_copy(t, i, buf):
        return remote(
            dsend.at[buf], dxn.at[t, chunk_rows(i)],
            dx_send.at[buf], dx_recv.at[t * n_chunk + i], across_y,
        )

    def dx_fetch(t, i):
        return pltpu.make_async_copy(dxn.at[t, chunk_rows(i)], dfetch, df.at[0])

    def dx_out(t, i):
        return pltpu.make_async_copy(dout, gfeat.at[t, chunk_rows(i)], dod.at[0])

    def mixed_out(h, i, buf):
        return pltpu.make_async_copy(
            mx.at[buf], mixed.at[:, part_rows(i), cols(h)], mxs.at[buf]
        )

    def tile_fetch(t, j, hk, start):
        lanes = pl.ds(mult(tile * j, tile), tile)
        near = pltpu.make_async_copy(feat.at[t, :, lanes], xsrc, tile_in.at[0])
        if not start:
            near.wait()
            return

        @pl.when(hk == y)
        def _():
            near.start()

        @pl.when(hk != y)
        def _():
            pltpu.make_async_copy(xn.at[t, :, lanes], xsrc, tile_in.at[0]).start()

    def core_copy(g):
        return remote(cstage, cland.at[g.buf], c_send.at[0], c_recv.at[g.buf], across_c)

    def across_copy(g, b):
        return remote(
            xstage.at[b], xland.at[g.buf, b], x_send.at[b], x_recv.at[g.buf, b], across_x
        )

    def piece(g, source, core, lanes, n_lanes):
        return gwt.at[
            g.t, source,
            pl.ds(mult(deep * core + tile * g.j, tile), tile),
            pl.ds(mult(hw * g.h + lanes, xw), n_lanes),
        ]

    def z_copy(g, to):
        return remote(
            zstage.at[g.buf, to], piece(g, z, c, xw * x, xw),
            z_send.at[g.buf, to], z_recv.at[g.g, z], at_z(to),
        )

    def z_in(g, frm):
        here = piece(g, frm, c, xw * x, xw)
        return remote(here, here, z_send.at[g.buf, frm], z_recv.at[g.g, frm], at_z(frm))

    def z_own(g):
        return pltpu.make_async_copy(
            zstage.at[g.buf, z], piece(g, z, c, xw * x, xw), zl.at[g.buf]
        )

    def ax_own(g):
        return remote(
            zstage.at[g.buf, z], piece(g, z, c, xw * x, xw),
            zx_send.at[g.buf], ax_recv.at[g.g, z], across_x,
        )

    def ax_copy(g, b):
        here = piece(g, b, c, xw * x, xw)
        return remote(here, here, ax_send.at[g.g, b], ax_recv.at[g.g, b], across_x)

    def ax_in(g, b):
        here = piece(g, b, c, xw * (1 - x), xw)
        return remote(here, here, ax_send.at[g.g, b], ax_recv.at[g.g, b], across_x)

    def ac_copy(g, b):
        here = piece(g, b, c, 0, hw)
        return remote(here, here, ac_send.at[g.g, b], ac_recv.at[g.g, b], across_c)

    def ac_in(g, b):
        here = piece(g, b, 1 - c, 0, hw)
        return remote(here, here, ac_send.at[g.g, b], ac_recv.at[g.g, b], across_c)

    def sum_copy(stage, device):
        return remote(
            sums.at[stage], sums_land.at[stage], t_send.at[stage], t_recv.at[stage], device
        )

    def prod_y():
        return remote(prods.at[0], prods_land.at[ZED], t_send.at[2], t_recv.at[2], across_y)

    def prod_z(to):
        return remote(
            prods.at[1], prods_land.at[z], t_send.at[3 + to], t_recv.at[3 + z], at_z(to)
        )

    def prod_z_in(frm):
        here = prods_land.at[frm]
        return remote(here, here, t_send.at[3 + frm], t_recv.at[3 + frm], at_z(frm))

    barrier = pltpu.get_barrier_semaphore()
    for device in [at_z(o) for o in others] + [across_y, across_x, across_c]:
        pl.semaphore_signal(barrier, inc=1, device_id=device, device_id_type=MESH)
    pl.semaphore_wait(barrier, 6)

    for to in others:
        w_z(0, to).start()
    x_copy(0, 0).start()
    x_copy(0, 1).start()
    w_own(0).start()
    cot_fetch(0, 0, 0).start()

    image_row = lax.broadcasted_iota(jnp.int32, (images, images), 0)
    image_col = lax.broadcasted_iota(jnp.int32, (images, images), 1)
    crops = counts[...].astype(F32)
    ends = jnp.dot(
        jnp.broadcast_to(crops, (8, images)), (image_row <= image_col).astype(F32),
        precision=lax.Precision.HIGHEST, preferred_element_type=F32,
    )[0:1]
    starts = ends - crops
    block = mask.shape[1]
    lane = scale.shape[1]

    for r in range(rows // block):
        index = (
            lax.broadcasted_iota(jnp.int32, (block, images), 0) + r * block
        ).astype(F32)
        inside = (index >= starts) & (index < ends)
        count_row = jnp.sum(jnp.where(inside, crops, 0.0), axis=1, keepdims=True)
        diagonal = lax.broadcasted_iota(jnp.int32, (block, block), 0) == (
            lax.broadcasted_iota(jnp.int32, (block, block), 1)
        )
        usable = jnp.sum(
            jnp.where(diagonal, mask[r : r + 1, :].astype(F32), 0.0),
            axis=1, keepdims=True,
        )
        live = (count_row > 0.0) & (usable == 1.0)
        share = jnp.where(live, 1.0 / jnp.maximum(count_row, 1.0), 0.0)
        scale[r * block : (r + 1) * block, :] = jnp.broadcast_to(share, (block, lane))

    for frm in others:
        w_z_in(0, frm).wait_recv()
        w_x(0, frm).start()
    for to in others:
        w_z(1, to).start()
    w_own(1).start()
    for frm in others:
        w_x_in(0, frm).wait_recv()
        w_c(0, frm).start()
    x_copy(0, 0).wait_recv()
    for copy in x_fetch(0, 0, 0):
        copy.start()

    def final(at, later):
        p, i, slot, t, h, buf = at.p, at.i, at.slot, at.t, at.h, at.buf
        cot_fetch(h, i, buf).wait()

        @pl.when(at.u >= 2 * n_part + 2)
        def _():
            mixed_out(h, i, buf).wait()

        @pl.when(i == 0)
        def _():
            stat[p] = jnp.zeros(stat.shape[1:], F32)

        lanes = cols(h)
        shift = bias[pl.ds(t, 1), lanes]
        st = [stitch[s, pl.ds(t, 1), lanes] for s in range(2)]
        band = min(BAND, part)

        def step(r, carry):
            here = part_rows_of(r, band)
            there = pl.ds(mult(i * part + r * band, band), band)
            value = pf[at.prod, z, here, :]
            below = wide(rs[slot, z + 1, here, :])
            above = wide(rs[slot, z, here, :])
            value = value + jnp.where(z > 0, below, 0.0) + jnp.where(z < ZED - 1, above, 0.0)
            pre = value + shift
            phi = 0.5 * (1.0 + lax.erf(pre * 0.7071067811865476))
            hidden = pre * phi
            slope = phi + pre * (jnp.exp(-0.5 * pre * pre) * 0.3989422804014327)
            weight = scale[there, 0:1]
            first = wide(cc[buf, 0, here, :]) * weight
            second = wide(cc[buf, 1, here, :]) * weight
            back0 = st[0] * first * slope
            back1 = st[1] * second * slope
            gl[p, there, cols(z)] = half(back0 + back1)

            def fold(v):
                return jnp.sum(v.reshape(band // 8, 8, hw), axis=0)

            stat[p, 0] += fold(back0)
            stat[p, 1] += fold(back1)
            stat[p, 2] += fold(first * hidden)
            stat[p, 3] += fold(second * hidden)

            @pl.when(t == 0)
            def _():
                h0[h, there, :] = hidden

            @pl.when(t == 1)
            def _():
                before = h0[h, there, :]
                for s in range(2):
                    mx[buf, s, here, :] = half(
                        stitch[s, 0:1, lanes] * before + st[s] * hidden
                    )

            return carry

        lax.fori_loop(0, part // band, step, 0)

        @pl.when(z < ZED - 1)
        def _():
            ag(at, z, 0, up).start()

        @pl.when(z > 0)
        def _():
            ag(at, z, 1, down).start()

        @pl.when(t == 1)
        def _():
            mixed_out(h, i, buf).start()

        @pl.when(at.u + 1 < parts)
        def _():
            cot_fetch(later.h, later.i, later.buf).start()

    def part_rows_of(r, band):
        return pl.ds(mult(r * band, band), band)

    def forward_ag(at, far):
        @pl.when((at.u >= 0) & (at.u < parts))
        def _():
            @pl.when(z - far >= 0)
            def _():
                ag(at, z - far, 0, up).wait_recv()

                @pl.when(z < ZED - 1)
                def _():
                    ag(at, z - far, 0, up).start()

            @pl.when(z + far < ZED)
            def _():
                ag(at, z + far, 1, down).wait_recv()

                @pl.when(z > 0)
                def _():
                    ag(at, z + far, 1, down).start()

    def dx_part(t, i, hk):
        there = chunk_rows(i)
        krows = pl.ds(mult(deep * hk, deep), deep)
        acc = None
        for h in range(HALVES):
            term = lax.dot_general(
                gl[2 * t + h, there, :], wv[2 * t + h, krows, :],
                (((1,), (1,)), ((), ())), preferred_element_type=F32,
            )
            acc = term if acc is None else acc + term
        return acc

    def dx_step(t, i, buf):
        @pl.when((i >= 2) | (t > 0))
        def _():
            dx_copy(t, i, buf).wait_send()

        dsend[buf] = half(dx_part(t, i, 1 - y))
        dx_copy(t, i, buf).start()
        own[buf] = dx_part(t, i, y)

    def dx_begin(t, i, buf):
        dx_copy(t, i, buf).wait_recv()
        dx_fetch(t, i).start()

    def dx_final(t, i, buf):
        @pl.when((i >= 1) | (t > 0))
        def _():
            dx_out(t, i).wait()

        dx_fetch(t, i).wait()

        def step(j, inner):
            lanes = pl.ds(mult(tile * j, tile), tile)
            dout[:, lanes] = half(own[buf, :, lanes] + wide(dfetch[:, lanes]))
            return inner

        lax.fori_loop(0, 3, step, 0)
        dx_out(t, i).start()

    def features_at(at, do):
        i = lax.div(at.i, SUB)

        @pl.when((at.u >= 0) & (at.u < parts) & (i * SUB == at.i) & (at.h == 1))
        def _():
            do(at.t, i, lax.rem(i, 2))

    def turn():
        lanes_at_once = min(128, tile)

        def step(q, carry):
            lanes = pl.ds(mult(q * lanes_at_once, lanes_at_once), lanes_at_once)
            xt[lanes, :] = xsrc[:, lanes].T
            return carry

        lax.fori_loop(0, tile // lanes_at_once, step, 0)

    def tile_dot(g):
        return jnp.dot(xt[...], gl[g.p], preferred_element_type=F32)

    def stage_one(g):
        tile_fetch(g.t, g.j, 1 - c, False)
        turn()
        tile_fetch(g.t, g.j, c, True)
        cstage[...] = half(tile_dot(g))
        core_copy(g).start()

    def stage_two(g):
        tile_fetch(g.t, g.j, c, False)
        turn()

        @pl.when(g.j < 2)
        def _():
            tile_fetch(g.t, g.j + 1, 1 - c, True)

        core_copy(g).wait()
        product = tile_dot(g)
        for b in range(ZED):
            block = product[:, b * hw : (b + 1) * hw] + wide(
                cland[g.buf, :, b * hw : (b + 1) * hw]
            )
            left, right = block[:, :xw], block[:, xw:]
            kept[b] = jnp.where(x == 0, left, right)
            xstage[b] = half(jnp.where(x == 0, right, left))

        def send(q, carry):
            across_copy(g, lax.rem(z + 3 + 3 * q, ZED)).start()
            return carry

        lax.fori_loop(0, ZED, send, 0)

    def stage_three(g):
        @pl.when(g.g >= 2)
        def _():
            for to in others:
                z_copy(g, to).wait_send()
            ax_own(g).wait_send()

        def add(b):
            across_copy(g, b).wait()
            zstage[g.buf, b] = half(kept[b] + wide(xland[g.buf, b]))

        def step(q, carry):
            b = lax.rem(z + 3 + 3 * q, ZED)
            add(b)
            z_copy(g, b).start()
            return carry

        lax.fori_loop(0, ZED - 1, step, 0)
        add(z)
        z_own(g).start()
        ax_own(g).start()

    def stage_four(g):
        def step(q, carry):
            b = lax.rem(z + 1 + q, ZED)
            z_in(g, b).wait_recv()
            ax_copy(g, b).start()
            return carry

        lax.fori_loop(0, ZED - 1, step, 0)
        z_own(g).wait()

    def stage_five(g):
        def step(q, carry):
            b = lax.rem(z + q, ZED)
            ax_in(g, b).wait_recv()
            ac_copy(g, b).start()
            return carry

        lax.fori_loop(0, ZED, step, 0)

    def stage_six(g):
        def step(b, carry):
            ac_in(g, b).wait_recv()
            return carry

        lax.fori_loop(0, ZED, step, 0)

    first_tile = n_part + 6

    def tiles_at(at, do):
        j = lax.div(at.i, 4)
        p = at.p - 1

        @pl.when((p >= 0) & (p < PHASES) & (4 * j == at.i))
        def _():
            t, h = tower(p)
            g = 3 * p + j
            do(Tile(g=g, p=p, t=t, h=h, j=j, buf=lax.rem(g, 2)))

    def body(u, carry):
        p0 = lax.div(u, n_part)
        i0 = u - p0 * n_part
        slot0, prod0 = lax.rem(u, RING), lax.rem(u, PRODUCTS)
        buf0 = lax.rem(u, 2)

        def before(lag):
            if isinstance(lag, int):
                whole, left = divmod(lag, n_part)
            else:
                whole, left = 0, lag
            under = i0 < left
            p = p0 - whole - jnp.where(under, 1, 0)
            i = i0 - left + jnp.where(under, n_part, 0)
            in_ring = lag % RING if isinstance(lag, int) else lag
            in_prods = lag % PRODUCTS if isinstance(lag, int) else lag
            slot = slot0 - in_ring + jnp.where(slot0 < in_ring, RING, 0)
            prod = prod0 - in_prods + jnp.where(prod0 < in_prods, PRODUCTS, 0)
            t, h = tower(p)
            return Part(u=u - lag, p=p, i=i, t=t, h=h, slot=slot, prod=prod, buf=lax.rem(i, 2))

        @pl.when((u >= 5) & (u < parts + 5))
        def _():
            slot = before(5).slot
            at_place(0, ZED - 2, lambda zz: rs_up(slot, zz).wait_send())
            at_place(1, ZED - 1, lambda zz: rs_down(slot, zz).wait_send())

        @pl.when((u >= 8) & (u < parts + 8))
        def _():
            at = before(8)

            def step(b, inner):
                @pl.when((z < ZED - 1) & (b <= z))
                def _():
                    ag(at, b, 0, up).wait_send()

                @pl.when((z > 0) & (b >= z))
                def _():
                    ag(at, b, 1, down).wait_send()

                return inner

            lax.fori_loop(0, ZED, step, 0)

        ck = lax.div(i0, SUB)
        fresh = ck * SUB == i0
        t0, h0_ = tower(p0)
        xbuf = lax.rem(ck, 2)

        @pl.when((u < parts) & fresh)
        def _():
            @pl.when(i0 == 0)
            def _():
                w_own(p0).wait()
                for frm in others:
                    w_c_in(p0, frm).wait_recv()

            for copy in x_fetch(t0, ck, xbuf):
                copy.wait()

            product = jnp.dot(xc[xbuf], wv[p0], preferred_element_type=F32)
            for b in range(ZED):
                for s in range(SUB):
                    pf[prod0 + s, b] = product[
                        s * part : (s + 1) * part, b * hw : (b + 1) * hw
                    ]

        going_up = before(z)

        @pl.when((going_up.u >= 0) & (going_up.u < parts))
        def _():
            slot, prod = going_up.slot, going_up.prod
            at_place(1, ZED - 1, lambda zz: rs_from_below(slot, zz).wait_recv())

            @pl.when(z == 0)
            def _():
                for b in range(1, ZED):
                    rs[slot, b + 1] = half(pf[prod, b])

            @pl.when(z > 0)
            def _():
                def step(b, inner):
                    rs[slot, b + 1] = half(wide(rs[slot, b + 1]) + pf[prod, b])
                    return inner

                lax.fori_loop(z + 1, ZED, step, 0)

            at_place(0, ZED - 2, lambda zz: rs_up(slot, zz).start())

        going_down = before(ZED - 1 - z)

        @pl.when((going_down.u >= 0) & (going_down.u < parts))
        def _():
            slot, prod = going_down.slot, going_down.prod
            at_place(0, ZED - 2, lambda zz: rs_from_above(slot, zz).wait_recv())

            @pl.when(z == ZED - 1)
            def _():
                for b in range(ZED - 1):
                    rs[slot, b] = half(pf[prod, b])

            @pl.when(z < ZED - 1)
            def _():
                def step(b, inner):
                    rs[slot, b] = half(wide(rs[slot, b]) + pf[prod, b])
                    return inner

                lax.fori_loop(0, z, step, 0)

            at_place(1, ZED - 1, lambda zz: rs_down(slot, zz).start())

        @pl.when(fresh & (u + 2 * SUB < 2 * n_part))
        def _():
            k = p0 * n_chunk + ck + 2
            over = jnp.where(k >= n_chunk, 1, 0)
            x_copy(over, k - over * n_chunk).start()

        @pl.when(fresh & (u + SUB < parts))
        def _():
            wrap = jnp.where(ck + 1 == n_chunk, 1, 0)
            i = ck + 1 - wrap * n_chunk
            t, h = tower(p0 + wrap)

            @pl.when(h == 0)
            def _():
                x_copy(t, i).wait_recv()

            for copy in x_fetch(t, i, lax.rem(i, 2)):
                copy.start()

        @pl.when((u >= 3) & (u < parts + 3))
        def _():
            final(before(3), before(2))

        forward_ag(before(4), 1)
        forward_ag(before(5), 2)
        forward_ag(before(6), 3)

        features_at(before(6 + 2 * SUB), dx_begin)
        features_at(before(7 + 2 * SUB), dx_final)
        features_at(before(7), dx_step)

        tiles_at(before(11), stage_three)
        tiles_at(before(8), stage_two)
        tiles_at(before(6), stage_one)
        tiles_at(before(14), stage_four)
        tiles_at(before(16), stage_five)
        tiles_at(before(18), stage_six)

        @pl.when((i0 == 5) & (p0 > 0) & (p0 < PHASES + 1))
        def _():
            t, _h = tower(p0 - 1)
            tile_fetch(t, 0, 1 - c, True)

        @pl.when(p0 + 1 < PHASES)
        def _():
            @pl.when((i0 < 6) & (p0 > 0))
            def _():
                for to in others:
                    w_z_strip(p0 + 1, to, i0).start()

            for q in range(3):
                @pl.when(i0 == q + 7)
                def _(q=q):
                    w_z_in(p0 + 1, others[q]).wait_recv()
                    w_x(p0 + 1, others[q]).start()

                @pl.when(i0 == q + 9)
                def _(q=q):
                    w_x_in(p0 + 1, others[q]).wait_recv()
                    w_c(p0 + 1, others[q]).start()

            @pl.when((i0 == 1) & (p0 > 0))
            def _():
                w_own(p0 + 1).start()

        @pl.when(u == parts + 3)
        def _():
            for p in range(PHASES):
                t, h = p // HALVES, p % HALVES
                for s in range(2):
                    for what in range(2):
                        sums[0, pl.ds(4 * what + 2 * s + t, 1), h * hw : (h + 1) * hw] = jnp.sum(
                            stat[p, 2 * what + s], axis=0, keepdims=True
                        )
            sum_copy(0, across_c).start()

        @pl.when(u == parts + 4)
        def _():
            sum_copy(0, across_c).wait()
            sums[1] = sums[0] + sums_land[0]
            sum_copy(1, across_x).start()

        @pl.when(u == parts + 5)
        def _():
            sum_copy(1, across_x).wait()
            both = sums[1] + sums_land[1]
            sums[2] = both
            member = (
                lax.broadcasted_iota(jnp.int32, (width, lane), 0) % FLAG_GROUPS
                == lax.broadcasted_iota(jnp.int32, (width, lane), 1) % FLAG_GROUPS
            ).astype(F32)
            bias_rows = both[0:4]
            inner = both[0:2] * both[2:4]
            stack = jnp.concatenate([inner, bias_rows * bias_rows, inner], axis=0)
            prods[0] = jnp.dot(
                stack, member, precision=lax.Precision.HIGHEST, preferred_element_type=F32
            )
            prod_y().start()

        @pl.when(u == parts + 6)
        def _():
            prod_y().wait()
            prods[1] = prods[0] + prods_land[ZED]
            for to in others:
                prod_z(to).start()

        @pl.when(u == parts + 7)
        def _():
            for frm in others:
                prod_z_in(frm).wait_recv()
            prods_land[z] = prods[1]
            whole = prods_land[0] + prods_land[1] + prods_land[2] + prods_land[3]
            both = sums[2]
            group = lax.broadcasted_iota(jnp.int32, (1, lane), 1) % FLAG_GROUPS

            def over(row):
                return jnp.concatenate([row] * (width // lane), axis=1)

            def flag_row(s, t):
                row = jnp.zeros((1, lane), F32)
                for g in range(FLAG_GROUPS):
                    row = jnp.where(group == g, flags[s, t, g].astype(F32), row)
                return row

            for t in range(2):
                task0, task1 = both[t : t + 1], both[2 + t : 3 + t]
                dots = whole[t : t + 1]
                coef0 = over(flag_row(0, t) * dots / (whole[4 + t : 5 + t] + 1e-06))
                coef1 = over(flag_row(1, t) * dots / (whole[2 + t : 3 + t] + 1e-06))
                gbias[t : t + 1] = (task0 - coef0 * task1) + (task1 - coef1 * task0)
            for s in range(2):
                gstitch[s] = both[4 + 2 * s : 6 + 2 * s]

        return carry

    lax.fori_loop(0, first_tile + n_part * (PHASES - 1) + 21, body, 0)

    last = 3 * PHASES - 1

    def tile_of(g):
        p, j = divmod(g, 3)
        return Tile(g=g, p=p, t=p // HALVES, h=p % HALVES, j=j, buf=g % 2)

    for g in (last - 1, last):
        for to in others:
            z_copy(tile_of(g), to).wait_send()
        ax_own(tile_of(g)).wait_send()
    for i in (n_chunk - 2, n_chunk - 1):
        dx_copy(1, i, i % 2).wait_send()
    for i in (n_part - 2, n_part - 1):
        mixed_out(1, i, i % 2).wait()
    dx_out(1, n_chunk - 1).wait()

    def drain_tiles(g, carry):
        p = lax.div(g, 3)
        t, h = tower(p)
        at = Tile(g=g, p=p, t=t, h=h, j=g - 3 * p, buf=lax.rem(g, 2))
        for b in others:
            ax_copy(at, b).wait_send()
        for b in range(ZED):
            ac_copy(at, b).wait_send()
        return carry

    lax.fori_loop(0, last + 1, drain_tiles, 0)

    def drain_x(i, carry):
        x_copy(0, i).wait_send()
        x_copy(1, i).wait_send()
        return carry

    lax.fori_loop(0, n_chunk, drain_x, 0)

    def drain_w(p, carry):
        for to in others:
            w_z(p, to).wait_send()
            w_x(p, to).wait_send()
            w_c(p, to).wait_send()
        return carry

    lax.fori_loop(0, PHASES, drain_w, 0)
    for to in others:
        prod_z(to).wait_send()


def fused_call(feat, wts, cot, bias, stitch, counts, mask, flags):
    rows, deep, width = feat.shape[1], feat.shape[2], wts.shape[2]
    chunk = rows // 6
    part = chunk // SUB
    hw, kz, tile = width // 2, 2 * deep, deep // 3
    cat, xw = 4 * hw, width // 4
    lane = min(128, width)
    dma = pltpu.SemaphoreType.DMA
    anywhere = pl.BlockSpec(memory_space=pl.ANY)
    inside = pl.BlockSpec(memory_space=pltpu.VMEM)
    scalars = pl.BlockSpec(memory_space=pltpu.SMEM)

    def v(shape, kind=BF16):
        return pltpu.VMEM(shape, kind)

    out_shape = [
        jax.ShapeDtypeStruct((2, rows, width), BF16),
        jax.ShapeDtypeStruct((2, rows, deep), BF16),
        jax.ShapeDtypeStruct((2, ZED, kz, width), BF16),
        jax.ShapeDtypeStruct((2, width), F32),
        jax.ShapeDtypeStruct((2, 2, width), F32),
        jax.ShapeDtypeStruct((2, rows, deep), BF16),
        jax.ShapeDtypeStruct((2, rows, deep), BF16),
    ]
    scratch = [
        v((PHASES, kz, cat)),
        v((PHASES, rows, cat)),
        v((RING, 5, part, hw)),
        v((2, rows, hw), F32),
        v((2, chunk, kz)),
        v((PRODUCTS, ZED, part, hw), F32),
        v((2, 2, part, hw)),
        v((2, 2, part, hw)),
        v((2, chunk, deep), F32),
        v((2, chunk, deep)),
        v((chunk, deep)),
        v((chunk, deep)),
        v((rows, tile)),
        v((tile, rows)),
        v((tile, cat)),
        v((2, tile, cat)),
        v((ZED, tile, xw)),
        v((2, ZED, tile, xw)),
        v((ZED, tile, xw), F32),
        v((2, ZED, tile, xw)),
        v((rows, lane), F32),
        v((PHASES, 4, 8, hw), F32),
        v((3, 8, width), F32),
        v((2, 8, width), F32),
        v((2, 8, lane), F32),
        v((5, 8, lane), F32),
        dma((RING, 2)), dma((RING, 2)), dma((RING, 8)), dma((RING, 4)),
        dma((12,)), dma((12,)),
        dma((4, 4)), dma((4, 4)), dma((4, 4)), dma((4, 4)), dma((4, 4)), dma((4, 4)), dma((4,)),
        dma((2, 2)), dma((2,)), dma((2,)), dma((2,)), dma((12,)), dma((1,)), dma((1,)),
        dma((1,)), dma((1,)), dma((2,)), dma((4,)), dma((2, 4)), dma((2, 4)), dma((12, 4)),
        dma((2,)), dma((2,)),
        dma((12, 4)), dma((12, 4)), dma((12, 4)), dma((12, 4)), dma((8,)), dma((8,)),
    ]
    flops = 3 * 2 * 2 * rows * kz * cat * 2
    return pl.pallas_call(
        functools.partial(fused_kernel, rows, deep, width, chunk),
        out_shape=out_shape,
        in_specs=[anywhere] * 3 + [inside] * 4 + [scalars],
        out_specs=[anywhere] * 3 + [inside] * 2 + [anywhere] * 2,
        scratch_shapes=scratch,
        compiler_params=pltpu.CompilerParams(
            collective_id=0, has_side_effects=True, vmem_limit_bytes=64 * 1024 * 1024
        ),
        cost_estimate=pl.CostEstimate(
            flops=flops, bytes_accessed=200_000_000, transcendentals=2 * rows * width * 2
        ),
        name="cross_stitch_step",
    )(feat, wts, cot, bias, stitch, counts, mask, flags)


def widen_kernel(block, low, out, taken, given, in_sem, out_sem):
    n_block = low.shape[0] // block

    def take(i):
        return pltpu.make_async_copy(
            low.at[pl.ds(i * block, block)], taken.at[i % WIDEN_SLOTS], in_sem.at[i % WIDEN_SLOTS]
        )

    def give(i):
        return pltpu.make_async_copy(
            given.at[i % WIDEN_SLOTS], out.at[pl.ds(i * block, block)], out_sem.at[i % WIDEN_SLOTS]
        )

    for i in range(min(WIDEN_SLOTS, n_block)):
        take(i).start()
    for i in range(n_block):
        slot = i % WIDEN_SLOTS
        take(i).wait()
        if i >= WIDEN_SLOTS:
            give(i - WIDEN_SLOTS).wait()
        given[slot] = wide(taken[slot])
        give(i).start()
        if i + WIDEN_SLOTS < n_block:
            take(i + WIDEN_SLOTS).start()
    for i in range(max(0, n_block - WIDEN_SLOTS), n_block):
        give(i).wait()


def widen(low):
    tall, width = low.shape
    block = tall // WIDEN_BLOCKS
    anywhere = pl.BlockSpec(memory_space=pl.ANY)
    return pl.pallas_call(
        functools.partial(widen_kernel, block),
        in_specs=[anywhere],
        out_specs=anywhere,
        out_shape=jax.ShapeDtypeStruct(low.shape, F32),
        scratch_shapes=[
            pltpu.VMEM((WIDEN_SLOTS, block, width), BF16),
            pltpu.VMEM((WIDEN_SLOTS, block, width), F32),
            pltpu.SemaphoreType.DMA((WIDEN_SLOTS,)),
            pltpu.SemaphoreType.DMA((WIDEN_SLOTS,)),
        ],
        compiler_params=pltpu.CompilerParams(vmem_limit_bytes=48 * 1024 * 1024),
        cost_estimate=pl.CostEstimate(
            flops=tall * width, bytes_accessed=6 * tall * width, transcendentals=0
        ),
        name="widen",
    )(low)


def fused_plan(mesh):
    def per_device(features, weights, bias, stitch, cotangent, crop_counts, row_mask, flags):
        rows, deep = features.shape[1:]
        width = weights.shape[2]
        mixed, gfeat, gwt, gbias, gstitch, _, _ = fused_call(
            features, weights, cotangent, bias, stitch,
            crop_counts.reshape(1, -1), row_mask.reshape(-1, min(128, rows // 6)), flags,
        )
        grad_weights = widen(gwt.reshape(-1, width)).reshape(2, ZED * 2 * deep, width)
        return mixed, gfeat, grad_weights, gbias, gstitch

    return per_device


def plan_for(mesh):
    if mesh.shape["batch"] == 4 and mesh.shape["mp"] == 2 * ZED:
        return fused_plan(mesh)
    return generic_plan(mesh)


def solution(mesh):
    in_specs = (
        P(None, "batch", "mp"),
        P(None, None, "mp"),
        P(None, "mp"),
        P(None, None, "mp"),
        P(None, "batch", "mp"),
        P("batch"),
        P("batch"),
        P(),
    )
    out_specs = (
        P(None, "batch", "mp"),
        P(None, "batch", "mp"),
        P(None, None, "mp"),
        P(None, "mp"),
        P(None, None, "mp"),
    )
    return jax.shard_map(
        plan_for(mesh), mesh=mesh, in_specs=in_specs, out_specs=out_specs, check_vma=False
    )
```

```python
import collections
import functools

import jax
import jax.numpy as jnp
from jax import lax
from jax.experimental import pallas as pl
from jax.experimental.pallas import tpu as pltpu
from jax.sharding import PartitionSpec as P

FLAG_GROUPS = 8
OUTER = 4


def row_weights(counts, mask):
    ends = jnp.cumsum(counts)
    starts = ends - counts
    index = lax.broadcasted_iota(jnp.int32, (mask.shape[0], counts.shape[0]), 0)
    inside = (index >= starts[None, :]) & (index < ends[None, :])
    count_row = jnp.sum(jnp.where(inside, counts[None, :], 0), axis=1)
    live = (count_row > 0) & (mask == 1)
    return jnp.where(live, 1.0 / jnp.maximum(count_row, 1).astype(jnp.float32), 0.0)


def project_bias(task_bias, flags):
    local_width = task_bias.shape[2]
    channel = lax.axis_index("mp") * local_width + lax.broadcasted_iota(
        jnp.int32, (local_width, FLAG_GROUPS), 0
    )
    member = (
        channel % FLAG_GROUPS == lax.broadcasted_iota(jnp.int32, (local_width, FLAG_GROUPS), 1)
    ).astype(jnp.float32)
    dots = jnp.dot(task_bias[0] * task_bias[1], member, precision=lax.Precision.HIGHEST)
    norms = jnp.einsum(
        "stc,cg->stg", task_bias * task_bias, member, precision=lax.Precision.HIGHEST
    )
    dots, norms = lax.psum((dots, norms), "mp")
    flag = flags.astype(jnp.float32)
    coef_first = jnp.dot(
        flag[0] * dots / (norms[1] + 1e-06), member.T, precision=lax.Precision.HIGHEST
    )
    coef_second = jnp.dot(
        flag[1] * dots / (norms[0] + 1e-06), member.T, precision=lax.Precision.HIGHEST
    )
    first = task_bias[0] - coef_first * task_bias[1]
    second = task_bias[1] - coef_second * task_bias[0]
    return first + second


def generic_plan(mesh):
    n_mp = mesh.shape["mp"]
    n_batch = mesh.shape["batch"]
    inner = n_mp // OUTER
    inner_groups = [[o * inner + i for i in range(inner)] for o in range(OUTER)]
    outer_groups = [[o * inner + i for o in range(OUTER)] for i in range(inner)]

    def per_device(features, weights, bias, stitch, cotangent, crop_counts, row_mask, flags):
        rows = features.shape[1]
        width = weights.shape[2]
        depth = features.shape[2] * inner
        held = lax.all_gather(
            features, "mp", axis=2, tiled=True, axis_index_groups=inner_groups
        )
        split = weights.reshape(2, OUTER, depth, width)
        block = lax.all_to_all(
            split, "mp", split_axis=1, concat_axis=1, axis_index_groups=outer_groups
        )
        block = block.reshape(2, OUTER, depth, width)
        part = jnp.einsum("trk,tokc->otrc", held, block, preferred_element_type=jnp.float32)
        linear = lax.psum_scatter(
            part.astype(jnp.bfloat16),
            "mp",
            scatter_dimension=0,
            axis_index_groups=outer_groups,
        ).astype(jnp.float32)
        pre = linear + bias[:, None, :]
        hidden, gelu_back = jax.vjp(lambda v: jax.nn.gelu(v, approximate=False), pre)
        mixed = stitch[:, 0, None, :] * hidden[0][None] + stitch[:, 1, None, :] * hidden[1][None]
        scale_rows = row_weights(crop_counts, row_mask)
        grad_out = cotangent.astype(jnp.float32) * scale_rows[None, :, None]
        first_task = gelu_back(stitch[0][:, None, :] * grad_out[0][None])[0]
        second_task = gelu_back(stitch[1][:, None, :] * grad_out[1][None])[0]
        task_bias = jnp.stack([jnp.sum(first_task, axis=1), jnp.sum(second_task, axis=1)])
        grad_linear = (first_task + second_task).astype(jnp.bfloat16)
        grad_stitch = jnp.sum(grad_out[:, None] * hidden[None], axis=2)
        every = lax.all_gather(grad_linear, "mp", axis_index_groups=outer_groups)
        grad_part = jnp.einsum(
            "otrc,tokc->trk", every, block, preferred_element_type=jnp.float32
        )
        grad_part = grad_part.astype(jnp.bfloat16).reshape(2, rows, inner, depth // inner)
        grad_features = lax.psum_scatter(
            grad_part.transpose(2, 0, 1, 3),
            "mp",
            scatter_dimension=0,
            axis_index_groups=inner_groups,
        )
        weight_part = jnp.einsum(
            "trk,otrc->otkc", held, every, preferred_element_type=jnp.float32
        )
        weight_part = weight_part.astype(jnp.bfloat16).reshape(
            OUTER, 2, n_batch, depth // n_batch, width
        )
        share = lax.psum_scatter(
            weight_part.transpose(2, 0, 1, 3, 4), "batch", scatter_dimension=0
        )
        share = lax.all_to_all(
            share, "mp", split_axis=0, concat_axis=0, axis_index_groups=outer_groups
        )
        share = share.reshape(OUTER, 2, depth // n_batch, width)
        whole = lax.all_gather(share, "batch")
        grad_weights = whole.transpose(2, 1, 0, 3, 4).reshape(2, OUTER * depth, width)
        task_bias, grad_stitch = lax.psum((task_bias, grad_stitch), "batch")
        grad_bias = project_bias(task_bias, flags)
        return (
            mixed.astype(jnp.bfloat16),
            grad_features.astype(jnp.bfloat16),
            grad_weights.astype(jnp.float32),
            grad_bias,
            grad_stitch,
        )

    return per_device


MESH = pl.DeviceIdType.MESH
BF16 = jnp.bfloat16
F32 = jnp.float32
ZED = 4
GROUPS = 4
PHASES = 8
RING = 8
BAND = 64
PRODUCTS = 4
HELD = 6
STRIPS = 4
WIDEN_BLOCKS = 12
WIDEN_SLOTS = 4


Part = collections.namedtuple("Part", ("u", "p", "i", "t", "h", "slot", "prod", "buf"))
Tile = collections.namedtuple("Tile", ("g", "p", "t", "h", "j", "buf", "ring"))


def half(value):
    return value.astype(BF16)


def wide(value):
    return value.astype(F32)


def fused_kernel(
    rows, deep, width, chunk,
    feat, wts, cot, bias, stitch, counts, mask, flags,
    mixed, gfeat, gwt, gbias, gstitch, xn, dxn, xturned,
    wv, gl, rs, h0, xc, pf, cc, mx, own, dsend, dfetch, dout,
    xsrc, xt, cstage, cland, xstage, xland, kept, zstage,
    scale, stat, sums, sums_land, prods, prods_land,
    rs_send, rs_recv, ag_send, ag_recv, xs_send, xs_recv,
    wz_send, wz_recv, wx_send, wx_recv, wc_send, wc_recv, wl,
    xf, cf, mxs, dx_send, dx_recv, df, dod,
    tile_in, tile_out, c_send, c_recv, x_send, x_recv, z_send, z_recv, zl, zx_send,
    ax_send, ax_recv, ac_send, ac_recv, t_send, t_recv,
):
    batch, mp = lax.axis_index("batch"), lax.axis_index("mp")
    z, y = mp // 2, mp % 2
    x, c = batch // 2, batch % 2
    up = {"mp": mp + 2}
    down = {"mp": mp - 2}
    across_y = {"mp": 2 * z + 1 - y}
    across_x = {"batch": 2 * (1 - x) + c}
    across_c = {"batch": 2 * x + 1 - c}

    def at_z(other):
        return {"mp": 2 * other + y}

    others = (3 - z, (z + 2) % 4, z + 1 - 2 * (z % 2))

    n_part = rows // chunk
    parts = PHASES * n_part
    images = counts.shape[1]
    hw = width // GROUPS
    kz = 2 * deep
    quarter = deep // 2
    tile = deep // 3
    strip = quarter // STRIPS
    sub = tile // 2
    cat = ZED * hw

    def mult(value, unit):
        return pl.multiple_of(value, unit)

    def remote(src, dst, send, recv, device):
        return pltpu.make_async_remote_copy(
            src_ref=src, dst_ref=dst, send_sem=send, recv_sem=recv,
            device_id=device, device_id_type=MESH,
        )

    def cols(h):
        return pl.ds(mult(h * hw, hw), hw)

    def lanes_of(h, b):
        return pl.ds(mult(h * cat + b * hw, hw), hw)

    def every(h):
        return pl.ds(mult(h * cat, cat), cat)

    def part_rows(i):
        return pl.ds(mult(i * chunk, chunk), chunk)

    def tower(p):
        t = jnp.where(p >= GROUPS, 1, 0)
        return t, p - GROUPS * t

    def x_copy(t, i):
        e = t * n_part + i
        return remote(
            feat.at[t, part_rows(i)], xn.at[t, part_rows(i)],
            xs_send.at[e], xs_recv.at[e], across_y,
        )

    def x_fetch(t, i, buf):
        return (
            pltpu.make_async_copy(
                feat.at[t, part_rows(i)],
                xc.at[buf, :, pl.ds(mult(deep * y, deep), deep)], xf.at[buf, 0],
            ),
            pltpu.make_async_copy(
                xn.at[t, part_rows(i)],
                xc.at[buf, :, pl.ds(mult(deep * (1 - y), deep), deep)], xf.at[buf, 1],
            ),
        )

    def cot_fetch(h, i, buf):
        return pltpu.make_async_copy(
            cot.at[:, part_rows(i), cols(h)], cc.at[buf], cf.at[buf]
        )

    def w_own(p):
        t, h = tower(p)
        return pltpu.make_async_copy(
            wts.at[t, pl.ds(mult(kz * z, kz), kz), cols(h)],
            wv.at[t, :, lanes_of(h, z)], wl.at[p],
        )

    def w_here(p, at, size, b):
        t, h = tower(p)
        return wv.at[t, pl.ds(mult(at, size), size), lanes_of(h, b)]

    def w_z(p, to):
        t, h = tower(p)
        at = deep * c + quarter * x
        return remote(
            wts.at[t, pl.ds(mult(kz * to + at, quarter), quarter), cols(h)],
            w_here(p, at, quarter, z),
            wz_send.at[p, to], wz_recv.at[p, z], at_z(to),
        )

    def w_z_strip(p, to, r):
        t, h = tower(p)
        at = deep * c + quarter * x + strip * r
        return remote(
            wts.at[t, pl.ds(mult(kz * to + at, strip), strip), cols(h)],
            w_here(p, at, strip, z),
            wz_send.at[p, to], wz_recv.at[p, z], at_z(to),
        )

    def w_z_in(p, frm):
        here = w_here(p, deep * c + quarter * x, quarter, frm)
        return remote(here, here, wz_send.at[p, frm], wz_recv.at[p, frm], at_z(frm))

    def w_x(p, b):
        here = w_here(p, deep * c + quarter * x, quarter, b)
        return remote(here, here, wx_send.at[p, b], wx_recv.at[p, b], across_x)

    def w_x_in(p, b):
        here = w_here(p, deep * c + quarter * (1 - x), quarter, b)
        return remote(here, here, wx_send.at[p, b], wx_recv.at[p, b], across_x)

    def w_c(p, b):
        here = w_here(p, deep * c, deep, b)
        return remote(here, here, wc_send.at[p, b], wc_recv.at[p, b], across_c)

    def w_c_in(p, b):
        here = w_here(p, deep * (1 - c), deep, b)
        return remote(here, here, wc_send.at[p, b], wc_recv.at[p, b], across_c)

    def rs_up(slot, zz):
        run = rs.at[slot, zz + 2 : ZED + 1]
        return remote(run, run, rs_send.at[slot, 0], rs_recv.at[slot, 0], up)

    def rs_down(slot, zz):
        run = rs.at[slot, 0:zz]
        return remote(run, run, rs_send.at[slot, 1], rs_recv.at[slot, 1], down)

    def rs_from_below(slot, zz):
        run = rs.at[slot, zz + 1 : ZED + 1]
        return remote(run, run, rs_send.at[slot, 0], rs_recv.at[slot, 0], down)

    def rs_from_above(slot, zz):
        run = rs.at[slot, 0 : zz + 1]
        return remote(run, run, rs_send.at[slot, 1], rs_recv.at[slot, 1], up)

    def at_place(first, last, do):
        for zz in range(first, last + 1):
            @pl.when(z == zz)
            def _(zz=zz):
                do(zz)

    def ag(at, b, going, device):
        here = gl.at[at.t, part_rows(at.i), lanes_of(at.h, b)]
        return remote(
            here, here, ag_send.at[at.slot, going * ZED + b], ag_recv.at[at.slot, b], device
        )

    def dx_copy(t, i, buf):
        return remote(
            dsend.at[buf], dxn.at[t, part_rows(i)],
            dx_send.at[buf], dx_recv.at[t * n_part + i], across_y,
        )

    def dx_fetch(t, i):
        return pltpu.make_async_copy(dxn.at[t, part_rows(i)], dfetch, df.at[0])

    def dx_out(t, i):
        return pltpu.make_async_copy(dout, gfeat.at[t, part_rows(i)], dod.at[0])

    def mixed_out(h, i, buf):
        return pltpu.make_async_copy(
            mx.at[buf], mixed.at[:, part_rows(i), cols(h)], mxs.at[buf]
        )

    def tile_fetch(g, hk, which):
        lanes = pl.ds(mult(tile * g.j, tile), tile)

        @pl.when((g.h == 0) & (hk == y))
        def _():
            pltpu.make_async_copy(feat.at[g.t, :, lanes], xsrc, tile_in.at[which]).start()

        @pl.when((g.h == 0) & (hk != y))
        def _():
            pltpu.make_async_copy(xn.at[g.t, :, lanes], xsrc, tile_in.at[which]).start()

        @pl.when(g.h > 0)
        def _():
            pltpu.make_async_copy(
                xturned.at[g.t, 3 * hk + g.j], xt.at[which], tile_in.at[which]
            ).start()

    def tile_save(g, hk, which):
        return pltpu.make_async_copy(
            xt.at[which], xturned.at[g.t, 3 * hk + g.j], tile_out.at[which]
        )

    def tile_ready(g, hk, which):
        @pl.when(g.h == 0)
        def _():
            pltpu.make_async_copy(
                feat.at[g.t, :, pl.ds(mult(tile * g.j, tile), tile)], xsrc, tile_in.at[which]
            ).wait()
            turn(which)
            tile_save(g, hk, which).start()

        @pl.when(g.h > 0)
        def _():
            pltpu.make_async_copy(
                xturned.at[g.t, 3 * hk + g.j], xt.at[which], tile_in.at[which]
            ).wait()

    def tile_done(g, hk, which):
        @pl.when(g.h == 0)
        def _():
            tile_save(g, hk, which).wait()

    def core_copy(g):
        return remote(cstage, cland.at[g.buf], c_send.at[0], c_recv.at[g.buf], across_c)

    def across_copy(g, b):
        return remote(
            xstage.at[b], xland.at[g.buf, b], x_send.at[b], x_recv.at[g.buf, b], across_x
        )

    def piece(g, source, core, at, size):
        return gwt.at[
            g.t, source, pl.ds(mult(deep * core + tile * g.j + at, sub), size), cols(g.h)
        ]

    def z_copy(g, to):
        return remote(
            zstage.at[g.j, to], piece(g, z, c, sub * x, sub),
            z_send.at[g.j, to], z_recv.at[g.ring, z], at_z(to),
        )

    def z_in(g, frm):
        here = piece(g, frm, c, sub * x, sub)
        return remote(here, here, z_send.at[g.j, frm], z_recv.at[g.ring, frm], at_z(frm))

    def z_own(g):
        return pltpu.make_async_copy(
            zstage.at[g.j, z], piece(g, z, c, sub * x, sub), zl.at[g.j]
        )

    def ax_own(g):
        return remote(
            zstage.at[g.j, z], piece(g, z, c, sub * x, sub),
            zx_send.at[g.j], ax_recv.at[g.ring, z], across_x,
        )

    def ax_copy(g, b):
        here = piece(g, b, c, sub * x, sub)
        return remote(here, here, ax_send.at[g.g, b], ax_recv.at[g.ring, b], across_x)

    def ax_in(g, b):
        here = piece(g, b, c, sub * (1 - x), sub)
        return remote(here, here, ax_send.at[g.g, b], ax_recv.at[g.ring, b], across_x)

    def ac_copy(g, b):
        here = piece(g, b, c, 0, tile)
        return remote(here, here, ac_send.at[g.g, b], ac_recv.at[g.ring, b], across_c)

    def ac_in(g, b):
        here = piece(g, b, 1 - c, 0, tile)
        return remote(here, here, ac_send.at[g.g, b], ac_recv.at[g.ring, b], across_c)

    def sum_copy(stage, device):
        return remote(
            sums.at[stage], sums_land.at[stage], t_send.at[stage], t_recv.at[stage], device
        )

    def prod_y():
        return remote(prods.at[0], prods_land.at[ZED], t_send.at[2], t_recv.at[2], across_y)

    def prod_z(to):
        return remote(
            prods.at[1], prods_land.at[z], t_send.at[3 + to], t_recv.at[3 + z], at_z(to)
        )

    def prod_z_in(frm):
        here = prods_land.at[frm]
        return remote(here, here, t_send.at[3 + frm], t_recv.at[3 + frm], at_z(frm))

    barrier = pltpu.get_barrier_semaphore()
    for device in [at_z(o) for o in others] + [across_y, across_x, across_c]:
        pl.semaphore_signal(barrier, inc=1, device_id=device, device_id_type=MESH)
    pl.semaphore_wait(barrier, 6)

    for to in others:
        w_z(0, to).start()
    x_copy(0, 0).start()
    x_copy(0, 1).start()
    w_own(0).start()
    cot_fetch(0, 0, 0).start()

    image_row = lax.broadcasted_iota(jnp.int32, (images, images), 0)
    image_col = lax.broadcasted_iota(jnp.int32, (images, images), 1)
    crops = counts[...].astype(F32)
    ends = jnp.dot(
        jnp.broadcast_to(crops, (8, images)), (image_row <= image_col).astype(F32),
        precision=lax.Precision.HIGHEST, preferred_element_type=F32,
    )[0:1]
    starts = ends - crops
    block = mask.shape[1]
    lane = scale.shape[1]

    for r in range(rows // block):
        index = (
            lax.broadcasted_iota(jnp.int32, (block, images), 0) + r * block
        ).astype(F32)
        inside = (index >= starts) & (index < ends)
        count_row = jnp.sum(jnp.where(inside, crops, 0.0), axis=1, keepdims=True)
        diagonal = lax.broadcasted_iota(jnp.int32, (block, block), 0) == (
            lax.broadcasted_iota(jnp.int32, (block, block), 1)
        )
        usable = jnp.sum(
            jnp.where(diagonal, mask[r : r + 1, :].astype(F32), 0.0),
            axis=1, keepdims=True,
        )
        live = (count_row > 0.0) & (usable == 1.0)
        share = jnp.where(live, 1.0 / jnp.maximum(count_row, 1.0), 0.0)
        scale[r * block : (r + 1) * block, :] = jnp.broadcast_to(share, (block, lane))

    for frm in others:
        w_z_in(0, frm).wait_recv()
        w_x(0, frm).start()
    for to in others:
        w_z(1, to).start()
    w_own(1).start()
    for frm in others:
        w_x_in(0, frm).wait_recv()
        w_c(0, frm).start()
    x_copy(0, 0).wait_recv()
    for copy in x_fetch(0, 0, 0):
        copy.start()

    def final(at, later):
        p, i, slot, t, h, buf = at.p, at.i, at.slot, at.t, at.h, at.buf
        cot_fetch(h, i, buf).wait()

        @pl.when(at.u >= parts // 2 + 2)
        def _():
            mixed_out(h, i, buf).wait()

        @pl.when(i == 0)
        def _():
            stat[p] = jnp.zeros(stat.shape[1:], F32)

        lanes = cols(h)

        def of_tower(pair):
            return jnp.where(t == 0, pair[0:1], pair[1:2])

        shift = of_tower(bias[:, lanes])
        st = [of_tower(stitch[s, :, lanes]) for s in range(2)]
        st_first = [stitch[s, :, lanes][0:1] for s in range(2)]
        band = min(BAND, chunk)

        def step(r, carry):
            here = part_rows_of(r, band)
            there = pl.ds(mult(i * chunk + r * band, band), band)
            value = pf[at.prod, z, here, :]
            below = wide(rs[slot, z + 1, here, :])
            above = wide(rs[slot, z, here, :])
            value = value + jnp.where(z > 0, below, 0.0) + jnp.where(z < ZED - 1, above, 0.0)
            pre = value + shift
            phi = 0.5 * (1.0 + lax.erf(pre * 0.7071067811865476))
            hidden = pre * phi
            slope = phi + pre * (jnp.exp(-0.5 * pre * pre) * 0.3989422804014327)
            weight = scale[there, 0:1]
            first = wide(cc[buf, 0, here, :]) * weight
            second = wide(cc[buf, 1, here, :]) * weight
            back0 = st[0] * first * slope
            back1 = st[1] * second * slope
            gl[t, there, lanes_of(h, z)] = half(back0 + back1)

            def fold(v):
                return jnp.sum(v.reshape(band // 8, 8, hw), axis=0)

            stat[p, 0] += fold(back0)
            stat[p, 1] += fold(back1)
            stat[p, 2] += fold(first * hidden)
            stat[p, 3] += fold(second * hidden)

            @pl.when(t == 0)
            def _():
                h0[h, there, :] = hidden

            @pl.when(t == 1)
            def _():
                before = h0[h, there, :]
                for s in range(2):
                    mx[buf, s, here, :] = half(
                        st_first[s] * before + st[s] * hidden
                    )

            return carry

        lax.fori_loop(0, chunk // band, step, 0)

        @pl.when(z < ZED - 1)
        def _():
            ag(at, z, 0, up).start()

        @pl.when(z > 0)
        def _():
            ag(at, z, 1, down).start()

        @pl.when(t == 1)
        def _():
            mixed_out(h, i, buf).start()

        @pl.when(at.u + 1 < parts)
        def _():
            cot_fetch(later.h, later.i, later.buf).start()

    def part_rows_of(r, band):
        return pl.ds(mult(r * band, band), band)

    def forward_ag(at, far):
        @pl.when((at.u >= 0) & (at.u < parts))
        def _():
            @pl.when(z - far >= 0)
            def _():
                ag(at, z - far, 0, up).wait_recv()

                @pl.when(z < ZED - 1)
                def _():
                    ag(at, z - far, 0, up).start()

            @pl.when(z + far < ZED)
            def _():
                ag(at, z + far, 1, down).wait_recv()

                @pl.when(z > 0)
                def _():
                    ag(at, z + far, 1, down).start()

    def dx_part(t, i, hk):
        return lax.dot_general(
            gl[t, part_rows(i), :], wv[t, pl.ds(mult(deep * hk, deep), deep), :],
            (((1,), (1,)), ((), ())), preferred_element_type=F32,
        )

    def dx_step(t, i):
        @pl.when(t > 0)
        def _():
            dx_copy(t, i, i).wait_send()

        dsend[i] = half(dx_part(t, i, 1 - y))
        dx_copy(t, i, i).start()
        own[i] = dx_part(t, i, y)

    def dx_begin(t, i):
        dx_copy(t, i, i).wait_recv()
        dx_fetch(t, i).start()

    def dx_final(t, i):
        @pl.when((i >= 1) | (t > 0))
        def _():
            dx_out(t, i).wait()

        dx_fetch(t, i).wait()

        def step(j, inner):
            lanes = pl.ds(mult(tile * j, tile), tile)
            dout[:, lanes] = half(own[i, :, lanes] + wide(dfetch[:, lanes]))
            return inner

        lax.fori_loop(0, 3, step, 0)
        dx_out(t, i).start()

    def listed(u, times, do):
        e, hit = 0, False
        for index, time in enumerate(times):
            same = u == time
            e = jnp.where(same, index, e)
            hit = hit | same

        @pl.when(hit)
        def _():
            t = jnp.where(e >= n_part, 1, 0)
            do(t, e - n_part * t)

    def turn(which):
        lanes_at_once = min(128, tile)

        def step(q, carry):
            lanes = pl.ds(mult(q * lanes_at_once, lanes_at_once), lanes_at_once)
            xt[which, lanes, :] = xsrc[:, lanes].T
            return carry

        lax.fori_loop(0, tile // lanes_at_once, step, 0)

    def tile_dot(g, which):
        return jnp.dot(xt[which], gl[g.t, :, every(g.h)], preferred_element_type=F32)

    def stage_one(g):
        tile_ready(g, 1 - c, 0)
        tile_fetch(g, c, 1)
        cstage[...] = half(tile_dot(g, 0))
        core_copy(g).start()
        tile_done(g, 1 - c, 0)

    def stage_two(g):
        tile_ready(g, c, 1)
        core_copy(g).wait()
        kept[...] = tile_dot(g, 1) + wide(cland[g.buf])
        away = pl.ds(mult(sub * (1 - x), sub), sub)
        for b in range(ZED):
            xstage[b] = half(kept[away, b * hw : (b + 1) * hw])

        def send(q, carry):
            across_copy(g, lax.rem(z + 3 + 3 * q, ZED)).start()
            return carry

        lax.fori_loop(0, ZED, send, 0)
        tile_done(g, c, 1)

    def stage_three(g):
        @pl.when(g.g >= 3)
        def _():
            for to in others:
                z_copy(g, to).wait_send()
            ax_own(g).wait_send()

        def add(b):
            across_copy(g, b).wait()
            stays = kept[pl.ds(mult(sub * x, sub), sub), pl.ds(mult(b * hw, hw), hw)]
            zstage[g.j, b] = half(stays + wide(xland[g.buf, b]))

        def step(q, carry):
            b = lax.rem(z + 3 + 3 * q, ZED)
            add(b)
            z_copy(g, b).start()
            return carry

        lax.fori_loop(0, ZED - 1, step, 0)
        add(z)
        z_own(g).start()
        ax_own(g).start()

    def stage_four(g):
        def step(q, carry):
            b = lax.rem(z + 1 + q, ZED)
            z_in(g, b).wait_recv()
            ax_copy(g, b).start()
            return carry

        lax.fori_loop(0, ZED - 1, step, 0)
        z_own(g).wait()

    def stage_five(g):
        def step(q, carry):
            b = lax.rem(z + q, ZED)
            ax_in(g, b).wait_recv()
            ac_copy(g, b).start()
            return carry

        lax.fori_loop(0, ZED, step, 0)

    def stage_six(g):
        def step(b, carry):
            ac_in(g, b).wait_recv()
            return carry

        lax.fori_loop(0, ZED, step, 0)

    stair = parts - 2 * n_part
    early = 2

    def phase_of(w):
        p = lax.div(w, n_part)
        i = w - n_part * p
        begins = w < stair + early
        middle = w < stair + early + n_part
        p = jnp.where(
            w < stair, p, jnp.where(begins, PHASES - 1, jnp.where(middle, PHASES - 2, PHASES - 1))
        )
        i = jnp.where(
            w < stair, i,
            jnp.where(begins, w - stair, jnp.where(middle, w - stair - early, w - stair - n_part)),
        )
        return p, i

    whole_six = stair + early + n_part + 5
    whole_seven = parts + 5

    def tile_at(v, do):
        w = v - 2 * n_part
        p = lax.div(w, n_part)
        r = w - n_part * p
        j = lax.div(r, 2)
        plain = (w >= 0) & (p < PHASES - 2) & (2 * j == r) & (j < 3)
        six = (v > whole_six) & (v < whole_six + 4)
        seven = (v > whole_seven) & (v < whole_seven + 4)
        p = jnp.where(six, PHASES - 2, jnp.where(seven, PHASES - 1, p))
        j = jnp.where(six, v - whole_six - 1, jnp.where(seven, v - whole_seven - 1, j))

        @pl.when(plain | six | seven)
        def _():
            t, h = tower(p)
            g = 3 * p + j
            do(Tile(g=g, p=p, t=t, h=h, j=j, buf=lax.rem(g, 2), ring=lax.rem(g, 12)))

    half_way = n_part * GROUPS
    dx_times = [half_way + 1 + 2 * e for e in range(n_part)]
    dx_times += [stair + early + 7 + e for e in range(early)]
    dx_times += [parts + 2 + e for e in range(n_part - early)]
    dx_ends = [time + 3 for time in dx_times[:n_part]]
    dx_ends += [stair + early + 11 + 2 * e for e in range(early)]
    dx_ends += [parts + 9 + 2 * e for e in range(n_part - early - 1)] + [parts + 16]

    def w_unit(n):
        return jnp.where(n == PHASES - 2, PHASES - 1, jnp.where(n == PHASES - 1, PHASES - 2, n))

    def body(u, carry):
        slot0, prod0 = lax.rem(u, RING), lax.rem(u, PRODUCTS)

        def before(lag):
            w = u - lag
            p, i = phase_of(w)
            in_ring = lag % RING if isinstance(lag, int) else lag
            in_prods = lag % PRODUCTS if isinstance(lag, int) else lag
            slot = slot0 - in_ring + jnp.where(slot0 < in_ring, RING, 0)
            prod = prod0 - in_prods + jnp.where(prod0 < in_prods, PRODUCTS, 0)
            t, h = tower(p)
            return Part(u=w, p=p, i=i, t=t, h=h, slot=slot, prod=prod, buf=lax.rem(i, 2))

        @pl.when((u >= 5) & (u < parts + 5))
        def _():
            slot = before(5).slot
            at_place(0, ZED - 2, lambda zz: rs_up(slot, zz).wait_send())
            at_place(1, ZED - 1, lambda zz: rs_down(slot, zz).wait_send())

        @pl.when((u >= 8) & (u < parts + 8))
        def _():
            at = before(8)

            def step(b, inner):
                @pl.when((z < ZED - 1) & (b <= z))
                def _():
                    ag(at, b, 0, up).wait_send()

                @pl.when((z > 0) & (b >= z))
                def _():
                    ag(at, b, 1, down).wait_send()

                return inner

            lax.fori_loop(0, ZED, step, 0)

        now = before(0)

        @pl.when(u < parts)
        def _():
            @pl.when(now.i == 0)
            def _():
                w_own(now.p).wait()
                for frm in others:
                    w_c_in(now.p, frm).wait_recv()

            for copy in x_fetch(now.t, now.i, now.buf):
                copy.wait()

            product = jnp.dot(
                xc[now.buf], wv[now.t, :, every(now.h)], preferred_element_type=F32
            )
            for b in range(ZED):
                pf[prod0, b] = product[:, b * hw : (b + 1) * hw]

        going_up = before(z)

        @pl.when((going_up.u >= 0) & (going_up.u < parts))
        def _():
            slot, prod = going_up.slot, going_up.prod
            at_place(1, ZED - 1, lambda zz: rs_from_below(slot, zz).wait_recv())

            @pl.when(z == 0)
            def _():
                for b in range(1, ZED):
                    rs[slot, b + 1] = half(pf[prod, b])

            @pl.when(z > 0)
            def _():
                def step(b, inner):
                    rs[slot, b + 1] = half(wide(rs[slot, b + 1]) + pf[prod, b])
                    return inner

                lax.fori_loop(z + 1, ZED, step, 0)

            at_place(0, ZED - 2, lambda zz: rs_up(slot, zz).start())

        going_down = before(ZED - 1 - z)

        @pl.when((going_down.u >= 0) & (going_down.u < parts))
        def _():
            slot, prod = going_down.slot, going_down.prod
            at_place(0, ZED - 2, lambda zz: rs_from_above(slot, zz).wait_recv())

            @pl.when(z == ZED - 1)
            def _():
                for b in range(ZED - 1):
                    rs[slot, b] = half(pf[prod, b])

            @pl.when(z < ZED - 1)
            def _():
                def step(b, inner):
                    rs[slot, b] = half(wide(rs[slot, b]) + pf[prod, b])
                    return inner

                lax.fori_loop(0, z, step, 0)

            at_place(1, ZED - 1, lambda zz: rs_down(slot, zz).start())

        @pl.when(u + 2 < 2 * n_part)
        def _():
            over = jnp.where(u + 2 >= n_part, 1, 0)
            x_copy(over, u + 2 - over * n_part).start()

        @pl.when(u + 1 < parts)
        def _():
            nxt = before(-1)

            @pl.when(nxt.h == 0)
            def _():
                x_copy(nxt.t, nxt.i).wait_recv()

            for copy in x_fetch(nxt.t, nxt.i, nxt.buf):
                copy.start()

        @pl.when((u >= 3) & (u < parts + 3))
        def _():
            final(before(3), before(2))

        forward_ag(before(4), 1)
        forward_ag(before(5), 2)
        forward_ag(before(6), 3)

        listed(u, [end - 1 for end in dx_ends], dx_begin)
        listed(u, dx_ends, dx_final)
        listed(u, dx_times, dx_step)

        tile_at(u - 2, stage_three)
        tile_at(u - 1, stage_two)
        tile_at(u, stage_one)
        tile_at(u - 4, stage_four)
        tile_at(u - 6, stage_five)
        tile_at(u - 7, stage_six)
        tile_at(u + 1, lambda g: tile_fetch(g, 1 - c, 0))

        n_sent = lax.div(u, STRIPS) + 2

        @pl.when(n_sent < PHASES)
        def _():
            r = u - STRIPS * (n_sent - 2)
            p = w_unit(n_sent)
            for to in others:
                w_z_strip(p, to, r).start()

            @pl.when(r == 1)
            def _():
                w_own(p).start()

        def spread_weights(v, do):
            n = lax.div(v, STRIPS) + 1
            for q in range(3):
                @pl.when((v >= 0) & (n < PHASES) & (v - STRIPS * (n - 1) == q))
                def _(q=q):
                    do(w_unit(n), others[q])

        def over_x(p, b):
            w_z_in(p, b).wait_recv()
            w_x(p, b).start()

        def over_c(p, b):
            w_x_in(p, b).wait_recv()
            w_c(p, b).start()

        spread_weights(u - 1, over_x)
        spread_weights(u - 3, over_c)

        @pl.when(u == parts + 3)
        def _():
            for p in range(PHASES):
                t, h = p // GROUPS, p % GROUPS
                for s in range(2):
                    for what in range(2):
                        sums[0, pl.ds(4 * what + 2 * s + t, 1), h * hw : (h + 1) * hw] = jnp.sum(
                            stat[p, 2 * what + s], axis=0, keepdims=True
                        )
            sum_copy(0, across_c).start()

        @pl.when(u == parts + 4)
        def _():
            sum_copy(0, across_c).wait()
            sums[1] = sums[0] + sums_land[0]
            sum_copy(1, across_x).start()

        @pl.when(u == parts + 5)
        def _():
            sum_copy(1, across_x).wait()
            both = sums[1] + sums_land[1]
            sums[2] = both
            member = (
                lax.broadcasted_iota(jnp.int32, (width, lane), 0) % FLAG_GROUPS
                == lax.broadcasted_iota(jnp.int32, (width, lane), 1) % FLAG_GROUPS
            ).astype(F32)
            bias_rows = both[0:4]
            inner = both[0:2] * both[2:4]
            stack = jnp.concatenate([inner, bias_rows * bias_rows, inner], axis=0)
            prods[0] = jnp.dot(
                stack, member, precision=lax.Precision.HIGHEST, preferred_element_type=F32
            )
            prod_y().start()

        @pl.when(u == parts + 6)
        def _():
            prod_y().wait()
            prods[1] = prods[0] + prods_land[ZED]
            for to in others:
                prod_z(to).start()

        @pl.when(u == parts + 7)
        def _():
            for frm in others:
                prod_z_in(frm).wait_recv()
            prods_land[z] = prods[1]
            whole = prods_land[0] + prods_land[1] + prods_land[2] + prods_land[3]
            both = sums[2]
            group = lax.broadcasted_iota(jnp.int32, (1, lane), 1) % FLAG_GROUPS

            def over(row):
                return jnp.concatenate([row] * (width // lane), axis=1)

            def flag_row(s, t):
                row = jnp.zeros((1, lane), F32)
                for g in range(FLAG_GROUPS):
                    row = jnp.where(group == g, flags[s, t, g].astype(F32), row)
                return row

            for t in range(2):
                task0, task1 = both[t : t + 1], both[2 + t : 3 + t]
                dots = whole[t : t + 1]
                coef0 = over(flag_row(0, t) * dots / (whole[4 + t : 5 + t] + 1e-06))
                coef1 = over(flag_row(1, t) * dots / (whole[2 + t : 3 + t] + 1e-06))
                gbias[t : t + 1] = (task0 - coef0 * task1) + (task1 - coef1 * task0)
            for s in range(2):
                gstitch[s] = both[4 + 2 * s : 6 + 2 * s]

        return carry

    lax.fori_loop(0, parts + 18, body, 0)

    last = 3 * PHASES - 1

    def tile_of(g):
        p, j = divmod(g, 3)
        return Tile(
            g=g, p=p, t=p // GROUPS, h=p % GROUPS, j=j, buf=g % 2, ring=g % 12
        )

    for g in (last - 2, last - 1, last):
        for to in others:
            z_copy(tile_of(g), to).wait_send()
        ax_own(tile_of(g)).wait_send()
    for i in range(n_part):
        dx_copy(1, i, i).wait_send()
    for i in (n_part - 2, n_part - 1):
        mixed_out(GROUPS - 1, i, i % 2).wait()
    dx_out(1, n_part - 1).wait()

    def drain_tiles(g, carry):
        p = lax.div(g, 3)
        t, h = tower(p)
        at = Tile(
            g=g, p=p, t=t, h=h, j=g - 3 * p, buf=lax.rem(g, 2), ring=lax.rem(g, 12)
        )
        for b in others:
            ax_copy(at, b).wait_send()
        for b in range(ZED):
            ac_copy(at, b).wait_send()
        return carry

    lax.fori_loop(0, last + 1, drain_tiles, 0)

    def drain_x(i, carry):
        x_copy(0, i).wait_send()
        x_copy(1, i).wait_send()
        return carry

    lax.fori_loop(0, n_part, drain_x, 0)

    def drain_w(p, carry):
        for to in others:
            w_z(p, to).wait_send()
            w_x(p, to).wait_send()
            w_c(p, to).wait_send()
        return carry

    lax.fori_loop(0, PHASES, drain_w, 0)
    for to in others:
        prod_z(to).wait_send()


def fused_call(feat, wts, cot, bias, stitch, counts, mask, flags):
    rows, deep, width = feat.shape[1], feat.shape[2], wts.shape[2]
    chunk = rows // 6
    hw, kz, tile = width // GROUPS, 2 * deep, deep // 3
    sub = tile // 2
    lane = min(128, width)
    dma = pltpu.SemaphoreType.DMA
    anywhere = pl.BlockSpec(memory_space=pl.ANY)
    inside = pl.BlockSpec(memory_space=pltpu.VMEM)
    scalars = pl.BlockSpec(memory_space=pltpu.SMEM)

    def v(shape, kind=BF16):
        return pltpu.VMEM(shape, kind)

    out_shape = [
        jax.ShapeDtypeStruct((2, rows, width), BF16),
        jax.ShapeDtypeStruct((2, rows, deep), BF16),
        jax.ShapeDtypeStruct((2, ZED, kz, width), BF16),
        jax.ShapeDtypeStruct((2, width), F32),
        jax.ShapeDtypeStruct((2, 2, width), F32),
        jax.ShapeDtypeStruct((2, rows, deep), BF16),
        jax.ShapeDtypeStruct((2, rows, deep), BF16),
        jax.ShapeDtypeStruct((2, 6, tile, rows), BF16),
    ]
    scratch = [
        v((2, kz, ZED * width)),
        v((2, rows, ZED * width)),
        v((RING, 5, chunk, hw)),
        v((GROUPS, rows, hw), F32),
        v((2, chunk, kz)),
        v((PRODUCTS, ZED, chunk, hw), F32),
        v((2, 2, chunk, hw)),
        v((2, 2, chunk, hw)),
        v((HELD, chunk, deep), F32),
        v((HELD, chunk, deep)),
        v((chunk, deep)),
        v((chunk, deep)),
        v((rows, tile)),
        v((2, tile, rows)),
        v((tile, ZED * hw)),
        v((2, tile, ZED * hw)),
        v((ZED, sub, hw)),
        v((2, ZED, sub, hw)),
        v((tile, ZED * hw), F32),
        v((3, ZED, sub, hw)),
        v((rows, lane), F32),
        v((PHASES, 4, 8, hw), F32),
        v((3, 8, width), F32),
        v((2, 8, width), F32),
        v((2, 8, lane), F32),
        v((5, 8, lane), F32),
        dma((RING, 2)), dma((RING, 2)), dma((RING, 8)), dma((RING, 4)),
        dma((12,)), dma((12,)),
        dma((8, 4)), dma((8, 4)), dma((8, 4)), dma((8, 4)), dma((8, 4)), dma((8, 4)), dma((8,)),
        dma((2, 2)), dma((2,)), dma((2,)), dma((HELD,)), dma((12,)), dma((1,)), dma((1,)),
        dma((2,)), dma((2,)),
        dma((1,)), dma((2,)), dma((4,)), dma((2, 4)), dma((3, 4)), dma((12, 4)),
        dma((3,)), dma((3,)),
        dma((24, 4)), dma((12, 4)), dma((24, 4)), dma((12, 4)), dma((8,)), dma((8,)),
    ]
    flops = 3 * 2 * 2 * rows * kz * ZED * width
    return pl.pallas_call(
        functools.partial(fused_kernel, rows, deep, width, chunk),
        out_shape=out_shape,
        in_specs=[anywhere] * 3 + [inside] * 4 + [scalars],
        out_specs=[anywhere] * 3 + [inside] * 2 + [anywhere] * 3,
        scratch_shapes=scratch,
        compiler_params=pltpu.CompilerParams(
            collective_id=0, has_side_effects=True, vmem_limit_bytes=64 * 1024 * 1024
        ),
        cost_estimate=pl.CostEstimate(
            flops=flops, bytes_accessed=200_000_000, transcendentals=2 * rows * width * 2
        ),
        name="cross_stitch_step",
    )(feat, wts, cot, bias, stitch, counts, mask, flags)


def widen_kernel(block, low, out, taken, given, in_sem, out_sem):
    n_block = low.shape[0] // block

    def take(i):
        return pltpu.make_async_copy(
            low.at[pl.ds(i * block, block)], taken.at[i % WIDEN_SLOTS], in_sem.at[i % WIDEN_SLOTS]
        )

    def give(i):
        return pltpu.make_async_copy(
            given.at[i % WIDEN_SLOTS], out.at[pl.ds(i * block, block)], out_sem.at[i % WIDEN_SLOTS]
        )

    for i in range(min(WIDEN_SLOTS, n_block)):
        take(i).start()
    for i in range(n_block):
        slot = i % WIDEN_SLOTS
        take(i).wait()
        if i >= WIDEN_SLOTS:
            give(i - WIDEN_SLOTS).wait()
        given[slot] = wide(taken[slot])
        give(i).start()
        if i + WIDEN_SLOTS < n_block:
            take(i + WIDEN_SLOTS).start()
    for i in range(max(0, n_block - WIDEN_SLOTS), n_block):
        give(i).wait()


def widen(low):
    tall, width = low.shape
    block = tall // WIDEN_BLOCKS
    anywhere = pl.BlockSpec(memory_space=pl.ANY)
    return pl.pallas_call(
        functools.partial(widen_kernel, block),
        in_specs=[anywhere],
        out_specs=anywhere,
        out_shape=jax.ShapeDtypeStruct(low.shape, F32),
        scratch_shapes=[
            pltpu.VMEM((WIDEN_SLOTS, block, width), BF16),
            pltpu.VMEM((WIDEN_SLOTS, block, width), F32),
            pltpu.SemaphoreType.DMA((WIDEN_SLOTS,)),
            pltpu.SemaphoreType.DMA((WIDEN_SLOTS,)),
        ],
        compiler_params=pltpu.CompilerParams(vmem_limit_bytes=48 * 1024 * 1024),
        cost_estimate=pl.CostEstimate(
            flops=tall * width, bytes_accessed=6 * tall * width, transcendentals=0
        ),
        name="widen",
    )(low)


def fused_plan(mesh):
    def per_device(features, weights, bias, stitch, cotangent, crop_counts, row_mask, flags):
        rows, deep = features.shape[1:]
        width = weights.shape[2]
        mixed, gfeat, gwt, gbias, gstitch, _, _, _ = fused_call(
            features, weights, cotangent, bias, stitch,
            crop_counts.reshape(1, -1), row_mask.reshape(-1, min(128, rows // 6)), flags,
        )
        grad_weights = widen(gwt.reshape(-1, width)).reshape(2, ZED * 2 * deep, width)
        return mixed, gfeat, grad_weights, gbias, gstitch

    return per_device


def plan_for(mesh):
    if mesh.shape["batch"] == 4 and mesh.shape["mp"] == 2 * ZED:
        return fused_plan(mesh)
    return generic_plan(mesh)


def solution(mesh):
    in_specs = (
        P(None, "batch", "mp"),
        P(None, None, "mp"),
        P(None, "mp"),
        P(None, None, "mp"),
        P(None, "batch", "mp"),
        P("batch"),
        P("batch"),
        P(),
    )
    out_specs = (
        P(None, "batch", "mp"),
        P(None, "batch", "mp"),
        P(None, None, "mp"),
        P(None, "mp"),
        P(None, None, "mp"),
    )
    return jax.shard_map(
        plan_for(mesh), mesh=mesh, in_specs=in_specs, out_specs=out_specs, check_vma=False
    )
```

```python
import collections
import functools

import jax
import jax.numpy as jnp
from jax import lax
from jax.experimental import pallas as pl
from jax.experimental.pallas import tpu as pltpu
from jax.sharding import PartitionSpec as P

FLAG_GROUPS = 8
OUTER = 4


def row_weights(counts, mask):
    ends = jnp.cumsum(counts)
    starts = ends - counts
    index = lax.broadcasted_iota(jnp.int32, (mask.shape[0], counts.shape[0]), 0)
    inside = (index >= starts[None, :]) & (index < ends[None, :])
    count_row = jnp.sum(jnp.where(inside, counts[None, :], 0), axis=1)
    live = (count_row > 0) & (mask == 1)
    return jnp.where(live, 1.0 / jnp.maximum(count_row, 1).astype(jnp.float32), 0.0)


def project_bias(task_bias, flags):
    local_width = task_bias.shape[2]
    channel = lax.axis_index("mp") * local_width + lax.broadcasted_iota(
        jnp.int32, (local_width, FLAG_GROUPS), 0
    )
    member = (
        channel % FLAG_GROUPS == lax.broadcasted_iota(jnp.int32, (local_width, FLAG_GROUPS), 1)
    ).astype(jnp.float32)
    dots = jnp.dot(task_bias[0] * task_bias[1], member, precision=lax.Precision.HIGHEST)
    norms = jnp.einsum(
        "stc,cg->stg", task_bias * task_bias, member, precision=lax.Precision.HIGHEST
    )
    dots, norms = lax.psum((dots, norms), "mp")
    flag = flags.astype(jnp.float32)
    coef_first = jnp.dot(
        flag[0] * dots / (norms[1] + 1e-06), member.T, precision=lax.Precision.HIGHEST
    )
    coef_second = jnp.dot(
        flag[1] * dots / (norms[0] + 1e-06), member.T, precision=lax.Precision.HIGHEST
    )
    first = task_bias[0] - coef_first * task_bias[1]
    second = task_bias[1] - coef_second * task_bias[0]
    return first + second


def generic_plan(mesh):
    n_mp = mesh.shape["mp"]
    n_batch = mesh.shape["batch"]
    inner = n_mp // OUTER
    inner_groups = [[o * inner + i for i in range(inner)] for o in range(OUTER)]
    outer_groups = [[o * inner + i for o in range(OUTER)] for i in range(inner)]

    def per_device(features, weights, bias, stitch, cotangent, crop_counts, row_mask, flags):
        rows = features.shape[1]
        width = weights.shape[2]
        depth = features.shape[2] * inner
        held = lax.all_gather(
            features, "mp", axis=2, tiled=True, axis_index_groups=inner_groups
        )
        split = weights.reshape(2, OUTER, depth, width)
        block = lax.all_to_all(
            split, "mp", split_axis=1, concat_axis=1, axis_index_groups=outer_groups
        )
        block = block.reshape(2, OUTER, depth, width)
        part = jnp.einsum("trk,tokc->otrc", held, block, preferred_element_type=jnp.float32)
        linear = lax.psum_scatter(
            part.astype(jnp.bfloat16),
            "mp",
            scatter_dimension=0,
            axis_index_groups=outer_groups,
        ).astype(jnp.float32)
        pre = linear + bias[:, None, :]
        hidden, gelu_back = jax.vjp(lambda v: jax.nn.gelu(v, approximate=False), pre)
        mixed = stitch[:, 0, None, :] * hidden[0][None] + stitch[:, 1, None, :] * hidden[1][None]
        scale_rows = row_weights(crop_counts, row_mask)
        grad_out = cotangent.astype(jnp.float32) * scale_rows[None, :, None]
        first_task = gelu_back(stitch[0][:, None, :] * grad_out[0][None])[0]
        second_task = gelu_back(stitch[1][:, None, :] * grad_out[1][None])[0]
        task_bias = jnp.stack([jnp.sum(first_task, axis=1), jnp.sum(second_task, axis=1)])
        grad_linear = (first_task + second_task).astype(jnp.bfloat16)
        grad_stitch = jnp.sum(grad_out[:, None] * hidden[None], axis=2)
        every = lax.all_gather(grad_linear, "mp", axis_index_groups=outer_groups)
        grad_part = jnp.einsum(
            "otrc,tokc->trk", every, block, preferred_element_type=jnp.float32
        )
        grad_part = grad_part.astype(jnp.bfloat16).reshape(2, rows, inner, depth // inner)
        grad_features = lax.psum_scatter(
            grad_part.transpose(2, 0, 1, 3),
            "mp",
            scatter_dimension=0,
            axis_index_groups=inner_groups,
        )
        weight_part = jnp.einsum(
            "trk,otrc->otkc", held, every, preferred_element_type=jnp.float32
        )
        weight_part = weight_part.astype(jnp.bfloat16).reshape(
            OUTER, 2, n_batch, depth // n_batch, width
        )
        share = lax.psum_scatter(
            weight_part.transpose(2, 0, 1, 3, 4), "batch", scatter_dimension=0
        )
        share = lax.all_to_all(
            share, "mp", split_axis=0, concat_axis=0, axis_index_groups=outer_groups
        )
        share = share.reshape(OUTER, 2, depth // n_batch, width)
        whole = lax.all_gather(share, "batch")
        grad_weights = whole.transpose(2, 1, 0, 3, 4).reshape(2, OUTER * depth, width)
        task_bias, grad_stitch = lax.psum((task_bias, grad_stitch), "batch")
        grad_bias = project_bias(task_bias, flags)
        return (
            mixed.astype(jnp.bfloat16),
            grad_features.astype(jnp.bfloat16),
            grad_weights.astype(jnp.float32),
            grad_bias,
            grad_stitch,
        )

    return per_device


MESH = pl.DeviceIdType.MESH
BF16 = jnp.bfloat16
F32 = jnp.float32
ZED = 4
HALVES = 2
PHASES = 4
RING = 8
BAND = 32
SUB = 2
PRODUCTS = 6
HELD = 4
WIDEN_BLOCKS = 12
WIDEN_SLOTS = 4


Part = collections.namedtuple("Part", ("u", "p", "i", "t", "h", "slot", "prod", "buf"))
Tile = collections.namedtuple("Tile", ("g", "p", "t", "h", "j", "buf", "trio", "quad"))


def half(value):
    return value.astype(BF16)


def wide(value):
    return value.astype(F32)


def fused_kernel(
    rows, deep, width, chunk,
    feat, wts, cot, bias, stitch, counts, mask, flags,
    mixed, gfeat, gwt, gbias, gstitch, xn, dxn,
    wv, gl, rs, h0, xc, pf, cc, mx, own, dsend, dfetch, dout,
    xsrc, xt, cstage, cland, xstage, xland, kept, zstage,
    scale, stat, sums, sums_land, prods, prods_land,
    rs_send, rs_recv, ag_send, ag_recv, xs_send, xs_recv,
    wz_send, wz_recv, wx_send, wx_recv, wc_send, wc_recv, wl,
    xf, cf, mxs, dx_send, dx_recv, df, dod,
    tile_in, c_send, c_recv, x_send, x_recv, z_send, z_recv, zl, zx_send,
    ax_send, ax_recv, ac_send, ac_recv, t_send, t_recv,
):
    batch, mp = lax.axis_index("batch"), lax.axis_index("mp")
    z, y = mp // 2, mp % 2
    x, c = batch // 2, batch % 2
    up = {"mp": mp + 2}
    down = {"mp": mp - 2}
    across_y = {"mp": 2 * z + 1 - y}
    across_x = {"batch": 2 * (1 - x) + c}
    across_c = {"batch": 2 * x + 1 - c}

    def at_z(other):
        return {"mp": 2 * other + y}

    others = (3 - z, (z + 2) % 4, z + 1 - 2 * (z % 2))

    n_chunk = rows // chunk
    total = PHASES * n_chunk
    part = chunk // SUB
    n_part = rows // part
    parts = PHASES * n_part
    images = counts.shape[1]
    hw = width // HALVES
    kz = 2 * deep
    quarter = deep // 2
    tile = deep // 3
    strip = quarter // 6
    xw = hw // 2

    def mult(value, unit):
        return pl.multiple_of(value, unit)

    def remote(src, dst, send, recv, device):
        return pltpu.make_async_remote_copy(
            src_ref=src, dst_ref=dst, send_sem=send, recv_sem=recv,
            device_id=device, device_id_type=MESH,
        )

    def cols(b):
        return pl.ds(mult(b * hw, hw), hw)

    def chunk_rows(i):
        return pl.ds(mult(i * chunk, chunk), chunk)

    def part_rows(i):
        return pl.ds(mult(i * part, part), part)

    def tower(p):
        t = jnp.where(p >= HALVES, 1, 0)
        return t, p - HALVES * t

    def x_copy(t, i):
        e = t * n_chunk + i
        return remote(
            feat.at[t, chunk_rows(i)], xn.at[t, chunk_rows(i)],
            xs_send.at[e], xs_recv.at[e], across_y,
        )

    def x_fetch(t, i, buf):
        return (
            pltpu.make_async_copy(
                feat.at[t, chunk_rows(i)],
                xc.at[buf, :, pl.ds(mult(deep * y, deep), deep)], xf.at[buf, 0],
            ),
            pltpu.make_async_copy(
                xn.at[t, chunk_rows(i)],
                xc.at[buf, :, pl.ds(mult(deep * (1 - y), deep), deep)], xf.at[buf, 1],
            ),
        )

    def cot_fetch(h, i, buf):
        return pltpu.make_async_copy(
            cot.at[:, part_rows(i), cols(h)], cc.at[buf], cf.at[buf]
        )

    def w_own(p):
        t, h = tower(p)
        return pltpu.make_async_copy(
            wts.at[t, pl.ds(mult(kz * z, kz), kz), cols(h)], wv.at[p, :, cols(z)], wl.at[p],
        )

    def w_rows():
        return pl.ds(mult(deep * c + quarter * x, quarter), quarter)

    def w_z(p, to):
        t, h = tower(p)
        return remote(
            wts.at[
                t, pl.ds(mult(kz * to + deep * c + quarter * x, quarter), quarter), cols(h)
            ],
            wv.at[p, w_rows(), cols(z)],
            wz_send.at[p, to], wz_recv.at[p, z], at_z(to),
        )

    def w_z_strip(p, to, r):
        t, h = tower(p)
        at = deep * c + quarter * x + strip * r
        return remote(
            wts.at[t, pl.ds(mult(kz * to + at, strip), strip), cols(h)],
            wv.at[p, pl.ds(mult(at, strip), strip), cols(z)],
            wz_send.at[p, to], wz_recv.at[p, z], at_z(to),
        )

    def w_z_in(p, frm):
        here = wv.at[p, w_rows(), cols(frm)]
        return remote(here, here, wz_send.at[p, frm], wz_recv.at[p, frm], at_z(frm))

    def w_x(p, b):
        here = wv.at[p, w_rows(), cols(b)]
        return remote(here, here, wx_send.at[p, b], wx_recv.at[p, b], across_x)

    def w_x_in(p, b):
        here = wv.at[
            p, pl.ds(mult(deep * c + quarter * (1 - x), quarter), quarter), cols(b)
        ]
        return remote(here, here, wx_send.at[p, b], wx_recv.at[p, b], across_x)

    def w_c(p, b):
        here = wv.at[p, pl.ds(mult(deep * c, deep), deep), cols(b)]
        return remote(here, here, wc_send.at[p, b], wc_recv.at[p, b], across_c)

    def w_c_in(p, b):
        here = wv.at[p, pl.ds(mult(deep * (1 - c), deep), deep), cols(b)]
        return remote(here, here, wc_send.at[p, b], wc_recv.at[p, b], across_c)

    def rs_up(slot, zz):
        run = rs.at[slot, zz + 2 : ZED + 1]
        return remote(run, run, rs_send.at[slot, 0], rs_recv.at[slot, 0], up)

    def rs_down(slot, zz):
        run = rs.at[slot, 0:zz]
        return remote(run, run, rs_send.at[slot, 1], rs_recv.at[slot, 1], down)

    def rs_from_below(slot, zz):
        run = rs.at[slot, zz + 1 : ZED + 1]
        return remote(run, run, rs_send.at[slot, 0], rs_recv.at[slot, 0], down)

    def rs_from_above(slot, zz):
        run = rs.at[slot, 0 : zz + 1]
        return remote(run, run, rs_send.at[slot, 1], rs_recv.at[slot, 1], up)

    def at_place(first, last, do):
        for zz in range(first, last + 1):
            @pl.when(z == zz)
            def _(zz=zz):
                do(zz)

    def ag(at, b, going, device):
        here = gl.at[at.p, part_rows(at.i), cols(b)]
        return remote(
            here, here, ag_send.at[at.slot, going * ZED + b], ag_recv.at[at.slot, b], device
        )

    def dx_copy(t, i, buf):
        return remote(
            dsend.at[buf], dxn.at[t, chunk_rows(i)],
            dx_send.at[buf], dx_recv.at[t * n_chunk + i], across_y,
        )

    def dx_fetch(t, i):
        return pltpu.make_async_copy(dxn.at[t, chunk_rows(i)], dfetch, df.at[0])

    def dx_out(t, i):
        return pltpu.make_async_copy(dout, gfeat.at[t, chunk_rows(i)], dod.at[0])

    def mixed_out(h, i, buf):
        return pltpu.make_async_copy(
            mx.at[buf], mixed.at[:, part_rows(i), cols(h)], mxs.at[buf]
        )

    def tile_fetch(t, j, hk, start):
        lanes = pl.ds(mult(tile * j, tile), tile)
        near = pltpu.make_async_copy(feat.at[t, :, lanes], xsrc, tile_in.at[0])
        if not start:
            near.wait()
            return

        @pl.when(hk == y)
        def _():
            near.start()

        @pl.when(hk != y)
        def _():
            pltpu.make_async_copy(xn.at[t, :, lanes], xsrc, tile_in.at[0]).start()

    def core_copy(g):
        return remote(cstage, cland.at[g.buf], c_send.at[0], c_recv.at[g.buf], across_c)

    def across_copy(g, b):
        return remote(
            xstage.at[g.trio, b], xland.at[g.quad, b],
            x_send.at[g.trio, b], x_recv.at[g.quad, b], across_x,
        )

    def piece(g, source, core, lanes, n_lanes):
        return gwt.at[
            g.t, source,
            pl.ds(mult(deep * core + tile * g.j, tile), tile),
            pl.ds(mult(hw * g.h + lanes, xw), n_lanes),
        ]

    def z_copy(g, to):
        return remote(
            zstage.at[g.trio, to], piece(g, z, c, xw * x, xw),
            z_send.at[g.trio, to], z_recv.at[g.g, z], at_z(to),
        )

    def z_in(g, frm):
        here = piece(g, frm, c, xw * x, xw)
        return remote(here, here, z_send.at[g.trio, frm], z_recv.at[g.g, frm], at_z(frm))

    def z_own(g):
        return pltpu.make_async_copy(
            zstage.at[g.trio, z], piece(g, z, c, xw * x, xw), zl.at[g.trio]
        )

    def ax_own(g):
        return remote(
            zstage.at[g.trio, z], piece(g, z, c, xw * x, xw),
            zx_send.at[g.trio], ax_recv.at[g.g, z], across_x,
        )

    def ax_copy(g, b):
        here = piece(g, b, c, xw * x, xw)
        return remote(here, here, ax_send.at[g.g, b], ax_recv.at[g.g, b], across_x)

    def ax_in(g, b):
        here = piece(g, b, c, xw * (1 - x), xw)
        return remote(here, here, ax_send.at[g.g, b], ax_recv.at[g.g, b], across_x)

    def ac_copy(g, b):
        here = piece(g, b, c, 0, hw)
        return remote(here, here, ac_send.at[g.g, b], ac_recv.at[g.g, b], across_c)

    def ac_in(g, b):
        here = piece(g, b, 1 - c, 0, hw)
        return remote(here, here, ac_send.at[g.g, b], ac_recv.at[g.g, b], across_c)

    def sum_copy(stage, device):
        return remote(
            sums.at[stage], sums_land.at[stage], t_send.at[stage], t_recv.at[stage], device
        )

    def prod_y():
        return remote(prods.at[0], prods_land.at[ZED], t_send.at[2], t_recv.at[2], across_y)

    def prod_z(to):
        return remote(
            prods.at[1], prods_land.at[z], t_send.at[3 + to], t_recv.at[3 + z], at_z(to)
        )

    def prod_z_in(frm):
        here = prods_land.at[frm]
        return remote(here, here, t_send.at[3 + frm], t_recv.at[3 + frm], at_z(frm))

    barrier = pltpu.get_barrier_semaphore()
    for device in [at_z(o) for o in others] + [across_y, across_x, across_c]:
        pl.semaphore_signal(barrier, inc=1, device_id=device, device_id_type=MESH)
    pl.semaphore_wait(barrier, 6)

    for to in others:
        w_z(0, to).start()
    x_copy(0, 0).start()
    x_copy(0, 1).start()
    w_own(0).start()
    cot_fetch(0, 0, 0).start()

    image_row = lax.broadcasted_iota(jnp.int32, (images, images), 0)
    image_col = lax.broadcasted_iota(jnp.int32, (images, images), 1)
    crops = counts[...].astype(F32)
    ends = jnp.dot(
        jnp.broadcast_to(crops, (8, images)), (image_row <= image_col).astype(F32),
        precision=lax.Precision.HIGHEST, preferred_element_type=F32,
    )[0:1]
    starts = ends - crops
    block = mask.shape[1]
    lane = scale.shape[1]

    for r in range(rows // block):
        index = (
            lax.broadcasted_iota(jnp.int32, (block, images), 0) + r * block
        ).astype(F32)
        inside = (index >= starts) & (index < ends)
        count_row = jnp.sum(jnp.where(inside, crops, 0.0), axis=1, keepdims=True)
        diagonal = lax.broadcasted_iota(jnp.int32, (block, block), 0) == (
            lax.broadcasted_iota(jnp.int32, (block, block), 1)
        )
        usable = jnp.sum(
            jnp.where(diagonal, mask[r : r + 1, :].astype(F32), 0.0),
            axis=1, keepdims=True,
        )
        live = (count_row > 0.0) & (usable == 1.0)
        share = jnp.where(live, 1.0 / jnp.maximum(count_row, 1.0), 0.0)
        scale[r * block : (r + 1) * block, :] = jnp.broadcast_to(share, (block, lane))

    for frm in others:
        w_z_in(0, frm).wait_recv()
        w_x(0, frm).start()
    for to in others:
        w_z(1, to).start()
    w_own(1).start()
    for frm in others:
        w_x_in(0, frm).wait_recv()
        w_c(0, frm).start()
    x_copy(0, 0).wait_recv()
    for copy in x_fetch(0, 0, 0):
        copy.start()

    def final(at, later):
        p, i, slot, t, h, buf = at.p, at.i, at.slot, at.t, at.h, at.buf
        cot_fetch(h, i, buf).wait()

        @pl.when(at.u >= 2 * n_part + 2)
        def _():
            mixed_out(h, i, buf).wait()

        @pl.when(i == 0)
        def _():
            stat[p] = jnp.zeros(stat.shape[1:], F32)

        lanes = cols(h)
        shift = bias[pl.ds(t, 1), lanes]
        st = [stitch[s, pl.ds(t, 1), lanes] for s in range(2)]
        band = min(BAND, part)

        def step(r, carry):
            here = part_rows_of(r, band)
            there = pl.ds(mult(i * part + r * band, band), band)
            value = pf[at.prod, z, here, :]
            below = wide(rs[slot, z + 1, here, :])
            above = wide(rs[slot, z, here, :])
            value = value + jnp.where(z > 0, below, 0.0) + jnp.where(z < ZED - 1, above, 0.0)
            pre = value + shift
            phi = 0.5 * (1.0 + lax.erf(pre * 0.7071067811865476))
            hidden = pre * phi
            slope = phi + pre * (jnp.exp(-0.5 * pre * pre) * 0.3989422804014327)
            weight = scale[there, 0:1]
            first = wide(cc[buf, 0, here, :]) * weight
            second = wide(cc[buf, 1, here, :]) * weight
            back0 = st[0] * first * slope
            back1 = st[1] * second * slope
            gl[p, there, cols(z)] = half(back0 + back1)

            def fold(v):
                return jnp.sum(v.reshape(band // 8, 8, hw), axis=0)

            stat[p, 0] += fold(back0)
            stat[p, 1] += fold(back1)
            stat[p, 2] += fold(first * hidden)
            stat[p, 3] += fold(second * hidden)

            @pl.when(t == 0)
            def _():
                h0[h, there, :] = hidden

            @pl.when(t == 1)
            def _():
                before = h0[h, there, :]
                for s in range(2):
                    mx[buf, s, here, :] = half(
                        stitch[s, 0:1, lanes] * before + st[s] * hidden
                    )

            return carry

        lax.fori_loop(0, part // band, step, 0)

        @pl.when(z < ZED - 1)
        def _():
            ag(at, z, 0, up).start()

        @pl.when(z > 0)
        def _():
            ag(at, z, 1, down).start()

        @pl.when(t == 1)
        def _():
            mixed_out(h, i, buf).start()

        @pl.when(at.u + 1 < parts)
        def _():
            cot_fetch(later.h, later.i, later.buf).start()

    def part_rows_of(r, band):
        return pl.ds(mult(r * band, band), band)

    def forward_ag(at, far):
        @pl.when((at.u >= 0) & (at.u < parts))
        def _():
            @pl.when(z - far >= 0)
            def _():
                ag(at, z - far, 0, up).wait_recv()

                @pl.when(z < ZED - 1)
                def _():
                    ag(at, z - far, 0, up).start()

            @pl.when(z + far < ZED)
            def _():
                ag(at, z + far, 1, down).wait_recv()

                @pl.when(z > 0)
                def _():
                    ag(at, z + far, 1, down).start()

    def dx_part(t, i, hk):
        there = chunk_rows(i)
        krows = pl.ds(mult(deep * hk, deep), deep)
        acc = None
        for h in range(HALVES):
            term = lax.dot_general(
                gl[2 * t + h, there, :], wv[2 * t + h, krows, :],
                (((1,), (1,)), ((), ())), preferred_element_type=F32,
            )
            acc = term if acc is None else acc + term
        return acc

    def dx_step(t, i, buf):
        @pl.when((i >= HELD) | (t > 0))
        def _():
            dx_copy(t, i, buf).wait_send()

        dsend[buf] = half(dx_part(t, i, 1 - y))
        dx_copy(t, i, buf).start()
        own[buf] = dx_part(t, i, y)

    def dx_begin(t, i, buf):
        dx_copy(t, i, buf).wait_recv()
        dx_fetch(t, i).start()

    def dx_final(t, i, buf):
        @pl.when((i >= 1) | (t > 0))
        def _():
            dx_out(t, i).wait()

        dx_fetch(t, i).wait()

        def step(j, inner):
            lanes = pl.ds(mult(tile * j, tile), tile)
            dout[:, lanes] = half(own[buf, :, lanes] + wide(dfetch[:, lanes]))
            return inner

        lax.fori_loop(0, 3, step, 0)
        dx_out(t, i).start()

    def listed(u, times, do):
        e, hit = 0, False
        for index, time in enumerate(times):
            same = u == time
            e = jnp.where(same, index, e)
            hit = hit | same

        @pl.when(hit)
        def _():
            do(e)

    def chunk_of(do):
        def run(e):
            t = jnp.where(e >= n_chunk, 1, 0)
            do(t, e - n_chunk * t, lax.rem(e, HELD))

        return run

    def turn():
        lanes_at_once = min(128, tile)

        def step(q, carry):
            lanes = pl.ds(mult(q * lanes_at_once, lanes_at_once), lanes_at_once)
            xt[lanes, :] = xsrc[:, lanes].T
            return carry

        lax.fori_loop(0, tile // lanes_at_once, step, 0)

    def tile_dot(g):
        return jnp.dot(xt[...], gl[g.p], preferred_element_type=F32)

    def stage_one(g):
        tile_fetch(g.t, g.j, 1 - c, False)
        turn()
        tile_fetch(g.t, g.j, c, True)
        cstage[...] = half(tile_dot(g))
        core_copy(g).start()

    def stage_two(g):
        tile_fetch(g.t, g.j, c, False)
        turn()

        @pl.when(g.j < 2)
        def _():
            tile_fetch(g.t, g.j + 1, 1 - c, True)

        core_copy(g).wait()
        product = tile_dot(g)
        for b in range(ZED):
            block = product[:, b * hw : (b + 1) * hw] + wide(
                cland[g.buf, :, b * hw : (b + 1) * hw]
            )
            left, right = block[:, :xw], block[:, xw:]
            kept[g.trio, b] = jnp.where(x == 0, left, right)
            xstage[g.trio, b] = half(jnp.where(x == 0, right, left))

        def send(q, carry):
            across_copy(g, lax.rem(z + 3 + 3 * q, ZED)).start()
            return carry

        lax.fori_loop(0, ZED, send, 0)

    def stage_three(g):
        @pl.when(g.g >= 3)
        def _():
            for to in others:
                z_copy(g, to).wait_send()
            ax_own(g).wait_send()

        def add(b):
            across_copy(g, b).wait()
            zstage[g.trio, b] = half(kept[g.trio, b] + wide(xland[g.quad, b]))

        def step(q, carry):
            b = lax.rem(z + 3 + 3 * q, ZED)
            add(b)
            z_copy(g, b).start()
            return carry

        lax.fori_loop(0, ZED - 1, step, 0)
        add(z)
        z_own(g).start()
        ax_own(g).start()

    def stage_four(g):
        def step(q, carry):
            b = lax.rem(z + 1 + q, ZED)
            z_in(g, b).wait_recv()
            ax_copy(g, b).start()
            return carry

        lax.fori_loop(0, ZED - 1, step, 0)
        z_own(g).wait()

    def stage_five(g):
        def step(q, carry):
            b = lax.rem(z + q, ZED)
            ax_in(g, b).wait_recv()
            ac_copy(g, b).start()
            return carry

        lax.fori_loop(0, ZED, step, 0)

    def stage_six(g):
        def step(b, carry):
            ac_in(g, b).wait_recv()
            return carry

        lax.fori_loop(0, ZED, step, 0)

    after = parts
    dx_times = [n_part + 7 + 2 * i for i in range(6)] + [3 * n_part + 7 + 2 * i for i in range(6)]
    dx_begins = [time + 3 for time in dx_times[:6]]
    dx_begins += [after - 2, after, after + 9, after + 11, after + 13, after + 15]
    dx_ends = [time + 4 for time in dx_times[:6]]
    dx_ends += [after - 1, after + 1, after + 10, after + 12, after + 14, after + 17]
    ones = [n_part * p + n_part + 6 + 4 * j for p in range(2) for j in range(3)]
    twos = [time + 2 for time in ones]
    threes = [time + 5 for time in ones]
    fours = [time + 8 for time in ones]
    fives = [time + 10 for time in ones]
    sixes = [time + 12 for time in ones]
    ones += [after - 6, after - 4, after - 2]
    twos += [after - 5, after - 3, after - 1]
    threes += [after - 2, after, after + 2]
    fours += [after + 2, after + 6, after + 7]
    fives += [after + 7, after + 9, after + 10]
    sixes += [after + 9, after + 11, after + 12]
    ones += [after + 6, after + 7, after + 8]
    twos += [after + 7, after + 8, after + 9]
    threes += [after + 10, after + 11, after + 13]
    fours += [after + 12, after + 14, after + 16]
    fives += [after + 15, after + 17, after + 18]
    sixes += [after + 16, after + 18, after + 19]

    def tile_of(g):
        p = lax.div(g, 3)
        t, h = tower(p)
        return Tile(
            g=g, p=p, t=t, h=h, j=g - 3 * p,
            buf=lax.rem(g, 2), trio=g - 3 * p, quad=lax.rem(g, 4),
        )

    def tile_in_hand(do):
        return lambda g: do(tile_of(g))

    def body(u, carry):
        p0 = lax.div(u, n_part)
        i0 = u - p0 * n_part
        slot0, prod0 = lax.rem(u, RING), lax.rem(u, PRODUCTS)
        buf0 = lax.rem(u, 2)

        def before(lag):
            if isinstance(lag, int):
                whole, left = divmod(lag, n_part)
            else:
                whole, left = 0, lag
            under = i0 < left
            p = p0 - whole - jnp.where(under, 1, 0)
            i = i0 - left + jnp.where(under, n_part, 0)
            in_ring = lag % RING if isinstance(lag, int) else lag
            in_prods = lag % PRODUCTS if isinstance(lag, int) else lag
            slot = slot0 - in_ring + jnp.where(slot0 < in_ring, RING, 0)
            prod = prod0 - in_prods + jnp.where(prod0 < in_prods, PRODUCTS, 0)
            t, h = tower(p)
            return Part(u=u - lag, p=p, i=i, t=t, h=h, slot=slot, prod=prod, buf=lax.rem(i, 2))

        @pl.when((u >= 5) & (u < parts + 5))
        def _():
            slot = before(5).slot
            at_place(0, ZED - 2, lambda zz: rs_up(slot, zz).wait_send())
            at_place(1, ZED - 1, lambda zz: rs_down(slot, zz).wait_send())

        @pl.when((u >= 8) & (u < parts + 8))
        def _():
            at = before(8)

            def step(b, inner):
                @pl.when((z < ZED - 1) & (b <= z))
                def _():
                    ag(at, b, 0, up).wait_send()

                @pl.when((z > 0) & (b >= z))
                def _():
                    ag(at, b, 1, down).wait_send()

                return inner

            lax.fori_loop(0, ZED, step, 0)

        ck = lax.div(i0, SUB)
        fresh = ck * SUB == i0
        t0, h0_ = tower(p0)
        xbuf = lax.rem(ck, 2)

        @pl.when((u < parts) & fresh)
        def _():
            @pl.when(i0 == 0)
            def _():
                w_own(p0).wait()
                for frm in others:
                    w_c_in(p0, frm).wait_recv()

            for copy in x_fetch(t0, ck, xbuf):
                copy.wait()

            product = jnp.dot(xc[xbuf], wv[p0], preferred_element_type=F32)
            for b in range(ZED):
                for s in range(SUB):
                    pf[prod0 + s, b] = product[
                        s * part : (s + 1) * part, b * hw : (b + 1) * hw
                    ]

        going_up = before(z)

        @pl.when((going_up.u >= 0) & (going_up.u < parts))
        def _():
            slot, prod = going_up.slot, going_up.prod
            at_place(1, ZED - 1, lambda zz: rs_from_below(slot, zz).wait_recv())

            @pl.when(z == 0)
            def _():
                for b in range(1, ZED):
                    rs[slot, b + 1] = half(pf[prod, b])

            @pl.when(z > 0)
            def _():
                def step(b, inner):
                    rs[slot, b + 1] = half(wide(rs[slot, b + 1]) + pf[prod, b])
                    return inner

                lax.fori_loop(z + 1, ZED, step, 0)

            at_place(0, ZED - 2, lambda zz: rs_up(slot, zz).start())

        going_down = before(ZED - 1 - z)

        @pl.when((going_down.u >= 0) & (going_down.u < parts))
        def _():
            slot, prod = going_down.slot, going_down.prod
            at_place(0, ZED - 2, lambda zz: rs_from_above(slot, zz).wait_recv())

            @pl.when(z == ZED - 1)
            def _():
                for b in range(ZED - 1):
                    rs[slot, b] = half(pf[prod, b])

            @pl.when(z < ZED - 1)
            def _():
                def step(b, inner):
                    rs[slot, b] = half(wide(rs[slot, b]) + pf[prod, b])
                    return inner

                lax.fori_loop(0, z, step, 0)

            at_place(1, ZED - 1, lambda zz: rs_down(slot, zz).start())

        @pl.when(fresh & (u + 2 * SUB < 2 * n_part))
        def _():
            k = p0 * n_chunk + ck + 2
            over = jnp.where(k >= n_chunk, 1, 0)
            x_copy(over, k - over * n_chunk).start()

        @pl.when(fresh & (u + SUB < parts))
        def _():
            wrap = jnp.where(ck + 1 == n_chunk, 1, 0)
            i = ck + 1 - wrap * n_chunk
            t, h = tower(p0 + wrap)

            @pl.when(h == 0)
            def _():
                x_copy(t, i).wait_recv()

            for copy in x_fetch(t, i, lax.rem(i, 2)):
                copy.start()

        @pl.when((u >= 3) & (u < parts + 3))
        def _():
            final(before(3), before(2))

        forward_ag(before(4), 1)
        forward_ag(before(5), 2)
        forward_ag(before(6), 3)

        listed(u, dx_begins, chunk_of(dx_begin))
        listed(u, dx_ends, chunk_of(dx_final))
        listed(u, dx_times, chunk_of(dx_step))

        listed(u, threes, tile_in_hand(stage_three))
        listed(u, twos, tile_in_hand(stage_two))
        listed(u, ones, tile_in_hand(stage_one))
        listed(u, fours, tile_in_hand(stage_four))
        listed(u, fives, tile_in_hand(stage_five))
        listed(u, sixes, tile_in_hand(stage_six))

        @pl.when((i0 == 5) & (p0 > 0) & (p0 < PHASES + 1))
        def _():
            t, _h = tower(p0 - 1)
            tile_fetch(t, 0, 1 - c, True)

        @pl.when(p0 + 1 < PHASES)
        def _():
            @pl.when((i0 < 6) & (p0 > 0))
            def _():
                for to in others:
                    w_z_strip(p0 + 1, to, i0).start()

            for q in range(3):
                @pl.when(i0 == q + 7)
                def _(q=q):
                    w_z_in(p0 + 1, others[q]).wait_recv()
                    w_x(p0 + 1, others[q]).start()

                @pl.when(i0 == q + 9)
                def _(q=q):
                    w_x_in(p0 + 1, others[q]).wait_recv()
                    w_c(p0 + 1, others[q]).start()

            @pl.when((i0 == 1) & (p0 > 0))
            def _():
                w_own(p0 + 1).start()

        @pl.when(u == parts + 3)
        def _():
            for p in range(PHASES):
                t, h = p // HALVES, p % HALVES
                for s in range(2):
                    for what in range(2):
                        sums[0, pl.ds(4 * what + 2 * s + t, 1), h * hw : (h + 1) * hw] = jnp.sum(
                            stat[p, 2 * what + s], axis=0, keepdims=True
                        )
            sum_copy(0, across_c).start()

        @pl.when(u == parts + 4)
        def _():
            sum_copy(0, across_c).wait()
            sums[1] = sums[0] + sums_land[0]
            sum_copy(1, across_x).start()

        @pl.when(u == parts + 5)
        def _():
            sum_copy(1, across_x).wait()
            both = sums[1] + sums_land[1]
            sums[2] = both
            member = (
                lax.broadcasted_iota(jnp.int32, (width, lane), 0) % FLAG_GROUPS
                == lax.broadcasted_iota(jnp.int32, (width, lane), 1) % FLAG_GROUPS
            ).astype(F32)
            bias_rows = both[0:4]
            inner = both[0:2] * both[2:4]
            stack = jnp.concatenate([inner, bias_rows * bias_rows, inner], axis=0)
            prods[0] = jnp.dot(
                stack, member, precision=lax.Precision.HIGHEST, preferred_element_type=F32
            )
            prod_y().start()

        @pl.when(u == parts + 6)
        def _():
            prod_y().wait()
            prods[1] = prods[0] + prods_land[ZED]
            for to in others:
                prod_z(to).start()

        @pl.when(u == parts + 7)
        def _():
            for frm in others:
                prod_z_in(frm).wait_recv()
            prods_land[z] = prods[1]
            whole = prods_land[0] + prods_land[1] + prods_land[2] + prods_land[3]
            both = sums[2]
            group = lax.broadcasted_iota(jnp.int32, (1, lane), 1) % FLAG_GROUPS

            def over(row):
                return jnp.concatenate([row] * (width // lane), axis=1)

            def flag_row(s, t):
                row = jnp.zeros((1, lane), F32)
                for g in range(FLAG_GROUPS):
                    row = jnp.where(group == g, flags[s, t, g].astype(F32), row)
                return row

            for t in range(2):
                task0, task1 = both[t : t + 1], both[2 + t : 3 + t]
                dots = whole[t : t + 1]
                coef0 = over(flag_row(0, t) * dots / (whole[4 + t : 5 + t] + 1e-06))
                coef1 = over(flag_row(1, t) * dots / (whole[2 + t : 3 + t] + 1e-06))
                gbias[t : t + 1] = (task0 - coef0 * task1) + (task1 - coef1 * task0)
            for s in range(2):
                gstitch[s] = both[4 + 2 * s : 6 + 2 * s]

        return carry

    lax.fori_loop(0, after + 20, body, 0)

    last = 3 * PHASES - 1

    for g in (last - 2, last - 1, last):
        for to in others:
            z_copy(tile_of(g), to).wait_send()
        ax_own(tile_of(g)).wait_send()
    for i in range(n_chunk - HELD, n_chunk):
        dx_copy(1, i, (n_chunk + i) % HELD).wait_send()
    for i in (n_part - 2, n_part - 1):
        mixed_out(1, i, i % 2).wait()
    dx_out(1, n_chunk - 1).wait()

    def drain_tiles(g, carry):
        at = tile_of(g)
        for b in others:
            ax_copy(at, b).wait_send()
        for b in range(ZED):
            ac_copy(at, b).wait_send()
        return carry

    lax.fori_loop(0, last + 1, drain_tiles, 0)

    def drain_x(i, carry):
        x_copy(0, i).wait_send()
        x_copy(1, i).wait_send()
        return carry

    lax.fori_loop(0, n_chunk, drain_x, 0)

    def drain_w(p, carry):
        for to in others:
            w_z(p, to).wait_send()
            w_x(p, to).wait_send()
            w_c(p, to).wait_send()
        return carry

    lax.fori_loop(0, PHASES, drain_w, 0)
    for to in others:
        prod_z(to).wait_send()


def fused_call(feat, wts, cot, bias, stitch, counts, mask, flags):
    rows, deep, width = feat.shape[1], feat.shape[2], wts.shape[2]
    chunk = rows // 6
    part = chunk // SUB
    hw, kz, tile = width // 2, 2 * deep, deep // 3
    cat, xw = 4 * hw, width // 4
    lane = min(128, width)
    dma = pltpu.SemaphoreType.DMA
    anywhere = pl.BlockSpec(memory_space=pl.ANY)
    inside = pl.BlockSpec(memory_space=pltpu.VMEM)
    scalars = pl.BlockSpec(memory_space=pltpu.SMEM)

    def v(shape, kind=BF16):
        return pltpu.VMEM(shape, kind)

    out_shape = [
        jax.ShapeDtypeStruct((2, rows, width), BF16),
        jax.ShapeDtypeStruct((2, rows, deep), BF16),
        jax.ShapeDtypeStruct((2, ZED, kz, width), BF16),
        jax.ShapeDtypeStruct((2, width), F32),
        jax.ShapeDtypeStruct((2, 2, width), F32),
        jax.ShapeDtypeStruct((2, rows, deep), BF16),
        jax.ShapeDtypeStruct((2, rows, deep), BF16),
    ]
    scratch = [
        v((PHASES, kz, cat)),
        v((PHASES, rows, cat)),
        v((RING, 5, part, hw)),
        v((2, rows, hw), F32),
        v((2, chunk, kz)),
        v((PRODUCTS, ZED, part, hw), F32),
        v((2, 2, part, hw)),
        v((2, 2, part, hw)),
        v((HELD, chunk, deep), F32),
        v((HELD, chunk, deep)),
        v((chunk, deep)),
        v((chunk, deep)),
        v((rows, tile)),
        v((tile, rows)),
        v((tile, cat)),
        v((2, tile, cat)),
        v((3, ZED, tile, xw)),
        v((4, ZED, tile, xw)),
        v((3, ZED, tile, xw), F32),
        v((3, ZED, tile, xw)),
        v((rows, lane), F32),
        v((PHASES, 4, 8, hw), F32),
        v((3, 8, width), F32),
        v((2, 8, width), F32),
        v((2, 8, lane), F32),
        v((5, 8, lane), F32),
        dma((RING, 2)), dma((RING, 2)), dma((RING, 8)), dma((RING, 4)),
        dma((12,)), dma((12,)),
        dma((4, 4)), dma((4, 4)), dma((4, 4)), dma((4, 4)), dma((4, 4)), dma((4, 4)), dma((4,)),
        dma((2, 2)), dma((2,)), dma((2,)), dma((HELD,)), dma((12,)), dma((1,)), dma((1,)),
        dma((1,)), dma((1,)), dma((2,)), dma((3, 4)), dma((4, 4)), dma((3, 4)), dma((12, 4)),
        dma((3,)), dma((3,)),
        dma((12, 4)), dma((12, 4)), dma((12, 4)), dma((12, 4)), dma((8,)), dma((8,)),
    ]
    flops = 3 * 2 * 2 * rows * kz * cat * 2
    return pl.pallas_call(
        functools.partial(fused_kernel, rows, deep, width, chunk),
        out_shape=out_shape,
        in_specs=[anywhere] * 3 + [inside] * 4 + [scalars],
        out_specs=[anywhere] * 3 + [inside] * 2 + [anywhere] * 2,
        scratch_shapes=scratch,
        compiler_params=pltpu.CompilerParams(
            collective_id=0, has_side_effects=True, vmem_limit_bytes=64 * 1024 * 1024
        ),
        cost_estimate=pl.CostEstimate(
            flops=flops, bytes_accessed=200_000_000, transcendentals=2 * rows * width * 2
        ),
        name="cross_stitch_step",
    )(feat, wts, cot, bias, stitch, counts, mask, flags)


def widen_kernel(block, low, out, taken, given, in_sem, out_sem):
    n_block = low.shape[0] // block

    def take(i):
        return pltpu.make_async_copy(
            low.at[pl.ds(i * block, block)], taken.at[i % WIDEN_SLOTS], in_sem.at[i % WIDEN_SLOTS]
        )

    def give(i):
        return pltpu.make_async_copy(
            given.at[i % WIDEN_SLOTS], out.at[pl.ds(i * block, block)], out_sem.at[i % WIDEN_SLOTS]
        )

    for i in range(min(WIDEN_SLOTS, n_block)):
        take(i).start()
    for i in range(n_block):
        slot = i % WIDEN_SLOTS
        take(i).wait()
        if i >= WIDEN_SLOTS:
            give(i - WIDEN_SLOTS).wait()
        given[slot] = wide(taken[slot])
        give(i).start()
        if i + WIDEN_SLOTS < n_block:
            take(i + WIDEN_SLOTS).start()
    for i in range(max(0, n_block - WIDEN_SLOTS), n_block):
        give(i).wait()


def widen(low):
    tall, width = low.shape
    block = tall // WIDEN_BLOCKS
    anywhere = pl.BlockSpec(memory_space=pl.ANY)
    return pl.pallas_call(
        functools.partial(widen_kernel, block),
        in_specs=[anywhere],
        out_specs=anywhere,
        out_shape=jax.ShapeDtypeStruct(low.shape, F32),
        scratch_shapes=[
            pltpu.VMEM((WIDEN_SLOTS, block, width), BF16),
            pltpu.VMEM((WIDEN_SLOTS, block, width), F32),
            pltpu.SemaphoreType.DMA((WIDEN_SLOTS,)),
            pltpu.SemaphoreType.DMA((WIDEN_SLOTS,)),
        ],
        compiler_params=pltpu.CompilerParams(vmem_limit_bytes=48 * 1024 * 1024),
        cost_estimate=pl.CostEstimate(
            flops=tall * width, bytes_accessed=6 * tall * width, transcendentals=0
        ),
        name="widen",
    )(low)


def fused_plan(mesh):
    def per_device(features, weights, bias, stitch, cotangent, crop_counts, row_mask, flags):
        rows, deep = features.shape[1:]
        width = weights.shape[2]
        mixed, gfeat, gwt, gbias, gstitch, _, _ = fused_call(
            features, weights, cotangent, bias, stitch,
            crop_counts.reshape(1, -1), row_mask.reshape(-1, min(128, rows // 6)), flags,
        )
        grad_weights = widen(gwt.reshape(-1, width)).reshape(2, ZED * 2 * deep, width)
        return mixed, gfeat, grad_weights, gbias, gstitch

    return per_device


def plan_for(mesh):
    if mesh.shape["batch"] == 4 and mesh.shape["mp"] == 2 * ZED:
        return fused_plan(mesh)
    return generic_plan(mesh)


def solution(mesh):
    in_specs = (
        P(None, "batch", "mp"),
        P(None, None, "mp"),
        P(None, "mp"),
        P(None, None, "mp"),
        P(None, "batch", "mp"),
        P("batch"),
        P("batch"),
        P(),
    )
    out_specs = (
        P(None, "batch", "mp"),
        P(None, "batch", "mp"),
        P(None, None, "mp"),
        P(None, "mp"),
        P(None, None, "mp"),
    )
    return jax.shard_map(
        plan_for(mesh), mesh=mesh, in_specs=in_specs, out_specs=out_specs, check_vma=False
    )
```

```python
import collections
import functools

import jax
import jax.numpy as jnp
from jax import lax
from jax.experimental import pallas as pl
from jax.experimental.pallas import tpu as pltpu
from jax.sharding import PartitionSpec as P

FLAG_GROUPS = 8
OUTER = 4


def row_weights(counts, mask):
    ends = jnp.cumsum(counts)
    starts = ends - counts
    index = lax.broadcasted_iota(jnp.int32, (mask.shape[0], counts.shape[0]), 0)
    inside = (index >= starts[None, :]) & (index < ends[None, :])
    count_row = jnp.sum(jnp.where(inside, counts[None, :], 0), axis=1)
    live = (count_row > 0) & (mask == 1)
    return jnp.where(live, 1.0 / jnp.maximum(count_row, 1).astype(jnp.float32), 0.0)


def project_bias(task_bias, flags):
    local_width = task_bias.shape[2]
    channel = lax.axis_index("mp") * local_width + lax.broadcasted_iota(
        jnp.int32, (local_width, FLAG_GROUPS), 0
    )
    member = (
        channel % FLAG_GROUPS == lax.broadcasted_iota(jnp.int32, (local_width, FLAG_GROUPS), 1)
    ).astype(jnp.float32)
    dots = jnp.dot(task_bias[0] * task_bias[1], member, precision=lax.Precision.HIGHEST)
    norms = jnp.einsum(
        "stc,cg->stg", task_bias * task_bias, member, precision=lax.Precision.HIGHEST
    )
    dots, norms = lax.psum((dots, norms), "mp")
    flag = flags.astype(jnp.float32)
    coef_first = jnp.dot(
        flag[0] * dots / (norms[1] + 1e-06), member.T, precision=lax.Precision.HIGHEST
    )
    coef_second = jnp.dot(
        flag[1] * dots / (norms[0] + 1e-06), member.T, precision=lax.Precision.HIGHEST
    )
    first = task_bias[0] - coef_first * task_bias[1]
    second = task_bias[1] - coef_second * task_bias[0]
    return first + second


def generic_plan(mesh):
    n_mp = mesh.shape["mp"]
    n_batch = mesh.shape["batch"]
    inner = n_mp // OUTER
    inner_groups = [[o * inner + i for i in range(inner)] for o in range(OUTER)]
    outer_groups = [[o * inner + i for o in range(OUTER)] for i in range(inner)]

    def per_device(features, weights, bias, stitch, cotangent, crop_counts, row_mask, flags):
        rows = features.shape[1]
        width = weights.shape[2]
        depth = features.shape[2] * inner
        held = lax.all_gather(
            features, "mp", axis=2, tiled=True, axis_index_groups=inner_groups
        )
        split = weights.reshape(2, OUTER, depth, width)
        block = lax.all_to_all(
            split, "mp", split_axis=1, concat_axis=1, axis_index_groups=outer_groups
        )
        block = block.reshape(2, OUTER, depth, width)
        part = jnp.einsum("trk,tokc->otrc", held, block, preferred_element_type=jnp.float32)
        linear = lax.psum_scatter(
            part.astype(jnp.bfloat16),
            "mp",
            scatter_dimension=0,
            axis_index_groups=outer_groups,
        ).astype(jnp.float32)
        pre = linear + bias[:, None, :]
        hidden, gelu_back = jax.vjp(lambda v: jax.nn.gelu(v, approximate=False), pre)
        mixed = stitch[:, 0, None, :] * hidden[0][None] + stitch[:, 1, None, :] * hidden[1][None]
        scale_rows = row_weights(crop_counts, row_mask)
        grad_out = cotangent.astype(jnp.float32) * scale_rows[None, :, None]
        first_task = gelu_back(stitch[0][:, None, :] * grad_out[0][None])[0]
        second_task = gelu_back(stitch[1][:, None, :] * grad_out[1][None])[0]
        task_bias = jnp.stack([jnp.sum(first_task, axis=1), jnp.sum(second_task, axis=1)])
        grad_linear = (first_task + second_task).astype(jnp.bfloat16)
        grad_stitch = jnp.sum(grad_out[:, None] * hidden[None], axis=2)
        every = lax.all_gather(grad_linear, "mp", axis_index_groups=outer_groups)
        grad_part = jnp.einsum(
            "otrc,tokc->trk", every, block, preferred_element_type=jnp.float32
        )
        grad_part = grad_part.astype(jnp.bfloat16).reshape(2, rows, inner, depth // inner)
        grad_features = lax.psum_scatter(
            grad_part.transpose(2, 0, 1, 3),
            "mp",
            scatter_dimension=0,
            axis_index_groups=inner_groups,
        )
        weight_part = jnp.einsum(
            "trk,otrc->otkc", held, every, preferred_element_type=jnp.float32
        )
        weight_part = weight_part.astype(jnp.bfloat16).reshape(
            OUTER, 2, n_batch, depth // n_batch, width
        )
        share = lax.psum_scatter(
            weight_part.transpose(2, 0, 1, 3, 4), "batch", scatter_dimension=0
        )
        share = lax.all_to_all(
            share, "mp", split_axis=0, concat_axis=0, axis_index_groups=outer_groups
        )
        share = share.reshape(OUTER, 2, depth // n_batch, width)
        whole = lax.all_gather(share, "batch")
        grad_weights = whole.transpose(2, 1, 0, 3, 4).reshape(2, OUTER * depth, width)
        task_bias, grad_stitch = lax.psum((task_bias, grad_stitch), "batch")
        grad_bias = project_bias(task_bias, flags)
        return (
            mixed.astype(jnp.bfloat16),
            grad_features.astype(jnp.bfloat16),
            grad_weights.astype(jnp.float32),
            grad_bias,
            grad_stitch,
        )

    return per_device


MESH = pl.DeviceIdType.MESH
BF16 = jnp.bfloat16
F32 = jnp.float32
ZED = 4
HALVES = 2
PHASES = 4
RING = 8
BAND = 32
SUB = 2
PRODUCTS = 6
HELD = 4
WIDEN_BLOCKS = 12
WIDEN_SLOTS = 4

DX_TIMES = (20, 21, 23, 25, 27, 29, 43, 45, 48, 50, 58, 64)
DX_BEGINS = (22, 24, 26, 28, 30, 34, 44, 48, 57, 60, 68, 76)
DX_ENDS = (23, 25, 27, 29, 31, 43, 45, 50, 59, 62, 71, 81)
ONES = (19, 23, 26, 30, 33, 40, 43, 45, 46, 54, 56, 57)
TWOS = (22, 26, 27, 32, 36, 42, 44, 46, 49, 55, 57, 61)
THREES = (23, 28, 33, 35, 42, 43, 45, 52, 55, 58, 59, 70)
FOURS = (25, 30, 35, 37, 44, 47, 50, 54, 60, 67, 68, 73)
FIVES = (33, 36, 44, 45, 51, 59, 62, 67, 74, 76, 82, 85)
SIXES = (35, 43, 47, 57, 64, 70, 75, 82, 84, 86, 87, 90)
W_STRIPS = {2: (5, 7, 8, 11, 12, 13), 3: (21, 22, 23, 24, 26, 27)}
W_ACROSS = {1: (0, 0, 2), 2: (16, 21, 22), 3: (29, 29, 34)}
W_CORES = {1: (1, 6, 7), 2: (21, 23, 23), 3: (33, 33, 35)}


Part = collections.namedtuple("Part", ("u", "p", "i", "t", "h", "slot", "prod", "buf"))
Tile = collections.namedtuple("Tile", ("g", "p", "t", "h", "j", "buf", "trio", "quad"))


def half(value):
    return value.astype(BF16)


def wide(value):
    return value.astype(F32)


def fused_kernel(
    rows, deep, width, chunk,
    feat, wts, cot, bias, stitch, counts, mask, flags,
    mixed, gfeat, gwt, gbias, gstitch, xn, dxn,
    wv, gl, rs, h0, xc, pf, cc, mx, own, dsend, dfetch, dout,
    xsrc, xt, cstage, cland, xstage, xland, kept, zstage,
    scale, stat, sums, sums_land, prods, prods_land,
    rs_send, rs_recv, ag_send, ag_recv, xs_send, xs_recv,
    wz_send, wz_recv, wx_send, wx_recv, wc_send, wc_recv, wl,
    xf, cf, mxs, dx_send, dx_recv, df, dod,
    tile_in, c_send, c_recv, x_send, x_recv, z_send, z_recv, zl, zx_send,
    ax_send, ax_recv, ac_send, ac_recv, t_send, t_recv,
):
    batch, mp = lax.axis_index("batch"), lax.axis_index("mp")
    z, y = mp // 2, mp % 2
    x, c = batch // 2, batch % 2
    up = {"mp": mp + 2}
    down = {"mp": mp - 2}
    across_y = {"mp": 2 * z + 1 - y}
    across_x = {"batch": 2 * (1 - x) + c}
    across_c = {"batch": 2 * x + 1 - c}

    def at_z(other):
        return {"mp": 2 * other + y}

    others = (3 - z, (z + 2) % 4, z + 1 - 2 * (z % 2))

    n_chunk = rows // chunk
    total = PHASES * n_chunk
    part = chunk // SUB
    n_part = rows // part
    parts = PHASES * n_part
    images = counts.shape[1]
    hw = width // HALVES
    kz = 2 * deep
    quarter = deep // 2
    tile = deep // 3
    strip = quarter // 6
    xw = hw // 2

    def mult(value, unit):
        return pl.multiple_of(value, unit)

    def remote(src, dst, send, recv, device):
        return pltpu.make_async_remote_copy(
            src_ref=src, dst_ref=dst, send_sem=send, recv_sem=recv,
            device_id=device, device_id_type=MESH,
        )

    def cols(b):
        return pl.ds(mult(b * hw, hw), hw)

    def chunk_rows(i):
        return pl.ds(mult(i * chunk, chunk), chunk)

    def part_rows(i):
        return pl.ds(mult(i * part, part), part)

    def tower(p):
        t = jnp.where(p >= HALVES, 1, 0)
        return t, p - HALVES * t

    def x_copy(t, i):
        e = t * n_chunk + i
        return remote(
            feat.at[t, chunk_rows(i)], xn.at[t, chunk_rows(i)],
            xs_send.at[e], xs_recv.at[e], across_y,
        )

    def x_fetch(t, i, buf):
        return (
            pltpu.make_async_copy(
                feat.at[t, chunk_rows(i)],
                xc.at[buf, :, pl.ds(mult(deep * y, deep), deep)], xf.at[buf, 0],
            ),
            pltpu.make_async_copy(
                xn.at[t, chunk_rows(i)],
                xc.at[buf, :, pl.ds(mult(deep * (1 - y), deep), deep)], xf.at[buf, 1],
            ),
        )

    def cot_fetch(h, i, buf):
        return pltpu.make_async_copy(
            cot.at[:, part_rows(i), cols(h)], cc.at[buf], cf.at[buf]
        )

    def w_own(p):
        t, h = tower(p)
        return pltpu.make_async_copy(
            wts.at[t, pl.ds(mult(kz * z, kz), kz), cols(h)], wv.at[p, :, cols(z)], wl.at[p],
        )

    def w_rows():
        return pl.ds(mult(deep * c + quarter * x, quarter), quarter)

    def w_z(p, to):
        t, h = tower(p)
        return remote(
            wts.at[
                t, pl.ds(mult(kz * to + deep * c + quarter * x, quarter), quarter), cols(h)
            ],
            wv.at[p, w_rows(), cols(z)],
            wz_send.at[p, to], wz_recv.at[p, z], at_z(to),
        )

    def w_z_strip(p, to, r):
        t, h = tower(p)
        at = deep * c + quarter * x + strip * r
        return remote(
            wts.at[t, pl.ds(mult(kz * to + at, strip), strip), cols(h)],
            wv.at[p, pl.ds(mult(at, strip), strip), cols(z)],
            wz_send.at[p, to], wz_recv.at[p, z], at_z(to),
        )

    def w_z_in(p, frm):
        here = wv.at[p, w_rows(), cols(frm)]
        return remote(here, here, wz_send.at[p, frm], wz_recv.at[p, frm], at_z(frm))

    def w_x(p, b):
        here = wv.at[p, w_rows(), cols(b)]
        return remote(here, here, wx_send.at[p, b], wx_recv.at[p, b], across_x)

    def w_x_in(p, b):
        here = wv.at[
            p, pl.ds(mult(deep * c + quarter * (1 - x), quarter), quarter), cols(b)
        ]
        return remote(here, here, wx_send.at[p, b], wx_recv.at[p, b], across_x)

    def w_c(p, b):
        here = wv.at[p, pl.ds(mult(deep * c, deep), deep), cols(b)]
        return remote(here, here, wc_send.at[p, b], wc_recv.at[p, b], across_c)

    def w_c_in(p, b):
        here = wv.at[p, pl.ds(mult(deep * (1 - c), deep), deep), cols(b)]
        return remote(here, here, wc_send.at[p, b], wc_recv.at[p, b], across_c)

    def rs_up(slot, zz):
        run = rs.at[slot, zz + 2 : ZED + 1]
        return remote(run, run, rs_send.at[slot, 0], rs_recv.at[slot, 0], up)

    def rs_down(slot, zz):
        run = rs.at[slot, 0:zz]
        return remote(run, run, rs_send.at[slot, 1], rs_recv.at[slot, 1], down)

    def rs_from_below(slot, zz):
        run = rs.at[slot, zz + 1 : ZED + 1]
        return remote(run, run, rs_send.at[slot, 0], rs_recv.at[slot, 0], down)

    def rs_from_above(slot, zz):
        run = rs.at[slot, 0 : zz + 1]
        return remote(run, run, rs_send.at[slot, 1], rs_recv.at[slot, 1], up)

    def at_place(first, last, do):
        for zz in range(first, last + 1):
            @pl.when(z == zz)
            def _(zz=zz):
                do(zz)

    def ag(at, b, going, device):
        here = gl.at[at.p, part_rows(at.i), cols(b)]
        return remote(
            here, here, ag_send.at[at.slot, going * ZED + b], ag_recv.at[at.slot, b], device
        )

    def dx_copy(t, i, buf):
        return remote(
            dsend.at[buf], dxn.at[t, chunk_rows(i)],
            dx_send.at[buf], dx_recv.at[t * n_chunk + i], across_y,
        )

    def dx_fetch(t, i):
        return pltpu.make_async_copy(dxn.at[t, chunk_rows(i)], dfetch, df.at[0])

    def dx_out(t, i):
        return pltpu.make_async_copy(dout, gfeat.at[t, chunk_rows(i)], dod.at[0])

    def mixed_out(h, i, buf):
        return pltpu.make_async_copy(
            mx.at[buf], mixed.at[:, part_rows(i), cols(h)], mxs.at[buf]
        )

    def tile_fetch(t, j, hk, start):
        lanes = pl.ds(mult(tile * j, tile), tile)
        near = pltpu.make_async_copy(feat.at[t, :, lanes], xsrc, tile_in.at[0])
        if not start:
            near.wait()
            return

        @pl.when(hk == y)
        def _():
            near.start()

        @pl.when(hk != y)
        def _():
            pltpu.make_async_copy(xn.at[t, :, lanes], xsrc, tile_in.at[0]).start()

    def core_copy(g):
        return remote(cstage, cland.at[g.buf], c_send.at[0], c_recv.at[g.buf], across_c)

    def across_copy(g, b):
        return remote(
            xstage.at[g.trio, b], xland.at[g.quad, b],
            x_send.at[g.trio, b], x_recv.at[g.quad, b], across_x,
        )

    def piece(g, source, core, lanes, n_lanes):
        return gwt.at[
            g.t, source,
            pl.ds(mult(deep * core + tile * g.j, tile), tile),
            pl.ds(mult(hw * g.h + lanes, xw), n_lanes),
        ]

    def z_copy(g, to):
        return remote(
            zstage.at[g.trio, to], piece(g, z, c, xw * x, xw),
            z_send.at[g.trio, to], z_recv.at[g.g, z], at_z(to),
        )

    def z_in(g, frm):
        here = piece(g, frm, c, xw * x, xw)
        return remote(here, here, z_send.at[g.trio, frm], z_recv.at[g.g, frm], at_z(frm))

    def z_own(g):
        return pltpu.make_async_copy(
            zstage.at[g.trio, z], piece(g, z, c, xw * x, xw), zl.at[g.trio]
        )

    def ax_own(g):
        return remote(
            zstage.at[g.trio, z], piece(g, z, c, xw * x, xw),
            zx_send.at[g.trio], ax_recv.at[g.g, z], across_x,
        )

    def ax_copy(g, b):
        here = piece(g, b, c, xw * x, xw)
        return remote(here, here, ax_send.at[g.g, b], ax_recv.at[g.g, b], across_x)

    def ax_in(g, b):
        here = piece(g, b, c, xw * (1 - x), xw)
        return remote(here, here, ax_send.at[g.g, b], ax_recv.at[g.g, b], across_x)

    def ac_copy(g, b):
        here = piece(g, b, c, 0, hw)
        return remote(here, here, ac_send.at[g.g, b], ac_recv.at[g.g, b], across_c)

    def ac_in(g, b):
        here = piece(g, b, 1 - c, 0, hw)
        return remote(here, here, ac_send.at[g.g, b], ac_recv.at[g.g, b], across_c)

    def sum_copy(stage, device):
        return remote(
            sums.at[stage], sums_land.at[stage], t_send.at[stage], t_recv.at[stage], device
        )

    def prod_y():
        return remote(prods.at[0], prods_land.at[ZED], t_send.at[2], t_recv.at[2], across_y)

    def prod_z(to):
        return remote(
            prods.at[1], prods_land.at[z], t_send.at[3 + to], t_recv.at[3 + z], at_z(to)
        )

    def prod_z_in(frm):
        here = prods_land.at[frm]
        return remote(here, here, t_send.at[3 + frm], t_recv.at[3 + frm], at_z(frm))

    barrier = pltpu.get_barrier_semaphore()
    for device in [at_z(o) for o in others] + [across_y, across_x, across_c]:
        pl.semaphore_signal(barrier, inc=1, device_id=device, device_id_type=MESH)
    pl.semaphore_wait(barrier, 6)

    for to in others:
        w_z(0, to).start()
    x_copy(0, 0).start()
    x_copy(0, 1).start()
    w_own(0).start()
    cot_fetch(0, 0, 0).start()

    image_row = lax.broadcasted_iota(jnp.int32, (images, images), 0)
    image_col = lax.broadcasted_iota(jnp.int32, (images, images), 1)
    crops = counts[...].astype(F32)
    ends = jnp.dot(
        jnp.broadcast_to(crops, (8, images)), (image_row <= image_col).astype(F32),
        precision=lax.Precision.HIGHEST, preferred_element_type=F32,
    )[0:1]
    starts = ends - crops
    block = mask.shape[1]
    lane = scale.shape[1]

    for r in range(rows // block):
        index = (
            lax.broadcasted_iota(jnp.int32, (block, images), 0) + r * block
        ).astype(F32)
        inside = (index >= starts) & (index < ends)
        count_row = jnp.sum(jnp.where(inside, crops, 0.0), axis=1, keepdims=True)
        diagonal = lax.broadcasted_iota(jnp.int32, (block, block), 0) == (
            lax.broadcasted_iota(jnp.int32, (block, block), 1)
        )
        usable = jnp.sum(
            jnp.where(diagonal, mask[r : r + 1, :].astype(F32), 0.0),
            axis=1, keepdims=True,
        )
        live = (count_row > 0.0) & (usable == 1.0)
        share = jnp.where(live, 1.0 / jnp.maximum(count_row, 1.0), 0.0)
        scale[r * block : (r + 1) * block, :] = jnp.broadcast_to(share, (block, lane))

    for frm in others:
        w_z_in(0, frm).wait_recv()
        w_x(0, frm).start()
    for to in others:
        w_z(1, to).start()
    w_own(1).start()
    for frm in others:
        w_x_in(0, frm).wait_recv()
        w_c(0, frm).start()
    x_copy(0, 0).wait_recv()
    for copy in x_fetch(0, 0, 0):
        copy.start()

    def final(at, later):
        p, i, slot, t, h, buf = at.p, at.i, at.slot, at.t, at.h, at.buf
        cot_fetch(h, i, buf).wait()

        @pl.when(at.u >= 2 * n_part + 2)
        def _():
            mixed_out(h, i, buf).wait()

        @pl.when(i == 0)
        def _():
            stat[p] = jnp.zeros(stat.shape[1:], F32)

        lanes = cols(h)
        shift = bias[pl.ds(t, 1), lanes]
        st = [stitch[s, pl.ds(t, 1), lanes] for s in range(2)]
        band = min(BAND, part)

        def step(r, carry):
            here = part_rows_of(r, band)
            there = pl.ds(mult(i * part + r * band, band), band)
            value = pf[at.prod, z, here, :]
            below = wide(rs[slot, z + 1, here, :])
            above = wide(rs[slot, z, here, :])
            value = value + jnp.where(z > 0, below, 0.0) + jnp.where(z < ZED - 1, above, 0.0)
            pre = value + shift
            phi = 0.5 * (1.0 + lax.erf(pre * 0.7071067811865476))
            hidden = pre * phi
            slope = phi + pre * (jnp.exp(-0.5 * pre * pre) * 0.3989422804014327)
            weight = scale[there, 0:1]
            first = wide(cc[buf, 0, here, :]) * weight
            second = wide(cc[buf, 1, here, :]) * weight
            back0 = st[0] * first * slope
            back1 = st[1] * second * slope
            gl[p, there, cols(z)] = half(back0 + back1)

            def fold(v):
                return jnp.sum(v.reshape(band // 8, 8, hw), axis=0)

            stat[p, 0] += fold(back0)
            stat[p, 1] += fold(back1)
            stat[p, 2] += fold(first * hidden)
            stat[p, 3] += fold(second * hidden)

            @pl.when(t == 0)
            def _():
                h0[h, there, :] = hidden

            @pl.when(t == 1)
            def _():
                before = h0[h, there, :]
                for s in range(2):
                    mx[buf, s, here, :] = half(
                        stitch[s, 0:1, lanes] * before + st[s] * hidden
                    )

            return carry

        lax.fori_loop(0, part // band, step, 0)

        @pl.when(z < ZED - 1)
        def _():
            ag(at, z, 0, up).start()

        @pl.when(z > 0)
        def _():
            ag(at, z, 1, down).start()

        @pl.when(t == 1)
        def _():
            mixed_out(h, i, buf).start()

        @pl.when(at.u + 1 < parts)
        def _():
            cot_fetch(later.h, later.i, later.buf).start()

    def part_rows_of(r, band):
        return pl.ds(mult(r * band, band), band)

    def forward_ag(at, far):
        @pl.when((at.u >= 0) & (at.u < parts))
        def _():
            @pl.when(z - far >= 0)
            def _():
                ag(at, z - far, 0, up).wait_recv()

                @pl.when(z < ZED - 1)
                def _():
                    ag(at, z - far, 0, up).start()

            @pl.when(z + far < ZED)
            def _():
                ag(at, z + far, 1, down).wait_recv()

                @pl.when(z > 0)
                def _():
                    ag(at, z + far, 1, down).start()

    def dx_part(t, i, hk):
        there = chunk_rows(i)
        krows = pl.ds(mult(deep * hk, deep), deep)
        acc = None
        for h in range(HALVES):
            term = lax.dot_general(
                gl[2 * t + h, there, :], wv[2 * t + h, krows, :],
                (((1,), (1,)), ((), ())), preferred_element_type=F32,
            )
            acc = term if acc is None else acc + term
        return acc

    def dx_step(t, i, buf):
        @pl.when((i >= HELD) | (t > 0))
        def _():
            dx_copy(t, i, buf).wait_send()

        dsend[buf] = half(dx_part(t, i, 1 - y))
        dx_copy(t, i, buf).start()
        own[buf] = dx_part(t, i, y)

    def dx_begin(t, i, buf):
        dx_copy(t, i, buf).wait_recv()
        dx_fetch(t, i).start()

    def dx_final(t, i, buf):
        @pl.when((i >= 1) | (t > 0))
        def _():
            dx_out(t, i).wait()

        dx_fetch(t, i).wait()

        def step(j, inner):
            lanes = pl.ds(mult(tile * j, tile), tile)
            dout[:, lanes] = half(own[buf, :, lanes] + wide(dfetch[:, lanes]))
            return inner

        lax.fori_loop(0, 3, step, 0)
        dx_out(t, i).start()

    def listed(u, times, do):
        e, hit = 0, False
        for index, time in enumerate(times):
            same = u == time
            e = jnp.where(same, index, e)
            hit = hit | same

        @pl.when(hit)
        def _():
            do(e)

    def chunk_of(do):
        def run(e):
            t = jnp.where(e >= n_chunk, 1, 0)
            do(t, e - n_chunk * t, lax.rem(e, HELD))

        return run

    def turn():
        lanes_at_once = min(128, tile)

        def step(q, carry):
            lanes = pl.ds(mult(q * lanes_at_once, lanes_at_once), lanes_at_once)
            xt[lanes, :] = xsrc[:, lanes].T
            return carry

        lax.fori_loop(0, tile // lanes_at_once, step, 0)

    def tile_dot(g):
        return jnp.dot(xt[...], gl[g.p], preferred_element_type=F32)

    def stage_one(g):
        tile_fetch(g.t, g.j, 1 - c, False)
        turn()
        tile_fetch(g.t, g.j, c, True)
        cstage[...] = half(tile_dot(g))
        core_copy(g).start()

    def stage_two(g):
        tile_fetch(g.t, g.j, c, False)
        turn()

        @pl.when(g.j < 2)
        def _():
            tile_fetch(g.t, g.j + 1, 1 - c, True)

        core_copy(g).wait()
        product = tile_dot(g)
        for b in range(ZED):
            block = product[:, b * hw : (b + 1) * hw] + wide(
                cland[g.buf, :, b * hw : (b + 1) * hw]
            )
            left, right = block[:, :xw], block[:, xw:]
            kept[g.trio, b] = jnp.where(x == 0, left, right)
            xstage[g.trio, b] = half(jnp.where(x == 0, right, left))

        def send(q, carry):
            across_copy(g, lax.rem(z + 3 + 3 * q, ZED)).start()
            return carry

        lax.fori_loop(0, ZED, send, 0)

    def stage_three(g):
        @pl.when(g.g >= 3)
        def _():
            for to in others:
                z_copy(g, to).wait_send()
            ax_own(g).wait_send()

        def add(b):
            across_copy(g, b).wait()
            zstage[g.trio, b] = half(kept[g.trio, b] + wide(xland[g.quad, b]))

        def step(q, carry):
            b = lax.rem(z + 3 + 3 * q, ZED)
            add(b)
            z_copy(g, b).start()
            return carry

        lax.fori_loop(0, ZED - 1, step, 0)
        add(z)
        z_own(g).start()
        ax_own(g).start()

    def stage_four(g):
        def step(q, carry):
            b = lax.rem(z + 1 + q, ZED)
            z_in(g, b).wait_recv()
            ax_copy(g, b).start()
            return carry

        lax.fori_loop(0, ZED - 1, step, 0)
        z_own(g).wait()

    def stage_five(g):
        def step(q, carry):
            b = lax.rem(z + q, ZED)
            ax_in(g, b).wait_recv()
            ac_copy(g, b).start()
            return carry

        lax.fori_loop(0, ZED, step, 0)

    def stage_six(g):
        def step(b, carry):
            ac_in(g, b).wait_recv()
            return carry

        lax.fori_loop(0, ZED, step, 0)

    def tile_of(g):
        p = lax.div(g, 3)
        t, h = tower(p)
        return Tile(
            g=g, p=p, t=t, h=h, j=g - 3 * p,
            buf=lax.rem(g, 2), trio=g - 3 * p, quad=lax.rem(g, 4),
        )

    def tile_in_hand(do):
        return lambda g: do(tile_of(g))

    def body(u, carry):
        p0 = lax.div(u, n_part)
        i0 = u - p0 * n_part
        slot0, prod0 = lax.rem(u, RING), lax.rem(u, PRODUCTS)
        buf0 = lax.rem(u, 2)

        def before(lag):
            if isinstance(lag, int):
                whole, left = divmod(lag, n_part)
            else:
                whole, left = 0, lag
            under = i0 < left
            p = p0 - whole - jnp.where(under, 1, 0)
            i = i0 - left + jnp.where(under, n_part, 0)
            in_ring = lag % RING if isinstance(lag, int) else lag
            in_prods = lag % PRODUCTS if isinstance(lag, int) else lag
            slot = slot0 - in_ring + jnp.where(slot0 < in_ring, RING, 0)
            prod = prod0 - in_prods + jnp.where(prod0 < in_prods, PRODUCTS, 0)
            t, h = tower(p)
            return Part(u=u - lag, p=p, i=i, t=t, h=h, slot=slot, prod=prod, buf=lax.rem(i, 2))

        @pl.when((u >= 5) & (u < parts + 5))
        def _():
            slot = before(5).slot
            at_place(0, ZED - 2, lambda zz: rs_up(slot, zz).wait_send())
            at_place(1, ZED - 1, lambda zz: rs_down(slot, zz).wait_send())

        @pl.when((u >= 8) & (u < parts + 8))
        def _():
            at = before(8)

            def step(b, inner):
                @pl.when((z < ZED - 1) & (b <= z))
                def _():
                    ag(at, b, 0, up).wait_send()

                @pl.when((z > 0) & (b >= z))
                def _():
                    ag(at, b, 1, down).wait_send()

                return inner

            lax.fori_loop(0, ZED, step, 0)

        ck = lax.div(i0, SUB)
        fresh = ck * SUB == i0
        t0, h0_ = tower(p0)
        xbuf = lax.rem(ck, 2)

        @pl.when((u < parts) & fresh)
        def _():
            @pl.when(i0 == 0)
            def _():
                w_own(p0).wait()
                for frm in others:
                    w_c_in(p0, frm).wait_recv()

            for copy in x_fetch(t0, ck, xbuf):
                copy.wait()

            product = jnp.dot(xc[xbuf], wv[p0], preferred_element_type=F32)
            for b in range(ZED):
                for s in range(SUB):
                    pf[prod0 + s, b] = product[
                        s * part : (s + 1) * part, b * hw : (b + 1) * hw
                    ]

        going_up = before(z)

        @pl.when((going_up.u >= 0) & (going_up.u < parts))
        def _():
            slot, prod = going_up.slot, going_up.prod
            at_place(1, ZED - 1, lambda zz: rs_from_below(slot, zz).wait_recv())

            @pl.when(z == 0)
            def _():
                for b in range(1, ZED):
                    rs[slot, b + 1] = half(pf[prod, b])

            @pl.when(z > 0)
            def _():
                def step(b, inner):
                    rs[slot, b + 1] = half(wide(rs[slot, b + 1]) + pf[prod, b])
                    return inner

                lax.fori_loop(z + 1, ZED, step, 0)

            at_place(0, ZED - 2, lambda zz: rs_up(slot, zz).start())

        going_down = before(ZED - 1 - z)

        @pl.when((going_down.u >= 0) & (going_down.u < parts))
        def _():
            slot, prod = going_down.slot, going_down.prod
            at_place(0, ZED - 2, lambda zz: rs_from_above(slot, zz).wait_recv())

            @pl.when(z == ZED - 1)
            def _():
                for b in range(ZED - 1):
                    rs[slot, b] = half(pf[prod, b])

            @pl.when(z < ZED - 1)
            def _():
                def step(b, inner):
                    rs[slot, b] = half(wide(rs[slot, b]) + pf[prod, b])
                    return inner

                lax.fori_loop(0, z, step, 0)

            at_place(1, ZED - 1, lambda zz: rs_down(slot, zz).start())

        @pl.when(fresh & (u + 2 * SUB < 2 * n_part))
        def _():
            k = p0 * n_chunk + ck + 2
            over = jnp.where(k >= n_chunk, 1, 0)
            x_copy(over, k - over * n_chunk).start()

        @pl.when(fresh & (u + SUB < parts))
        def _():
            wrap = jnp.where(ck + 1 == n_chunk, 1, 0)
            i = ck + 1 - wrap * n_chunk
            t, h = tower(p0 + wrap)

            @pl.when(h == 0)
            def _():
                x_copy(t, i).wait_recv()

            for copy in x_fetch(t, i, lax.rem(i, 2)):
                copy.start()

        @pl.when((u >= 3) & (u < parts + 3))
        def _():
            final(before(3), before(2))

        forward_ag(before(4), 1)
        forward_ag(before(5), 2)
        forward_ag(before(6), 3)

        listed(u, DX_BEGINS, chunk_of(dx_begin))
        listed(u, DX_ENDS, chunk_of(dx_final))
        listed(u, DX_TIMES, chunk_of(dx_step))

        listed(u, THREES, tile_in_hand(stage_three))
        listed(u, TWOS, tile_in_hand(stage_two))
        listed(u, ONES, tile_in_hand(stage_one))
        listed(u, FOURS, tile_in_hand(stage_four))
        listed(u, FIVES, tile_in_hand(stage_five))
        listed(u, SIXES, tile_in_hand(stage_six))

        def first_fetch(p):
            tile_fetch(lax.div(p, HALVES), 0, 1 - c, True)

        listed(u, [time - 1 for time in ONES[::3]], first_fetch)

        for p, times in W_STRIPS.items():
            def send_strip(r, p=p):
                for to in others:
                    w_z_strip(p, to, r).start()

                @pl.when(r == 0)
                def _():
                    w_own(p).start()

            listed(u, times, send_strip)

        for p, times in W_ACROSS.items():
            for q, time in enumerate(times):
                @pl.when(u == time)
                def _(p=p, q=q):
                    w_z_in(p, others[q]).wait_recv()
                    w_x(p, others[q]).start()

        for p, times in W_CORES.items():
            for q, time in enumerate(times):
                @pl.when(u == time)
                def _(p=p, q=q):
                    w_x_in(p, others[q]).wait_recv()
                    w_c(p, others[q]).start()

        @pl.when(u == parts + 3)
        def _():
            for p in range(PHASES):
                t, h = p // HALVES, p % HALVES
                for s in range(2):
                    for what in range(2):
                        sums[0, pl.ds(4 * what + 2 * s + t, 1), h * hw : (h + 1) * hw] = jnp.sum(
                            stat[p, 2 * what + s], axis=0, keepdims=True
                        )
            sum_copy(0, across_c).start()

        @pl.when(u == parts + 4)
        def _():
            sum_copy(0, across_c).wait()
            sums[1] = sums[0] + sums_land[0]
            sum_copy(1, across_x).start()

        @pl.when(u == parts + 5)
        def _():
            sum_copy(1, across_x).wait()
            both = sums[1] + sums_land[1]
            sums[2] = both
            member = (
                lax.broadcasted_iota(jnp.int32, (width, lane), 0) % FLAG_GROUPS
                == lax.broadcasted_iota(jnp.int32, (width, lane), 1) % FLAG_GROUPS
            ).astype(F32)
            bias_rows = both[0:4]
            inner = both[0:2] * both[2:4]
            stack = jnp.concatenate([inner, bias_rows * bias_rows, inner], axis=0)
            prods[0] = jnp.dot(
                stack, member, precision=lax.Precision.HIGHEST, preferred_element_type=F32
            )
            prod_y().start()

        @pl.when(u == parts + 6)
        def _():
            prod_y().wait()
            prods[1] = prods[0] + prods_land[ZED]
            for to in others:
                prod_z(to).start()

        @pl.when(u == parts + 7)
        def _():
            for frm in others:
                prod_z_in(frm).wait_recv()
            prods_land[z] = prods[1]
            whole = prods_land[0] + prods_land[1] + prods_land[2] + prods_land[3]
            both = sums[2]
            group = lax.broadcasted_iota(jnp.int32, (1, lane), 1) % FLAG_GROUPS

            def over(row):
                return jnp.concatenate([row] * (width // lane), axis=1)

            def flag_row(s, t):
                row = jnp.zeros((1, lane), F32)
                for g in range(FLAG_GROUPS):
                    row = jnp.where(group == g, flags[s, t, g].astype(F32), row)
                return row

            for t in range(2):
                task0, task1 = both[t : t + 1], both[2 + t : 3 + t]
                dots = whole[t : t + 1]
                coef0 = over(flag_row(0, t) * dots / (whole[4 + t : 5 + t] + 1e-06))
                coef1 = over(flag_row(1, t) * dots / (whole[2 + t : 3 + t] + 1e-06))
                gbias[t : t + 1] = (task0 - coef0 * task1) + (task1 - coef1 * task0)
            for s in range(2):
                gstitch[s] = both[4 + 2 * s : 6 + 2 * s]

        return carry

    lax.fori_loop(0, max(SIXES + DX_ENDS) + 1, body, 0)

    last = 3 * PHASES - 1

    for g in (last - 2, last - 1, last):
        for to in others:
            z_copy(tile_of(g), to).wait_send()
        ax_own(tile_of(g)).wait_send()
    for i in range(n_chunk - HELD, n_chunk):
        dx_copy(1, i, (n_chunk + i) % HELD).wait_send()
    for i in (n_part - 2, n_part - 1):
        mixed_out(1, i, i % 2).wait()
    dx_out(1, n_chunk - 1).wait()

    def drain_tiles(g, carry):
        at = tile_of(g)
        for b in others:
            ax_copy(at, b).wait_send()
        for b in range(ZED):
            ac_copy(at, b).wait_send()
        return carry

    lax.fori_loop(0, last + 1, drain_tiles, 0)

    def drain_x(i, carry):
        x_copy(0, i).wait_send()
        x_copy(1, i).wait_send()
        return carry

    lax.fori_loop(0, n_chunk, drain_x, 0)

    def drain_w(p, carry):
        for to in others:
            w_z(p, to).wait_send()
            w_x(p, to).wait_send()
            w_c(p, to).wait_send()
        return carry

    lax.fori_loop(0, PHASES, drain_w, 0)
    for to in others:
        prod_z(to).wait_send()


def fused_call(feat, wts, cot, bias, stitch, counts, mask, flags):
    rows, deep, width = feat.shape[1], feat.shape[2], wts.shape[2]
    chunk = rows // 6
    part = chunk // SUB
    hw, kz, tile = width // 2, 2 * deep, deep // 3
    cat, xw = 4 * hw, width // 4
    lane = min(128, width)
    dma = pltpu.SemaphoreType.DMA
    anywhere = pl.BlockSpec(memory_space=pl.ANY)
    inside = pl.BlockSpec(memory_space=pltpu.VMEM)
    scalars = pl.BlockSpec(memory_space=pltpu.SMEM)

    def v(shape, kind=BF16):
        return pltpu.VMEM(shape, kind)

    out_shape = [
        jax.ShapeDtypeStruct((2, rows, width), BF16),
        jax.ShapeDtypeStruct((2, rows, deep), BF16),
        jax.ShapeDtypeStruct((2, ZED, kz, width), BF16),
        jax.ShapeDtypeStruct((2, width), F32),
        jax.ShapeDtypeStruct((2, 2, width), F32),
        jax.ShapeDtypeStruct((2, rows, deep), BF16),
        jax.ShapeDtypeStruct((2, rows, deep), BF16),
    ]
    scratch = [
        v((PHASES, kz, cat)),
        v((PHASES, rows, cat)),
        v((RING, 5, part, hw)),
        v((2, rows, hw), F32),
        v((2, chunk, kz)),
        v((PRODUCTS, ZED, part, hw), F32),
        v((2, 2, part, hw)),
        v((2, 2, part, hw)),
        v((HELD, chunk, deep), F32),
        v((HELD, chunk, deep)),
        v((chunk, deep)),
        v((chunk, deep)),
        v((rows, tile)),
        v((tile, rows)),
        v((tile, cat)),
        v((2, tile, cat)),
        v((3, ZED, tile, xw)),
        v((4, ZED, tile, xw)),
        v((3, ZED, tile, xw), F32),
        v((3, ZED, tile, xw)),
        v((rows, lane), F32),
        v((PHASES, 4, 8, hw), F32),
        v((3, 8, width), F32),
        v((2, 8, width), F32),
        v((2, 8, lane), F32),
        v((5, 8, lane), F32),
        dma((RING, 2)), dma((RING, 2)), dma((RING, 8)), dma((RING, 4)),
        dma((12,)), dma((12,)),
        dma((4, 4)), dma((4, 4)), dma((4, 4)), dma((4, 4)), dma((4, 4)), dma((4, 4)), dma((4,)),
        dma((2, 2)), dma((2,)), dma((2,)), dma((HELD,)), dma((12,)), dma((1,)), dma((1,)),
        dma((1,)), dma((1,)), dma((2,)), dma((3, 4)), dma((4, 4)), dma((3, 4)), dma((12, 4)),
        dma((3,)), dma((3,)),
        dma((12, 4)), dma((12, 4)), dma((12, 4)), dma((12, 4)), dma((8,)), dma((8,)),
    ]
    flops = 3 * 2 * 2 * rows * kz * cat * 2
    return pl.pallas_call(
        functools.partial(fused_kernel, rows, deep, width, chunk),
        out_shape=out_shape,
        in_specs=[anywhere] * 3 + [inside] * 4 + [scalars],
        out_specs=[anywhere] * 3 + [inside] * 2 + [anywhere] * 2,
        scratch_shapes=scratch,
        compiler_params=pltpu.CompilerParams(
            collective_id=0, has_side_effects=True, vmem_limit_bytes=64 * 1024 * 1024
        ),
        cost_estimate=pl.CostEstimate(
            flops=flops, bytes_accessed=200_000_000, transcendentals=2 * rows * width * 2
        ),
        name="cross_stitch_step",
    )(feat, wts, cot, bias, stitch, counts, mask, flags)


def finish_kernel(
    block, low, mixed, gfeat, gbias, gstitch,
    out, mixed_out, gfeat_out, gbias_out, gstitch_out,
    taken, given, in_sem, out_sem, pass_sem,
):
    n_block = low.shape[0] // block
    passed = (
        pltpu.make_async_copy(mixed, mixed_out, pass_sem.at[0]),
        pltpu.make_async_copy(gfeat, gfeat_out, pass_sem.at[1]),
    )

    def take(i):
        return pltpu.make_async_copy(
            low.at[pl.ds(i * block, block)], taken.at[i % WIDEN_SLOTS], in_sem.at[i % WIDEN_SLOTS]
        )

    def give(i):
        return pltpu.make_async_copy(
            given.at[i % WIDEN_SLOTS], out.at[pl.ds(i * block, block)], out_sem.at[i % WIDEN_SLOTS]
        )

    for i in range(min(WIDEN_SLOTS, n_block)):
        take(i).start()
    for copy in passed:
        copy.start()
    gbias_out[...] = gbias[...]
    gstitch_out[...] = gstitch[...]
    for i in range(n_block):
        slot = i % WIDEN_SLOTS
        take(i).wait()
        if i >= WIDEN_SLOTS:
            give(i - WIDEN_SLOTS).wait()
        given[slot] = wide(taken[slot])
        give(i).start()
        if i + WIDEN_SLOTS < n_block:
            take(i + WIDEN_SLOTS).start()
    for i in range(max(0, n_block - WIDEN_SLOTS), n_block):
        give(i).wait()
    for copy in passed:
        copy.wait()


def finish(low, mixed, gfeat, gbias, gstitch):
    tall, width = low.shape
    block = tall // WIDEN_BLOCKS
    anywhere = pl.BlockSpec(memory_space=pl.ANY)
    inside = pl.BlockSpec(memory_space=pltpu.VMEM)
    moved = sum(a.size * a.dtype.itemsize for a in (mixed, gfeat))
    return pl.pallas_call(
        functools.partial(finish_kernel, block),
        in_specs=[anywhere] * 3 + [inside] * 2,
        out_specs=[anywhere] * 3 + [inside] * 2,
        out_shape=[
            jax.ShapeDtypeStruct(a.shape, kind)
            for a, kind in ((low, F32), (mixed, BF16), (gfeat, BF16), (gbias, F32), (gstitch, F32))
        ],
        scratch_shapes=[
            pltpu.VMEM((WIDEN_SLOTS, block, width), BF16),
            pltpu.VMEM((WIDEN_SLOTS, block, width), F32),
            pltpu.SemaphoreType.DMA((WIDEN_SLOTS,)),
            pltpu.SemaphoreType.DMA((WIDEN_SLOTS,)),
            pltpu.SemaphoreType.DMA((2,)),
        ],
        compiler_params=pltpu.CompilerParams(vmem_limit_bytes=60 * 1024 * 1024),
        cost_estimate=pl.CostEstimate(
            flops=tall * width, bytes_accessed=6 * tall * width + 2 * moved, transcendentals=0
        ),
        name="finish",
    )(low, mixed, gfeat, gbias, gstitch)


def fused_plan(mesh):
    def per_device(features, weights, bias, stitch, cotangent, crop_counts, row_mask, flags):
        rows, deep = features.shape[1:]
        width = weights.shape[2]
        mixed, gfeat, gwt, gbias, gstitch, _, _ = fused_call(
            features, weights, cotangent, bias, stitch,
            crop_counts.reshape(1, -1), row_mask.reshape(-1, min(128, rows // 6)), flags,
        )
        grad_weights, mixed, gfeat, gbias, gstitch = finish(
            gwt.reshape(-1, width), mixed, gfeat, gbias, gstitch
        )
        return mixed, gfeat, grad_weights.reshape(2, ZED * 2 * deep, width), gbias, gstitch

    return per_device


def plan_for(mesh):
    if mesh.shape["batch"] == 4 and mesh.shape["mp"] == 2 * ZED:
        return fused_plan(mesh)
    return generic_plan(mesh)


def solution(mesh):
    in_specs = (
        P(None, "batch", "mp"),
        P(None, None, "mp"),
        P(None, "mp"),
        P(None, None, "mp"),
        P(None, "batch", "mp"),
        P("batch"),
        P("batch"),
        P(),
    )
    out_specs = (
        P(None, "batch", "mp"),
        P(None, "batch", "mp"),
        P(None, None, "mp"),
        P(None, "mp"),
        P(None, None, "mp"),
    )
    return jax.shard_map(
        plan_for(mesh), mesh=mesh, in_specs=in_specs, out_specs=out_specs, check_vma=False
    )
```

```python
import collections
import functools

import jax
import jax.numpy as jnp
from jax import lax
from jax.experimental import pallas as pl
from jax.experimental.pallas import tpu as pltpu
from jax.sharding import PartitionSpec as P

FLAG_GROUPS = 8
OUTER = 4


def row_weights(counts, mask):
    ends = jnp.cumsum(counts)
    starts = ends - counts
    index = lax.broadcasted_iota(jnp.int32, (mask.shape[0], counts.shape[0]), 0)
    inside = (index >= starts[None, :]) & (index < ends[None, :])
    count_row = jnp.sum(jnp.where(inside, counts[None, :], 0), axis=1)
    live = (count_row > 0) & (mask == 1)
    return jnp.where(live, 1.0 / jnp.maximum(count_row, 1).astype(jnp.float32), 0.0)


def project_bias(task_bias, flags):
    local_width = task_bias.shape[2]
    channel = lax.axis_index("mp") * local_width + lax.broadcasted_iota(
        jnp.int32, (local_width, FLAG_GROUPS), 0
    )
    member = (
        channel % FLAG_GROUPS == lax.broadcasted_iota(jnp.int32, (local_width, FLAG_GROUPS), 1)
    ).astype(jnp.float32)
    dots = jnp.dot(task_bias[0] * task_bias[1], member, precision=lax.Precision.HIGHEST)
    norms = jnp.einsum(
        "stc,cg->stg", task_bias * task_bias, member, precision=lax.Precision.HIGHEST
    )
    dots, norms = lax.psum((dots, norms), "mp")
    flag = flags.astype(jnp.float32)
    coef_first = jnp.dot(
        flag[0] * dots / (norms[1] + 1e-06), member.T, precision=lax.Precision.HIGHEST
    )
    coef_second = jnp.dot(
        flag[1] * dots / (norms[0] + 1e-06), member.T, precision=lax.Precision.HIGHEST
    )
    first = task_bias[0] - coef_first * task_bias[1]
    second = task_bias[1] - coef_second * task_bias[0]
    return first + second


def generic_plan(mesh):
    n_mp = mesh.shape["mp"]
    n_batch = mesh.shape["batch"]
    inner = n_mp // OUTER
    inner_groups = [[o * inner + i for i in range(inner)] for o in range(OUTER)]
    outer_groups = [[o * inner + i for o in range(OUTER)] for i in range(inner)]

    def per_device(features, weights, bias, stitch, cotangent, crop_counts, row_mask, flags):
        rows = features.shape[1]
        width = weights.shape[2]
        depth = features.shape[2] * inner
        held = lax.all_gather(
            features, "mp", axis=2, tiled=True, axis_index_groups=inner_groups
        )
        split = weights.reshape(2, OUTER, depth, width)
        block = lax.all_to_all(
            split, "mp", split_axis=1, concat_axis=1, axis_index_groups=outer_groups
        )
        block = block.reshape(2, OUTER, depth, width)
        part = jnp.einsum("trk,tokc->otrc", held, block, preferred_element_type=jnp.float32)
        linear = lax.psum_scatter(
            part.astype(jnp.bfloat16),
            "mp",
            scatter_dimension=0,
            axis_index_groups=outer_groups,
        ).astype(jnp.float32)
        pre = linear + bias[:, None, :]
        hidden, gelu_back = jax.vjp(lambda v: jax.nn.gelu(v, approximate=False), pre)
        mixed = stitch[:, 0, None, :] * hidden[0][None] + stitch[:, 1, None, :] * hidden[1][None]
        scale_rows = row_weights(crop_counts, row_mask)
        grad_out = cotangent.astype(jnp.float32) * scale_rows[None, :, None]
        first_task = gelu_back(stitch[0][:, None, :] * grad_out[0][None])[0]
        second_task = gelu_back(stitch[1][:, None, :] * grad_out[1][None])[0]
        task_bias = jnp.stack([jnp.sum(first_task, axis=1), jnp.sum(second_task, axis=1)])
        grad_linear = (first_task + second_task).astype(jnp.bfloat16)
        grad_stitch = jnp.sum(grad_out[:, None] * hidden[None], axis=2)
        every = lax.all_gather(grad_linear, "mp", axis_index_groups=outer_groups)
        grad_part = jnp.einsum(
            "otrc,tokc->trk", every, block, preferred_element_type=jnp.float32
        )
        grad_part = grad_part.astype(jnp.bfloat16).reshape(2, rows, inner, depth // inner)
        grad_features = lax.psum_scatter(
            grad_part.transpose(2, 0, 1, 3),
            "mp",
            scatter_dimension=0,
            axis_index_groups=inner_groups,
        )
        weight_part = jnp.einsum(
            "trk,otrc->otkc", held, every, preferred_element_type=jnp.float32
        )
        weight_part = weight_part.astype(jnp.bfloat16).reshape(
            OUTER, 2, n_batch, depth // n_batch, width
        )
        share = lax.psum_scatter(
            weight_part.transpose(2, 0, 1, 3, 4), "batch", scatter_dimension=0
        )
        share = lax.all_to_all(
            share, "mp", split_axis=0, concat_axis=0, axis_index_groups=outer_groups
        )
        share = share.reshape(OUTER, 2, depth // n_batch, width)
        whole = lax.all_gather(share, "batch")
        grad_weights = whole.transpose(2, 1, 0, 3, 4).reshape(2, OUTER * depth, width)
        task_bias, grad_stitch = lax.psum((task_bias, grad_stitch), "batch")
        grad_bias = project_bias(task_bias, flags)
        return (
            mixed.astype(jnp.bfloat16),
            grad_features.astype(jnp.bfloat16),
            grad_weights.astype(jnp.float32),
            grad_bias,
            grad_stitch,
        )

    return per_device


MESH = pl.DeviceIdType.MESH
BF16 = jnp.bfloat16
F32 = jnp.float32
ZED = 4
HALVES = 2
PHASES = 4
RING = 8
BAND = 32
SUB = 2
PRODUCTS = 6
HELD = 4
WIDEN_BLOCKS = 12
WIDEN_SLOTS = 4

DX_TIMES = (19, 22, 24, 25, 28, 29, 43, 46, 48, 51, 60, 71)
DX_BEGINS = (22, 24, 26, 28, 30, 44, 48, 52, 62, 68, 71, 85)
DX_ENDS = (23, 25, 27, 29, 39, 45, 49, 57, 65, 70, 72, 109)
ONES = (20, 23, 26, 30, 35, 38, 43, 44, 47, 54, 58, 61)
TWOS = (21, 26, 29, 31, 36, 42, 44, 45, 50, 58, 61, 66)
THREES = (23, 28, 30, 34, 42, 43, 45, 52, 56, 63, 68, 79)
FOURS = (27, 31, 34, 38, 44, 45, 46, 57, 69, 73, 75, 87)
FIVES = (35, 48, 49, 57, 65, 68, 74, 78, 91, 98, 102, 117)
SIXES = (48, 49, 62, 63, 73, 83, 99, 107, 108, 116, 118, 123)
W_STRIPS = {2: (0, 2, 7, 8, 10, 14), 3: (14, 19, 20, 22, 24, 25)}
W_ACROSS = {1: (0, 0, 0), 2: (18, 18, 22), 3: (28, 29, 31)}
W_CORES = {1: (2, 3, 10), 2: (20, 21, 23), 3: (30, 31, 34)}


Part = collections.namedtuple("Part", ("u", "p", "i", "t", "h", "slot", "prod", "buf"))
Tile = collections.namedtuple("Tile", ("g", "p", "t", "h", "j", "buf", "trio", "quad"))


def half(value):
    return value.astype(BF16)


def wide(value):
    return value.astype(F32)


def fused_kernel(
    rows, deep, width, chunk,
    feat, wts, cot, bias, stitch, counts, mask, flags,
    mixed, gfeat, gwt, gbias, gstitch, xn, dxn,
    wv, gl, rs, h0, xc, pf, cc, mx, own, dsend, dfetch, dout,
    xsrc, xt, cstage, cland, xstage, xland, kept, zstage,
    scale, stat, sums, sums_land, prods, prods_land,
    rs_send, rs_recv, ag_send, ag_recv, xs_send, xs_recv,
    wz_send, wz_recv, wx_send, wx_recv, wc_send, wc_recv, wl,
    xf, cf, mxs, dx_send, dx_recv, df, dod,
    tile_in, c_send, c_recv, x_send, x_recv, z_send, z_recv, zl, zx_send,
    ax_send, ax_recv, ac_send, ac_recv, t_send, t_recv,
):
    batch, mp = lax.axis_index("batch"), lax.axis_index("mp")
    z, y = mp // 2, mp % 2
    x, c = batch // 2, batch % 2
    up = {"mp": mp + 2}
    down = {"mp": mp - 2}
    across_y = {"mp": 2 * z + 1 - y}
    across_x = {"batch": 2 * (1 - x) + c}
    across_c = {"batch": 2 * x + 1 - c}

    def at_z(other):
        return {"mp": 2 * other + y}

    others = (3 - z, (z + 2) % 4, z + 1 - 2 * (z % 2))

    n_chunk = rows // chunk
    total = PHASES * n_chunk
    part = chunk // SUB
    n_part = rows // part
    parts = PHASES * n_part
    images = counts.shape[1]
    hw = width // HALVES
    kz = 2 * deep
    quarter = deep // 2
    tile = deep // 3
    strip = quarter // 6
    xw = hw // 2

    def mult(value, unit):
        return pl.multiple_of(value, unit)

    def remote(src, dst, send, recv, device):
        return pltpu.make_async_remote_copy(
            src_ref=src, dst_ref=dst, send_sem=send, recv_sem=recv,
            device_id=device, device_id_type=MESH,
        )

    def cols(b):
        return pl.ds(mult(b * hw, hw), hw)

    def chunk_rows(i):
        return pl.ds(mult(i * chunk, chunk), chunk)

    def part_rows(i):
        return pl.ds(mult(i * part, part), part)

    def tower(p):
        t = jnp.where(p >= HALVES, 1, 0)
        return t, p - HALVES * t

    def x_copy(t, i):
        e = t * n_chunk + i
        return remote(
            feat.at[t, chunk_rows(i)], xn.at[t, chunk_rows(i)],
            xs_send.at[e], xs_recv.at[e], across_y,
        )

    def x_fetch(t, i, buf):
        return (
            pltpu.make_async_copy(
                feat.at[t, chunk_rows(i)],
                xc.at[buf, :, pl.ds(mult(deep * y, deep), deep)], xf.at[buf, 0],
            ),
            pltpu.make_async_copy(
                xn.at[t, chunk_rows(i)],
                xc.at[buf, :, pl.ds(mult(deep * (1 - y), deep), deep)], xf.at[buf, 1],
            ),
        )

    def cot_fetch(h, i, buf):
        return pltpu.make_async_copy(
            cot.at[:, part_rows(i), cols(h)], cc.at[buf], cf.at[buf]
        )

    def w_own(p):
        t, h = tower(p)
        return pltpu.make_async_copy(
            wts.at[t, pl.ds(mult(kz * z, kz), kz), cols(h)], wv.at[p, :, cols(z)], wl.at[p],
        )

    def w_rows():
        return pl.ds(mult(deep * c + quarter * x, quarter), quarter)

    def w_z(p, to):
        t, h = tower(p)
        return remote(
            wts.at[
                t, pl.ds(mult(kz * to + deep * c + quarter * x, quarter), quarter), cols(h)
            ],
            wv.at[p, w_rows(), cols(z)],
            wz_send.at[p, to], wz_recv.at[p, z], at_z(to),
        )

    def w_z_strip(p, to, r):
        t, h = tower(p)
        at = deep * c + quarter * x + strip * r
        return remote(
            wts.at[t, pl.ds(mult(kz * to + at, strip), strip), cols(h)],
            wv.at[p, pl.ds(mult(at, strip), strip), cols(z)],
            wz_send.at[p, to], wz_recv.at[p, z], at_z(to),
        )

    def w_z_in(p, frm):
        here = wv.at[p, w_rows(), cols(frm)]
        return remote(here, here, wz_send.at[p, frm], wz_recv.at[p, frm], at_z(frm))

    def w_x(p, b):
        here = wv.at[p, w_rows(), cols(b)]
        return remote(here, here, wx_send.at[p, b], wx_recv.at[p, b], across_x)

    def w_x_in(p, b):
        here = wv.at[
            p, pl.ds(mult(deep * c + quarter * (1 - x), quarter), quarter), cols(b)
        ]
        return remote(here, here, wx_send.at[p, b], wx_recv.at[p, b], across_x)

    def w_c(p, b):
        here = wv.at[p, pl.ds(mult(deep * c, deep), deep), cols(b)]
        return remote(here, here, wc_send.at[p, b], wc_recv.at[p, b], across_c)

    def w_c_in(p, b):
        here = wv.at[p, pl.ds(mult(deep * (1 - c), deep), deep), cols(b)]
        return remote(here, here, wc_send.at[p, b], wc_recv.at[p, b], across_c)

    def rs_up(slot, zz):
        run = rs.at[slot, zz + 2 : ZED + 1]
        return remote(run, run, rs_send.at[slot, 0], rs_recv.at[slot, 0], up)

    def rs_down(slot, zz):
        run = rs.at[slot, 0:zz]
        return remote(run, run, rs_send.at[slot, 1], rs_recv.at[slot, 1], down)

    def rs_from_below(slot, zz):
        run = rs.at[slot, zz + 1 : ZED + 1]
        return remote(run, run, rs_send.at[slot, 0], rs_recv.at[slot, 0], down)

    def rs_from_above(slot, zz):
        run = rs.at[slot, 0 : zz + 1]
        return remote(run, run, rs_send.at[slot, 1], rs_recv.at[slot, 1], up)

    def at_place(first, last, do):
        for zz in range(first, last + 1):
            @pl.when(z == zz)
            def _(zz=zz):
                do(zz)

    def ag(at, b, going, device):
        here = gl.at[at.p, part_rows(at.i), cols(b)]
        return remote(
            here, here, ag_send.at[at.slot, going * ZED + b], ag_recv.at[at.slot, b], device
        )

    def dx_copy(t, i, buf):
        return remote(
            dsend.at[buf], dxn.at[t, chunk_rows(i)],
            dx_send.at[buf], dx_recv.at[t * n_chunk + i], across_y,
        )

    def dx_fetch(t, i):
        return pltpu.make_async_copy(dxn.at[t, chunk_rows(i)], dfetch, df.at[0])

    def dx_out(t, i):
        return pltpu.make_async_copy(dout, gfeat.at[t, chunk_rows(i)], dod.at[0])

    def mixed_out(h, i, buf):
        return pltpu.make_async_copy(
            mx.at[buf], mixed.at[:, part_rows(i), cols(h)], mxs.at[buf]
        )

    def tile_fetch(t, j, hk, start):
        lanes = pl.ds(mult(tile * j, tile), tile)
        near = pltpu.make_async_copy(feat.at[t, :, lanes], xsrc, tile_in.at[0])
        if not start:
            near.wait()
            return

        @pl.when(hk == y)
        def _():
            near.start()

        @pl.when(hk != y)
        def _():
            pltpu.make_async_copy(xn.at[t, :, lanes], xsrc, tile_in.at[0]).start()

    def core_copy(g):
        return remote(cstage, cland.at[g.buf], c_send.at[0], c_recv.at[g.buf], across_c)

    def across_copy(g, b):
        return remote(
            xstage.at[g.trio, b], xland.at[g.quad, b],
            x_send.at[g.trio, b], x_recv.at[g.quad, b], across_x,
        )

    def piece(g, source, core, lanes, n_lanes):
        return gwt.at[
            g.t, source,
            pl.ds(mult(deep * core + tile * g.j, tile), tile),
            pl.ds(mult(hw * g.h + lanes, xw), n_lanes),
        ]

    def z_copy(g, to):
        return remote(
            zstage.at[g.trio, to], piece(g, z, c, xw * x, xw),
            z_send.at[g.trio, to], z_recv.at[g.g, z], at_z(to),
        )

    def z_in(g, frm):
        here = piece(g, frm, c, xw * x, xw)
        return remote(here, here, z_send.at[g.trio, frm], z_recv.at[g.g, frm], at_z(frm))

    def z_own(g):
        return pltpu.make_async_copy(
            zstage.at[g.trio, z], piece(g, z, c, xw * x, xw), zl.at[g.trio]
        )

    def ax_own(g):
        return remote(
            zstage.at[g.trio, z], piece(g, z, c, xw * x, xw),
            zx_send.at[g.trio], ax_recv.at[g.g, z], across_x,
        )

    def ax_copy(g, b):
        here = piece(g, b, c, xw * x, xw)
        return remote(here, here, ax_send.at[g.g, b], ax_recv.at[g.g, b], across_x)

    def ax_in(g, b):
        here = piece(g, b, c, xw * (1 - x), xw)
        return remote(here, here, ax_send.at[g.g, b], ax_recv.at[g.g, b], across_x)

    def ac_copy(g, b):
        here = piece(g, b, c, 0, hw)
        return remote(here, here, ac_send.at[g.g, b], ac_recv.at[g.g, b], across_c)

    def ac_in(g, b):
        here = piece(g, b, 1 - c, 0, hw)
        return remote(here, here, ac_send.at[g.g, b], ac_recv.at[g.g, b], across_c)

    def sum_copy(stage, device):
        return remote(
            sums.at[stage], sums_land.at[stage], t_send.at[stage], t_recv.at[stage], device
        )

    def prod_y():
        return remote(prods.at[0], prods_land.at[ZED], t_send.at[2], t_recv.at[2], across_y)

    def prod_z(to):
        return remote(
            prods.at[1], prods_land.at[z], t_send.at[3 + to], t_recv.at[3 + z], at_z(to)
        )

    def prod_z_in(frm):
        here = prods_land.at[frm]
        return remote(here, here, t_send.at[3 + frm], t_recv.at[3 + frm], at_z(frm))

    barrier = pltpu.get_barrier_semaphore()
    for device in [at_z(o) for o in others] + [across_y, across_x, across_c]:
        pl.semaphore_signal(barrier, inc=1, device_id=device, device_id_type=MESH)
    pl.semaphore_wait(barrier, 6)

    for to in others:
        w_z(0, to).start()
    x_copy(0, 0).start()
    x_copy(0, 1).start()
    w_own(0).start()
    cot_fetch(0, 0, 0).start()

    image_row = lax.broadcasted_iota(jnp.int32, (images, images), 0)
    image_col = lax.broadcasted_iota(jnp.int32, (images, images), 1)
    crops = counts[...].astype(F32)
    ends = jnp.dot(
        jnp.broadcast_to(crops, (8, images)), (image_row <= image_col).astype(F32),
        precision=lax.Precision.HIGHEST, preferred_element_type=F32,
    )[0:1]
    starts = ends - crops
    block = mask.shape[1]
    lane = scale.shape[1]

    for r in range(rows // block):
        index = (
            lax.broadcasted_iota(jnp.int32, (block, images), 0) + r * block
        ).astype(F32)
        inside = (index >= starts) & (index < ends)
        count_row = jnp.sum(jnp.where(inside, crops, 0.0), axis=1, keepdims=True)
        diagonal = lax.broadcasted_iota(jnp.int32, (block, block), 0) == (
            lax.broadcasted_iota(jnp.int32, (block, block), 1)
        )
        usable = jnp.sum(
            jnp.where(diagonal, mask[r : r + 1, :].astype(F32), 0.0),
            axis=1, keepdims=True,
        )
        live = (count_row > 0.0) & (usable == 1.0)
        share = jnp.where(live, 1.0 / jnp.maximum(count_row, 1.0), 0.0)
        scale[r * block : (r + 1) * block, :] = jnp.broadcast_to(share, (block, lane))

    for frm in others:
        w_z_in(0, frm).wait_recv()
        w_x(0, frm).start()
    for to in others:
        w_z(1, to).start()
    w_own(1).start()
    for frm in others:
        w_x_in(0, frm).wait_recv()
        w_c(0, frm).start()
    x_copy(0, 0).wait_recv()
    for copy in x_fetch(0, 0, 0):
        copy.start()

    def final(at, later):
        p, i, slot, t, h, buf = at.p, at.i, at.slot, at.t, at.h, at.buf
        cot_fetch(h, i, buf).wait()

        @pl.when(at.u >= 2 * n_part + 2)
        def _():
            mixed_out(h, i, buf).wait()

        @pl.when(i == 0)
        def _():
            stat[p] = jnp.zeros(stat.shape[1:], F32)

        lanes = cols(h)
        shift = bias[pl.ds(t, 1), lanes]
        st = [stitch[s, pl.ds(t, 1), lanes] for s in range(2)]
        band = min(BAND, part)

        def step(r, carry):
            here = part_rows_of(r, band)
            there = pl.ds(mult(i * part + r * band, band), band)
            value = pf[at.prod, z, here, :]
            below = wide(rs[slot, z + 1, here, :])
            above = wide(rs[slot, z, here, :])
            value = value + jnp.where(z > 0, below, 0.0) + jnp.where(z < ZED - 1, above, 0.0)
            pre = value + shift
            phi = 0.5 * (1.0 + lax.erf(pre * 0.7071067811865476))
            hidden = pre * phi
            slope = phi + pre * (jnp.exp(-0.5 * pre * pre) * 0.3989422804014327)
            weight = scale[there, 0:1]
            first = wide(cc[buf, 0, here, :]) * weight
            second = wide(cc[buf, 1, here, :]) * weight
            back0 = st[0] * first * slope
            back1 = st[1] * second * slope
            gl[p, there, cols(z)] = half(back0 + back1)

            def fold(v):
                return jnp.sum(v.reshape(band // 8, 8, hw), axis=0)

            stat[p, 0] += fold(back0)
            stat[p, 1] += fold(back1)
            stat[p, 2] += fold(first * hidden)
            stat[p, 3] += fold(second * hidden)

            @pl.when(t == 0)
            def _():
                h0[h, there, :] = hidden

            @pl.when(t == 1)
            def _():
                before = h0[h, there, :]
                for s in range(2):
                    mx[buf, s, here, :] = half(
                        stitch[s, 0:1, lanes] * before + st[s] * hidden
                    )

            return carry

        lax.fori_loop(0, part // band, step, 0)

        @pl.when(z < ZED - 1)
        def _():
            ag(at, z, 0, up).start()

        @pl.when(z > 0)
        def _():
            ag(at, z, 1, down).start()

        @pl.when(t == 1)
        def _():
            mixed_out(h, i, buf).start()

        @pl.when(at.u + 1 < parts)
        def _():
            cot_fetch(later.h, later.i, later.buf).start()

    def part_rows_of(r, band):
        return pl.ds(mult(r * band, band), band)

    def forward_ag(at, far):
        @pl.when((at.u >= 0) & (at.u < parts))
        def _():
            @pl.when(z - far >= 0)
            def _():
                ag(at, z - far, 0, up).wait_recv()

                @pl.when(z < ZED - 1)
                def _():
                    ag(at, z - far, 0, up).start()

            @pl.when(z + far < ZED)
            def _():
                ag(at, z + far, 1, down).wait_recv()

                @pl.when(z > 0)
                def _():
                    ag(at, z + far, 1, down).start()

    def dx_part(t, i, hk):
        there = chunk_rows(i)
        krows = pl.ds(mult(deep * hk, deep), deep)
        acc = None
        for h in range(HALVES):
            term = lax.dot_general(
                gl[2 * t + h, there, :], wv[2 * t + h, krows, :],
                (((1,), (1,)), ((), ())), preferred_element_type=F32,
            )
            acc = term if acc is None else acc + term
        return acc

    def dx_step(t, i, buf):
        @pl.when((i >= HELD) | (t > 0))
        def _():
            dx_copy(t, i, buf).wait_send()

        dsend[buf] = half(dx_part(t, i, 1 - y))
        dx_copy(t, i, buf).start()
        own[buf] = dx_part(t, i, y)

    def dx_begin(t, i, buf):
        dx_copy(t, i, buf).wait_recv()
        dx_fetch(t, i).start()

    def dx_final(t, i, buf):
        @pl.when((i >= 1) | (t > 0))
        def _():
            dx_out(t, i).wait()

        dx_fetch(t, i).wait()

        def step(j, inner):
            lanes = pl.ds(mult(tile * j, tile), tile)
            dout[:, lanes] = half(own[buf, :, lanes] + wide(dfetch[:, lanes]))
            return inner

        lax.fori_loop(0, 3, step, 0)
        dx_out(t, i).start()

    def listed(u, times, do):
        e, hit = 0, False
        for index, time in enumerate(times):
            same = u == time
            e = jnp.where(same, index, e)
            hit = hit | same

        @pl.when(hit)
        def _():
            do(e)

    def chunk_of(do):
        def run(e):
            t = jnp.where(e >= n_chunk, 1, 0)
            do(t, e - n_chunk * t, lax.rem(e, HELD))

        return run

    def turn():
        lanes_at_once = min(128, tile)

        def step(q, carry):
            lanes = pl.ds(mult(q * lanes_at_once, lanes_at_once), lanes_at_once)
            xt[lanes, :] = xsrc[:, lanes].T
            return carry

        lax.fori_loop(0, tile // lanes_at_once, step, 0)

    def tile_dot(g):
        return jnp.dot(xt[...], gl[g.p], preferred_element_type=F32)

    def stage_one(g):
        tile_fetch(g.t, g.j, 1 - c, False)
        turn()
        tile_fetch(g.t, g.j, c, True)
        cstage[...] = half(tile_dot(g))
        core_copy(g).start()

    def stage_two(g):
        tile_fetch(g.t, g.j, c, False)
        turn()

        @pl.when(g.j < 2)
        def _():
            tile_fetch(g.t, g.j + 1, 1 - c, True)

        core_copy(g).wait()
        product = tile_dot(g)
        for b in range(ZED):
            block = product[:, b * hw : (b + 1) * hw] + wide(
                cland[g.buf, :, b * hw : (b + 1) * hw]
            )
            left, right = block[:, :xw], block[:, xw:]
            kept[g.trio, b] = jnp.where(x == 0, left, right)
            xstage[g.trio, b] = half(jnp.where(x == 0, right, left))

        def send(q, carry):
            across_copy(g, lax.rem(z + 3 + 3 * q, ZED)).start()
            return carry

        lax.fori_loop(0, ZED, send, 0)

    def stage_three(g):
        @pl.when(g.g >= 3)
        def _():
            for to in others:
                z_copy(g, to).wait_send()
            ax_own(g).wait_send()

        def add(b):
            across_copy(g, b).wait()
            zstage[g.trio, b] = half(kept[g.trio, b] + wide(xland[g.quad, b]))

        def step(q, carry):
            b = lax.rem(z + 3 + 3 * q, ZED)
            add(b)
            z_copy(g, b).start()
            return carry

        lax.fori_loop(0, ZED - 1, step, 0)
        add(z)
        z_own(g).start()
        ax_own(g).start()

    def stage_four(g):
        def step(q, carry):
            b = lax.rem(z + 1 + q, ZED)
            z_in(g, b).wait_recv()
            ax_copy(g, b).start()
            return carry

        lax.fori_loop(0, ZED - 1, step, 0)
        z_own(g).wait()

    def stage_five(g):
        def step(q, carry):
            b = lax.rem(z + q, ZED)
            ax_in(g, b).wait_recv()
            ac_copy(g, b).start()
            return carry

        lax.fori_loop(0, ZED, step, 0)

    def stage_six(g):
        def step(b, carry):
            ac_in(g, b).wait_recv()
            return carry

        lax.fori_loop(0, ZED, step, 0)

    def tile_of(g):
        p = lax.div(g, 3)
        t, h = tower(p)
        return Tile(
            g=g, p=p, t=t, h=h, j=g - 3 * p,
            buf=lax.rem(g, 2), trio=g - 3 * p, quad=lax.rem(g, 4),
        )

    def tile_in_hand(do):
        return lambda g: do(tile_of(g))

    def body(u, carry):
        p0 = lax.div(u, n_part)
        i0 = u - p0 * n_part
        slot0, prod0 = lax.rem(u, RING), lax.rem(u, PRODUCTS)
        buf0 = lax.rem(u, 2)

        def before(lag):
            if isinstance(lag, int):
                whole, left = divmod(lag, n_part)
            else:
                whole, left = 0, lag
            under = i0 < left
            p = p0 - whole - jnp.where(under, 1, 0)
            i = i0 - left + jnp.where(under, n_part, 0)
            in_ring = lag % RING if isinstance(lag, int) else lag
            in_prods = lag % PRODUCTS if isinstance(lag, int) else lag
            slot = slot0 - in_ring + jnp.where(slot0 < in_ring, RING, 0)
            prod = prod0 - in_prods + jnp.where(prod0 < in_prods, PRODUCTS, 0)
            t, h = tower(p)
            return Part(u=u - lag, p=p, i=i, t=t, h=h, slot=slot, prod=prod, buf=lax.rem(i, 2))

        @pl.when((u >= 5) & (u < parts + 5))
        def _():
            slot = before(5).slot
            at_place(0, ZED - 2, lambda zz: rs_up(slot, zz).wait_send())
            at_place(1, ZED - 1, lambda zz: rs_down(slot, zz).wait_send())

        @pl.when((u >= 8) & (u < parts + 8))
        def _():
            at = before(8)

            def step(b, inner):
                @pl.when((z < ZED - 1) & (b <= z))
                def _():
                    ag(at, b, 0, up).wait_send()

                @pl.when((z > 0) & (b >= z))
                def _():
                    ag(at, b, 1, down).wait_send()

                return inner

            lax.fori_loop(0, ZED, step, 0)

        ck = lax.div(i0, SUB)
        fresh = ck * SUB == i0
        t0, h0_ = tower(p0)
        xbuf = lax.rem(ck, 2)

        @pl.when((u < parts) & fresh)
        def _():
            @pl.when(i0 == 0)
            def _():
                w_own(p0).wait()
                for frm in others:
                    w_c_in(p0, frm).wait_recv()

            for copy in x_fetch(t0, ck, xbuf):
                copy.wait()

            product = jnp.dot(xc[xbuf], wv[p0], preferred_element_type=F32)
            for b in range(ZED):
                for s in range(SUB):
                    pf[prod0 + s, b] = product[
                        s * part : (s + 1) * part, b * hw : (b + 1) * hw
                    ]

        going_up = before(z)

        @pl.when((going_up.u >= 0) & (going_up.u < parts))
        def _():
            slot, prod = going_up.slot, going_up.prod
            at_place(1, ZED - 1, lambda zz: rs_from_below(slot, zz).wait_recv())

            @pl.when(z == 0)
            def _():
                for b in range(1, ZED):
                    rs[slot, b + 1] = half(pf[prod, b])

            @pl.when(z > 0)
            def _():
                def step(b, inner):
                    rs[slot, b + 1] = half(wide(rs[slot, b + 1]) + pf[prod, b])
                    return inner

                lax.fori_loop(z + 1, ZED, step, 0)

            at_place(0, ZED - 2, lambda zz: rs_up(slot, zz).start())

        going_down = before(ZED - 1 - z)

        @pl.when((going_down.u >= 0) & (going_down.u < parts))
        def _():
            slot, prod = going_down.slot, going_down.prod
            at_place(0, ZED - 2, lambda zz: rs_from_above(slot, zz).wait_recv())

            @pl.when(z == ZED - 1)
            def _():
                for b in range(ZED - 1):
                    rs[slot, b] = half(pf[prod, b])

            @pl.when(z < ZED - 1)
            def _():
                def step(b, inner):
                    rs[slot, b] = half(wide(rs[slot, b]) + pf[prod, b])
                    return inner

                lax.fori_loop(0, z, step, 0)

            at_place(1, ZED - 1, lambda zz: rs_down(slot, zz).start())

        @pl.when(fresh & (u + 2 * SUB < 2 * n_part))
        def _():
            k = p0 * n_chunk + ck + 2
            over = jnp.where(k >= n_chunk, 1, 0)
            x_copy(over, k - over * n_chunk).start()

        @pl.when(fresh & (u + SUB < parts))
        def _():
            wrap = jnp.where(ck + 1 == n_chunk, 1, 0)
            i = ck + 1 - wrap * n_chunk
            t, h = tower(p0 + wrap)

            @pl.when(h == 0)
            def _():
                x_copy(t, i).wait_recv()

            for copy in x_fetch(t, i, lax.rem(i, 2)):
                copy.start()

        @pl.when((u >= 3) & (u < parts + 3))
        def _():
            final(before(3), before(2))

        forward_ag(before(4), 1)
        forward_ag(before(5), 2)
        forward_ag(before(6), 3)

        listed(u, DX_BEGINS, chunk_of(dx_begin))
        listed(u, DX_ENDS, chunk_of(dx_final))
        listed(u, DX_TIMES, chunk_of(dx_step))

        listed(u, THREES, tile_in_hand(stage_three))
        listed(u, TWOS, tile_in_hand(stage_two))
        listed(u, ONES, tile_in_hand(stage_one))
        listed(u, FOURS, tile_in_hand(stage_four))
        listed(u, FIVES, tile_in_hand(stage_five))
        listed(u, SIXES, tile_in_hand(stage_six))

        def first_fetch(p):
            tile_fetch(lax.div(p, HALVES), 0, 1 - c, True)

        listed(u, [time - 1 for time in ONES[::3]], first_fetch)

        for p, times in W_STRIPS.items():
            def send_strip(r, p=p):
                for to in others:
                    w_z_strip(p, to, r).start()

                @pl.when(r == 0)
                def _():
                    w_own(p).start()

            listed(u, times, send_strip)

        for p, times in W_ACROSS.items():
            for q, time in enumerate(times):
                @pl.when(u == time)
                def _(p=p, q=q):
                    w_z_in(p, others[q]).wait_recv()
                    w_x(p, others[q]).start()

        for p, times in W_CORES.items():
            for q, time in enumerate(times):
                @pl.when(u == time)
                def _(p=p, q=q):
                    w_x_in(p, others[q]).wait_recv()
                    w_c(p, others[q]).start()

        @pl.when(u == parts + 3)
        def _():
            for p in range(PHASES):
                t, h = p // HALVES, p % HALVES
                for s in range(2):
                    for what in range(2):
                        sums[0, pl.ds(4 * what + 2 * s + t, 1), h * hw : (h + 1) * hw] = jnp.sum(
                            stat[p, 2 * what + s], axis=0, keepdims=True
                        )
            sum_copy(0, across_c).start()

        @pl.when(u == parts + 4)
        def _():
            sum_copy(0, across_c).wait()
            sums[1] = sums[0] + sums_land[0]
            sum_copy(1, across_x).start()

        @pl.when(u == parts + 5)
        def _():
            sum_copy(1, across_x).wait()
            both = sums[1] + sums_land[1]
            sums[2] = both
            member = (
                lax.broadcasted_iota(jnp.int32, (width, lane), 0) % FLAG_GROUPS
                == lax.broadcasted_iota(jnp.int32, (width, lane), 1) % FLAG_GROUPS
            ).astype(F32)
            bias_rows = both[0:4]
            inner = both[0:2] * both[2:4]
            stack = jnp.concatenate([inner, bias_rows * bias_rows, inner], axis=0)
            prods[0] = jnp.dot(
                stack, member, precision=lax.Precision.HIGHEST, preferred_element_type=F32
            )
            prod_y().start()

        @pl.when(u == parts + 6)
        def _():
            prod_y().wait()
            prods[1] = prods[0] + prods_land[ZED]
            for to in others:
                prod_z(to).start()

        @pl.when(u == parts + 7)
        def _():
            for frm in others:
                prod_z_in(frm).wait_recv()
            prods_land[z] = prods[1]
            whole = prods_land[0] + prods_land[1] + prods_land[2] + prods_land[3]
            both = sums[2]
            group = lax.broadcasted_iota(jnp.int32, (1, lane), 1) % FLAG_GROUPS

            def over(row):
                return jnp.concatenate([row] * (width // lane), axis=1)

            def flag_row(s, t):
                row = jnp.zeros((1, lane), F32)
                for g in range(FLAG_GROUPS):
                    row = jnp.where(group == g, flags[s, t, g].astype(F32), row)
                return row

            for t in range(2):
                task0, task1 = both[t : t + 1], both[2 + t : 3 + t]
                dots = whole[t : t + 1]
                coef0 = over(flag_row(0, t) * dots / (whole[4 + t : 5 + t] + 1e-06))
                coef1 = over(flag_row(1, t) * dots / (whole[2 + t : 3 + t] + 1e-06))
                gbias[t : t + 1] = (task0 - coef0 * task1) + (task1 - coef1 * task0)
            for s in range(2):
                gstitch[s] = both[4 + 2 * s : 6 + 2 * s]

        return carry

    lax.fori_loop(0, max(SIXES + DX_ENDS) + 1, body, 0)

    last = 3 * PHASES - 1

    for g in (last - 2, last - 1, last):
        for to in others:
            z_copy(tile_of(g), to).wait_send()
        ax_own(tile_of(g)).wait_send()
    for i in range(n_chunk - HELD, n_chunk):
        dx_copy(1, i, (n_chunk + i) % HELD).wait_send()
    for i in (n_part - 2, n_part - 1):
        mixed_out(1, i, i % 2).wait()
    dx_out(1, n_chunk - 1).wait()

    def drain_tiles(g, carry):
        at = tile_of(g)
        for b in others:
            ax_copy(at, b).wait_send()
        for b in range(ZED):
            ac_copy(at, b).wait_send()
        return carry

    lax.fori_loop(0, last + 1, drain_tiles, 0)

    def drain_x(i, carry):
        x_copy(0, i).wait_send()
        x_copy(1, i).wait_send()
        return carry

    lax.fori_loop(0, n_chunk, drain_x, 0)

    def drain_w(p, carry):
        for to in others:
            w_z(p, to).wait_send()
            w_x(p, to).wait_send()
            w_c(p, to).wait_send()
        return carry

    lax.fori_loop(0, PHASES, drain_w, 0)
    for to in others:
        prod_z(to).wait_send()


def fused_call(feat, wts, cot, bias, stitch, counts, mask, flags):
    rows, deep, width = feat.shape[1], feat.shape[2], wts.shape[2]
    chunk = rows // 6
    part = chunk // SUB
    hw, kz, tile = width // 2, 2 * deep, deep // 3
    cat, xw = 4 * hw, width // 4
    lane = min(128, width)
    dma = pltpu.SemaphoreType.DMA
    anywhere = pl.BlockSpec(memory_space=pl.ANY)
    inside = pl.BlockSpec(memory_space=pltpu.VMEM)
    scalars = pl.BlockSpec(memory_space=pltpu.SMEM)

    def v(shape, kind=BF16):
        return pltpu.VMEM(shape, kind)

    out_shape = [
        jax.ShapeDtypeStruct((2, rows, width), BF16),
        jax.ShapeDtypeStruct((2, rows, deep), BF16),
        jax.ShapeDtypeStruct((2, ZED, kz, width), BF16),
        jax.ShapeDtypeStruct((2, width), F32),
        jax.ShapeDtypeStruct((2, 2, width), F32),
        jax.ShapeDtypeStruct((2, rows, deep), BF16),
        jax.ShapeDtypeStruct((2, rows, deep), BF16),
    ]
    scratch = [
        v((PHASES, kz, cat)),
        v((PHASES, rows, cat)),
        v((RING, 5, part, hw)),
        v((2, rows, hw), F32),
        v((2, chunk, kz)),
        v((PRODUCTS, ZED, part, hw), F32),
        v((2, 2, part, hw)),
        v((2, 2, part, hw)),
        v((HELD, chunk, deep), F32),
        v((HELD, chunk, deep)),
        v((chunk, deep)),
        v((chunk, deep)),
        v((rows, tile)),
        v((tile, rows)),
        v((tile, cat)),
        v((2, tile, cat)),
        v((3, ZED, tile, xw)),
        v((4, ZED, tile, xw)),
        v((3, ZED, tile, xw), F32),
        v((3, ZED, tile, xw)),
        v((rows, lane), F32),
        v((PHASES, 4, 8, hw), F32),
        v((3, 8, width), F32),
        v((2, 8, width), F32),
        v((2, 8, lane), F32),
        v((5, 8, lane), F32),
        dma((RING, 2)), dma((RING, 2)), dma((RING, 8)), dma((RING, 4)),
        dma((12,)), dma((12,)),
        dma((4, 4)), dma((4, 4)), dma((4, 4)), dma((4, 4)), dma((4, 4)), dma((4, 4)), dma((4,)),
        dma((2, 2)), dma((2,)), dma((2,)), dma((HELD,)), dma((12,)), dma((1,)), dma((1,)),
        dma((1,)), dma((1,)), dma((2,)), dma((3, 4)), dma((4, 4)), dma((3, 4)), dma((12, 4)),
        dma((3,)), dma((3,)),
        dma((12, 4)), dma((12, 4)), dma((12, 4)), dma((12, 4)), dma((8,)), dma((8,)),
    ]
    flops = 3 * 2 * 2 * rows * kz * cat * 2
    return pl.pallas_call(
        functools.partial(fused_kernel, rows, deep, width, chunk),
        out_shape=out_shape,
        in_specs=[anywhere] * 3 + [inside] * 4 + [scalars],
        out_specs=[anywhere] * 3 + [inside] * 2 + [anywhere] * 2,
        scratch_shapes=scratch,
        compiler_params=pltpu.CompilerParams(
            collective_id=0, has_side_effects=True, vmem_limit_bytes=64 * 1024 * 1024
        ),
        cost_estimate=pl.CostEstimate(
            flops=flops, bytes_accessed=200_000_000, transcendentals=2 * rows * width * 2
        ),
        name="cross_stitch_step",
    )(feat, wts, cot, bias, stitch, counts, mask, flags)


def finish_kernel(
    block, low, mixed, gfeat, gbias, gstitch,
    out, mixed_out, gfeat_out, gbias_out, gstitch_out,
    taken, given, held_mixed, held_gfeat, in_sem, out_sem, pass_sem,
):
    n_block = low.shape[0] // block
    fetched = (
        pltpu.make_async_copy(mixed, held_mixed, pass_sem.at[0]),
        pltpu.make_async_copy(gfeat, held_gfeat, pass_sem.at[1]),
    )
    passed = (
        pltpu.make_async_copy(held_mixed, mixed_out, pass_sem.at[2]),
        pltpu.make_async_copy(held_gfeat, gfeat_out, pass_sem.at[3]),
    )

    def take(i):
        return pltpu.make_async_copy(
            low.at[pl.ds(i * block, block)], taken.at[i % WIDEN_SLOTS], in_sem.at[i % WIDEN_SLOTS]
        )

    def give(i):
        return pltpu.make_async_copy(
            given.at[i % WIDEN_SLOTS], out.at[pl.ds(i * block, block)], out_sem.at[i % WIDEN_SLOTS]
        )

    for i in range(min(WIDEN_SLOTS, n_block)):
        take(i).start()
    for copy in fetched:
        copy.start()
    gbias_out[...] = gbias[...]
    gstitch_out[...] = gstitch[...]
    for i in range(n_block):
        slot = i % WIDEN_SLOTS
        take(i).wait()
        if i >= WIDEN_SLOTS:
            give(i - WIDEN_SLOTS).wait()
        given[slot] = wide(taken[slot])
        give(i).start()
        if i + WIDEN_SLOTS < n_block:
            take(i + WIDEN_SLOTS).start()
        if i == n_block // 2:
            for arrived, copy in zip(fetched, passed):
                arrived.wait()
                copy.start()
    for i in range(max(0, n_block - WIDEN_SLOTS), n_block):
        give(i).wait()
    for copy in passed:
        copy.wait()


def finish(low, mixed, gfeat, gbias, gstitch):
    tall, width = low.shape
    block = tall // WIDEN_BLOCKS
    anywhere = pl.BlockSpec(memory_space=pl.ANY)
    inside = pl.BlockSpec(memory_space=pltpu.VMEM)
    moved = sum(a.size * a.dtype.itemsize for a in (mixed, gfeat))
    return pl.pallas_call(
        functools.partial(finish_kernel, block),
        in_specs=[anywhere] * 3 + [inside] * 2,
        out_specs=[anywhere] * 3 + [inside] * 2,
        out_shape=[
            jax.ShapeDtypeStruct(a.shape, kind)
            for a, kind in ((low, F32), (mixed, BF16), (gfeat, BF16), (gbias, F32), (gstitch, F32))
        ],
        scratch_shapes=[
            pltpu.VMEM((WIDEN_SLOTS, block, width), BF16),
            pltpu.VMEM((WIDEN_SLOTS, block, width), F32),
            pltpu.VMEM(mixed.shape, BF16),
            pltpu.VMEM(gfeat.shape, BF16),
            pltpu.SemaphoreType.DMA((WIDEN_SLOTS,)),
            pltpu.SemaphoreType.DMA((WIDEN_SLOTS,)),
            pltpu.SemaphoreType.DMA((4,)),
        ],
        compiler_params=pltpu.CompilerParams(vmem_limit_bytes=60 * 1024 * 1024),
        cost_estimate=pl.CostEstimate(
            flops=tall * width, bytes_accessed=6 * tall * width + 2 * moved, transcendentals=0
        ),
        name="finish",
    )(low, mixed, gfeat, gbias, gstitch)


def fused_plan(mesh):
    def per_device(features, weights, bias, stitch, cotangent, crop_counts, row_mask, flags):
        rows, deep = features.shape[1:]
        width = weights.shape[2]
        mixed, gfeat, gwt, gbias, gstitch, _, _ = fused_call(
            features, weights, cotangent, bias, stitch,
            crop_counts.reshape(1, -1), row_mask.reshape(-1, min(128, rows // 6)), flags,
        )
        grad_weights, mixed, gfeat, gbias, gstitch = finish(
            gwt.reshape(-1, width), mixed, gfeat, gbias, gstitch
        )
        return mixed, gfeat, grad_weights.reshape(2, ZED * 2 * deep, width), gbias, gstitch

    return per_device


def plan_for(mesh):
    if mesh.shape["batch"] == 4 and mesh.shape["mp"] == 2 * ZED:
        return fused_plan(mesh)
    return generic_plan(mesh)


def solution(mesh):
    in_specs = (
        P(None, "batch", "mp"),
        P(None, None, "mp"),
        P(None, "mp"),
        P(None, None, "mp"),
        P(None, "batch", "mp"),
        P("batch"),
        P("batch"),
        P(),
    )
    out_specs = (
        P(None, "batch", "mp"),
        P(None, "batch", "mp"),
        P(None, None, "mp"),
        P(None, "mp"),
        P(None, None, "mp"),
    )
    return jax.shard_map(
        plan_for(mesh), mesh=mesh, in_specs=in_specs, out_specs=out_specs, check_vma=False
    )
```

```python
import collections
import functools

import jax
import jax.numpy as jnp
from jax import lax
from jax.experimental import pallas as pl
from jax.experimental.pallas import tpu as pltpu
from jax.sharding import PartitionSpec as P

FLAG_GROUPS = 8
OUTER = 4


def row_weights(counts, mask):
    ends = jnp.cumsum(counts)
    starts = ends - counts
    index = lax.broadcasted_iota(jnp.int32, (mask.shape[0], counts.shape[0]), 0)
    inside = (index >= starts[None, :]) & (index < ends[None, :])
    count_row = jnp.sum(jnp.where(inside, counts[None, :], 0), axis=1)
    live = (count_row > 0) & (mask == 1)
    return jnp.where(live, 1.0 / jnp.maximum(count_row, 1).astype(jnp.float32), 0.0)


def project_bias(task_bias, flags):
    local_width = task_bias.shape[2]
    channel = lax.axis_index("mp") * local_width + lax.broadcasted_iota(
        jnp.int32, (local_width, FLAG_GROUPS), 0
    )
    member = (
        channel % FLAG_GROUPS == lax.broadcasted_iota(jnp.int32, (local_width, FLAG_GROUPS), 1)
    ).astype(jnp.float32)
    dots = jnp.dot(task_bias[0] * task_bias[1], member, precision=lax.Precision.HIGHEST)
    norms = jnp.einsum(
        "stc,cg->stg", task_bias * task_bias, member, precision=lax.Precision.HIGHEST
    )
    dots, norms = lax.psum((dots, norms), "mp")
    flag = flags.astype(jnp.float32)
    coef_first = jnp.dot(
        flag[0] * dots / (norms[1] + 1e-06), member.T, precision=lax.Precision.HIGHEST
    )
    coef_second = jnp.dot(
        flag[1] * dots / (norms[0] + 1e-06), member.T, precision=lax.Precision.HIGHEST
    )
    first = task_bias[0] - coef_first * task_bias[1]
    second = task_bias[1] - coef_second * task_bias[0]
    return first + second


def generic_plan(mesh):
    n_mp = mesh.shape["mp"]
    n_batch = mesh.shape["batch"]
    inner = n_mp // OUTER
    inner_groups = [[o * inner + i for i in range(inner)] for o in range(OUTER)]
    outer_groups = [[o * inner + i for o in range(OUTER)] for i in range(inner)]

    def per_device(features, weights, bias, stitch, cotangent, crop_counts, row_mask, flags):
        rows = features.shape[1]
        width = weights.shape[2]
        depth = features.shape[2] * inner
        held = lax.all_gather(
            features, "mp", axis=2, tiled=True, axis_index_groups=inner_groups
        )
        split = weights.reshape(2, OUTER, depth, width)
        block = lax.all_to_all(
            split, "mp", split_axis=1, concat_axis=1, axis_index_groups=outer_groups
        )
        block = block.reshape(2, OUTER, depth, width)
        part = jnp.einsum("trk,tokc->otrc", held, block, preferred_element_type=jnp.float32)
        linear = lax.psum_scatter(
            part.astype(jnp.bfloat16),
            "mp",
            scatter_dimension=0,
            axis_index_groups=outer_groups,
        ).astype(jnp.float32)
        pre = linear + bias[:, None, :]
        hidden, gelu_back = jax.vjp(lambda v: jax.nn.gelu(v, approximate=False), pre)
        mixed = stitch[:, 0, None, :] * hidden[0][None] + stitch[:, 1, None, :] * hidden[1][None]
        scale_rows = row_weights(crop_counts, row_mask)
        grad_out = cotangent.astype(jnp.float32) * scale_rows[None, :, None]
        first_task = gelu_back(stitch[0][:, None, :] * grad_out[0][None])[0]
        second_task = gelu_back(stitch[1][:, None, :] * grad_out[1][None])[0]
        task_bias = jnp.stack([jnp.sum(first_task, axis=1), jnp.sum(second_task, axis=1)])
        grad_linear = (first_task + second_task).astype(jnp.bfloat16)
        grad_stitch = jnp.sum(grad_out[:, None] * hidden[None], axis=2)
        every = lax.all_gather(grad_linear, "mp", axis_index_groups=outer_groups)
        grad_part = jnp.einsum(
            "otrc,tokc->trk", every, block, preferred_element_type=jnp.float32
        )
        grad_part = grad_part.astype(jnp.bfloat16).reshape(2, rows, inner, depth // inner)
        grad_features = lax.psum_scatter(
            grad_part.transpose(2, 0, 1, 3),
            "mp",
            scatter_dimension=0,
            axis_index_groups=inner_groups,
        )
        weight_part = jnp.einsum(
            "trk,otrc->otkc", held, every, preferred_element_type=jnp.float32
        )
        weight_part = weight_part.astype(jnp.bfloat16).reshape(
            OUTER, 2, n_batch, depth // n_batch, width
        )
        share = lax.psum_scatter(
            weight_part.transpose(2, 0, 1, 3, 4), "batch", scatter_dimension=0
        )
        share = lax.all_to_all(
            share, "mp", split_axis=0, concat_axis=0, axis_index_groups=outer_groups
        )
        share = share.reshape(OUTER, 2, depth // n_batch, width)
        whole = lax.all_gather(share, "batch")
        grad_weights = whole.transpose(2, 1, 0, 3, 4).reshape(2, OUTER * depth, width)
        task_bias, grad_stitch = lax.psum((task_bias, grad_stitch), "batch")
        grad_bias = project_bias(task_bias, flags)
        return (
            mixed.astype(jnp.bfloat16),
            grad_features.astype(jnp.bfloat16),
            grad_weights.astype(jnp.float32),
            grad_bias,
            grad_stitch,
        )

    return per_device


MESH = pl.DeviceIdType.MESH
BF16 = jnp.bfloat16
F32 = jnp.float32
ZED = 4
HALVES = 2
PHASES = 4
RING = 8
BAND = 32
SUB = 2
PRODUCTS = 6
HELD = 4
WIDEN_BLOCKS = 12
WIDEN_SLOTS = 4

DX_TIMES = (20, 21, 24, 25, 27, 32, 43, 46, 47, 58, 60, 61)
DX_BEGINS = (22, 24, 27, 30, 37, 41, 44, 50, 52, 66, 75, 82)
DX_ENDS = (23, 25, 29, 35, 39, 42, 48, 51, 53, 69, 78, 95)
ONES = (21, 24, 28, 31, 36, 40, 43, 45, 46, 54, 57, 63)
TWOS = (22, 26, 30, 33, 38, 42, 44, 46, 50, 56, 58, 65)
THREES = (24, 31, 32, 35, 43, 44, 45, 52, 55, 62, 64, 80)
FOURS = (27, 33, 37, 38, 44, 46, 48, 54, 64, 71, 74, 85)
FIVES = (31, 40, 49, 51, 64, 69, 73, 80, 84, 86, 94, 105)
SIXES = (36, 60, 64, 66, 68, 81, 85, 97, 98, 99, 110, 111)
W_STRIPS = {2: (5, 6, 7, 8, 10, 11), 3: (20, 21, 23, 24, 25, 27)}
W_ACROSS = {1: (3, 3, 3), 2: (15, 16, 17), 3: (30, 31, 32)}
W_CORES = {1: (5, 7, 9), 2: (18, 21, 23), 3: (33, 33, 35)}


Part = collections.namedtuple("Part", ("u", "p", "i", "t", "h", "slot", "prod", "buf"))
Tile = collections.namedtuple("Tile", ("g", "p", "t", "h", "j", "buf", "trio", "quad"))


def half(value):
    return value.astype(BF16)


def wide(value):
    return value.astype(F32)


def fused_kernel(
    rows, deep, width, chunk,
    feat, wts, cot, bias, stitch, counts, mask, flags,
    mixed, gfeat, gwt, gbias, gstitch, xn, dxn,
    wv, gl, rs, h0, xc, pf, cc, mx, own, dsend, dfetch, dout,
    xsrc, xt, cstage, cland, xstage, xland, kept, zstage,
    scale, stat, sums, sums_land, prods, prods_land,
    rs_send, rs_recv, ag_send, ag_recv, xs_send, xs_recv,
    wz_send, wz_recv, wx_send, wx_recv, wc_send, wc_recv, wl,
    xf, cf, mxs, dx_send, dx_recv, df, dod,
    tile_in, c_send, c_recv, x_send, x_recv, z_send, z_recv, zl, zx_send,
    ax_send, ax_recv, ac_send, ac_recv, t_send, t_recv,
):
    batch, mp = lax.axis_index("batch"), lax.axis_index("mp")
    z, y = mp // 2, mp % 2
    x, c = batch // 2, batch % 2
    up = {"mp": mp + 2}
    down = {"mp": mp - 2}
    across_y = {"mp": 2 * z + 1 - y}
    across_x = {"batch": 2 * (1 - x) + c}
    across_c = {"batch": 2 * x + 1 - c}

    def at_z(other):
        return {"mp": 2 * other + y}

    others = (3 - z, (z + 2) % 4, z + 1 - 2 * (z % 2))

    n_chunk = rows // chunk
    total = PHASES * n_chunk
    part = chunk // SUB
    n_part = rows // part
    parts = PHASES * n_part
    images = counts.shape[1]
    hw = width // HALVES
    kz = 2 * deep
    quarter = deep // 2
    tile = deep // 3
    strip = quarter // 6
    xw = hw // 2

    def mult(value, unit):
        return pl.multiple_of(value, unit)

    def remote(src, dst, send, recv, device):
        return pltpu.make_async_remote_copy(
            src_ref=src, dst_ref=dst, send_sem=send, recv_sem=recv,
            device_id=device, device_id_type=MESH,
        )

    def cols(b):
        return pl.ds(mult(b * hw, hw), hw)

    def chunk_rows(i):
        return pl.ds(mult(i * chunk, chunk), chunk)

    def part_rows(i):
        return pl.ds(mult(i * part, part), part)

    def tower(p):
        t = jnp.where(p >= HALVES, 1, 0)
        return t, p - HALVES * t

    def x_copy(t, i):
        e = t * n_chunk + i
        return remote(
            feat.at[t, chunk_rows(i)], xn.at[t, chunk_rows(i)],
            xs_send.at[e], xs_recv.at[e], across_y,
        )

    def x_fetch(t, i, buf):
        return (
            pltpu.make_async_copy(
                feat.at[t, chunk_rows(i)],
                xc.at[buf, :, pl.ds(mult(deep * y, deep), deep)], xf.at[buf, 0],
            ),
            pltpu.make_async_copy(
                xn.at[t, chunk_rows(i)],
                xc.at[buf, :, pl.ds(mult(deep * (1 - y), deep), deep)], xf.at[buf, 1],
            ),
        )

    def cot_fetch(h, i, buf):
        return pltpu.make_async_copy(
            cot.at[:, part_rows(i), cols(h)], cc.at[buf], cf.at[buf]
        )

    def w_own(p):
        t, h = tower(p)
        return pltpu.make_async_copy(
            wts.at[t, pl.ds(mult(kz * z, kz), kz), cols(h)], wv.at[p, :, cols(z)], wl.at[p],
        )

    def w_rows():
        return pl.ds(mult(deep * c + quarter * x, quarter), quarter)

    def w_z(p, to):
        t, h = tower(p)
        return remote(
            wts.at[
                t, pl.ds(mult(kz * to + deep * c + quarter * x, quarter), quarter), cols(h)
            ],
            wv.at[p, w_rows(), cols(z)],
            wz_send.at[p, to], wz_recv.at[p, z], at_z(to),
        )

    def w_z_strip(p, to, r):
        t, h = tower(p)
        at = deep * c + quarter * x + strip * r
        return remote(
            wts.at[t, pl.ds(mult(kz * to + at, strip), strip), cols(h)],
            wv.at[p, pl.ds(mult(at, strip), strip), cols(z)],
            wz_send.at[p, to], wz_recv.at[p, z], at_z(to),
        )

    def w_z_in(p, frm):
        here = wv.at[p, w_rows(), cols(frm)]
        return remote(here, here, wz_send.at[p, frm], wz_recv.at[p, frm], at_z(frm))

    def w_x(p, b):
        here = wv.at[p, w_rows(), cols(b)]
        return remote(here, here, wx_send.at[p, b], wx_recv.at[p, b], across_x)

    def w_x_in(p, b):
        here = wv.at[
            p, pl.ds(mult(deep * c + quarter * (1 - x), quarter), quarter), cols(b)
        ]
        return remote(here, here, wx_send.at[p, b], wx_recv.at[p, b], across_x)

    def w_c(p, b):
        here = wv.at[p, pl.ds(mult(deep * c, deep), deep), cols(b)]
        return remote(here, here, wc_send.at[p, b], wc_recv.at[p, b], across_c)

    def w_c_in(p, b):
        here = wv.at[p, pl.ds(mult(deep * (1 - c), deep), deep), cols(b)]
        return remote(here, here, wc_send.at[p, b], wc_recv.at[p, b], across_c)

    def rs_up(slot, zz):
        run = rs.at[slot, zz + 2 : ZED + 1]
        return remote(run, run, rs_send.at[slot, 0], rs_recv.at[slot, 0], up)

    def rs_down(slot, zz):
        run = rs.at[slot, 0:zz]
        return remote(run, run, rs_send.at[slot, 1], rs_recv.at[slot, 1], down)

    def rs_from_below(slot, zz):
        run = rs.at[slot, zz + 1 : ZED + 1]
        return remote(run, run, rs_send.at[slot, 0], rs_recv.at[slot, 0], down)

    def rs_from_above(slot, zz):
        run = rs.at[slot, 0 : zz + 1]
        return remote(run, run, rs_send.at[slot, 1], rs_recv.at[slot, 1], up)

    def at_place(first, last, do):
        for zz in range(first, last + 1):
            @pl.when(z == zz)
            def _(zz=zz):
                do(zz)

    def ag(at, b, going, device):
        here = gl.at[at.p, part_rows(at.i), cols(b)]
        return remote(
            here, here, ag_send.at[at.slot, going * ZED + b], ag_recv.at[at.slot, b], device
        )

    def dx_copy(t, i, buf):
        return remote(
            dsend.at[buf], dxn.at[t, chunk_rows(i)],
            dx_send.at[buf], dx_recv.at[t * n_chunk + i], across_y,
        )

    def dx_fetch(t, i):
        return pltpu.make_async_copy(dxn.at[t, chunk_rows(i)], dfetch, df.at[0])

    def dx_out(t, i):
        return pltpu.make_async_copy(dout, gfeat.at[t, chunk_rows(i)], dod.at[0])

    def mixed_out(h, i, buf):
        return pltpu.make_async_copy(
            mx.at[buf], mixed.at[:, part_rows(i), cols(h)], mxs.at[buf]
        )

    def tile_fetch(t, j, hk, start):
        lanes = pl.ds(mult(tile * j, tile), tile)
        near = pltpu.make_async_copy(feat.at[t, :, lanes], xsrc, tile_in.at[0])
        if not start:
            near.wait()
            return

        @pl.when(hk == y)
        def _():
            near.start()

        @pl.when(hk != y)
        def _():
            pltpu.make_async_copy(xn.at[t, :, lanes], xsrc, tile_in.at[0]).start()

    def core_copy(g):
        return remote(cstage, cland.at[g.buf], c_send.at[0], c_recv.at[g.buf], across_c)

    def across_copy(g, b):
        return remote(
            xstage.at[g.trio, b], xland.at[g.quad, b],
            x_send.at[g.trio, b], x_recv.at[g.quad, b], across_x,
        )

    def piece(g, source, core, lanes, n_lanes):
        return gwt.at[
            g.t, source,
            pl.ds(mult(deep * core + tile * g.j, tile), tile),
            pl.ds(mult(hw * g.h + lanes, xw), n_lanes),
        ]

    def z_copy(g, to):
        return remote(
            zstage.at[g.trio, to], piece(g, z, c, xw * x, xw),
            z_send.at[g.trio, to], z_recv.at[g.g, z], at_z(to),
        )

    def z_in(g, frm):
        here = piece(g, frm, c, xw * x, xw)
        return remote(here, here, z_send.at[g.trio, frm], z_recv.at[g.g, frm], at_z(frm))

    def z_own(g):
        return pltpu.make_async_copy(
            zstage.at[g.trio, z], piece(g, z, c, xw * x, xw), zl.at[g.trio]
        )

    def ax_own(g):
        return remote(
            zstage.at[g.trio, z], piece(g, z, c, xw * x, xw),
            zx_send.at[g.trio], ax_recv.at[g.g, z], across_x,
        )

    def ax_copy(g, b):
        here = piece(g, b, c, xw * x, xw)
        return remote(here, here, ax_send.at[g.g, b], ax_recv.at[g.g, b], across_x)

    def ax_in(g, b):
        here = piece(g, b, c, xw * (1 - x), xw)
        return remote(here, here, ax_send.at[g.g, b], ax_recv.at[g.g, b], across_x)

    def ac_copy(g, b):
        here = piece(g, b, c, 0, hw)
        return remote(here, here, ac_send.at[g.g, b], ac_recv.at[g.g, b], across_c)

    def ac_in(g, b):
        here = piece(g, b, 1 - c, 0, hw)
        return remote(here, here, ac_send.at[g.g, b], ac_recv.at[g.g, b], across_c)

    def sum_copy(stage, device):
        return remote(
            sums.at[stage], sums_land.at[stage], t_send.at[stage], t_recv.at[stage], device
        )

    def prod_y():
        return remote(prods.at[0], prods_land.at[ZED], t_send.at[2], t_recv.at[2], across_y)

    def prod_z(to):
        return remote(
            prods.at[1], prods_land.at[z], t_send.at[3 + to], t_recv.at[3 + z], at_z(to)
        )

    def prod_z_in(frm):
        here = prods_land.at[frm]
        return remote(here, here, t_send.at[3 + frm], t_recv.at[3 + frm], at_z(frm))

    barrier = pltpu.get_barrier_semaphore()
    for device in [at_z(o) for o in others] + [across_y, across_x, across_c]:
        pl.semaphore_signal(barrier, inc=1, device_id=device, device_id_type=MESH)
    pl.semaphore_wait(barrier, 6)

    for to in others:
        w_z(0, to).start()
    x_copy(0, 0).start()
    x_copy(0, 1).start()
    w_own(0).start()
    cot_fetch(0, 0, 0).start()

    image_row = lax.broadcasted_iota(jnp.int32, (images, images), 0)
    image_col = lax.broadcasted_iota(jnp.int32, (images, images), 1)
    crops = counts[...].astype(F32)
    ends = jnp.dot(
        jnp.broadcast_to(crops, (8, images)), (image_row <= image_col).astype(F32),
        precision=lax.Precision.HIGHEST, preferred_element_type=F32,
    )[0:1]
    starts = ends - crops
    block = mask.shape[1]
    lane = scale.shape[1]

    for r in range(rows // block):
        index = (
            lax.broadcasted_iota(jnp.int32, (block, images), 0) + r * block
        ).astype(F32)
        inside = (index >= starts) & (index < ends)
        count_row = jnp.sum(jnp.where(inside, crops, 0.0), axis=1, keepdims=True)
        diagonal = lax.broadcasted_iota(jnp.int32, (block, block), 0) == (
            lax.broadcasted_iota(jnp.int32, (block, block), 1)
        )
        usable = jnp.sum(
            jnp.where(diagonal, mask[r : r + 1, :].astype(F32), 0.0),
            axis=1, keepdims=True,
        )
        live = (count_row > 0.0) & (usable == 1.0)
        share = jnp.where(live, 1.0 / jnp.maximum(count_row, 1.0), 0.0)
        scale[r * block : (r + 1) * block, :] = jnp.broadcast_to(share, (block, lane))

    for frm in others:
        w_z_in(0, frm).wait_recv()
        w_x(0, frm).start()
    for to in others:
        w_z(1, to).start()
    w_own(1).start()
    for frm in others:
        w_x_in(0, frm).wait_recv()
        w_c(0, frm).start()
    x_copy(0, 0).wait_recv()
    for copy in x_fetch(0, 0, 0):
        copy.start()

    def final(at, later):
        p, i, slot, t, h, buf = at.p, at.i, at.slot, at.t, at.h, at.buf
        cot_fetch(h, i, buf).wait()

        @pl.when(at.u >= 2 * n_part + 2)
        def _():
            mixed_out(h, i, buf).wait()

        @pl.when(i == 0)
        def _():
            stat[p] = jnp.zeros(stat.shape[1:], F32)

        lanes = cols(h)
        shift = bias[pl.ds(t, 1), lanes]
        st = [stitch[s, pl.ds(t, 1), lanes] for s in range(2)]
        band = min(BAND, part)

        def step(r, carry):
            here = part_rows_of(r, band)
            there = pl.ds(mult(i * part + r * band, band), band)
            value = pf[at.prod, z, here, :]
            below = wide(rs[slot, z + 1, here, :])
            above = wide(rs[slot, z, here, :])
            value = value + jnp.where(z > 0, below, 0.0) + jnp.where(z < ZED - 1, above, 0.0)
            pre = value + shift
            phi = 0.5 * (1.0 + lax.erf(pre * 0.7071067811865476))
            hidden = pre * phi
            slope = phi + pre * (jnp.exp(-0.5 * pre * pre) * 0.3989422804014327)
            weight = scale[there, 0:1]
            first = wide(cc[buf, 0, here, :]) * weight
            second = wide(cc[buf, 1, here, :]) * weight
            back0 = st[0] * first * slope
            back1 = st[1] * second * slope
            gl[p, there, cols(z)] = half(back0 + back1)

            def fold(v):
                return jnp.sum(v.reshape(band // 8, 8, hw), axis=0)

            stat[p, 0] += fold(back0)
            stat[p, 1] += fold(back1)
            stat[p, 2] += fold(first * hidden)
            stat[p, 3] += fold(second * hidden)

            @pl.when(t == 0)
            def _():
                h0[h, there, :] = hidden

            @pl.when(t == 1)
            def _():
                before = h0[h, there, :]
                for s in range(2):
                    mx[buf, s, here, :] = half(
                        stitch[s, 0:1, lanes] * before + st[s] * hidden
                    )

            return carry

        lax.fori_loop(0, part // band, step, 0)

        @pl.when(z < ZED - 1)
        def _():
            ag(at, z, 0, up).start()

        @pl.when(z > 0)
        def _():
            ag(at, z, 1, down).start()

        @pl.when(t == 1)
        def _():
            mixed_out(h, i, buf).start()

        @pl.when(at.u + 1 < parts)
        def _():
            cot_fetch(later.h, later.i, later.buf).start()

    def part_rows_of(r, band):
        return pl.ds(mult(r * band, band), band)

    def forward_ag(at, far):
        @pl.when((at.u >= 0) & (at.u < parts))
        def _():
            @pl.when(z - far >= 0)
            def _():
                ag(at, z - far, 0, up).wait_recv()

                @pl.when(z < ZED - 1)
                def _():
                    ag(at, z - far, 0, up).start()

            @pl.when(z + far < ZED)
            def _():
                ag(at, z + far, 1, down).wait_recv()

                @pl.when(z > 0)
                def _():
                    ag(at, z + far, 1, down).start()

    def dx_part(t, i, hk):
        there = chunk_rows(i)
        krows = pl.ds(mult(deep * hk, deep), deep)
        acc = None
        for h in range(HALVES):
            term = lax.dot_general(
                gl[2 * t + h, there, :], wv[2 * t + h, krows, :],
                (((1,), (1,)), ((), ())), preferred_element_type=F32,
            )
            acc = term if acc is None else acc + term
        return acc

    def dx_step(t, i, buf):
        @pl.when((i >= HELD) | (t > 0))
        def _():
            dx_copy(t, i, buf).wait_send()

        dsend[buf] = half(dx_part(t, i, 1 - y))
        dx_copy(t, i, buf).start()
        own[buf] = dx_part(t, i, y)

    def dx_begin(t, i, buf):
        dx_copy(t, i, buf).wait_recv()
        dx_fetch(t, i).start()

    def dx_final(t, i, buf):
        @pl.when((i >= 1) | (t > 0))
        def _():
            dx_out(t, i).wait()

        dx_fetch(t, i).wait()

        def step(j, inner):
            lanes = pl.ds(mult(tile * j, tile), tile)
            dout[:, lanes] = half(own[buf, :, lanes] + wide(dfetch[:, lanes]))
            return inner

        lax.fori_loop(0, 3, step, 0)
        dx_out(t, i).start()

    def listed(u, times, do):
        e, hit = 0, False
        for index, time in enumerate(times):
            same = u == time
            e = jnp.where(same, index, e)
            hit = hit | same

        @pl.when(hit)
        def _():
            do(e)

    def chunk_of(do):
        def run(e):
            t = jnp.where(e >= n_chunk, 1, 0)
            do(t, e - n_chunk * t, lax.rem(e, HELD))

        return run

    def turn():
        lanes_at_once = min(128, tile)

        def step(q, carry):
            lanes = pl.ds(mult(q * lanes_at_once, lanes_at_once), lanes_at_once)
            xt[lanes, :] = xsrc[:, lanes].T
            return carry

        lax.fori_loop(0, tile // lanes_at_once, step, 0)

    def tile_dot(g):
        return jnp.dot(xt[...], gl[g.p], preferred_element_type=F32)

    def stage_one(g):
        tile_fetch(g.t, g.j, 1 - c, False)
        turn()
        tile_fetch(g.t, g.j, c, True)
        cstage[...] = half(tile_dot(g))
        core_copy(g).start()

    def stage_two(g):
        tile_fetch(g.t, g.j, c, False)
        turn()

        @pl.when(g.j < 2)
        def _():
            tile_fetch(g.t, g.j + 1, 1 - c, True)

        core_copy(g).wait()
        product = tile_dot(g)
        for b in range(ZED):
            block = product[:, b * hw : (b + 1) * hw] + wide(
                cland[g.buf, :, b * hw : (b + 1) * hw]
            )
            left, right = block[:, :xw], block[:, xw:]
            kept[g.trio, b] = jnp.where(x == 0, left, right)
            xstage[g.trio, b] = half(jnp.where(x == 0, right, left))

        def send(q, carry):
            across_copy(g, lax.rem(z + 3 + 3 * q, ZED)).start()
            return carry

        lax.fori_loop(0, ZED, send, 0)

    def stage_three(g):
        @pl.when(g.g >= 3)
        def _():
            for to in others:
                z_copy(g, to).wait_send()
            ax_own(g).wait_send()

        def add(b):
            across_copy(g, b).wait()
            zstage[g.trio, b] = half(kept[g.trio, b] + wide(xland[g.quad, b]))

        def step(q, carry):
            b = lax.rem(z + 3 + 3 * q, ZED)
            add(b)
            z_copy(g, b).start()
            return carry

        lax.fori_loop(0, ZED - 1, step, 0)
        add(z)
        z_own(g).start()
        ax_own(g).start()

    def stage_four(g):
        def step(q, carry):
            b = lax.rem(z + 1 + q, ZED)
            z_in(g, b).wait_recv()
            ax_copy(g, b).start()
            return carry

        lax.fori_loop(0, ZED - 1, step, 0)
        z_own(g).wait()

    def stage_five(g):
        def step(q, carry):
            b = lax.rem(z + q, ZED)
            ax_in(g, b).wait_recv()
            ac_copy(g, b).start()
            return carry

        lax.fori_loop(0, ZED, step, 0)

    def stage_six(g):
        def step(b, carry):
            ac_in(g, b).wait_recv()
            return carry

        lax.fori_loop(0, ZED, step, 0)

    def tile_of(g):
        p = lax.div(g, 3)
        t, h = tower(p)
        return Tile(
            g=g, p=p, t=t, h=h, j=g - 3 * p,
            buf=lax.rem(g, 2), trio=g - 3 * p, quad=lax.rem(g, 4),
        )

    def tile_in_hand(do):
        return lambda g: do(tile_of(g))

    def body(u, carry):
        p0 = lax.div(u, n_part)
        i0 = u - p0 * n_part
        slot0, prod0 = lax.rem(u, RING), lax.rem(u, PRODUCTS)
        buf0 = lax.rem(u, 2)

        def before(lag):
            if isinstance(lag, int):
                whole, left = divmod(lag, n_part)
            else:
                whole, left = 0, lag
            under = i0 < left
            p = p0 - whole - jnp.where(under, 1, 0)
            i = i0 - left + jnp.where(under, n_part, 0)
            in_ring = lag % RING if isinstance(lag, int) else lag
            in_prods = lag % PRODUCTS if isinstance(lag, int) else lag
            slot = slot0 - in_ring + jnp.where(slot0 < in_ring, RING, 0)
            prod = prod0 - in_prods + jnp.where(prod0 < in_prods, PRODUCTS, 0)
            t, h = tower(p)
            return Part(u=u - lag, p=p, i=i, t=t, h=h, slot=slot, prod=prod, buf=lax.rem(i, 2))

        @pl.when((u >= 5) & (u < parts + 5))
        def _():
            slot = before(5).slot
            at_place(0, ZED - 2, lambda zz: rs_up(slot, zz).wait_send())
            at_place(1, ZED - 1, lambda zz: rs_down(slot, zz).wait_send())

        @pl.when((u >= 8) & (u < parts + 8))
        def _():
            at = before(8)

            def step(b, inner):
                @pl.when((z < ZED - 1) & (b <= z))
                def _():
                    ag(at, b, 0, up).wait_send()

                @pl.when((z > 0) & (b >= z))
                def _():
                    ag(at, b, 1, down).wait_send()

                return inner

            lax.fori_loop(0, ZED, step, 0)

        ck = lax.div(i0, SUB)
        fresh = ck * SUB == i0
        t0, h0_ = tower(p0)
        xbuf = lax.rem(ck, 2)

        @pl.when((u < parts) & fresh)
        def _():
            @pl.when(i0 == 0)
            def _():
                w_own(p0).wait()
                for frm in others:
                    w_c_in(p0, frm).wait_recv()

            for copy in x_fetch(t0, ck, xbuf):
                copy.wait()

            product = jnp.dot(xc[xbuf], wv[p0], preferred_element_type=F32)
            for b in range(ZED):
                for s in range(SUB):
                    pf[prod0 + s, b] = product[
                        s * part : (s + 1) * part, b * hw : (b + 1) * hw
                    ]

        going_up = before(z)

        @pl.when((going_up.u >= 0) & (going_up.u < parts))
        def _():
            slot, prod = going_up.slot, going_up.prod
            at_place(1, ZED - 1, lambda zz: rs_from_below(slot, zz).wait_recv())

            @pl.when(z == 0)
            def _():
                for b in range(1, ZED):
                    rs[slot, b + 1] = half(pf[prod, b])

            @pl.when(z > 0)
            def _():
                def step(b, inner):
                    rs[slot, b + 1] = half(wide(rs[slot, b + 1]) + pf[prod, b])
                    return inner

                lax.fori_loop(z + 1, ZED, step, 0)

            at_place(0, ZED - 2, lambda zz: rs_up(slot, zz).start())

        going_down = before(ZED - 1 - z)

        @pl.when((going_down.u >= 0) & (going_down.u < parts))
        def _():
            slot, prod = going_down.slot, going_down.prod
            at_place(0, ZED - 2, lambda zz: rs_from_above(slot, zz).wait_recv())

            @pl.when(z == ZED - 1)
            def _():
                for b in range(ZED - 1):
                    rs[slot, b] = half(pf[prod, b])

            @pl.when(z < ZED - 1)
            def _():
                def step(b, inner):
                    rs[slot, b] = half(wide(rs[slot, b]) + pf[prod, b])
                    return inner

                lax.fori_loop(0, z, step, 0)

            at_place(1, ZED - 1, lambda zz: rs_down(slot, zz).start())

        @pl.when(fresh & (u + 2 * SUB < 2 * n_part))
        def _():
            k = p0 * n_chunk + ck + 2
            over = jnp.where(k >= n_chunk, 1, 0)
            x_copy(over, k - over * n_chunk).start()

        @pl.when(fresh & (u + SUB < parts))
        def _():
            wrap = jnp.where(ck + 1 == n_chunk, 1, 0)
            i = ck + 1 - wrap * n_chunk
            t, h = tower(p0 + wrap)

            @pl.when(h == 0)
            def _():
                x_copy(t, i).wait_recv()

            for copy in x_fetch(t, i, lax.rem(i, 2)):
                copy.start()

        @pl.when((u >= 3) & (u < parts + 3))
        def _():
            final(before(3), before(2))

        forward_ag(before(4), 1)
        forward_ag(before(5), 2)
        forward_ag(before(6), 3)

        listed(u, DX_BEGINS, chunk_of(dx_begin))
        listed(u, DX_ENDS, chunk_of(dx_final))
        listed(u, DX_TIMES, chunk_of(dx_step))

        listed(u, THREES, tile_in_hand(stage_three))
        listed(u, TWOS, tile_in_hand(stage_two))
        listed(u, ONES, tile_in_hand(stage_one))
        listed(u, FOURS, tile_in_hand(stage_four))
        listed(u, FIVES, tile_in_hand(stage_five))
        listed(u, SIXES, tile_in_hand(stage_six))

        def first_fetch(p):
            tile_fetch(lax.div(p, HALVES), 0, 1 - c, True)

        listed(u, [time - 1 for time in ONES[::3]], first_fetch)

        for p, times in W_STRIPS.items():
            def send_strip(r, p=p):
                for to in others:
                    w_z_strip(p, to, r).start()

                @pl.when(r == 0)
                def _():
                    w_own(p).start()

            listed(u, times, send_strip)

        for p, times in W_ACROSS.items():
            for q, time in enumerate(times):
                @pl.when(u == time)
                def _(p=p, q=q):
                    w_z_in(p, others[q]).wait_recv()
                    w_x(p, others[q]).start()

        for p, times in W_CORES.items():
            for q, time in enumerate(times):
                @pl.when(u == time)
                def _(p=p, q=q):
                    w_x_in(p, others[q]).wait_recv()
                    w_c(p, others[q]).start()

        @pl.when(u == parts + 3)
        def _():
            for p in range(PHASES):
                t, h = p // HALVES, p % HALVES
                for s in range(2):
                    for what in range(2):
                        sums[0, pl.ds(4 * what + 2 * s + t, 1), h * hw : (h + 1) * hw] = jnp.sum(
                            stat[p, 2 * what + s], axis=0, keepdims=True
                        )
            sum_copy(0, across_c).start()

        @pl.when(u == parts + 4)
        def _():
            sum_copy(0, across_c).wait()
            sums[1] = sums[0] + sums_land[0]
            sum_copy(1, across_x).start()

        @pl.when(u == parts + 5)
        def _():
            sum_copy(1, across_x).wait()
            both = sums[1] + sums_land[1]
            sums[2] = both
            member = (
                lax.broadcasted_iota(jnp.int32, (width, lane), 0) % FLAG_GROUPS
                == lax.broadcasted_iota(jnp.int32, (width, lane), 1) % FLAG_GROUPS
            ).astype(F32)
            bias_rows = both[0:4]
            inner = both[0:2] * both[2:4]
            stack = jnp.concatenate([inner, bias_rows * bias_rows, inner], axis=0)
            prods[0] = jnp.dot(
                stack, member, precision=lax.Precision.HIGHEST, preferred_element_type=F32
            )
            prod_y().start()

        @pl.when(u == parts + 6)
        def _():
            prod_y().wait()
            prods[1] = prods[0] + prods_land[ZED]
            for to in others:
                prod_z(to).start()

        @pl.when(u == parts + 7)
        def _():
            for frm in others:
                prod_z_in(frm).wait_recv()
            prods_land[z] = prods[1]
            whole = prods_land[0] + prods_land[1] + prods_land[2] + prods_land[3]
            both = sums[2]
            group = lax.broadcasted_iota(jnp.int32, (1, lane), 1) % FLAG_GROUPS

            def over(row):
                return jnp.concatenate([row] * (width // lane), axis=1)

            def flag_row(s, t):
                row = jnp.zeros((1, lane), F32)
                for g in range(FLAG_GROUPS):
                    row = jnp.where(group == g, flags[s, t, g].astype(F32), row)
                return row

            for t in range(2):
                task0, task1 = both[t : t + 1], both[2 + t : 3 + t]
                dots = whole[t : t + 1]
                coef0 = over(flag_row(0, t) * dots / (whole[4 + t : 5 + t] + 1e-06))
                coef1 = over(flag_row(1, t) * dots / (whole[2 + t : 3 + t] + 1e-06))
                gbias[t : t + 1] = (task0 - coef0 * task1) + (task1 - coef1 * task0)
            for s in range(2):
                gstitch[s] = both[4 + 2 * s : 6 + 2 * s]

        return carry

    lax.fori_loop(0, max(SIXES + DX_ENDS) + 1, body, 0)

    last = 3 * PHASES - 1

    for g in (last - 2, last - 1, last):
        for to in others:
            z_copy(tile_of(g), to).wait_send()
        ax_own(tile_of(g)).wait_send()
    for i in range(n_chunk - HELD, n_chunk):
        dx_copy(1, i, (n_chunk + i) % HELD).wait_send()
    for i in (n_part - 2, n_part - 1):
        mixed_out(1, i, i % 2).wait()
    dx_out(1, n_chunk - 1).wait()

    def drain_tiles(g, carry):
        at = tile_of(g)
        for b in others:
            ax_copy(at, b).wait_send()
        for b in range(ZED):
            ac_copy(at, b).wait_send()
        return carry

    lax.fori_loop(0, last + 1, drain_tiles, 0)

    def drain_x(i, carry):
        x_copy(0, i).wait_send()
        x_copy(1, i).wait_send()
        return carry

    lax.fori_loop(0, n_chunk, drain_x, 0)

    def drain_w(p, carry):
        for to in others:
            w_z(p, to).wait_send()
            w_x(p, to).wait_send()
            w_c(p, to).wait_send()
        return carry

    lax.fori_loop(0, PHASES, drain_w, 0)
    for to in others:
        prod_z(to).wait_send()


def fused_call(feat, wts, cot, bias, stitch, counts, mask, flags):
    rows, deep, width = feat.shape[1], feat.shape[2], wts.shape[2]
    chunk = rows // 6
    part = chunk // SUB
    hw, kz, tile = width // 2, 2 * deep, deep // 3
    cat, xw = 4 * hw, width // 4
    lane = min(128, width)
    dma = pltpu.SemaphoreType.DMA
    anywhere = pl.BlockSpec(memory_space=pl.ANY)
    inside = pl.BlockSpec(memory_space=pltpu.VMEM)
    scalars = pl.BlockSpec(memory_space=pltpu.SMEM)

    def v(shape, kind=BF16):
        return pltpu.VMEM(shape, kind)

    out_shape = [
        jax.ShapeDtypeStruct((2, rows, width), BF16),
        jax.ShapeDtypeStruct((2, rows, deep), BF16),
        jax.ShapeDtypeStruct((2, ZED, kz, width), BF16),
        jax.ShapeDtypeStruct((2, width), F32),
        jax.ShapeDtypeStruct((2, 2, width), F32),
        jax.ShapeDtypeStruct((2, rows, deep), BF16),
        jax.ShapeDtypeStruct((2, rows, deep), BF16),
    ]
    scratch = [
        v((PHASES, kz, cat)),
        v((PHASES, rows, cat)),
        v((RING, 5, part, hw)),
        v((2, rows, hw), F32),
        v((2, chunk, kz)),
        v((PRODUCTS, ZED, part, hw), F32),
        v((2, 2, part, hw)),
        v((2, 2, part, hw)),
        v((HELD, chunk, deep), F32),
        v((HELD, chunk, deep)),
        v((chunk, deep)),
        v((chunk, deep)),
        v((rows, tile)),
        v((tile, rows)),
        v((tile, cat)),
        v((2, tile, cat)),
        v((3, ZED, tile, xw)),
        v((4, ZED, tile, xw)),
        v((3, ZED, tile, xw), F32),
        v((3, ZED, tile, xw)),
        v((rows, lane), F32),
        v((PHASES, 4, 8, hw), F32),
        v((3, 8, width), F32),
        v((2, 8, width), F32),
        v((2, 8, lane), F32),
        v((5, 8, lane), F32),
        dma((RING, 2)), dma((RING, 2)), dma((RING, 8)), dma((RING, 4)),
        dma((12,)), dma((12,)),
        dma((4, 4)), dma((4, 4)), dma((4, 4)), dma((4, 4)), dma((4, 4)), dma((4, 4)), dma((4,)),
        dma((2, 2)), dma((2,)), dma((2,)), dma((HELD,)), dma((12,)), dma((1,)), dma((1,)),
        dma((1,)), dma((1,)), dma((2,)), dma((3, 4)), dma((4, 4)), dma((3, 4)), dma((12, 4)),
        dma((3,)), dma((3,)),
        dma((12, 4)), dma((12, 4)), dma((12, 4)), dma((12, 4)), dma((8,)), dma((8,)),
    ]
    flops = 3 * 2 * 2 * rows * kz * cat * 2
    return pl.pallas_call(
        functools.partial(fused_kernel, rows, deep, width, chunk),
        out_shape=out_shape,
        in_specs=[anywhere] * 3 + [inside] * 4 + [scalars],
        out_specs=[anywhere] * 3 + [inside] * 2 + [anywhere] * 2,
        scratch_shapes=scratch,
        compiler_params=pltpu.CompilerParams(
            collective_id=0, has_side_effects=True, vmem_limit_bytes=64 * 1024 * 1024
        ),
        cost_estimate=pl.CostEstimate(
            flops=flops, bytes_accessed=200_000_000, transcendentals=2 * rows * width * 2
        ),
        name="cross_stitch_step",
    )(feat, wts, cot, bias, stitch, counts, mask, flags)


def finish_kernel(
    block, low, mixed, gfeat, gbias, gstitch,
    out, mixed_out, gfeat_out, gbias_out, gstitch_out,
    taken, given, held_mixed, held_gfeat, in_sem, out_sem, pass_sem,
):
    n_block = low.shape[0] // block
    fetched = (
        pltpu.make_async_copy(mixed, held_mixed, pass_sem.at[0]),
        pltpu.make_async_copy(gfeat, held_gfeat, pass_sem.at[1]),
    )
    passed = (
        pltpu.make_async_copy(held_mixed, mixed_out, pass_sem.at[2]),
        pltpu.make_async_copy(held_gfeat, gfeat_out, pass_sem.at[3]),
    )

    def take(i):
        return pltpu.make_async_copy(
            low.at[pl.ds(i * block, block)], taken.at[i % WIDEN_SLOTS], in_sem.at[i % WIDEN_SLOTS]
        )

    def give(i):
        return pltpu.make_async_copy(
            given.at[i % WIDEN_SLOTS], out.at[pl.ds(i * block, block)], out_sem.at[i % WIDEN_SLOTS]
        )

    for i in range(min(WIDEN_SLOTS, n_block)):
        take(i).start()
    for copy in fetched:
        copy.start()
    gbias_out[...] = gbias[...]
    gstitch_out[...] = gstitch[...]
    for i in range(n_block):
        slot = i % WIDEN_SLOTS
        take(i).wait()
        if i >= WIDEN_SLOTS:
            give(i - WIDEN_SLOTS).wait()
        given[slot] = wide(taken[slot])
        give(i).start()
        if i + WIDEN_SLOTS < n_block:
            take(i + WIDEN_SLOTS).start()
        if i == 2:
            for arrived, copy in zip(fetched, passed):
                arrived.wait()
                copy.start()
    for i in range(max(0, n_block - WIDEN_SLOTS), n_block):
        give(i).wait()
    for copy in passed:
        copy.wait()


def finish(low, mixed, gfeat, gbias, gstitch):
    tall, width = low.shape
    block = tall // WIDEN_BLOCKS
    anywhere = pl.BlockSpec(memory_space=pl.ANY)
    inside = pl.BlockSpec(memory_space=pltpu.VMEM)
    moved = sum(a.size * a.dtype.itemsize for a in (mixed, gfeat))
    return pl.pallas_call(
        functools.partial(finish_kernel, block),
        in_specs=[anywhere] * 3 + [inside] * 2,
        out_specs=[anywhere] * 3 + [inside] * 2,
        out_shape=[
            jax.ShapeDtypeStruct(a.shape, kind)
            for a, kind in ((low, F32), (mixed, BF16), (gfeat, BF16), (gbias, F32), (gstitch, F32))
        ],
        scratch_shapes=[
            pltpu.VMEM((WIDEN_SLOTS, block, width), BF16),
            pltpu.VMEM((WIDEN_SLOTS, block, width), F32),
            pltpu.VMEM(mixed.shape, BF16),
            pltpu.VMEM(gfeat.shape, BF16),
            pltpu.SemaphoreType.DMA((WIDEN_SLOTS,)),
            pltpu.SemaphoreType.DMA((WIDEN_SLOTS,)),
            pltpu.SemaphoreType.DMA((4,)),
        ],
        compiler_params=pltpu.CompilerParams(vmem_limit_bytes=60 * 1024 * 1024),
        cost_estimate=pl.CostEstimate(
            flops=tall * width, bytes_accessed=6 * tall * width + 2 * moved, transcendentals=0
        ),
        name="finish",
    )(low, mixed, gfeat, gbias, gstitch)


def fused_plan(mesh):
    def per_device(features, weights, bias, stitch, cotangent, crop_counts, row_mask, flags):
        rows, deep = features.shape[1:]
        width = weights.shape[2]
        mixed, gfeat, gwt, gbias, gstitch, _, _ = fused_call(
            features, weights, cotangent, bias, stitch,
            crop_counts.reshape(1, -1), row_mask.reshape(-1, min(128, rows // 6)), flags,
        )
        grad_weights, mixed, gfeat, gbias, gstitch = finish(
            gwt.reshape(-1, width), mixed, gfeat, gbias, gstitch
        )
        return mixed, gfeat, grad_weights.reshape(2, ZED * 2 * deep, width), gbias, gstitch

    return per_device


def plan_for(mesh):
    if mesh.shape["batch"] == 4 and mesh.shape["mp"] == 2 * ZED:
        return fused_plan(mesh)
    return generic_plan(mesh)


def solution(mesh):
    in_specs = (
        P(None, "batch", "mp"),
        P(None, None, "mp"),
        P(None, "mp"),
        P(None, None, "mp"),
        P(None, "batch", "mp"),
        P("batch"),
        P("batch"),
        P(),
    )
    out_specs = (
        P(None, "batch", "mp"),
        P(None, "batch", "mp"),
        P(None, None, "mp"),
        P(None, "mp"),
        P(None, None, "mp"),
    )
    return jax.shard_map(
        plan_for(mesh), mesh=mesh, in_specs=in_specs, out_specs=out_specs, check_vma=False
    )
```

```python
import collections
import functools

import jax
import jax.numpy as jnp
from jax import lax
from jax.experimental import pallas as pl
from jax.experimental.pallas import tpu as pltpu
from jax.sharding import PartitionSpec as P

FLAG_GROUPS = 8
OUTER = 4


def row_weights(counts, mask):
    ends = jnp.cumsum(counts)
    starts = ends - counts
    index = lax.broadcasted_iota(jnp.int32, (mask.shape[0], counts.shape[0]), 0)
    inside = (index >= starts[None, :]) & (index < ends[None, :])
    count_row = jnp.sum(jnp.where(inside, counts[None, :], 0), axis=1)
    live = (count_row > 0) & (mask == 1)
    return jnp.where(live, 1.0 / jnp.maximum(count_row, 1).astype(jnp.float32), 0.0)


def project_bias(task_bias, flags):
    local_width = task_bias.shape[2]
    channel = lax.axis_index("mp") * local_width + lax.broadcasted_iota(
        jnp.int32, (local_width, FLAG_GROUPS), 0
    )
    member = (
        channel % FLAG_GROUPS == lax.broadcasted_iota(jnp.int32, (local_width, FLAG_GROUPS), 1)
    ).astype(jnp.float32)
    dots = jnp.dot(task_bias[0] * task_bias[1], member, precision=lax.Precision.HIGHEST)
    norms = jnp.einsum(
        "stc,cg->stg", task_bias * task_bias, member, precision=lax.Precision.HIGHEST
    )
    dots, norms = lax.psum((dots, norms), "mp")
    flag = flags.astype(jnp.float32)
    coef_first = jnp.dot(
        flag[0] * dots / (norms[1] + 1e-06), member.T, precision=lax.Precision.HIGHEST
    )
    coef_second = jnp.dot(
        flag[1] * dots / (norms[0] + 1e-06), member.T, precision=lax.Precision.HIGHEST
    )
    first = task_bias[0] - coef_first * task_bias[1]
    second = task_bias[1] - coef_second * task_bias[0]
    return first + second


def generic_plan(mesh):
    n_mp = mesh.shape["mp"]
    n_batch = mesh.shape["batch"]
    inner = n_mp // OUTER
    inner_groups = [[o * inner + i for i in range(inner)] for o in range(OUTER)]
    outer_groups = [[o * inner + i for o in range(OUTER)] for i in range(inner)]

    def per_device(features, weights, bias, stitch, cotangent, crop_counts, row_mask, flags):
        rows = features.shape[1]
        width = weights.shape[2]
        depth = features.shape[2] * inner
        held = lax.all_gather(
            features, "mp", axis=2, tiled=True, axis_index_groups=inner_groups
        )
        split = weights.reshape(2, OUTER, depth, width)
        block = lax.all_to_all(
            split, "mp", split_axis=1, concat_axis=1, axis_index_groups=outer_groups
        )
        block = block.reshape(2, OUTER, depth, width)
        part = jnp.einsum("trk,tokc->otrc", held, block, preferred_element_type=jnp.float32)
        linear = lax.psum_scatter(
            part.astype(jnp.bfloat16),
            "mp",
            scatter_dimension=0,
            axis_index_groups=outer_groups,
        ).astype(jnp.float32)
        pre = linear + bias[:, None, :]
        hidden, gelu_back = jax.vjp(lambda v: jax.nn.gelu(v, approximate=False), pre)
        mixed = stitch[:, 0, None, :] * hidden[0][None] + stitch[:, 1, None, :] * hidden[1][None]
        scale_rows = row_weights(crop_counts, row_mask)
        grad_out = cotangent.astype(jnp.float32) * scale_rows[None, :, None]
        first_task = gelu_back(stitch[0][:, None, :] * grad_out[0][None])[0]
        second_task = gelu_back(stitch[1][:, None, :] * grad_out[1][None])[0]
        task_bias = jnp.stack([jnp.sum(first_task, axis=1), jnp.sum(second_task, axis=1)])
        grad_linear = (first_task + second_task).astype(jnp.bfloat16)
        grad_stitch = jnp.sum(grad_out[:, None] * hidden[None], axis=2)
        every = lax.all_gather(grad_linear, "mp", axis_index_groups=outer_groups)
        grad_part = jnp.einsum(
            "otrc,tokc->trk", every, block, preferred_element_type=jnp.float32
        )
        grad_part = grad_part.astype(jnp.bfloat16).reshape(2, rows, inner, depth // inner)
        grad_features = lax.psum_scatter(
            grad_part.transpose(2, 0, 1, 3),
            "mp",
            scatter_dimension=0,
            axis_index_groups=inner_groups,
        )
        weight_part = jnp.einsum(
            "trk,otrc->otkc", held, every, preferred_element_type=jnp.float32
        )
        weight_part = weight_part.astype(jnp.bfloat16).reshape(
            OUTER, 2, n_batch, depth // n_batch, width
        )
        share = lax.psum_scatter(
            weight_part.transpose(2, 0, 1, 3, 4), "batch", scatter_dimension=0
        )
        share = lax.all_to_all(
            share, "mp", split_axis=0, concat_axis=0, axis_index_groups=outer_groups
        )
        share = share.reshape(OUTER, 2, depth // n_batch, width)
        whole = lax.all_gather(share, "batch")
        grad_weights = whole.transpose(2, 1, 0, 3, 4).reshape(2, OUTER * depth, width)
        task_bias, grad_stitch = lax.psum((task_bias, grad_stitch), "batch")
        grad_bias = project_bias(task_bias, flags)
        return (
            mixed.astype(jnp.bfloat16),
            grad_features.astype(jnp.bfloat16),
            grad_weights.astype(jnp.float32),
            grad_bias,
            grad_stitch,
        )

    return per_device


MESH = pl.DeviceIdType.MESH
BF16 = jnp.bfloat16
F32 = jnp.float32
ZED = 4
HALVES = 2
PHASES = 4
RING = 8
BAND = 32
SUB = 2
PRODUCTS = 6
HELD = 4
WIDEN_BLOCKS = 18
WIDEN_SLOTS = 6

DX_TIMES = (20, 21, 23, 25, 27, 29, 43, 45, 48, 50, 58, 64)
DX_BEGINS = (22, 24, 26, 28, 30, 34, 44, 48, 57, 60, 68, 76)
DX_ENDS = (23, 25, 27, 29, 31, 43, 45, 50, 59, 62, 71, 81)
ONES = (19, 23, 26, 30, 33, 40, 43, 45, 46, 54, 56, 57)
TWOS = (22, 26, 27, 32, 36, 42, 44, 46, 49, 55, 57, 61)
THREES = (23, 28, 33, 35, 42, 43, 45, 52, 55, 58, 59, 70)
FOURS = (25, 30, 35, 37, 44, 47, 50, 54, 60, 67, 68, 73)
FIVES = (33, 36, 44, 45, 51, 59, 62, 67, 74, 76, 82, 85)
SIXES = (35, 43, 47, 57, 64, 70, 75, 82, 84, 86, 87, 90)
W_STRIPS = {2: (5, 7, 8, 11, 12, 13), 3: (21, 22, 23, 24, 26, 27)}
W_ACROSS = {1: (0, 0, 2), 2: (16, 21, 22), 3: (29, 29, 34)}
W_CORES = {1: (1, 6, 7), 2: (21, 23, 23), 3: (33, 33, 35)}


Part = collections.namedtuple("Part", ("u", "p", "i", "t", "h", "slot", "prod", "buf"))
Tile = collections.namedtuple("Tile", ("g", "p", "t", "h", "j", "buf", "trio", "quad"))


def half(value):
    return value.astype(BF16)


def wide(value):
    return value.astype(F32)


def fused_kernel(
    rows, deep, width, chunk,
    feat, wts, cot, bias, stitch, counts, mask, flags,
    mixed, gfeat, gwt, gbias, gstitch, xn, dxn,
    wv, gl, rs, h0, xc, pf, cc, mx, own, dsend, dfetch, dout,
    xsrc, xt, cstage, cland, xstage, xland, kept, zstage,
    scale, stat, sums, sums_land, prods, prods_land,
    rs_send, rs_recv, ag_send, ag_recv, xs_send, xs_recv,
    wz_send, wz_recv, wx_send, wx_recv, wc_send, wc_recv, wl,
    xf, cf, mxs, dx_send, dx_recv, df, dod,
    tile_in, c_send, c_recv, x_send, x_recv, z_send, z_recv, zl, zx_send,
    ax_send, ax_recv, ac_send, ac_recv, t_send, t_recv,
):
    batch, mp = lax.axis_index("batch"), lax.axis_index("mp")
    z, y = mp // 2, mp % 2
    x, c = batch // 2, batch % 2
    up = {"mp": mp + 2}
    down = {"mp": mp - 2}
    across_y = {"mp": 2 * z + 1 - y}
    across_x = {"batch": 2 * (1 - x) + c}
    across_c = {"batch": 2 * x + 1 - c}

    def at_z(other):
        return {"mp": 2 * other + y}

    others = (3 - z, (z + 2) % 4, z + 1 - 2 * (z % 2))

    n_chunk = rows // chunk
    total = PHASES * n_chunk
    part = chunk // SUB
    n_part = rows // part
    parts = PHASES * n_part
    images = counts.shape[1]
    hw = width // HALVES
    kz = 2 * deep
    quarter = deep // 2
    tile = deep // 3
    strip = quarter // 6
    xw = hw // 2

    def mult(value, unit):
        return pl.multiple_of(value, unit)

    def remote(src, dst, send, recv, device):
        return pltpu.make_async_remote_copy(
            src_ref=src, dst_ref=dst, send_sem=send, recv_sem=recv,
            device_id=device, device_id_type=MESH,
        )

    def cols(b):
        return pl.ds(mult(b * hw, hw), hw)

    def chunk_rows(i):
        return pl.ds(mult(i * chunk, chunk), chunk)

    def part_rows(i):
        return pl.ds(mult(i * part, part), part)

    def tower(p):
        t = jnp.where(p >= HALVES, 1, 0)
        return t, p - HALVES * t

    def x_copy(t, i):
        e = t * n_chunk + i
        return remote(
            feat.at[t, chunk_rows(i)], xn.at[t, chunk_rows(i)],
            xs_send.at[e], xs_recv.at[e], across_y,
        )

    def x_fetch(t, i, buf):
        return (
            pltpu.make_async_copy(
                feat.at[t, chunk_rows(i)],
                xc.at[buf, :, pl.ds(mult(deep * y, deep), deep)], xf.at[buf, 0],
            ),
            pltpu.make_async_copy(
                xn.at[t, chunk_rows(i)],
                xc.at[buf, :, pl.ds(mult(deep * (1 - y), deep), deep)], xf.at[buf, 1],
            ),
        )

    def cot_fetch(h, i, buf):
        return pltpu.make_async_copy(
            cot.at[:, part_rows(i), cols(h)], cc.at[buf], cf.at[buf]
        )

    def w_own(p):
        t, h = tower(p)
        return pltpu.make_async_copy(
            wts.at[t, pl.ds(mult(kz * z, kz), kz), cols(h)], wv.at[p, :, cols(z)], wl.at[p],
        )

    def w_rows():
        return pl.ds(mult(deep * c + quarter * x, quarter), quarter)

    def w_z(p, to):
        t, h = tower(p)
        return remote(
            wts.at[
                t, pl.ds(mult(kz * to + deep * c + quarter * x, quarter), quarter), cols(h)
            ],
            wv.at[p, w_rows(), cols(z)],
            wz_send.at[p, to], wz_recv.at[p, z], at_z(to),
        )

    def w_z_strip(p, to, r):
        t, h = tower(p)
        at = deep * c + quarter * x + strip * r
        return remote(
            wts.at[t, pl.ds(mult(kz * to + at, strip), strip), cols(h)],
            wv.at[p, pl.ds(mult(at, strip), strip), cols(z)],
            wz_send.at[p, to], wz_recv.at[p, z], at_z(to),
        )

    def w_z_in(p, frm):
        here = wv.at[p, w_rows(), cols(frm)]
        return remote(here, here, wz_send.at[p, frm], wz_recv.at[p, frm], at_z(frm))

    def w_x(p, b):
        here = wv.at[p, w_rows(), cols(b)]
        return remote(here, here, wx_send.at[p, b], wx_recv.at[p, b], across_x)

    def w_x_in(p, b):
        here = wv.at[
            p, pl.ds(mult(deep * c + quarter * (1 - x), quarter), quarter), cols(b)
        ]
        return remote(here, here, wx_send.at[p, b], wx_recv.at[p, b], across_x)

    def w_c(p, b):
        here = wv.at[p, pl.ds(mult(deep * c, deep), deep), cols(b)]
        return remote(here, here, wc_send.at[p, b], wc_recv.at[p, b], across_c)

    def w_c_in(p, b):
        here = wv.at[p, pl.ds(mult(deep * (1 - c), deep), deep), cols(b)]
        return remote(here, here, wc_send.at[p, b], wc_recv.at[p, b], across_c)

    def rs_up(slot, zz):
        run = rs.at[slot, zz + 2 : ZED + 1]
        return remote(run, run, rs_send.at[slot, 0], rs_recv.at[slot, 0], up)

    def rs_down(slot, zz):
        run = rs.at[slot, 0:zz]
        return remote(run, run, rs_send.at[slot, 1], rs_recv.at[slot, 1], down)

    def rs_from_below(slot, zz):
        run = rs.at[slot, zz + 1 : ZED + 1]
        return remote(run, run, rs_send.at[slot, 0], rs_recv.at[slot, 0], down)

    def rs_from_above(slot, zz):
        run = rs.at[slot, 0 : zz + 1]
        return remote(run, run, rs_send.at[slot, 1], rs_recv.at[slot, 1], up)

    def at_place(first, last, do):
        for zz in range(first, last + 1):
            @pl.when(z == zz)
            def _(zz=zz):
                do(zz)

    def ag(at, b, going, device):
        here = gl.at[at.p, part_rows(at.i), cols(b)]
        return remote(
            here, here, ag_send.at[at.slot, going * ZED + b], ag_recv.at[at.slot, b], device
        )

    def dx_copy(t, i, buf):
        return remote(
            dsend.at[buf], dxn.at[t, chunk_rows(i)],
            dx_send.at[buf], dx_recv.at[t * n_chunk + i], across_y,
        )

    def dx_fetch(t, i):
        return pltpu.make_async_copy(dxn.at[t, chunk_rows(i)], dfetch, df.at[0])

    def dx_out(t, i):
        return pltpu.make_async_copy(dout, gfeat.at[t, chunk_rows(i)], dod.at[0])

    def mixed_out(h, i, buf):
        return pltpu.make_async_copy(
            mx.at[buf], mixed.at[:, part_rows(i), cols(h)], mxs.at[buf]
        )

    def tile_fetch(t, j, hk, start):
        lanes = pl.ds(mult(tile * j, tile), tile)
        near = pltpu.make_async_copy(feat.at[t, :, lanes], xsrc, tile_in.at[0])
        if not start:
            near.wait()
            return

        @pl.when(hk == y)
        def _():
            near.start()

        @pl.when(hk != y)
        def _():
            pltpu.make_async_copy(xn.at[t, :, lanes], xsrc, tile_in.at[0]).start()

    def core_copy(g):
        return remote(cstage, cland.at[g.buf], c_send.at[0], c_recv.at[g.buf], across_c)

    def across_copy(g, b):
        return remote(
            xstage.at[g.trio, b], xland.at[g.quad, b],
            x_send.at[g.trio, b], x_recv.at[g.quad, b], across_x,
        )

    def piece(g, source, core, lanes, n_lanes):
        return gwt.at[
            g.t, source,
            pl.ds(mult(deep * core + tile * g.j, tile), tile),
            pl.ds(mult(hw * g.h + lanes, xw), n_lanes),
        ]

    def z_copy(g, to):
        return remote(
            zstage.at[g.trio, to], piece(g, z, c, xw * x, xw),
            z_send.at[g.trio, to], z_recv.at[g.g, z], at_z(to),
        )

    def z_in(g, frm):
        here = piece(g, frm, c, xw * x, xw)
        return remote(here, here, z_send.at[g.trio, frm], z_recv.at[g.g, frm], at_z(frm))

    def z_own(g):
        return pltpu.make_async_copy(
            zstage.at[g.trio, z], piece(g, z, c, xw * x, xw), zl.at[g.trio]
        )

    def ax_own(g):
        return remote(
            zstage.at[g.trio, z], piece(g, z, c, xw * x, xw),
            zx_send.at[g.trio], ax_recv.at[g.g, z], across_x,
        )

    def ax_copy(g, b):
        here = piece(g, b, c, xw * x, xw)
        return remote(here, here, ax_send.at[g.g, b], ax_recv.at[g.g, b], across_x)

    def ax_in(g, b):
        here = piece(g, b, c, xw * (1 - x), xw)
        return remote(here, here, ax_send.at[g.g, b], ax_recv.at[g.g, b], across_x)

    def ac_copy(g, b):
        here = piece(g, b, c, 0, hw)
        return remote(here, here, ac_send.at[g.g, b], ac_recv.at[g.g, b], across_c)

    def ac_in(g, b):
        here = piece(g, b, 1 - c, 0, hw)
        return remote(here, here, ac_send.at[g.g, b], ac_recv.at[g.g, b], across_c)

    def sum_copy(stage, device):
        return remote(
            sums.at[stage], sums_land.at[stage], t_send.at[stage], t_recv.at[stage], device
        )

    def prod_y():
        return remote(prods.at[0], prods_land.at[ZED], t_send.at[2], t_recv.at[2], across_y)

    def prod_z(to):
        return remote(
            prods.at[1], prods_land.at[z], t_send.at[3 + to], t_recv.at[3 + z], at_z(to)
        )

    def prod_z_in(frm):
        here = prods_land.at[frm]
        return remote(here, here, t_send.at[3 + frm], t_recv.at[3 + frm], at_z(frm))

    barrier = pltpu.get_barrier_semaphore()
    for device in [at_z(o) for o in others] + [across_y, across_x, across_c]:
        pl.semaphore_signal(barrier, inc=1, device_id=device, device_id_type=MESH)
    pl.semaphore_wait(barrier, 6)

    for to in others:
        w_z(0, to).start()
    x_copy(0, 0).start()
    x_copy(0, 1).start()
    w_own(0).start()
    cot_fetch(0, 0, 0).start()

    image_row = lax.broadcasted_iota(jnp.int32, (images, images), 0)
    image_col = lax.broadcasted_iota(jnp.int32, (images, images), 1)
    crops = counts[...].astype(F32)
    ends = jnp.dot(
        jnp.broadcast_to(crops, (8, images)), (image_row <= image_col).astype(F32),
        precision=lax.Precision.HIGHEST, preferred_element_type=F32,
    )[0:1]
    starts = ends - crops
    block = mask.shape[1]
    lane = scale.shape[1]

    for r in range(rows // block):
        index = (
            lax.broadcasted_iota(jnp.int32, (block, images), 0) + r * block
        ).astype(F32)
        inside = (index >= starts) & (index < ends)
        count_row = jnp.sum(jnp.where(inside, crops, 0.0), axis=1, keepdims=True)
        diagonal = lax.broadcasted_iota(jnp.int32, (block, block), 0) == (
            lax.broadcasted_iota(jnp.int32, (block, block), 1)
        )
        usable = jnp.sum(
            jnp.where(diagonal, mask[r : r + 1, :].astype(F32), 0.0),
            axis=1, keepdims=True,
        )
        live = (count_row > 0.0) & (usable == 1.0)
        share = jnp.where(live, 1.0 / jnp.maximum(count_row, 1.0), 0.0)
        scale[r * block : (r + 1) * block, :] = jnp.broadcast_to(share, (block, lane))

    for frm in others:
        w_z_in(0, frm).wait_recv()
        w_x(0, frm).start()
    for to in others:
        w_z(1, to).start()
    w_own(1).start()
    for frm in others:
        w_x_in(0, frm).wait_recv()
        w_c(0, frm).start()
    x_copy(0, 0).wait_recv()
    for copy in x_fetch(0, 0, 0):
        copy.start()

    def final(at, later):
        p, i, slot, t, h, buf = at.p, at.i, at.slot, at.t, at.h, at.buf
        cot_fetch(h, i, buf).wait()

        @pl.when(at.u >= 2 * n_part + 2)
        def _():
            mixed_out(h, i, buf).wait()

        @pl.when(i == 0)
        def _():
            stat[p] = jnp.zeros(stat.shape[1:], F32)

        lanes = cols(h)
        shift = bias[pl.ds(t, 1), lanes]
        st = [stitch[s, pl.ds(t, 1), lanes] for s in range(2)]
        band = min(BAND, part)

        def step(r, carry):
            here = part_rows_of(r, band)
            there = pl.ds(mult(i * part + r * band, band), band)
            value = pf[at.prod, z, here, :]
            below = wide(rs[slot, z + 1, here, :])
            above = wide(rs[slot, z, here, :])
            value = value + jnp.where(z > 0, below, 0.0) + jnp.where(z < ZED - 1, above, 0.0)
            pre = value + shift
            phi = 0.5 * (1.0 + lax.erf(pre * 0.7071067811865476))
            hidden = pre * phi
            slope = phi + pre * (jnp.exp(-0.5 * pre * pre) * 0.3989422804014327)
            weight = scale[there, 0:1]
            first = wide(cc[buf, 0, here, :]) * weight
            second = wide(cc[buf, 1, here, :]) * weight
            back0 = st[0] * first * slope
            back1 = st[1] * second * slope
            gl[p, there, cols(z)] = half(back0 + back1)

            def fold(v):
                return jnp.sum(v.reshape(band // 8, 8, hw), axis=0)

            stat[p, 0] += fold(back0)
            stat[p, 1] += fold(back1)
            stat[p, 2] += fold(first * hidden)
            stat[p, 3] += fold(second * hidden)

            @pl.when(t == 0)
            def _():
                h0[h, there, :] = hidden

            @pl.when(t == 1)
            def _():
                before = h0[h, there, :]
                for s in range(2):
                    mx[buf, s, here, :] = half(
                        stitch[s, 0:1, lanes] * before + st[s] * hidden
                    )

            return carry

        lax.fori_loop(0, part // band, step, 0)

        @pl.when(z < ZED - 1)
        def _():
            ag(at, z, 0, up).start()

        @pl.when(z > 0)
        def _():
            ag(at, z, 1, down).start()

        @pl.when(t == 1)
        def _():
            mixed_out(h, i, buf).start()

        @pl.when(at.u + 1 < parts)
        def _():
            cot_fetch(later.h, later.i, later.buf).start()

    def part_rows_of(r, band):
        return pl.ds(mult(r * band, band), band)

    def forward_ag(at, far):
        @pl.when((at.u >= 0) & (at.u < parts))
        def _():
            @pl.when(z - far >= 0)
            def _():
                ag(at, z - far, 0, up).wait_recv()

                @pl.when(z < ZED - 1)
                def _():
                    ag(at, z - far, 0, up).start()

            @pl.when(z + far < ZED)
            def _():
                ag(at, z + far, 1, down).wait_recv()

                @pl.when(z > 0)
                def _():
                    ag(at, z + far, 1, down).start()

    def dx_part(t, i, hk):
        there = chunk_rows(i)
        krows = pl.ds(mult(deep * hk, deep), deep)
        acc = None
        for h in range(HALVES):
            term = lax.dot_general(
                gl[2 * t + h, there, :], wv[2 * t + h, krows, :],
                (((1,), (1,)), ((), ())), preferred_element_type=F32,
            )
            acc = term if acc is None else acc + term
        return acc

    def dx_step(t, i, buf):
        @pl.when((i >= HELD) | (t > 0))
        def _():
            dx_copy(t, i, buf).wait_send()

        dsend[buf] = half(dx_part(t, i, 1 - y))
        dx_copy(t, i, buf).start()
        own[buf] = dx_part(t, i, y)

    def dx_begin(t, i, buf):
        dx_copy(t, i, buf).wait_recv()
        dx_fetch(t, i).start()

    def dx_final(t, i, buf):
        @pl.when((i >= 1) | (t > 0))
        def _():
            dx_out(t, i).wait()

        dx_fetch(t, i).wait()

        def step(j, inner):
            lanes = pl.ds(mult(tile * j, tile), tile)
            dout[:, lanes] = half(own[buf, :, lanes] + wide(dfetch[:, lanes]))
            return inner

        lax.fori_loop(0, 3, step, 0)
        dx_out(t, i).start()

    def listed(u, times, do):
        e, hit = 0, False
        for index, time in enumerate(times):
            same = u == time
            e = jnp.where(same, index, e)
            hit = hit | same

        @pl.when(hit)
        def _():
            do(e)

    def chunk_of(do):
        def run(e):
            t = jnp.where(e >= n_chunk, 1, 0)
            do(t, e - n_chunk * t, lax.rem(e, HELD))

        return run

    def turn():
        lanes_at_once = min(128, tile)

        def step(q, carry):
            lanes = pl.ds(mult(q * lanes_at_once, lanes_at_once), lanes_at_once)
            xt[lanes, :] = xsrc[:, lanes].T
            return carry

        lax.fori_loop(0, tile // lanes_at_once, step, 0)

    def tile_dot(g):
        return jnp.dot(xt[...], gl[g.p], preferred_element_type=F32)

    def stage_one(g):
        tile_fetch(g.t, g.j, 1 - c, False)
        turn()
        tile_fetch(g.t, g.j, c, True)
        cstage[...] = half(tile_dot(g))
        core_copy(g).start()

    def stage_two(g):
        tile_fetch(g.t, g.j, c, False)
        turn()

        @pl.when(g.j < 2)
        def _():
            tile_fetch(g.t, g.j + 1, 1 - c, True)

        core_copy(g).wait()
        product = tile_dot(g)
        for b in range(ZED):
            block = product[:, b * hw : (b + 1) * hw] + wide(
                cland[g.buf, :, b * hw : (b + 1) * hw]
            )
            left, right = block[:, :xw], block[:, xw:]
            kept[g.trio, b] = jnp.where(x == 0, left, right)
            xstage[g.trio, b] = half(jnp.where(x == 0, right, left))

        def send(q, carry):
            across_copy(g, lax.rem(z + 3 + 3 * q, ZED)).start()
            return carry

        lax.fori_loop(0, ZED, send, 0)

    def stage_three(g):
        @pl.when(g.g >= 3)
        def _():
            for to in others:
                z_copy(g, to).wait_send()
            ax_own(g).wait_send()

        def add(b):
            across_copy(g, b).wait()
            zstage[g.trio, b] = half(kept[g.trio, b] + wide(xland[g.quad, b]))

        def step(q, carry):
            b = lax.rem(z + 3 + 3 * q, ZED)
            add(b)
            z_copy(g, b).start()
            return carry

        lax.fori_loop(0, ZED - 1, step, 0)
        add(z)
        z_own(g).start()
        ax_own(g).start()

    def stage_four(g):
        def step(q, carry):
            b = lax.rem(z + 1 + q, ZED)
            z_in(g, b).wait_recv()
            ax_copy(g, b).start()
            return carry

        lax.fori_loop(0, ZED - 1, step, 0)
        z_own(g).wait()

    def stage_five(g):
        def step(q, carry):
            b = lax.rem(z + q, ZED)
            ax_in(g, b).wait_recv()
            ac_copy(g, b).start()
            return carry

        lax.fori_loop(0, ZED, step, 0)

    def stage_six(g):
        def step(b, carry):
            ac_in(g, b).wait_recv()
            return carry

        lax.fori_loop(0, ZED, step, 0)

    def tile_of(g):
        p = lax.div(g, 3)
        t, h = tower(p)
        return Tile(
            g=g, p=p, t=t, h=h, j=g - 3 * p,
            buf=lax.rem(g, 2), trio=g - 3 * p, quad=lax.rem(g, 4),
        )

    def tile_in_hand(do):
        return lambda g: do(tile_of(g))

    def body(u, carry):
        p0 = lax.div(u, n_part)
        i0 = u - p0 * n_part
        slot0, prod0 = lax.rem(u, RING), lax.rem(u, PRODUCTS)
        buf0 = lax.rem(u, 2)

        def before(lag):
            if isinstance(lag, int):
                whole, left = divmod(lag, n_part)
            else:
                whole, left = 0, lag
            under = i0 < left
            p = p0 - whole - jnp.where(under, 1, 0)
            i = i0 - left + jnp.where(under, n_part, 0)
            in_ring = lag % RING if isinstance(lag, int) else lag
            in_prods = lag % PRODUCTS if isinstance(lag, int) else lag
            slot = slot0 - in_ring + jnp.where(slot0 < in_ring, RING, 0)
            prod = prod0 - in_prods + jnp.where(prod0 < in_prods, PRODUCTS, 0)
            t, h = tower(p)
            return Part(u=u - lag, p=p, i=i, t=t, h=h, slot=slot, prod=prod, buf=lax.rem(i, 2))

        @pl.when((u >= 5) & (u < parts + 5))
        def _():
            slot = before(5).slot
            at_place(0, ZED - 2, lambda zz: rs_up(slot, zz).wait_send())
            at_place(1, ZED - 1, lambda zz: rs_down(slot, zz).wait_send())

        @pl.when((u >= 8) & (u < parts + 8))
        def _():
            at = before(8)

            def step(b, inner):
                @pl.when((z < ZED - 1) & (b <= z))
                def _():
                    ag(at, b, 0, up).wait_send()

                @pl.when((z > 0) & (b >= z))
                def _():
                    ag(at, b, 1, down).wait_send()

                return inner

            lax.fori_loop(0, ZED, step, 0)

        ck = lax.div(i0, SUB)
        fresh = ck * SUB == i0
        t0, h0_ = tower(p0)
        xbuf = lax.rem(ck, 2)

        @pl.when((u < parts) & fresh)
        def _():
            @pl.when(i0 == 0)
            def _():
                w_own(p0).wait()
                for frm in others:
                    w_c_in(p0, frm).wait_recv()

            for copy in x_fetch(t0, ck, xbuf):
                copy.wait()

            product = jnp.dot(xc[xbuf], wv[p0], preferred_element_type=F32)
            for b in range(ZED):
                for s in range(SUB):
                    pf[prod0 + s, b] = product[
                        s * part : (s + 1) * part, b * hw : (b + 1) * hw
                    ]

        going_up = before(z)

        @pl.when((going_up.u >= 0) & (going_up.u < parts))
        def _():
            slot, prod = going_up.slot, going_up.prod
            at_place(1, ZED - 1, lambda zz: rs_from_below(slot, zz).wait_recv())

            @pl.when(z == 0)
            def _():
                for b in range(1, ZED):
                    rs[slot, b + 1] = half(pf[prod, b])

            @pl.when(z > 0)
            def _():
                def step(b, inner):
                    rs[slot, b + 1] = half(wide(rs[slot, b + 1]) + pf[prod, b])
                    return inner

                lax.fori_loop(z + 1, ZED, step, 0)

            at_place(0, ZED - 2, lambda zz: rs_up(slot, zz).start())

        going_down = before(ZED - 1 - z)

        @pl.when((going_down.u >= 0) & (going_down.u < parts))
        def _():
            slot, prod = going_down.slot, going_down.prod
            at_place(0, ZED - 2, lambda zz: rs_from_above(slot, zz).wait_recv())

            @pl.when(z == ZED - 1)
            def _():
                for b in range(ZED - 1):
                    rs[slot, b] = half(pf[prod, b])

            @pl.when(z < ZED - 1)
            def _():
                def step(b, inner):
                    rs[slot, b] = half(wide(rs[slot, b]) + pf[prod, b])
                    return inner

                lax.fori_loop(0, z, step, 0)

            at_place(1, ZED - 1, lambda zz: rs_down(slot, zz).start())

        @pl.when(fresh & (u + 2 * SUB < 2 * n_part))
        def _():
            k = p0 * n_chunk + ck + 2
            over = jnp.where(k >= n_chunk, 1, 0)
            x_copy(over, k - over * n_chunk).start()

        @pl.when(fresh & (u + SUB < parts))
        def _():
            wrap = jnp.where(ck + 1 == n_chunk, 1, 0)
            i = ck + 1 - wrap * n_chunk
            t, h = tower(p0 + wrap)

            @pl.when(h == 0)
            def _():
                x_copy(t, i).wait_recv()

            for copy in x_fetch(t, i, lax.rem(i, 2)):
                copy.start()

        @pl.when((u >= 3) & (u < parts + 3))
        def _():
            final(before(3), before(2))

        forward_ag(before(4), 1)
        forward_ag(before(5), 2)
        forward_ag(before(6), 3)

        listed(u, DX_BEGINS, chunk_of(dx_begin))
        listed(u, DX_ENDS, chunk_of(dx_final))
        listed(u, DX_TIMES, chunk_of(dx_step))

        listed(u, THREES, tile_in_hand(stage_three))
        listed(u, TWOS, tile_in_hand(stage_two))
        listed(u, ONES, tile_in_hand(stage_one))
        listed(u, FOURS, tile_in_hand(stage_four))
        listed(u, FIVES, tile_in_hand(stage_five))
        listed(u, SIXES, tile_in_hand(stage_six))

        def first_fetch(p):
            tile_fetch(lax.div(p, HALVES), 0, 1 - c, True)

        listed(u, [time - 1 for time in ONES[::3]], first_fetch)

        for p, times in W_STRIPS.items():
            def send_strip(r, p=p):
                for to in others:
                    w_z_strip(p, to, r).start()

                @pl.when(r == 0)
                def _():
                    w_own(p).start()

            listed(u, times, send_strip)

        for p, times in W_ACROSS.items():
            for q, time in enumerate(times):
                @pl.when(u == time)
                def _(p=p, q=q):
                    w_z_in(p, others[q]).wait_recv()
                    w_x(p, others[q]).start()

        for p, times in W_CORES.items():
            for q, time in enumerate(times):
                @pl.when(u == time)
                def _(p=p, q=q):
                    w_x_in(p, others[q]).wait_recv()
                    w_c(p, others[q]).start()

        @pl.when(u == parts + 3)
        def _():
            for p in range(PHASES):
                t, h = p // HALVES, p % HALVES
                for s in range(2):
                    for what in range(2):
                        sums[0, pl.ds(4 * what + 2 * s + t, 1), h * hw : (h + 1) * hw] = jnp.sum(
                            stat[p, 2 * what + s], axis=0, keepdims=True
                        )
            sum_copy(0, across_c).start()

        @pl.when(u == parts + 4)
        def _():
            sum_copy(0, across_c).wait()
            sums[1] = sums[0] + sums_land[0]
            sum_copy(1, across_x).start()

        @pl.when(u == parts + 5)
        def _():
            sum_copy(1, across_x).wait()
            both = sums[1] + sums_land[1]
            sums[2] = both
            member = (
                lax.broadcasted_iota(jnp.int32, (width, lane), 0) % FLAG_GROUPS
                == lax.broadcasted_iota(jnp.int32, (width, lane), 1) % FLAG_GROUPS
            ).astype(F32)
            bias_rows = both[0:4]
            inner = both[0:2] * both[2:4]
            stack = jnp.concatenate([inner, bias_rows * bias_rows, inner], axis=0)
            prods[0] = jnp.dot(
                stack, member, precision=lax.Precision.HIGHEST, preferred_element_type=F32
            )
            prod_y().start()

        @pl.when(u == parts + 6)
        def _():
            prod_y().wait()
            prods[1] = prods[0] + prods_land[ZED]
            for to in others:
                prod_z(to).start()

        @pl.when(u == parts + 7)
        def _():
            for frm in others:
                prod_z_in(frm).wait_recv()
            prods_land[z] = prods[1]
            whole = prods_land[0] + prods_land[1] + prods_land[2] + prods_land[3]
            both = sums[2]
            group = lax.broadcasted_iota(jnp.int32, (1, lane), 1) % FLAG_GROUPS

            def over(row):
                return jnp.concatenate([row] * (width // lane), axis=1)

            def flag_row(s, t):
                row = jnp.zeros((1, lane), F32)
                for g in range(FLAG_GROUPS):
                    row = jnp.where(group == g, flags[s, t, g].astype(F32), row)
                return row

            for t in range(2):
                task0, task1 = both[t : t + 1], both[2 + t : 3 + t]
                dots = whole[t : t + 1]
                coef0 = over(flag_row(0, t) * dots / (whole[4 + t : 5 + t] + 1e-06))
                coef1 = over(flag_row(1, t) * dots / (whole[2 + t : 3 + t] + 1e-06))
                gbias[t : t + 1] = (task0 - coef0 * task1) + (task1 - coef1 * task0)
            for s in range(2):
                gstitch[s] = both[4 + 2 * s : 6 + 2 * s]

        return carry

    lax.fori_loop(0, max(SIXES + DX_ENDS) + 1, body, 0)

    last = 3 * PHASES - 1

    for g in (last - 2, last - 1, last):
        for to in others:
            z_copy(tile_of(g), to).wait_send()
        ax_own(tile_of(g)).wait_send()
    for i in range(n_chunk - HELD, n_chunk):
        dx_copy(1, i, (n_chunk + i) % HELD).wait_send()
    for i in (n_part - 2, n_part - 1):
        mixed_out(1, i, i % 2).wait()
    dx_out(1, n_chunk - 1).wait()

    def drain_tiles(g, carry):
        at = tile_of(g)
        for b in others:
            ax_copy(at, b).wait_send()
        for b in range(ZED):
            ac_copy(at, b).wait_send()
        return carry

    lax.fori_loop(0, last + 1, drain_tiles, 0)

    def drain_x(i, carry):
        x_copy(0, i).wait_send()
        x_copy(1, i).wait_send()
        return carry

    lax.fori_loop(0, n_chunk, drain_x, 0)

    def drain_w(p, carry):
        for to in others:
            w_z(p, to).wait_send()
            w_x(p, to).wait_send()
            w_c(p, to).wait_send()
        return carry

    lax.fori_loop(0, PHASES, drain_w, 0)
    for to in others:
        prod_z(to).wait_send()


def fused_call(feat, wts, cot, bias, stitch, counts, mask, flags):
    rows, deep, width = feat.shape[1], feat.shape[2], wts.shape[2]
    chunk = rows // 6
    part = chunk // SUB
    hw, kz, tile = width // 2, 2 * deep, deep // 3
    cat, xw = 4 * hw, width // 4
    lane = min(128, width)
    dma = pltpu.SemaphoreType.DMA
    anywhere = pl.BlockSpec(memory_space=pl.ANY)
    inside = pl.BlockSpec(memory_space=pltpu.VMEM)
    scalars = pl.BlockSpec(memory_space=pltpu.SMEM)

    def v(shape, kind=BF16):
        return pltpu.VMEM(shape, kind)

    out_shape = [
        jax.ShapeDtypeStruct((2, rows, width), BF16),
        jax.ShapeDtypeStruct((2, rows, deep), BF16),
        jax.ShapeDtypeStruct((2, ZED, kz, width), BF16),
        jax.ShapeDtypeStruct((2, width), F32),
        jax.ShapeDtypeStruct((2, 2, width), F32),
        jax.ShapeDtypeStruct((2, rows, deep), BF16),
        jax.ShapeDtypeStruct((2, rows, deep), BF16),
    ]
    scratch = [
        v((PHASES, kz, cat)),
        v((PHASES, rows, cat)),
        v((RING, 5, part, hw)),
        v((2, rows, hw), F32),
        v((2, chunk, kz)),
        v((PRODUCTS, ZED, part, hw), F32),
        v((2, 2, part, hw)),
        v((2, 2, part, hw)),
        v((HELD, chunk, deep), F32),
        v((HELD, chunk, deep)),
        v((chunk, deep)),
        v((chunk, deep)),
        v((rows, tile)),
        v((tile, rows)),
        v((tile, cat)),
        v((2, tile, cat)),
        v((3, ZED, tile, xw)),
        v((4, ZED, tile, xw)),
        v((3, ZED, tile, xw), F32),
        v((3, ZED, tile, xw)),
        v((rows, lane), F32),
        v((PHASES, 4, 8, hw), F32),
        v((3, 8, width), F32),
        v((2, 8, width), F32),
        v((2, 8, lane), F32),
        v((5, 8, lane), F32),
        dma((RING, 2)), dma((RING, 2)), dma((RING, 8)), dma((RING, 4)),
        dma((12,)), dma((12,)),
        dma((4, 4)), dma((4, 4)), dma((4, 4)), dma((4, 4)), dma((4, 4)), dma((4, 4)), dma((4,)),
        dma((2, 2)), dma((2,)), dma((2,)), dma((HELD,)), dma((12,)), dma((1,)), dma((1,)),
        dma((1,)), dma((1,)), dma((2,)), dma((3, 4)), dma((4, 4)), dma((3, 4)), dma((12, 4)),
        dma((3,)), dma((3,)),
        dma((12, 4)), dma((12, 4)), dma((12, 4)), dma((12, 4)), dma((8,)), dma((8,)),
    ]
    flops = 3 * 2 * 2 * rows * kz * cat * 2
    return pl.pallas_call(
        functools.partial(fused_kernel, rows, deep, width, chunk),
        out_shape=out_shape,
        in_specs=[anywhere] * 3 + [inside] * 4 + [scalars],
        out_specs=[anywhere] * 3 + [inside] * 2 + [anywhere] * 2,
        scratch_shapes=scratch,
        compiler_params=pltpu.CompilerParams(
            collective_id=0, has_side_effects=True, vmem_limit_bytes=64 * 1024 * 1024
        ),
        cost_estimate=pl.CostEstimate(
            flops=flops, bytes_accessed=200_000_000, transcendentals=2 * rows * width * 2
        ),
        name="cross_stitch_step",
    )(feat, wts, cot, bias, stitch, counts, mask, flags)


def finish_kernel(
    block, low, mixed, gfeat, gbias, gstitch,
    out, mixed_out, gfeat_out, gbias_out, gstitch_out,
    taken, given, held_mixed, held_gfeat, in_sem, out_sem, pass_sem,
):
    n_block = low.shape[0] // block
    fetched = (
        pltpu.make_async_copy(mixed, held_mixed, pass_sem.at[0]),
        pltpu.make_async_copy(gfeat, held_gfeat, pass_sem.at[1]),
    )
    passed = (
        pltpu.make_async_copy(held_mixed, mixed_out, pass_sem.at[2]),
        pltpu.make_async_copy(held_gfeat, gfeat_out, pass_sem.at[3]),
    )

    def take(i):
        return pltpu.make_async_copy(
            low.at[pl.ds(i * block, block)], taken.at[i % WIDEN_SLOTS], in_sem.at[i % WIDEN_SLOTS]
        )

    def give(i):
        return pltpu.make_async_copy(
            given.at[i % WIDEN_SLOTS], out.at[pl.ds(i * block, block)], out_sem.at[i % WIDEN_SLOTS]
        )

    for i in range(min(WIDEN_SLOTS, n_block)):
        take(i).start()
    for copy in fetched:
        copy.start()
    gbias_out[...] = gbias[...]
    gstitch_out[...] = gstitch[...]
    for i in range(n_block):
        slot = i % WIDEN_SLOTS
        take(i).wait()
        if i >= WIDEN_SLOTS:
            give(i - WIDEN_SLOTS).wait()
        given[slot] = wide(taken[slot])
        give(i).start()
        if i + WIDEN_SLOTS < n_block:
            take(i + WIDEN_SLOTS).start()
        if i == 2:
            for arrived, copy in zip(fetched, passed):
                arrived.wait()
                copy.start()
    for i in range(max(0, n_block - WIDEN_SLOTS), n_block):
        give(i).wait()
    for copy in passed:
        copy.wait()


def finish(low, mixed, gfeat, gbias, gstitch):
    tall, width = low.shape
    block = tall // WIDEN_BLOCKS
    anywhere = pl.BlockSpec(memory_space=pl.ANY)
    inside = pl.BlockSpec(memory_space=pltpu.VMEM)
    moved = sum(a.size * a.dtype.itemsize for a in (mixed, gfeat))
    return pl.pallas_call(
        functools.partial(finish_kernel, block),
        in_specs=[anywhere] * 3 + [inside] * 2,
        out_specs=[anywhere] * 3 + [inside] * 2,
        out_shape=[
            jax.ShapeDtypeStruct(a.shape, kind)
            for a, kind in ((low, F32), (mixed, BF16), (gfeat, BF16), (gbias, F32), (gstitch, F32))
        ],
        scratch_shapes=[
            pltpu.VMEM((WIDEN_SLOTS, block, width), BF16),
            pltpu.VMEM((WIDEN_SLOTS, block, width), F32),
            pltpu.VMEM(mixed.shape, BF16),
            pltpu.VMEM(gfeat.shape, BF16),
            pltpu.SemaphoreType.DMA((WIDEN_SLOTS,)),
            pltpu.SemaphoreType.DMA((WIDEN_SLOTS,)),
            pltpu.SemaphoreType.DMA((4,)),
        ],
        compiler_params=pltpu.CompilerParams(vmem_limit_bytes=60 * 1024 * 1024),
        cost_estimate=pl.CostEstimate(
            flops=tall * width, bytes_accessed=6 * tall * width + 2 * moved, transcendentals=0
        ),
        name="finish",
    )(low, mixed, gfeat, gbias, gstitch)


def fused_plan(mesh):
    def per_device(features, weights, bias, stitch, cotangent, crop_counts, row_mask, flags):
        rows, deep = features.shape[1:]
        width = weights.shape[2]
        mixed, gfeat, gwt, gbias, gstitch, _, _ = fused_call(
            features, weights, cotangent, bias, stitch,
            crop_counts.reshape(1, -1), row_mask.reshape(-1, min(128, rows // 6)), flags,
        )
        grad_weights, mixed, gfeat, gbias, gstitch = finish(
            gwt.reshape(-1, width), mixed, gfeat, gbias, gstitch
        )
        return mixed, gfeat, grad_weights.reshape(2, ZED * 2 * deep, width), gbias, gstitch

    return per_device


def plan_for(mesh):
    if mesh.shape["batch"] == 4 and mesh.shape["mp"] == 2 * ZED:
        return fused_plan(mesh)
    return generic_plan(mesh)


def solution(mesh):
    in_specs = (
        P(None, "batch", "mp"),
        P(None, None, "mp"),
        P(None, "mp"),
        P(None, None, "mp"),
        P(None, "batch", "mp"),
        P("batch"),
        P("batch"),
        P(),
    )
    out_specs = (
        P(None, "batch", "mp"),
        P(None, "batch", "mp"),
        P(None, None, "mp"),
        P(None, "mp"),
        P(None, None, "mp"),
    )
    return jax.shard_map(
        plan_for(mesh), mesh=mesh, in_specs=in_specs, out_specs=out_specs, check_vma=False
    )
```

```python
import collections
import functools

import jax
import jax.numpy as jnp
from jax import lax
from jax.experimental import pallas as pl
from jax.experimental.pallas import tpu as pltpu
from jax.sharding import PartitionSpec as P

FLAG_GROUPS = 8
OUTER = 4


def row_weights(counts, mask):
    ends = jnp.cumsum(counts)
    starts = ends - counts
    index = lax.broadcasted_iota(jnp.int32, (mask.shape[0], counts.shape[0]), 0)
    inside = (index >= starts[None, :]) & (index < ends[None, :])
    count_row = jnp.sum(jnp.where(inside, counts[None, :], 0), axis=1)
    live = (count_row > 0) & (mask == 1)
    return jnp.where(live, 1.0 / jnp.maximum(count_row, 1).astype(jnp.float32), 0.0)


def project_bias(task_bias, flags):
    local_width = task_bias.shape[2]
    channel = lax.axis_index("mp") * local_width + lax.broadcasted_iota(
        jnp.int32, (local_width, FLAG_GROUPS), 0
    )
    member = (
        channel % FLAG_GROUPS == lax.broadcasted_iota(jnp.int32, (local_width, FLAG_GROUPS), 1)
    ).astype(jnp.float32)
    dots = jnp.dot(task_bias[0] * task_bias[1], member, precision=lax.Precision.HIGHEST)
    norms = jnp.einsum(
        "stc,cg->stg", task_bias * task_bias, member, precision=lax.Precision.HIGHEST
    )
    dots, norms = lax.psum((dots, norms), "mp")
    flag = flags.astype(jnp.float32)
    coef_first = jnp.dot(
        flag[0] * dots / (norms[1] + 1e-06), member.T, precision=lax.Precision.HIGHEST
    )
    coef_second = jnp.dot(
        flag[1] * dots / (norms[0] + 1e-06), member.T, precision=lax.Precision.HIGHEST
    )
    first = task_bias[0] - coef_first * task_bias[1]
    second = task_bias[1] - coef_second * task_bias[0]
    return first + second


def generic_plan(mesh):
    n_mp = mesh.shape["mp"]
    n_batch = mesh.shape["batch"]
    inner = n_mp // OUTER
    inner_groups = [[o * inner + i for i in range(inner)] for o in range(OUTER)]
    outer_groups = [[o * inner + i for o in range(OUTER)] for i in range(inner)]

    def per_device(features, weights, bias, stitch, cotangent, crop_counts, row_mask, flags):
        rows = features.shape[1]
        width = weights.shape[2]
        depth = features.shape[2] * inner
        held = lax.all_gather(
            features, "mp", axis=2, tiled=True, axis_index_groups=inner_groups
        )
        split = weights.reshape(2, OUTER, depth, width)
        block = lax.all_to_all(
            split, "mp", split_axis=1, concat_axis=1, axis_index_groups=outer_groups
        )
        block = block.reshape(2, OUTER, depth, width)
        part = jnp.einsum("trk,tokc->otrc", held, block, preferred_element_type=jnp.float32)
        linear = lax.psum_scatter(
            part.astype(jnp.bfloat16),
            "mp",
            scatter_dimension=0,
            axis_index_groups=outer_groups,
        ).astype(jnp.float32)
        pre = linear + bias[:, None, :]
        hidden, gelu_back = jax.vjp(lambda v: jax.nn.gelu(v, approximate=False), pre)
        mixed = stitch[:, 0, None, :] * hidden[0][None] + stitch[:, 1, None, :] * hidden[1][None]
        scale_rows = row_weights(crop_counts, row_mask)
        grad_out = cotangent.astype(jnp.float32) * scale_rows[None, :, None]
        first_task = gelu_back(stitch[0][:, None, :] * grad_out[0][None])[0]
        second_task = gelu_back(stitch[1][:, None, :] * grad_out[1][None])[0]
        task_bias = jnp.stack([jnp.sum(first_task, axis=1), jnp.sum(second_task, axis=1)])
        grad_linear = (first_task + second_task).astype(jnp.bfloat16)
        grad_stitch = jnp.sum(grad_out[:, None] * hidden[None], axis=2)
        every = lax.all_gather(grad_linear, "mp", axis_index_groups=outer_groups)
        grad_part = jnp.einsum(
            "otrc,tokc->trk", every, block, preferred_element_type=jnp.float32
        )
        grad_part = grad_part.astype(jnp.bfloat16).reshape(2, rows, inner, depth // inner)
        grad_features = lax.psum_scatter(
            grad_part.transpose(2, 0, 1, 3),
            "mp",
            scatter_dimension=0,
            axis_index_groups=inner_groups,
        )
        weight_part = jnp.einsum(
            "trk,otrc->otkc", held, every, preferred_element_type=jnp.float32
        )
        weight_part = weight_part.astype(jnp.bfloat16).reshape(
            OUTER, 2, n_batch, depth // n_batch, width
        )
        share = lax.psum_scatter(
            weight_part.transpose(2, 0, 1, 3, 4), "batch", scatter_dimension=0
        )
        share = lax.all_to_all(
            share, "mp", split_axis=0, concat_axis=0, axis_index_groups=outer_groups
        )
        share = share.reshape(OUTER, 2, depth // n_batch, width)
        whole = lax.all_gather(share, "batch")
        grad_weights = whole.transpose(2, 1, 0, 3, 4).reshape(2, OUTER * depth, width)
        task_bias, grad_stitch = lax.psum((task_bias, grad_stitch), "batch")
        grad_bias = project_bias(task_bias, flags)
        return (
            mixed.astype(jnp.bfloat16),
            grad_features.astype(jnp.bfloat16),
            grad_weights.astype(jnp.float32),
            grad_bias,
            grad_stitch,
        )

    return per_device


MESH = pl.DeviceIdType.MESH
BF16 = jnp.bfloat16
F32 = jnp.float32
ZED = 4
HALVES = 2
PHASES = 4
RING = 8
BAND = 32
SUB = 2
PRODUCTS = 6
HELD = 4
WIDEN_SLOTS = 4

DX_TIMES = (20, 21, 23, 25, 27, 29, 43, 45, 48, 50, 58, 64)
DX_BEGINS = (22, 24, 26, 28, 30, 34, 44, 48, 57, 60, 68, 76)
DX_ENDS = (23, 25, 27, 29, 31, 43, 45, 50, 59, 62, 71, 81)
ONES = (19, 23, 26, 30, 33, 40, 43, 45, 46, 54, 56, 57)
TWOS = (22, 26, 27, 32, 36, 42, 44, 46, 49, 55, 57, 61)
THREES = (23, 28, 33, 35, 42, 43, 45, 52, 55, 58, 59, 70)
FOURS = (25, 30, 35, 37, 44, 47, 50, 54, 60, 67, 68, 73)
FIVES = (33, 36, 44, 45, 51, 59, 62, 67, 74, 76, 82, 85)
SIXES = (35, 43, 47, 57, 64, 70, 75, 82, 84, 86, 87, 90)
W_STRIPS = {2: (5, 7, 8, 11, 12, 13), 3: (21, 22, 23, 24, 26, 27)}
W_ACROSS = {1: (0, 0, 2), 2: (16, 21, 22), 3: (29, 29, 34)}
W_CORES = {1: (1, 6, 7), 2: (21, 23, 23), 3: (33, 33, 35)}


Part = collections.namedtuple("Part", ("u", "p", "i", "t", "h", "slot", "prod", "buf"))
Tile = collections.namedtuple("Tile", ("g", "p", "t", "h", "j", "buf", "trio", "quad"))


def half(value):
    return value.astype(BF16)


def wide(value):
    return value.astype(F32)


def fused_kernel(
    rows, deep, width, chunk,
    feat, wts, cot, bias, stitch, counts, mask, flags,
    mixed, gfeat, gwt, gbias, gstitch, xn, dxn,
    wv, gl, rs, h0, xc, pf, cc, mx, own, dsend, dfetch, dout,
    xsrc, xt, cstage, cland, xstage, xland, kept, zstage,
    scale, stat, sums, sums_land, prods, prods_land,
    rs_send, rs_recv, ag_send, ag_recv, xs_send, xs_recv,
    wz_send, wz_recv, wx_send, wx_recv, wc_send, wc_recv, wl,
    xf, cf, mxs, dx_send, dx_recv, df, dod,
    tile_in, c_send, c_recv, x_send, x_recv, z_send, z_recv, zl, zx_send,
    ax_send, ax_recv, ac_send, ac_recv, t_send, t_recv,
):
    batch, mp = lax.axis_index("batch"), lax.axis_index("mp")
    z, y = mp // 2, mp % 2
    x, c = batch // 2, batch % 2
    up = {"mp": mp + 2}
    down = {"mp": mp - 2}
    across_y = {"mp": 2 * z + 1 - y}
    across_x = {"batch": 2 * (1 - x) + c}
    across_c = {"batch": 2 * x + 1 - c}

    def at_z(other):
        return {"mp": 2 * other + y}

    others = (3 - z, (z + 2) % 4, z + 1 - 2 * (z % 2))

    n_chunk = rows // chunk
    total = PHASES * n_chunk
    part = chunk // SUB
    n_part = rows // part
    parts = PHASES * n_part
    images = counts.shape[1]
    hw = width // HALVES
    kz = 2 * deep
    quarter = deep // 2
    tile = deep // 3
    strip = quarter // 6
    xw = hw // 2

    def mult(value, unit):
        return pl.multiple_of(value, unit)

    def remote(src, dst, send, recv, device):
        return pltpu.make_async_remote_copy(
            src_ref=src, dst_ref=dst, send_sem=send, recv_sem=recv,
            device_id=device, device_id_type=MESH,
        )

    def cols(b):
        return pl.ds(mult(b * hw, hw), hw)

    def chunk_rows(i):
        return pl.ds(mult(i * chunk, chunk), chunk)

    def part_rows(i):
        return pl.ds(mult(i * part, part), part)

    def tower(p):
        t = jnp.where(p >= HALVES, 1, 0)
        return t, p - HALVES * t

    def x_copy(t, i):
        e = t * n_chunk + i
        return remote(
            feat.at[t, chunk_rows(i)], xn.at[t, chunk_rows(i)],
            xs_send.at[e], xs_recv.at[e], across_y,
        )

    def x_fetch(t, i, buf):
        return (
            pltpu.make_async_copy(
                feat.at[t, chunk_rows(i)],
                xc.at[buf, :, pl.ds(mult(deep * y, deep), deep)], xf.at[buf, 0],
            ),
            pltpu.make_async_copy(
                xn.at[t, chunk_rows(i)],
                xc.at[buf, :, pl.ds(mult(deep * (1 - y), deep), deep)], xf.at[buf, 1],
            ),
        )

    def cot_fetch(h, i, buf):
        return pltpu.make_async_copy(
            cot.at[:, part_rows(i), cols(h)], cc.at[buf], cf.at[buf]
        )

    def w_own(p):
        t, h = tower(p)
        return pltpu.make_async_copy(
            wts.at[t, pl.ds(mult(kz * z, kz), kz), cols(h)], wv.at[p, :, cols(z)], wl.at[p],
        )

    def w_rows():
        return pl.ds(mult(deep * c + quarter * x, quarter), quarter)

    def w_z(p, to):
        t, h = tower(p)
        return remote(
            wts.at[
                t, pl.ds(mult(kz * to + deep * c + quarter * x, quarter), quarter), cols(h)
            ],
            wv.at[p, w_rows(), cols(z)],
            wz_send.at[p, to], wz_recv.at[p, z], at_z(to),
        )

    def w_z_strip(p, to, r):
        t, h = tower(p)
        at = deep * c + quarter * x + strip * r
        return remote(
            wts.at[t, pl.ds(mult(kz * to + at, strip), strip), cols(h)],
            wv.at[p, pl.ds(mult(at, strip), strip), cols(z)],
            wz_send.at[p, to], wz_recv.at[p, z], at_z(to),
        )

    def w_z_in(p, frm):
        here = wv.at[p, w_rows(), cols(frm)]
        return remote(here, here, wz_send.at[p, frm], wz_recv.at[p, frm], at_z(frm))

    def w_x(p, b):
        here = wv.at[p, w_rows(), cols(b)]
        return remote(here, here, wx_send.at[p, b], wx_recv.at[p, b], across_x)

    def w_x_in(p, b):
        here = wv.at[
            p, pl.ds(mult(deep * c + quarter * (1 - x), quarter), quarter), cols(b)
        ]
        return remote(here, here, wx_send.at[p, b], wx_recv.at[p, b], across_x)

    def w_c(p, b):
        here = wv.at[p, pl.ds(mult(deep * c, deep), deep), cols(b)]
        return remote(here, here, wc_send.at[p, b], wc_recv.at[p, b], across_c)

    def w_c_in(p, b):
        here = wv.at[p, pl.ds(mult(deep * (1 - c), deep), deep), cols(b)]
        return remote(here, here, wc_send.at[p, b], wc_recv.at[p, b], across_c)

    def rs_up(slot, zz):
        run = rs.at[slot, zz + 2 : ZED + 1]
        return remote(run, run, rs_send.at[slot, 0], rs_recv.at[slot, 0], up)

    def rs_down(slot, zz):
        run = rs.at[slot, 0:zz]
        return remote(run, run, rs_send.at[slot, 1], rs_recv.at[slot, 1], down)

    def rs_from_below(slot, zz):
        run = rs.at[slot, zz + 1 : ZED + 1]
        return remote(run, run, rs_send.at[slot, 0], rs_recv.at[slot, 0], down)

    def rs_from_above(slot, zz):
        run = rs.at[slot, 0 : zz + 1]
        return remote(run, run, rs_send.at[slot, 1], rs_recv.at[slot, 1], up)

    def at_place(first, last, do):
        for zz in range(first, last + 1):
            @pl.when(z == zz)
            def _(zz=zz):
                do(zz)

    def ag(at, b, going, device):
        here = gl.at[at.p, b, part_rows(at.i)]
        return remote(
            here, here, ag_send.at[at.slot, going * ZED + b], ag_recv.at[at.slot, b], device
        )

    def dx_copy(t, i, buf):
        return remote(
            dsend.at[buf], dxn.at[t, chunk_rows(i)],
            dx_send.at[buf], dx_recv.at[t * n_chunk + i], across_y,
        )

    def dx_fetch(t, i):
        return pltpu.make_async_copy(dxn.at[t, chunk_rows(i)], dfetch, df.at[0])

    def dx_out(t, i):
        return pltpu.make_async_copy(dout, gfeat.at[t, chunk_rows(i)], dod.at[0])

    def mixed_out(h, i, buf):
        return pltpu.make_async_copy(
            mx.at[buf], mixed.at[:, part_rows(i), cols(h)], mxs.at[buf]
        )

    def tile_fetch(t, j, hk, start):
        lanes = pl.ds(mult(tile * j, tile), tile)
        near = pltpu.make_async_copy(feat.at[t, :, lanes], xsrc, tile_in.at[0])
        if not start:
            near.wait()
            return

        @pl.when(hk == y)
        def _():
            near.start()

        @pl.when(hk != y)
        def _():
            pltpu.make_async_copy(xn.at[t, :, lanes], xsrc, tile_in.at[0]).start()

    def core_copy(g):
        return remote(cstage, cland.at[g.buf], c_send.at[0], c_recv.at[g.buf], across_c)

    def across_copy(g, b):
        return remote(
            xstage.at[g.trio, b], xland.at[g.quad, b],
            x_send.at[g.trio, b], x_recv.at[g.quad, b], across_x,
        )

    def piece(g, source, core, side):
        return gwt.at[g.p, source, core, g.j, side]

    def z_copy(g, to):
        return remote(
            zstage.at[g.trio, to], piece(g, z, c, x),
            z_send.at[g.trio, to], z_recv.at[g.g, z], at_z(to),
        )

    def z_in(g, frm):
        here = piece(g, frm, c, x)
        return remote(here, here, z_send.at[g.trio, frm], z_recv.at[g.g, frm], at_z(frm))

    def z_own(g):
        return pltpu.make_async_copy(
            zstage.at[g.trio, z], piece(g, z, c, x), zl.at[g.trio]
        )

    def ax_own(g):
        return remote(
            zstage.at[g.trio, z], piece(g, z, c, x),
            zx_send.at[g.trio], ax_recv.at[g.g, z], across_x,
        )

    def ax_copy(g, b):
        here = piece(g, b, c, x)
        return remote(here, here, ax_send.at[g.g, b], ax_recv.at[g.g, b], across_x)

    def ax_in(g, b):
        here = piece(g, b, c, 1 - x)
        return remote(here, here, ax_send.at[g.g, b], ax_recv.at[g.g, b], across_x)

    def ac_copy(g, b):
        here = gwt.at[g.p, b, c, g.j]
        return remote(here, here, ac_send.at[g.g, b], ac_recv.at[g.g, b], across_c)

    def ac_in(g, b):
        here = gwt.at[g.p, b, 1 - c, g.j]
        return remote(here, here, ac_send.at[g.g, b], ac_recv.at[g.g, b], across_c)

    def sum_copy(stage, device):
        return remote(
            sums.at[stage], sums_land.at[stage], t_send.at[stage], t_recv.at[stage], device
        )

    def prod_y():
        return remote(prods.at[0], prods_land.at[ZED], t_send.at[2], t_recv.at[2], across_y)

    def prod_z(to):
        return remote(
            prods.at[1], prods_land.at[z], t_send.at[3 + to], t_recv.at[3 + z], at_z(to)
        )

    def prod_z_in(frm):
        here = prods_land.at[frm]
        return remote(here, here, t_send.at[3 + frm], t_recv.at[3 + frm], at_z(frm))

    barrier = pltpu.get_barrier_semaphore()
    for device in [at_z(o) for o in others] + [across_y, across_x, across_c]:
        pl.semaphore_signal(barrier, inc=1, device_id=device, device_id_type=MESH)
    pl.semaphore_wait(barrier, 6)

    for to in others:
        w_z(0, to).start()
    x_copy(0, 0).start()
    x_copy(0, 1).start()
    w_own(0).start()
    cot_fetch(0, 0, 0).start()

    image_row = lax.broadcasted_iota(jnp.int32, (images, images), 0)
    image_col = lax.broadcasted_iota(jnp.int32, (images, images), 1)
    crops = counts[...].astype(F32)
    ends = jnp.dot(
        jnp.broadcast_to(crops, (8, images)), (image_row <= image_col).astype(F32),
        precision=lax.Precision.HIGHEST, preferred_element_type=F32,
    )[0:1]
    starts = ends - crops
    block = mask.shape[1]
    lane = scale.shape[1]

    for r in range(rows // block):
        index = (
            lax.broadcasted_iota(jnp.int32, (block, images), 0) + r * block
        ).astype(F32)
        inside = (index >= starts) & (index < ends)
        count_row = jnp.sum(jnp.where(inside, crops, 0.0), axis=1, keepdims=True)
        diagonal = lax.broadcasted_iota(jnp.int32, (block, block), 0) == (
            lax.broadcasted_iota(jnp.int32, (block, block), 1)
        )
        usable = jnp.sum(
            jnp.where(diagonal, mask[r : r + 1, :].astype(F32), 0.0),
            axis=1, keepdims=True,
        )
        live = (count_row > 0.0) & (usable == 1.0)
        share = jnp.where(live, 1.0 / jnp.maximum(count_row, 1.0), 0.0)
        scale[r * block : (r + 1) * block, :] = jnp.broadcast_to(share, (block, lane))

    for frm in others:
        w_z_in(0, frm).wait_recv()
        w_x(0, frm).start()
    for to in others:
        w_z(1, to).start()
    w_own(1).start()
    for frm in others:
        w_x_in(0, frm).wait_recv()
        w_c(0, frm).start()
    x_copy(0, 0).wait_recv()
    for copy in x_fetch(0, 0, 0):
        copy.start()

    def final(at, later):
        p, i, slot, t, h, buf = at.p, at.i, at.slot, at.t, at.h, at.buf
        cot_fetch(h, i, buf).wait()

        @pl.when(at.u >= 2 * n_part + 2)
        def _():
            mixed_out(h, i, buf).wait()

        @pl.when(i == 0)
        def _():
            stat[p] = jnp.zeros(stat.shape[1:], F32)

        lanes = cols(h)
        shift = bias[pl.ds(t, 1), lanes]
        st = [stitch[s, pl.ds(t, 1), lanes] for s in range(2)]
        band = min(BAND, part)

        def step(r, carry):
            here = part_rows_of(r, band)
            there = pl.ds(mult(i * part + r * band, band), band)
            value = pf[at.prod, z, here, :]
            below = wide(rs[slot, z + 1, here, :])
            above = wide(rs[slot, z, here, :])
            value = value + jnp.where(z > 0, below, 0.0) + jnp.where(z < ZED - 1, above, 0.0)
            pre = value + shift
            phi = 0.5 * (1.0 + lax.erf(pre * 0.7071067811865476))
            hidden = pre * phi
            slope = phi + pre * (jnp.exp(-0.5 * pre * pre) * 0.3989422804014327)
            weight = scale[there, 0:1]
            first = wide(cc[buf, 0, here, :]) * weight
            second = wide(cc[buf, 1, here, :]) * weight
            back0 = st[0] * first * slope
            back1 = st[1] * second * slope
            gl[p, z, there, :] = half(back0 + back1)

            def fold(v):
                return jnp.sum(v.reshape(band // 8, 8, hw), axis=0)

            stat[p, 0] += fold(back0)
            stat[p, 1] += fold(back1)
            stat[p, 2] += fold(first * hidden)
            stat[p, 3] += fold(second * hidden)

            @pl.when(t == 0)
            def _():
                h0[h, there, :] = hidden

            @pl.when(t == 1)
            def _():
                before = h0[h, there, :]
                for s in range(2):
                    mx[buf, s, here, :] = half(
                        stitch[s, 0:1, lanes] * before + st[s] * hidden
                    )

            return carry

        lax.fori_loop(0, part // band, step, 0)

        @pl.when(z < ZED - 1)
        def _():
            ag(at, z, 0, up).start()

        @pl.when(z > 0)
        def _():
            ag(at, z, 1, down).start()

        @pl.when(t == 1)
        def _():
            mixed_out(h, i, buf).start()

        @pl.when(at.u + 1 < parts)
        def _():
            cot_fetch(later.h, later.i, later.buf).start()

    def part_rows_of(r, band):
        return pl.ds(mult(r * band, band), band)

    def forward_ag(at, far):
        @pl.when((at.u >= 0) & (at.u < parts))
        def _():
            @pl.when(z - far >= 0)
            def _():
                ag(at, z - far, 0, up).wait_recv()

                @pl.when(z < ZED - 1)
                def _():
                    ag(at, z - far, 0, up).start()

            @pl.when(z + far < ZED)
            def _():
                ag(at, z + far, 1, down).wait_recv()

                @pl.when(z > 0)
                def _():
                    ag(at, z + far, 1, down).start()

    def dx_step(t, i, buf):
        @pl.when((i >= HELD) | (t > 0))
        def _():
            dx_copy(t, i, buf).wait_send()

        def line_up(h):
            for b in range(ZED):
                xt[0:chunk, b * hw : (b + 1) * hw] = gl[2 * t + h, b, part_rows_of(i, chunk), :]

        def term(h, hk):
            return lax.dot_general(
                xt[0:chunk, 0 : ZED * hw],
                wv[2 * t + h, pl.ds(mult(deep * hk, deep), deep), :],
                (((1,), (1,)), ((), ())), preferred_element_type=F32,
            )

        line_up(0)
        far = term(0, 1 - y)
        own[buf] = term(0, y)
        line_up(1)
        dsend[buf] = half(far + term(1, 1 - y))
        dx_copy(t, i, buf).start()
        own[buf] += term(1, y)

    def dx_begin(t, i, buf):
        dx_copy(t, i, buf).wait_recv()
        dx_fetch(t, i).start()

    def dx_final(t, i, buf):
        @pl.when((i >= 1) | (t > 0))
        def _():
            dx_out(t, i).wait()

        dx_fetch(t, i).wait()

        def step(j, inner):
            lanes = pl.ds(mult(tile * j, tile), tile)
            dout[:, lanes] = half(own[buf, :, lanes] + wide(dfetch[:, lanes]))
            return inner

        lax.fori_loop(0, 3, step, 0)
        dx_out(t, i).start()

    def listed(u, times, do):
        e, hit = 0, False
        for index, time in enumerate(times):
            same = u == time
            e = jnp.where(same, index, e)
            hit = hit | same

        @pl.when(hit)
        def _():
            do(e)

    def chunk_of(do):
        def run(e):
            t = jnp.where(e >= n_chunk, 1, 0)
            do(t, e - n_chunk * t, lax.rem(e, HELD))

        return run

    def turn():
        lanes_at_once = min(128, tile)

        def step(q, carry):
            lanes = pl.ds(mult(q * lanes_at_once, lanes_at_once), lanes_at_once)
            xt[lanes, :] = xsrc[:, lanes].T
            return carry

        lax.fori_loop(0, tile // lanes_at_once, step, 0)

    def tile_dot(g, b):
        return jnp.dot(xt[...], gl[g.p, b], preferred_element_type=F32)

    def stage_one(g):
        tile_fetch(g.t, g.j, 1 - c, False)
        turn()
        tile_fetch(g.t, g.j, c, True)
        for b in range(ZED):
            cstage[:, b * hw : (b + 1) * hw] = half(tile_dot(g, b))
        core_copy(g).start()

    def stage_two(g):
        tile_fetch(g.t, g.j, c, False)
        turn()

        @pl.when(g.j < 2)
        def _():
            tile_fetch(g.t, g.j + 1, 1 - c, True)

        core_copy(g).wait()
        for b in range(ZED):
            block = tile_dot(g, b) + wide(cland[g.buf, :, b * hw : (b + 1) * hw])
            left, right = block[:, :xw], block[:, xw:]
            kept[g.trio, b] = jnp.where(x == 0, left, right)
            xstage[g.trio, b] = half(jnp.where(x == 0, right, left))

        def send(q, carry):
            across_copy(g, lax.rem(z + 3 + 3 * q, ZED)).start()
            return carry

        lax.fori_loop(0, ZED, send, 0)

    def stage_three(g):
        @pl.when(g.g >= 3)
        def _():
            for to in others:
                z_copy(g, to).wait_send()
            ax_own(g).wait_send()

        def add(b):
            across_copy(g, b).wait()
            zstage[g.trio, b] = half(kept[g.trio, b] + wide(xland[g.quad, b]))

        def step(q, carry):
            b = lax.rem(z + 3 + 3 * q, ZED)
            add(b)
            z_copy(g, b).start()
            return carry

        lax.fori_loop(0, ZED - 1, step, 0)
        add(z)
        z_own(g).start()
        ax_own(g).start()

    def stage_four(g):
        def step(q, carry):
            b = lax.rem(z + 1 + q, ZED)
            z_in(g, b).wait_recv()
            ax_copy(g, b).start()
            return carry

        lax.fori_loop(0, ZED - 1, step, 0)
        z_own(g).wait()

    def stage_five(g):
        def step(q, carry):
            b = lax.rem(z + q, ZED)
            ax_in(g, b).wait_recv()
            ac_copy(g, b).start()
            return carry

        lax.fori_loop(0, ZED, step, 0)

    def stage_six(g):
        def step(b, carry):
            ac_in(g, b).wait_recv()
            return carry

        lax.fori_loop(0, ZED, step, 0)

    def tile_of(g):
        p = lax.div(g, 3)
        t, h = tower(p)
        return Tile(
            g=g, p=p, t=t, h=h, j=g - 3 * p,
            buf=lax.rem(g, 2), trio=g - 3 * p, quad=lax.rem(g, 4),
        )

    def tile_in_hand(do):
        return lambda g: do(tile_of(g))

    def body(u, carry):
        p0 = lax.div(u, n_part)
        i0 = u - p0 * n_part
        slot0, prod0 = lax.rem(u, RING), lax.rem(u, PRODUCTS)
        buf0 = lax.rem(u, 2)

        def before(lag):
            if isinstance(lag, int):
                whole, left = divmod(lag, n_part)
            else:
                whole, left = 0, lag
            under = i0 < left
            p = p0 - whole - jnp.where(under, 1, 0)
            i = i0 - left + jnp.where(under, n_part, 0)
            in_ring = lag % RING if isinstance(lag, int) else lag
            in_prods = lag % PRODUCTS if isinstance(lag, int) else lag
            slot = slot0 - in_ring + jnp.where(slot0 < in_ring, RING, 0)
            prod = prod0 - in_prods + jnp.where(prod0 < in_prods, PRODUCTS, 0)
            t, h = tower(p)
            return Part(u=u - lag, p=p, i=i, t=t, h=h, slot=slot, prod=prod, buf=lax.rem(i, 2))

        @pl.when((u >= 5) & (u < parts + 5))
        def _():
            slot = before(5).slot
            at_place(0, ZED - 2, lambda zz: rs_up(slot, zz).wait_send())
            at_place(1, ZED - 1, lambda zz: rs_down(slot, zz).wait_send())

        @pl.when((u >= 8) & (u < parts + 8))
        def _():
            at = before(8)

            def step(b, inner):
                @pl.when((z < ZED - 1) & (b <= z))
                def _():
                    ag(at, b, 0, up).wait_send()

                @pl.when((z > 0) & (b >= z))
                def _():
                    ag(at, b, 1, down).wait_send()

                return inner

            lax.fori_loop(0, ZED, step, 0)

        ck = lax.div(i0, SUB)
        fresh = ck * SUB == i0
        t0, h0_ = tower(p0)
        xbuf = lax.rem(ck, 2)

        @pl.when((u < parts) & fresh)
        def _():
            @pl.when(i0 == 0)
            def _():
                w_own(p0).wait()
                for frm in others:
                    w_c_in(p0, frm).wait_recv()

            for copy in x_fetch(t0, ck, xbuf):
                copy.wait()

            product = jnp.dot(xc[xbuf], wv[p0], preferred_element_type=F32)
            for b in range(ZED):
                for s in range(SUB):
                    pf[prod0 + s, b] = product[
                        s * part : (s + 1) * part, b * hw : (b + 1) * hw
                    ]

        going_up = before(z)

        @pl.when((going_up.u >= 0) & (going_up.u < parts))
        def _():
            slot, prod = going_up.slot, going_up.prod
            at_place(1, ZED - 1, lambda zz: rs_from_below(slot, zz).wait_recv())

            @pl.when(z == 0)
            def _():
                for b in range(1, ZED):
                    rs[slot, b + 1] = half(pf[prod, b])

            @pl.when(z > 0)
            def _():
                def step(b, inner):
                    rs[slot, b + 1] = half(wide(rs[slot, b + 1]) + pf[prod, b])
                    return inner

                lax.fori_loop(z + 1, ZED, step, 0)

            at_place(0, ZED - 2, lambda zz: rs_up(slot, zz).start())

        going_down = before(ZED - 1 - z)

        @pl.when((going_down.u >= 0) & (going_down.u < parts))
        def _():
            slot, prod = going_down.slot, going_down.prod
            at_place(0, ZED - 2, lambda zz: rs_from_above(slot, zz).wait_recv())

            @pl.when(z == ZED - 1)
            def _():
                for b in range(ZED - 1):
                    rs[slot, b] = half(pf[prod, b])

            @pl.when(z < ZED - 1)
            def _():
                def step(b, inner):
                    rs[slot, b] = half(wide(rs[slot, b]) + pf[prod, b])
                    return inner

                lax.fori_loop(0, z, step, 0)

            at_place(1, ZED - 1, lambda zz: rs_down(slot, zz).start())

        @pl.when(fresh & (u + 2 * SUB < 2 * n_part))
        def _():
            k = p0 * n_chunk + ck + 2
            over = jnp.where(k >= n_chunk, 1, 0)
            x_copy(over, k - over * n_chunk).start()

        @pl.when(fresh & (u + SUB < parts))
        def _():
            wrap = jnp.where(ck + 1 == n_chunk, 1, 0)
            i = ck + 1 - wrap * n_chunk
            t, h = tower(p0 + wrap)

            @pl.when(h == 0)
            def _():
                x_copy(t, i).wait_recv()

            for copy in x_fetch(t, i, lax.rem(i, 2)):
                copy.start()

        @pl.when((u >= 3) & (u < parts + 3))
        def _():
            final(before(3), before(2))

        forward_ag(before(4), 1)
        forward_ag(before(5), 2)
        forward_ag(before(6), 3)

        listed(u, DX_BEGINS, chunk_of(dx_begin))
        listed(u, DX_ENDS, chunk_of(dx_final))
        listed(u, DX_TIMES, chunk_of(dx_step))

        listed(u, THREES, tile_in_hand(stage_three))
        listed(u, TWOS, tile_in_hand(stage_two))
        listed(u, ONES, tile_in_hand(stage_one))
        listed(u, FOURS, tile_in_hand(stage_four))
        listed(u, FIVES, tile_in_hand(stage_five))
        listed(u, SIXES, tile_in_hand(stage_six))

        def first_fetch(p):
            tile_fetch(lax.div(p, HALVES), 0, 1 - c, True)

        listed(u, [time - 1 for time in ONES[::3]], first_fetch)

        for p, times in W_STRIPS.items():
            def send_strip(r, p=p):
                for to in others:
                    w_z_strip(p, to, r).start()

                @pl.when(r == 0)
                def _():
                    w_own(p).start()

            listed(u, times, send_strip)

        for p, times in W_ACROSS.items():
            for q, time in enumerate(times):
                @pl.when(u == time)
                def _(p=p, q=q):
                    w_z_in(p, others[q]).wait_recv()
                    w_x(p, others[q]).start()

        for p, times in W_CORES.items():
            for q, time in enumerate(times):
                @pl.when(u == time)
                def _(p=p, q=q):
                    w_x_in(p, others[q]).wait_recv()
                    w_c(p, others[q]).start()

        @pl.when(u == parts + 3)
        def _():
            for p in range(PHASES):
                t, h = p // HALVES, p % HALVES
                for s in range(2):
                    for what in range(2):
                        sums[0, pl.ds(4 * what + 2 * s + t, 1), h * hw : (h + 1) * hw] = jnp.sum(
                            stat[p, 2 * what + s], axis=0, keepdims=True
                        )
            sum_copy(0, across_c).start()

        @pl.when(u == parts + 4)
        def _():
            sum_copy(0, across_c).wait()
            sums[1] = sums[0] + sums_land[0]
            sum_copy(1, across_x).start()

        @pl.when(u == parts + 5)
        def _():
            sum_copy(1, across_x).wait()
            both = sums[1] + sums_land[1]
            sums[2] = both
            member = (
                lax.broadcasted_iota(jnp.int32, (width, lane), 0) % FLAG_GROUPS
                == lax.broadcasted_iota(jnp.int32, (width, lane), 1) % FLAG_GROUPS
            ).astype(F32)
            bias_rows = both[0:4]
            inner = both[0:2] * both[2:4]
            stack = jnp.concatenate([inner, bias_rows * bias_rows, inner], axis=0)
            prods[0] = jnp.dot(
                stack, member, precision=lax.Precision.HIGHEST, preferred_element_type=F32
            )
            prod_y().start()

        @pl.when(u == parts + 6)
        def _():
            prod_y().wait()
            prods[1] = prods[0] + prods_land[ZED]
            for to in others:
                prod_z(to).start()

        @pl.when(u == parts + 7)
        def _():
            for frm in others:
                prod_z_in(frm).wait_recv()
            prods_land[z] = prods[1]
            whole = prods_land[0] + prods_land[1] + prods_land[2] + prods_land[3]
            both = sums[2]
            group = lax.broadcasted_iota(jnp.int32, (1, lane), 1) % FLAG_GROUPS

            def over(row):
                return jnp.concatenate([row] * (width // lane), axis=1)

            def flag_row(s, t):
                row = jnp.zeros((1, lane), F32)
                for g in range(FLAG_GROUPS):
                    row = jnp.where(group == g, flags[s, t, g].astype(F32), row)
                return row

            for t in range(2):
                task0, task1 = both[t : t + 1], both[2 + t : 3 + t]
                dots = whole[t : t + 1]
                coef0 = over(flag_row(0, t) * dots / (whole[4 + t : 5 + t] + 1e-06))
                coef1 = over(flag_row(1, t) * dots / (whole[2 + t : 3 + t] + 1e-06))
                gbias[t : t + 1] = (task0 - coef0 * task1) + (task1 - coef1 * task0)
            for s in range(2):
                gstitch[s] = both[4 + 2 * s : 6 + 2 * s]

        return carry

    lax.fori_loop(0, max(SIXES + DX_ENDS) + 1, body, 0)

    last = 3 * PHASES - 1

    for g in (last - 2, last - 1, last):
        for to in others:
            z_copy(tile_of(g), to).wait_send()
        ax_own(tile_of(g)).wait_send()
    for i in range(n_chunk - HELD, n_chunk):
        dx_copy(1, i, (n_chunk + i) % HELD).wait_send()
    for i in (n_part - 2, n_part - 1):
        mixed_out(1, i, i % 2).wait()
    dx_out(1, n_chunk - 1).wait()

    def drain_tiles(g, carry):
        at = tile_of(g)
        for b in others:
            ax_copy(at, b).wait_send()
        for b in range(ZED):
            ac_copy(at, b).wait_send()
        return carry

    lax.fori_loop(0, last + 1, drain_tiles, 0)

    def drain_x(i, carry):
        x_copy(0, i).wait_send()
        x_copy(1, i).wait_send()
        return carry

    lax.fori_loop(0, n_chunk, drain_x, 0)

    def drain_w(p, carry):
        for to in others:
            w_z(p, to).wait_send()
            w_x(p, to).wait_send()
            w_c(p, to).wait_send()
        return carry

    lax.fori_loop(0, PHASES, drain_w, 0)
    for to in others:
        prod_z(to).wait_send()


def fused_call(feat, wts, cot, bias, stitch, counts, mask, flags):
    rows, deep, width = feat.shape[1], feat.shape[2], wts.shape[2]
    chunk = rows // 6
    part = chunk // SUB
    hw, kz, tile = width // 2, 2 * deep, deep // 3
    cat, xw = 4 * hw, width // 4
    lane = min(128, width)
    dma = pltpu.SemaphoreType.DMA
    anywhere = pl.BlockSpec(memory_space=pl.ANY)
    inside = pl.BlockSpec(memory_space=pltpu.VMEM)
    scalars = pl.BlockSpec(memory_space=pltpu.SMEM)

    def v(shape, kind=BF16):
        return pltpu.VMEM(shape, kind)

    out_shape = [
        jax.ShapeDtypeStruct((2, rows, width), BF16),
        jax.ShapeDtypeStruct((2, rows, deep), BF16),
        jax.ShapeDtypeStruct((PHASES, ZED, 2, 3, 2, tile, xw), BF16),
        jax.ShapeDtypeStruct((2, width), F32),
        jax.ShapeDtypeStruct((2, 2, width), F32),
        jax.ShapeDtypeStruct((2, rows, deep), BF16),
        jax.ShapeDtypeStruct((2, rows, deep), BF16),
    ]
    scratch = [
        v((PHASES, kz, cat)),
        v((PHASES, ZED, rows, hw)),
        v((RING, 5, part, hw)),
        v((2, rows, hw), F32),
        v((2, chunk, kz)),
        v((PRODUCTS, ZED, part, hw), F32),
        v((2, 2, part, hw)),
        v((2, 2, part, hw)),
        v((HELD, chunk, deep), F32),
        v((HELD, chunk, deep)),
        v((chunk, deep)),
        v((chunk, deep)),
        v((rows, tile)),
        v((tile, rows)),
        v((tile, cat)),
        v((2, tile, cat)),
        v((3, ZED, tile, xw)),
        v((4, ZED, tile, xw)),
        v((3, ZED, tile, xw), F32),
        v((3, ZED, tile, xw)),
        v((rows, lane), F32),
        v((PHASES, 4, 8, hw), F32),
        v((3, 8, width), F32),
        v((2, 8, width), F32),
        v((2, 8, lane), F32),
        v((5, 8, lane), F32),
        dma((RING, 2)), dma((RING, 2)), dma((RING, 8)), dma((RING, 4)),
        dma((12,)), dma((12,)),
        dma((4, 4)), dma((4, 4)), dma((4, 4)), dma((4, 4)), dma((4, 4)), dma((4, 4)), dma((4,)),
        dma((2, 2)), dma((2,)), dma((2,)), dma((HELD,)), dma((12,)), dma((1,)), dma((1,)),
        dma((1,)), dma((1,)), dma((2,)), dma((3, 4)), dma((4, 4)), dma((3, 4)), dma((12, 4)),
        dma((3,)), dma((3,)),
        dma((12, 4)), dma((12, 4)), dma((12, 4)), dma((12, 4)), dma((8,)), dma((8,)),
    ]
    flops = 3 * 2 * 2 * rows * kz * cat * 2
    return pl.pallas_call(
        functools.partial(fused_kernel, rows, deep, width, chunk),
        out_shape=out_shape,
        in_specs=[anywhere] * 3 + [inside] * 4 + [scalars],
        out_specs=[anywhere] * 3 + [inside] * 2 + [anywhere] * 2,
        scratch_shapes=scratch,
        compiler_params=pltpu.CompilerParams(
            collective_id=0, has_side_effects=True, vmem_limit_bytes=64 * 1024 * 1024
        ),
        cost_estimate=pl.CostEstimate(
            flops=flops, bytes_accessed=200_000_000, transcendentals=2 * rows * width * 2
        ),
        name="cross_stitch_step",
    )(feat, wts, cot, bias, stitch, counts, mask, flags)


def finish_kernel(
    low, mixed, gfeat, gbias, gstitch,
    out, mixed_out, gfeat_out, gbias_out, gstitch_out,
    taken, given, held_mixed, held_gfeat, in_sem, out_sem, pass_sem,
):
    places, tile, xw = low.shape[1], low.shape[5], low.shape[6]
    n_block = 2 * places * 2
    block = 3 * tile
    fetched = (
        pltpu.make_async_copy(mixed, held_mixed, pass_sem.at[0]),
        pltpu.make_async_copy(gfeat, held_gfeat, pass_sem.at[1]),
    )
    passed = (
        pltpu.make_async_copy(held_mixed, mixed_out, pass_sem.at[2]),
        pltpu.make_async_copy(held_gfeat, gfeat_out, pass_sem.at[3]),
    )

    class take:
        def __init__(self, i):
            t, rest = divmod(i, places * 2)
            source, core = divmod(rest, 2)
            slot = i % WIDEN_SLOTS
            self.copies = [
                pltpu.make_async_copy(
                    low.at[2 * t + h, source, core], taken.at[slot, h], in_sem.at[slot, h]
                )
                for h in range(HALVES)
            ]

        def start(self):
            for copy in self.copies:
                copy.start()

        def wait(self):
            for copy in self.copies:
                copy.wait()

    def give(i):
        return pltpu.make_async_copy(
            given.at[i % WIDEN_SLOTS], out.at[pl.ds(i * block, block)], out_sem.at[i % WIDEN_SLOTS]
        )

    for i in range(min(WIDEN_SLOTS, n_block)):
        take(i).start()
    for copy in fetched:
        copy.start()
    gbias_out[...] = gbias[...]
    gstitch_out[...] = gstitch[...]
    for i in range(n_block):
        slot = i % WIDEN_SLOTS
        take(i).wait()
        if i >= WIDEN_SLOTS:
            give(i - WIDEN_SLOTS).wait()
        for h in range(HALVES):
            for j in range(3):
                for side in range(2):
                    lanes = (2 * h + side) * xw
                    given[slot, j * tile : (j + 1) * tile, lanes : lanes + xw] = wide(
                        taken[slot, h, j, side]
                    )
        give(i).start()
        if i + WIDEN_SLOTS < n_block:
            take(i + WIDEN_SLOTS).start()
        if i == 2:
            for arrived, copy in zip(fetched, passed):
                arrived.wait()
                copy.start()
    for i in range(max(0, n_block - WIDEN_SLOTS), n_block):
        give(i).wait()
    for copy in passed:
        copy.wait()


def finish(low, mixed, gfeat, gbias, gstitch):
    tile, xw = low.shape[5:]
    block, width = 3 * tile, 4 * xw
    tall = low.size // width
    anywhere = pl.BlockSpec(memory_space=pl.ANY)
    inside = pl.BlockSpec(memory_space=pltpu.VMEM)
    moved = sum(a.size * a.dtype.itemsize for a in (mixed, gfeat))
    return pl.pallas_call(
        finish_kernel,
        in_specs=[anywhere] * 3 + [inside] * 2,
        out_specs=[anywhere] * 3 + [inside] * 2,
        out_shape=[jax.ShapeDtypeStruct((tall, width), F32)]
        + [
            jax.ShapeDtypeStruct(a.shape, kind)
            for a, kind in ((mixed, BF16), (gfeat, BF16), (gbias, F32), (gstitch, F32))
        ],
        scratch_shapes=[
            pltpu.VMEM((WIDEN_SLOTS, HALVES, 3, 2, tile, xw), BF16),
            pltpu.VMEM((WIDEN_SLOTS, block, width), F32),
            pltpu.VMEM(mixed.shape, BF16),
            pltpu.VMEM(gfeat.shape, BF16),
            pltpu.SemaphoreType.DMA((WIDEN_SLOTS, HALVES)),
            pltpu.SemaphoreType.DMA((WIDEN_SLOTS,)),
            pltpu.SemaphoreType.DMA((4,)),
        ],
        compiler_params=pltpu.CompilerParams(vmem_limit_bytes=60 * 1024 * 1024),
        cost_estimate=pl.CostEstimate(
            flops=tall * width, bytes_accessed=6 * tall * width + 2 * moved, transcendentals=0
        ),
        name="finish",
    )(low, mixed, gfeat, gbias, gstitch)


def fused_plan(mesh):
    def per_device(features, weights, bias, stitch, cotangent, crop_counts, row_mask, flags):
        rows, deep = features.shape[1:]
        width = weights.shape[2]
        mixed, gfeat, gwt, gbias, gstitch, _, _ = fused_call(
            features, weights, cotangent, bias, stitch,
            crop_counts.reshape(1, -1), row_mask.reshape(-1, min(128, rows // 6)), flags,
        )
        grad_weights, mixed, gfeat, gbias, gstitch = finish(
            gwt, mixed, gfeat, gbias, gstitch
        )
        return mixed, gfeat, grad_weights.reshape(2, ZED * 2 * deep, width), gbias, gstitch

    return per_device


def plan_for(mesh):
    if mesh.shape["batch"] == 4 and mesh.shape["mp"] == 2 * ZED:
        return fused_plan(mesh)
    return generic_plan(mesh)


def solution(mesh):
    in_specs = (
        P(None, "batch", "mp"),
        P(None, None, "mp"),
        P(None, "mp"),
        P(None, None, "mp"),
        P(None, "batch", "mp"),
        P("batch"),
        P("batch"),
        P(),
    )
    out_specs = (
        P(None, "batch", "mp"),
        P(None, "batch", "mp"),
        P(None, None, "mp"),
        P(None, "mp"),
        P(None, None, "mp"),
    )
    return jax.shard_map(
        plan_for(mesh), mesh=mesh, in_specs=in_specs, out_specs=out_specs, check_vma=False
    )
```

```python
import collections
import functools

import jax
import jax.numpy as jnp
from jax import lax
from jax.experimental import pallas as pl
from jax.experimental.pallas import tpu as pltpu
from jax.sharding import PartitionSpec as P

FLAG_GROUPS = 8
OUTER = 4


def row_weights(counts, mask):
    ends = jnp.cumsum(counts)
    starts = ends - counts
    index = lax.broadcasted_iota(jnp.int32, (mask.shape[0], counts.shape[0]), 0)
    inside = (index >= starts[None, :]) & (index < ends[None, :])
    count_row = jnp.sum(jnp.where(inside, counts[None, :], 0), axis=1)
    live = (count_row > 0) & (mask == 1)
    return jnp.where(live, 1.0 / jnp.maximum(count_row, 1).astype(jnp.float32), 0.0)


def project_bias(task_bias, flags):
    local_width = task_bias.shape[2]
    channel = lax.axis_index("mp") * local_width + lax.broadcasted_iota(
        jnp.int32, (local_width, FLAG_GROUPS), 0
    )
    member = (
        channel % FLAG_GROUPS == lax.broadcasted_iota(jnp.int32, (local_width, FLAG_GROUPS), 1)
    ).astype(jnp.float32)
    dots = jnp.dot(task_bias[0] * task_bias[1], member, precision=lax.Precision.HIGHEST)
    norms = jnp.einsum(
        "stc,cg->stg", task_bias * task_bias, member, precision=lax.Precision.HIGHEST
    )
    dots, norms = lax.psum((dots, norms), "mp")
    flag = flags.astype(jnp.float32)
    coef_first = jnp.dot(
        flag[0] * dots / (norms[1] + 1e-06), member.T, precision=lax.Precision.HIGHEST
    )
    coef_second = jnp.dot(
        flag[1] * dots / (norms[0] + 1e-06), member.T, precision=lax.Precision.HIGHEST
    )
    first = task_bias[0] - coef_first * task_bias[1]
    second = task_bias[1] - coef_second * task_bias[0]
    return first + second


def generic_plan(mesh):
    n_mp = mesh.shape["mp"]
    n_batch = mesh.shape["batch"]
    inner = n_mp // OUTER
    inner_groups = [[o * inner + i for i in range(inner)] for o in range(OUTER)]
    outer_groups = [[o * inner + i for o in range(OUTER)] for i in range(inner)]

    def per_device(features, weights, bias, stitch, cotangent, crop_counts, row_mask, flags):
        rows = features.shape[1]
        width = weights.shape[2]
        depth = features.shape[2] * inner
        held = lax.all_gather(
            features, "mp", axis=2, tiled=True, axis_index_groups=inner_groups
        )
        split = weights.reshape(2, OUTER, depth, width)
        block = lax.all_to_all(
            split, "mp", split_axis=1, concat_axis=1, axis_index_groups=outer_groups
        )
        block = block.reshape(2, OUTER, depth, width)
        part = jnp.einsum("trk,tokc->otrc", held, block, preferred_element_type=jnp.float32)
        linear = lax.psum_scatter(
            part.astype(jnp.bfloat16),
            "mp",
            scatter_dimension=0,
            axis_index_groups=outer_groups,
        ).astype(jnp.float32)
        pre = linear + bias[:, None, :]
        hidden, gelu_back = jax.vjp(lambda v: jax.nn.gelu(v, approximate=False), pre)
        mixed = stitch[:, 0, None, :] * hidden[0][None] + stitch[:, 1, None, :] * hidden[1][None]
        scale_rows = row_weights(crop_counts, row_mask)
        grad_out = cotangent.astype(jnp.float32) * scale_rows[None, :, None]
        first_task = gelu_back(stitch[0][:, None, :] * grad_out[0][None])[0]
        second_task = gelu_back(stitch[1][:, None, :] * grad_out[1][None])[0]
        task_bias = jnp.stack([jnp.sum(first_task, axis=1), jnp.sum(second_task, axis=1)])
        grad_linear = (first_task + second_task).astype(jnp.bfloat16)
        grad_stitch = jnp.sum(grad_out[:, None] * hidden[None], axis=2)
        every = lax.all_gather(grad_linear, "mp", axis_index_groups=outer_groups)
        grad_part = jnp.einsum(
            "otrc,tokc->trk", every, block, preferred_element_type=jnp.float32
        )
        grad_part = grad_part.astype(jnp.bfloat16).reshape(2, rows, inner, depth // inner)
        grad_features = lax.psum_scatter(
            grad_part.transpose(2, 0, 1, 3),
            "mp",
            scatter_dimension=0,
            axis_index_groups=inner_groups,
        )
        weight_part = jnp.einsum(
            "trk,otrc->otkc", held, every, preferred_element_type=jnp.float32
        )
        weight_part = weight_part.astype(jnp.bfloat16).reshape(
            OUTER, 2, n_batch, depth // n_batch, width
        )
        share = lax.psum_scatter(
            weight_part.transpose(2, 0, 1, 3, 4), "batch", scatter_dimension=0
        )
        share = lax.all_to_all(
            share, "mp", split_axis=0, concat_axis=0, axis_index_groups=outer_groups
        )
        share = share.reshape(OUTER, 2, depth // n_batch, width)
        whole = lax.all_gather(share, "batch")
        grad_weights = whole.transpose(2, 1, 0, 3, 4).reshape(2, OUTER * depth, width)
        task_bias, grad_stitch = lax.psum((task_bias, grad_stitch), "batch")
        grad_bias = project_bias(task_bias, flags)
        return (
            mixed.astype(jnp.bfloat16),
            grad_features.astype(jnp.bfloat16),
            grad_weights.astype(jnp.float32),
            grad_bias,
            grad_stitch,
        )

    return per_device


MESH = pl.DeviceIdType.MESH
BF16 = jnp.bfloat16
F32 = jnp.float32
ZED = 4
HALVES = 2
PHASES = 4
RING = 8
BAND = 32
SUB = 2
PRODUCTS = 6
HELD = 4
WIDEN_BLOCKS = 12
WIDEN_SLOTS = 4

DX_TIMES = (20, 21, 24, 25, 27, 32, 43, 46, 47, 58, 60, 61)
DX_BEGINS = (22, 24, 27, 30, 37, 41, 44, 50, 52, 66, 75, 82)
DX_ENDS = (23, 25, 29, 35, 39, 42, 48, 51, 53, 69, 78, 95)
ONES = (21, 24, 28, 31, 36, 40, 43, 45, 46, 54, 57, 63)
TWOS = (22, 26, 30, 33, 38, 42, 44, 46, 50, 56, 58, 65)
THREES = (24, 31, 32, 35, 43, 44, 45, 52, 55, 62, 64, 80)
FOURS = (27, 33, 37, 38, 44, 46, 48, 54, 64, 71, 74, 85)
FIVES = (31, 40, 49, 51, 64, 69, 73, 80, 84, 86, 94, 105)
SIXES = (36, 60, 64, 66, 68, 81, 85, 97, 98, 99, 110, 111)
W_STRIPS = {2: (5, 6, 7, 8, 10, 11), 3: (20, 21, 23, 24, 25, 27)}
W_ACROSS = {1: (3, 3, 3), 2: (15, 16, 17), 3: (30, 31, 32)}
W_CORES = {1: (5, 7, 9), 2: (18, 21, 23), 3: (33, 33, 35)}


Part = collections.namedtuple("Part", ("u", "p", "i", "t", "h", "slot", "prod", "buf"))
Tile = collections.namedtuple("Tile", ("g", "p", "t", "h", "j", "buf", "trio", "quad"))


def half(value):
    return value.astype(BF16)


def wide(value):
    return value.astype(F32)


def fused_kernel(
    rows, deep, width, chunk,
    feat, wts, cot, bias, stitch, counts, mask, flags,
    mixed, gfeat, gwt, gbias, gstitch, xn, dxn,
    wv, gl, rs, h0, xc, pf, cc, mx, own, dsend, dfetch, dout,
    xsrc, xt, cstage, cland, xstage, xland, kept, zstage,
    scale, stat, sums, sums_land, prods, prods_land,
    rs_send, rs_recv, ag_send, ag_recv, xs_send, xs_recv,
    fz_send, fz_recv, fx_send, fx_recv,
    wz_send, wz_recv, wx_send, wx_recv, wc_send, wc_recv, wl,
    xf, cf, mxs, dx_send, dx_recv, df, dod,
    tile_in, c_send, c_recv, x_send, x_recv, z_send, z_recv, zl, zx_send,
    ax_send, ax_recv, ac_send, ac_recv, t_send, t_recv,
):
    batch, mp = lax.axis_index("batch"), lax.axis_index("mp")
    z, y = mp // 2, mp % 2
    x, c = batch // 2, batch % 2
    up = {"mp": mp + 2}
    down = {"mp": mp - 2}
    across_y = {"mp": 2 * z + 1 - y}
    across_x = {"batch": 2 * (1 - x) + c}
    across_c = {"batch": 2 * x + 1 - c}

    def at_z(other):
        return {"mp": 2 * other + y}

    others = (3 - z, (z + 2) % 4, z + 1 - 2 * (z % 2))

    n_chunk = rows // chunk
    total = PHASES * n_chunk
    part = chunk // SUB
    n_part = rows // part
    parts = PHASES * n_part
    images = counts.shape[1]
    hw = width // HALVES
    kz = 2 * deep
    quarter = deep // 2
    tile = deep // 3
    strip = quarter // 6
    xw = hw // 2

    def mult(value, unit):
        return pl.multiple_of(value, unit)

    def remote(src, dst, send, recv, device):
        return pltpu.make_async_remote_copy(
            src_ref=src, dst_ref=dst, send_sem=send, recv_sem=recv,
            device_id=device, device_id_type=MESH,
        )

    def cols(b):
        return pl.ds(mult(b * hw, hw), hw)

    def chunk_rows(i):
        return pl.ds(mult(i * chunk, chunk), chunk)

    def part_rows(i):
        return pl.ds(mult(i * part, part), part)

    def tower(p):
        t = jnp.where(p >= HALVES, 1, 0)
        return t, p - HALVES * t

    def x_copy(t, i):
        e = t * n_chunk + i
        return remote(
            feat.at[t, chunk_rows(i)], xn.at[t, chunk_rows(i)],
            xs_send.at[e], xs_recv.at[e], across_y,
        )

    def x_fetch(t, i, buf):
        return (
            pltpu.make_async_copy(
                feat.at[t, chunk_rows(i)],
                xc.at[buf, :, pl.ds(mult(deep * y, deep), deep)], xf.at[buf, 0],
            ),
            pltpu.make_async_copy(
                xn.at[t, chunk_rows(i)],
                xc.at[buf, :, pl.ds(mult(deep * (1 - y), deep), deep)], xf.at[buf, 1],
            ),
        )

    def cot_fetch(h, i, buf):
        return pltpu.make_async_copy(
            cot.at[:, part_rows(i), cols(h)], cc.at[buf], cf.at[buf]
        )

    def w_own(p):
        t, h = tower(p)
        return pltpu.make_async_copy(
            wts.at[t, pl.ds(mult(kz * z, kz), kz), cols(h)], wv.at[p, :, cols(z)], wl.at[p],
        )

    def w_rows():
        return pl.ds(mult(deep * c + quarter * x, quarter), quarter)

    def w_z(p, to):
        t, h = tower(p)
        return remote(
            wts.at[
                t, pl.ds(mult(kz * to + deep * c + quarter * x, quarter), quarter), cols(h)
            ],
            wv.at[p, w_rows(), cols(z)],
            wz_send.at[p, to], wz_recv.at[p, z], at_z(to),
        )

    def w_z_strip(p, to, r):
        t, h = tower(p)
        at = deep * c + quarter * x + strip * r
        return remote(
            wts.at[t, pl.ds(mult(kz * to + at, strip), strip), cols(h)],
            wv.at[p, pl.ds(mult(at, strip), strip), cols(z)],
            wz_send.at[p, to], wz_recv.at[p, z], at_z(to),
        )

    def first_rows(side, r):
        part_of = quarter // 2
        return pl.ds(mult(deep * c + quarter * side + part_of * r, part_of), part_of)

    def first_z(to, r):
        part_of = quarter // 2
        at = kz * to + deep * c + quarter * x + part_of * r
        return remote(
            wts.at[0, pl.ds(mult(at, part_of), part_of), cols(0)],
            wv.at[0, first_rows(x, r), cols(z)],
            fz_send.at[r, to], fz_recv.at[r, z], at_z(to),
        )

    def first_z_in(frm, r):
        here = wv.at[0, first_rows(x, r), cols(frm)]
        return remote(here, here, fz_send.at[r, frm], fz_recv.at[r, frm], at_z(frm))

    def first_x(b, r, side):
        here = wv.at[0, first_rows(side, r), cols(b)]
        return remote(here, here, fx_send.at[r, b], fx_recv.at[r, b], across_x)

    def w_z_in(p, frm):
        here = wv.at[p, w_rows(), cols(frm)]
        return remote(here, here, wz_send.at[p, frm], wz_recv.at[p, frm], at_z(frm))

    def w_x(p, b):
        here = wv.at[p, w_rows(), cols(b)]
        return remote(here, here, wx_send.at[p, b], wx_recv.at[p, b], across_x)

    def w_x_in(p, b):
        here = wv.at[
            p, pl.ds(mult(deep * c + quarter * (1 - x), quarter), quarter), cols(b)
        ]
        return remote(here, here, wx_send.at[p, b], wx_recv.at[p, b], across_x)

    def w_c(p, b):
        here = wv.at[p, pl.ds(mult(deep * c, deep), deep), cols(b)]
        return remote(here, here, wc_send.at[p, b], wc_recv.at[p, b], across_c)

    def w_c_in(p, b):
        here = wv.at[p, pl.ds(mult(deep * (1 - c), deep), deep), cols(b)]
        return remote(here, here, wc_send.at[p, b], wc_recv.at[p, b], across_c)

    def rs_up(slot, zz):
        run = rs.at[slot, zz + 2 : ZED + 1]
        return remote(run, run, rs_send.at[slot, 0], rs_recv.at[slot, 0], up)

    def rs_down(slot, zz):
        run = rs.at[slot, 0:zz]
        return remote(run, run, rs_send.at[slot, 1], rs_recv.at[slot, 1], down)

    def rs_from_below(slot, zz):
        run = rs.at[slot, zz + 1 : ZED + 1]
        return remote(run, run, rs_send.at[slot, 0], rs_recv.at[slot, 0], down)

    def rs_from_above(slot, zz):
        run = rs.at[slot, 0 : zz + 1]
        return remote(run, run, rs_send.at[slot, 1], rs_recv.at[slot, 1], up)

    def at_place(first, last, do):
        for zz in range(first, last + 1):
            @pl.when(z == zz)
            def _(zz=zz):
                do(zz)

    def ag(at, b, going, device):
        here = gl.at[at.p, part_rows(at.i), cols(b)]
        return remote(
            here, here, ag_send.at[at.slot, going * ZED + b], ag_recv.at[at.slot, b], device
        )

    def dx_copy(t, i, buf):
        return remote(
            dsend.at[buf], dxn.at[t, chunk_rows(i)],
            dx_send.at[buf], dx_recv.at[t * n_chunk + i], across_y,
        )

    def dx_fetch(t, i):
        return pltpu.make_async_copy(dxn.at[t, chunk_rows(i)], dfetch, df.at[0])

    def dx_out(t, i):
        return pltpu.make_async_copy(dout, gfeat.at[t, chunk_rows(i)], dod.at[0])

    def mixed_out(h, i, buf):
        return pltpu.make_async_copy(
            mx.at[buf], mixed.at[:, part_rows(i), cols(h)], mxs.at[buf]
        )

    def tile_fetch(t, j, hk, start):
        lanes = pl.ds(mult(tile * j, tile), tile)
        near = pltpu.make_async_copy(feat.at[t, :, lanes], xsrc, tile_in.at[0])
        if not start:
            near.wait()
            return

        @pl.when(hk == y)
        def _():
            near.start()

        @pl.when(hk != y)
        def _():
            pltpu.make_async_copy(xn.at[t, :, lanes], xsrc, tile_in.at[0]).start()

    def core_copy(g):
        return remote(cstage, cland.at[g.buf], c_send.at[0], c_recv.at[g.buf], across_c)

    def across_copy(g, b):
        return remote(
            xstage.at[g.trio, b], xland.at[g.quad, b],
            x_send.at[g.trio, b], x_recv.at[g.quad, b], across_x,
        )

    def piece(g, source, core, lanes, n_lanes):
        return gwt.at[
            g.t, source,
            pl.ds(mult(deep * core + tile * g.j, tile), tile),
            pl.ds(mult(hw * g.h + lanes, xw), n_lanes),
        ]

    def z_copy(g, to):
        return remote(
            zstage.at[g.trio, to], piece(g, z, c, xw * x, xw),
            z_send.at[g.trio, to], z_recv.at[g.g, z], at_z(to),
        )

    def z_in(g, frm):
        here = piece(g, frm, c, xw * x, xw)
        return remote(here, here, z_send.at[g.trio, frm], z_recv.at[g.g, frm], at_z(frm))

    def z_own(g):
        return pltpu.make_async_copy(
            zstage.at[g.trio, z], piece(g, z, c, xw * x, xw), zl.at[g.trio]
        )

    def ax_own(g):
        return remote(
            zstage.at[g.trio, z], piece(g, z, c, xw * x, xw),
            zx_send.at[g.trio], ax_recv.at[g.g, z], across_x,
        )

    def ax_copy(g, b):
        here = piece(g, b, c, xw * x, xw)
        return remote(here, here, ax_send.at[g.g, b], ax_recv.at[g.g, b], across_x)

    def ax_in(g, b):
        here = piece(g, b, c, xw * (1 - x), xw)
        return remote(here, here, ax_send.at[g.g, b], ax_recv.at[g.g, b], across_x)

    def ac_copy(g, b):
        here = piece(g, b, c, 0, hw)
        return remote(here, here, ac_send.at[g.g, b], ac_recv.at[g.g, b], across_c)

    def ac_in(g, b):
        here = piece(g, b, 1 - c, 0, hw)
        return remote(here, here, ac_send.at[g.g, b], ac_recv.at[g.g, b], across_c)

    def sum_copy(stage, device):
        return remote(
            sums.at[stage], sums_land.at[stage], t_send.at[stage], t_recv.at[stage], device
        )

    def prod_y():
        return remote(prods.at[0], prods_land.at[ZED], t_send.at[2], t_recv.at[2], across_y)

    def prod_z(to):
        return remote(
            prods.at[1], prods_land.at[z], t_send.at[3 + to], t_recv.at[3 + z], at_z(to)
        )

    def prod_z_in(frm):
        here = prods_land.at[frm]
        return remote(here, here, t_send.at[3 + frm], t_recv.at[3 + frm], at_z(frm))

    barrier = pltpu.get_barrier_semaphore()
    for device in [at_z(o) for o in others] + [across_y, across_x, across_c]:
        pl.semaphore_signal(barrier, inc=1, device_id=device, device_id_type=MESH)
    pl.semaphore_wait(barrier, 6)

    for r in range(2):
        for to in others:
            first_z(to, r).start()
    x_copy(0, 0).start()
    x_copy(0, 1).start()
    w_own(0).start()
    for to in others:
        w_z(1, to).start()
    w_own(1).start()
    cot_fetch(0, 0, 0).start()

    image_row = lax.broadcasted_iota(jnp.int32, (images, images), 0)
    image_col = lax.broadcasted_iota(jnp.int32, (images, images), 1)
    crops = counts[...].astype(F32)
    ends = jnp.dot(
        jnp.broadcast_to(crops, (8, images)), (image_row <= image_col).astype(F32),
        precision=lax.Precision.HIGHEST, preferred_element_type=F32,
    )[0:1]
    starts = ends - crops
    block = mask.shape[1]
    lane = scale.shape[1]

    for r in range(rows // block):
        index = (
            lax.broadcasted_iota(jnp.int32, (block, images), 0) + r * block
        ).astype(F32)
        inside = (index >= starts) & (index < ends)
        count_row = jnp.sum(jnp.where(inside, crops, 0.0), axis=1, keepdims=True)
        diagonal = lax.broadcasted_iota(jnp.int32, (block, block), 0) == (
            lax.broadcasted_iota(jnp.int32, (block, block), 1)
        )
        usable = jnp.sum(
            jnp.where(diagonal, mask[r : r + 1, :].astype(F32), 0.0),
            axis=1, keepdims=True,
        )
        live = (count_row > 0.0) & (usable == 1.0)
        share = jnp.where(live, 1.0 / jnp.maximum(count_row, 1.0), 0.0)
        scale[r * block : (r + 1) * block, :] = jnp.broadcast_to(share, (block, lane))

    for r in range(2):
        for frm in others:
            first_z_in(frm, r).wait_recv()
            first_x(frm, r, x).start()
    for frm in others:
        for r in range(2):
            first_x(frm, r, 1 - x).wait_recv()
        w_c(0, frm).start()
    x_copy(0, 0).wait_recv()
    for copy in x_fetch(0, 0, 0):
        copy.start()

    def final(at, later):
        p, i, slot, t, h, buf = at.p, at.i, at.slot, at.t, at.h, at.buf
        cot_fetch(h, i, buf).wait()

        @pl.when(at.u >= 2 * n_part + 2)
        def _():
            mixed_out(h, i, buf).wait()

        @pl.when(i == 0)
        def _():
            stat[p] = jnp.zeros(stat.shape[1:], F32)

        lanes = cols(h)
        shift = bias[pl.ds(t, 1), lanes]
        st = [stitch[s, pl.ds(t, 1), lanes] for s in range(2)]
        band = min(BAND, part)

        def step(r, carry):
            here = part_rows_of(r, band)
            there = pl.ds(mult(i * part + r * band, band), band)
            value = pf[at.prod, z, here, :]
            below = wide(rs[slot, z + 1, here, :])
            above = wide(rs[slot, z, here, :])
            value = value + jnp.where(z > 0, below, 0.0) + jnp.where(z < ZED - 1, above, 0.0)
            pre = value + shift
            phi = 0.5 * (1.0 + lax.erf(pre * 0.7071067811865476))
            hidden = pre * phi
            slope = phi + pre * (jnp.exp(-0.5 * pre * pre) * 0.3989422804014327)
            weight = scale[there, 0:1]
            first = wide(cc[buf, 0, here, :]) * weight
            second = wide(cc[buf, 1, here, :]) * weight
            back0 = st[0] * first * slope
            back1 = st[1] * second * slope
            gl[p, there, cols(z)] = half(back0 + back1)

            def fold(v):
                return jnp.sum(v.reshape(band // 8, 8, hw), axis=0)

            stat[p, 0] += fold(back0)
            stat[p, 1] += fold(back1)
            stat[p, 2] += fold(first * hidden)
            stat[p, 3] += fold(second * hidden)

            @pl.when(t == 0)
            def _():
                h0[h, there, :] = hidden

            @pl.when(t == 1)
            def _():
                before = h0[h, there, :]
                for s in range(2):
                    mx[buf, s, here, :] = half(
                        stitch[s, 0:1, lanes] * before + st[s] * hidden
                    )

            return carry

        lax.fori_loop(0, part // band, step, 0)

        @pl.when(z < ZED - 1)
        def _():
            ag(at, z, 0, up).start()

        @pl.when(z > 0)
        def _():
            ag(at, z, 1, down).start()

        @pl.when(t == 1)
        def _():
            mixed_out(h, i, buf).start()

        @pl.when(at.u + 1 < parts)
        def _():
            cot_fetch(later.h, later.i, later.buf).start()

    def part_rows_of(r, band):
        return pl.ds(mult(r * band, band), band)

    def forward_ag(at, far):
        @pl.when((at.u >= 0) & (at.u < parts))
        def _():
            @pl.when(z - far >= 0)
            def _():
                ag(at, z - far, 0, up).wait_recv()

                @pl.when(z < ZED - 1)
                def _():
                    ag(at, z - far, 0, up).start()

            @pl.when(z + far < ZED)
            def _():
                ag(at, z + far, 1, down).wait_recv()

                @pl.when(z > 0)
                def _():
                    ag(at, z + far, 1, down).start()

    def dx_part(t, i, hk):
        there = chunk_rows(i)
        krows = pl.ds(mult(deep * hk, deep), deep)
        acc = None
        for h in range(HALVES):
            term = lax.dot_general(
                gl[2 * t + h, there, :], wv[2 * t + h, krows, :],
                (((1,), (1,)), ((), ())), preferred_element_type=F32,
            )
            acc = term if acc is None else acc + term
        return acc

    def dx_step(t, i, buf):
        @pl.when((i >= HELD) | (t > 0))
        def _():
            dx_copy(t, i, buf).wait_send()

        dsend[buf] = half(dx_part(t, i, 1 - y))
        dx_copy(t, i, buf).start()
        own[buf] = dx_part(t, i, y)

    def dx_begin(t, i, buf):
        dx_copy(t, i, buf).wait_recv()
        dx_fetch(t, i).start()

    def dx_final(t, i, buf):
        @pl.when((i >= 1) | (t > 0))
        def _():
            dx_out(t, i).wait()

        dx_fetch(t, i).wait()

        def step(j, inner):
            lanes = pl.ds(mult(tile * j, tile), tile)
            dout[:, lanes] = half(own[buf, :, lanes] + wide(dfetch[:, lanes]))
            return inner

        lax.fori_loop(0, 3, step, 0)
        dx_out(t, i).start()

    def listed(u, times, do):
        e, hit = 0, False
        for index, time in enumerate(times):
            same = u == time
            e = jnp.where(same, index, e)
            hit = hit | same

        @pl.when(hit)
        def _():
            do(e)

    def chunk_of(do):
        def run(e):
            t = jnp.where(e >= n_chunk, 1, 0)
            do(t, e - n_chunk * t, lax.rem(e, HELD))

        return run

    def turn():
        lanes_at_once = min(128, tile)

        def step(q, carry):
            lanes = pl.ds(mult(q * lanes_at_once, lanes_at_once), lanes_at_once)
            xt[lanes, :] = xsrc[:, lanes].T
            return carry

        lax.fori_loop(0, tile // lanes_at_once, step, 0)

    def tile_dot(g):
        return jnp.dot(xt[...], gl[g.p], preferred_element_type=F32)

    def stage_one(g):
        tile_fetch(g.t, g.j, 1 - c, False)
        turn()
        tile_fetch(g.t, g.j, c, True)
        cstage[...] = half(tile_dot(g))
        core_copy(g).start()

    def stage_two(g):
        tile_fetch(g.t, g.j, c, False)
        turn()

        @pl.when(g.j < 2)
        def _():
            tile_fetch(g.t, g.j + 1, 1 - c, True)

        core_copy(g).wait()
        product = tile_dot(g)
        for b in range(ZED):
            block = product[:, b * hw : (b + 1) * hw] + wide(
                cland[g.buf, :, b * hw : (b + 1) * hw]
            )
            left, right = block[:, :xw], block[:, xw:]
            kept[g.trio, b] = jnp.where(x == 0, left, right)
            xstage[g.trio, b] = half(jnp.where(x == 0, right, left))

        def send(q, carry):
            across_copy(g, lax.rem(z + 3 + 3 * q, ZED)).start()
            return carry

        lax.fori_loop(0, ZED, send, 0)

    def stage_three(g):
        @pl.when(g.g >= 3)
        def _():
            for to in others:
                z_copy(g, to).wait_send()
            ax_own(g).wait_send()

        def add(b):
            across_copy(g, b).wait()
            zstage[g.trio, b] = half(kept[g.trio, b] + wide(xland[g.quad, b]))

        def step(q, carry):
            b = lax.rem(z + 3 + 3 * q, ZED)
            add(b)
            z_copy(g, b).start()
            return carry

        lax.fori_loop(0, ZED - 1, step, 0)
        add(z)
        z_own(g).start()
        ax_own(g).start()

    def stage_four(g):
        def step(q, carry):
            b = lax.rem(z + 1 + q, ZED)
            z_in(g, b).wait_recv()
            ax_copy(g, b).start()
            return carry

        lax.fori_loop(0, ZED - 1, step, 0)
        z_own(g).wait()

    def stage_five(g):
        def step(q, carry):
            b = lax.rem(z + q, ZED)
            ax_in(g, b).wait_recv()
            ac_copy(g, b).start()
            return carry

        lax.fori_loop(0, ZED, step, 0)

    def stage_six(g):
        def step(b, carry):
            ac_in(g, b).wait_recv()
            return carry

        lax.fori_loop(0, ZED, step, 0)

    def tile_of(g):
        p = lax.div(g, 3)
        t, h = tower(p)
        return Tile(
            g=g, p=p, t=t, h=h, j=g - 3 * p,
            buf=lax.rem(g, 2), trio=g - 3 * p, quad=lax.rem(g, 4),
        )

    def tile_in_hand(do):
        return lambda g: do(tile_of(g))

    def body(u, carry):
        p0 = lax.div(u, n_part)
        i0 = u - p0 * n_part
        slot0, prod0 = lax.rem(u, RING), lax.rem(u, PRODUCTS)
        buf0 = lax.rem(u, 2)

        def before(lag):
            if isinstance(lag, int):
                whole, left = divmod(lag, n_part)
            else:
                whole, left = 0, lag
            under = i0 < left
            p = p0 - whole - jnp.where(under, 1, 0)
            i = i0 - left + jnp.where(under, n_part, 0)
            in_ring = lag % RING if isinstance(lag, int) else lag
            in_prods = lag % PRODUCTS if isinstance(lag, int) else lag
            slot = slot0 - in_ring + jnp.where(slot0 < in_ring, RING, 0)
            prod = prod0 - in_prods + jnp.where(prod0 < in_prods, PRODUCTS, 0)
            t, h = tower(p)
            return Part(u=u - lag, p=p, i=i, t=t, h=h, slot=slot, prod=prod, buf=lax.rem(i, 2))

        @pl.when((u >= 5) & (u < parts + 5))
        def _():
            slot = before(5).slot
            at_place(0, ZED - 2, lambda zz: rs_up(slot, zz).wait_send())
            at_place(1, ZED - 1, lambda zz: rs_down(slot, zz).wait_send())

        @pl.when((u >= 8) & (u < parts + 8))
        def _():
            at = before(8)

            def step(b, inner):
                @pl.when((z < ZED - 1) & (b <= z))
                def _():
                    ag(at, b, 0, up).wait_send()

                @pl.when((z > 0) & (b >= z))
                def _():
                    ag(at, b, 1, down).wait_send()

                return inner

            lax.fori_loop(0, ZED, step, 0)

        ck = lax.div(i0, SUB)
        fresh = ck * SUB == i0
        t0, h0_ = tower(p0)
        xbuf = lax.rem(ck, 2)

        @pl.when((u < parts) & fresh)
        def _():
            @pl.when(i0 == 0)
            def _():
                w_own(p0).wait()
                for frm in others:
                    w_c_in(p0, frm).wait_recv()

            for copy in x_fetch(t0, ck, xbuf):
                copy.wait()

            product = jnp.dot(xc[xbuf], wv[p0], preferred_element_type=F32)
            for b in range(ZED):
                for s in range(SUB):
                    pf[prod0 + s, b] = product[
                        s * part : (s + 1) * part, b * hw : (b + 1) * hw
                    ]

        going_up = before(z)

        @pl.when((going_up.u >= 0) & (going_up.u < parts))
        def _():
            slot, prod = going_up.slot, going_up.prod
            at_place(1, ZED - 1, lambda zz: rs_from_below(slot, zz).wait_recv())

            @pl.when(z == 0)
            def _():
                for b in range(1, ZED):
                    rs[slot, b + 1] = half(pf[prod, b])

            @pl.when(z > 0)
            def _():
                def step(b, inner):
                    rs[slot, b + 1] = half(wide(rs[slot, b + 1]) + pf[prod, b])
                    return inner

                lax.fori_loop(z + 1, ZED, step, 0)

            at_place(0, ZED - 2, lambda zz: rs_up(slot, zz).start())

        going_down = before(ZED - 1 - z)

        @pl.when((going_down.u >= 0) & (going_down.u < parts))
        def _():
            slot, prod = going_down.slot, going_down.prod
            at_place(0, ZED - 2, lambda zz: rs_from_above(slot, zz).wait_recv())

            @pl.when(z == ZED - 1)
            def _():
                for b in range(ZED - 1):
                    rs[slot, b] = half(pf[prod, b])

            @pl.when(z < ZED - 1)
            def _():
                def step(b, inner):
                    rs[slot, b] = half(wide(rs[slot, b]) + pf[prod, b])
                    return inner

                lax.fori_loop(0, z, step, 0)

            at_place(1, ZED - 1, lambda zz: rs_down(slot, zz).start())

        @pl.when(fresh & (u + 2 * SUB < 2 * n_part))
        def _():
            k = p0 * n_chunk + ck + 2
            over = jnp.where(k >= n_chunk, 1, 0)
            x_copy(over, k - over * n_chunk).start()

        @pl.when(fresh & (u + SUB < parts))
        def _():
            wrap = jnp.where(ck + 1 == n_chunk, 1, 0)
            i = ck + 1 - wrap * n_chunk
            t, h = tower(p0 + wrap)

            @pl.when(h == 0)
            def _():
                x_copy(t, i).wait_recv()

            for copy in x_fetch(t, i, lax.rem(i, 2)):
                copy.start()

        @pl.when((u >= 3) & (u < parts + 3))
        def _():
            final(before(3), before(2))

        forward_ag(before(4), 1)
        forward_ag(before(5), 2)
        forward_ag(before(6), 3)

        listed(u, DX_BEGINS, chunk_of(dx_begin))
        listed(u, DX_ENDS, chunk_of(dx_final))
        listed(u, DX_TIMES, chunk_of(dx_step))

        listed(u, THREES, tile_in_hand(stage_three))
        listed(u, TWOS, tile_in_hand(stage_two))
        listed(u, ONES, tile_in_hand(stage_one))
        listed(u, FOURS, tile_in_hand(stage_four))
        listed(u, FIVES, tile_in_hand(stage_five))
        listed(u, SIXES, tile_in_hand(stage_six))

        def first_fetch(p):
            tile_fetch(lax.div(p, HALVES), 0, 1 - c, True)

        listed(u, [time - 1 for time in ONES[::3]], first_fetch)

        for p, times in W_STRIPS.items():
            def send_strip(r, p=p):
                for to in others:
                    w_z_strip(p, to, r).start()

                @pl.when(r == 0)
                def _():
                    w_own(p).start()

            listed(u, times, send_strip)

        for p, times in W_ACROSS.items():
            for q, time in enumerate(times):
                @pl.when(u == time)
                def _(p=p, q=q):
                    w_z_in(p, others[q]).wait_recv()
                    w_x(p, others[q]).start()

        for p, times in W_CORES.items():
            for q, time in enumerate(times):
                @pl.when(u == time)
                def _(p=p, q=q):
                    w_x_in(p, others[q]).wait_recv()
                    w_c(p, others[q]).start()

        @pl.when(u == parts + 3)
        def _():
            for p in range(PHASES):
                t, h = p // HALVES, p % HALVES
                for s in range(2):
                    for what in range(2):
                        sums[0, pl.ds(4 * what + 2 * s + t, 1), h * hw : (h + 1) * hw] = jnp.sum(
                            stat[p, 2 * what + s], axis=0, keepdims=True
                        )
            sum_copy(0, across_c).start()

        @pl.when(u == parts + 4)
        def _():
            sum_copy(0, across_c).wait()
            sums[1] = sums[0] + sums_land[0]
            sum_copy(1, across_x).start()

        @pl.when(u == parts + 5)
        def _():
            sum_copy(1, across_x).wait()
            both = sums[1] + sums_land[1]
            sums[2] = both
            member = (
                lax.broadcasted_iota(jnp.int32, (width, lane), 0) % FLAG_GROUPS
                == lax.broadcasted_iota(jnp.int32, (width, lane), 1) % FLAG_GROUPS
            ).astype(F32)
            bias_rows = both[0:4]
            inner = both[0:2] * both[2:4]
            stack = jnp.concatenate([inner, bias_rows * bias_rows, inner], axis=0)
            prods[0] = jnp.dot(
                stack, member, precision=lax.Precision.HIGHEST, preferred_element_type=F32
            )
            prod_y().start()

        @pl.when(u == parts + 6)
        def _():
            prod_y().wait()
            prods[1] = prods[0] + prods_land[ZED]
            for to in others:
                prod_z(to).start()

        @pl.when(u == parts + 7)
        def _():
            for frm in others:
                prod_z_in(frm).wait_recv()
            prods_land[z] = prods[1]
            whole = prods_land[0] + prods_land[1] + prods_land[2] + prods_land[3]
            both = sums[2]
            group = lax.broadcasted_iota(jnp.int32, (1, lane), 1) % FLAG_GROUPS

            def over(row):
                return jnp.concatenate([row] * (width // lane), axis=1)

            def flag_row(s, t):
                row = jnp.zeros((1, lane), F32)
                for g in range(FLAG_GROUPS):
                    row = jnp.where(group == g, flags[s, t, g].astype(F32), row)
                return row

            for t in range(2):
                task0, task1 = both[t : t + 1], both[2 + t : 3 + t]
                dots = whole[t : t + 1]
                coef0 = over(flag_row(0, t) * dots / (whole[4 + t : 5 + t] + 1e-06))
                coef1 = over(flag_row(1, t) * dots / (whole[2 + t : 3 + t] + 1e-06))
                gbias[t : t + 1] = (task0 - coef0 * task1) + (task1 - coef1 * task0)
            for s in range(2):
                gstitch[s] = both[4 + 2 * s : 6 + 2 * s]

        return carry

    lax.fori_loop(0, max(SIXES + DX_ENDS) + 1, body, 0)

    last = 3 * PHASES - 1

    for g in (last - 2, last - 1, last):
        for to in others:
            z_copy(tile_of(g), to).wait_send()
        ax_own(tile_of(g)).wait_send()
    for i in range(n_chunk - HELD, n_chunk):
        dx_copy(1, i, (n_chunk + i) % HELD).wait_send()
    for i in (n_part - 2, n_part - 1):
        mixed_out(1, i, i % 2).wait()
    dx_out(1, n_chunk - 1).wait()

    def drain_tiles(g, carry):
        at = tile_of(g)
        for b in others:
            ax_copy(at, b).wait_send()
        for b in range(ZED):
            ac_copy(at, b).wait_send()
        return carry

    lax.fori_loop(0, last + 1, drain_tiles, 0)

    def drain_x(i, carry):
        x_copy(0, i).wait_send()
        x_copy(1, i).wait_send()
        return carry

    lax.fori_loop(0, n_chunk, drain_x, 0)

    def drain_w(p, carry):
        for to in others:
            w_z(p, to).wait_send()
            w_x(p, to).wait_send()
            w_c(p, to).wait_send()
        return carry

    lax.fori_loop(1, PHASES, drain_w, 0)
    for b in others:
        w_c(0, b).wait_send()
        for r in range(2):
            first_z(b, r).wait_send()
            first_x(b, r, x).wait_send()
    for to in others:
        prod_z(to).wait_send()


def fused_call(feat, wts, cot, bias, stitch, counts, mask, flags):
    rows, deep, width = feat.shape[1], feat.shape[2], wts.shape[2]
    chunk = rows // 6
    part = chunk // SUB
    hw, kz, tile = width // 2, 2 * deep, deep // 3
    cat, xw = 4 * hw, width // 4
    lane = min(128, width)
    dma = pltpu.SemaphoreType.DMA
    anywhere = pl.BlockSpec(memory_space=pl.ANY)
    inside = pl.BlockSpec(memory_space=pltpu.VMEM)
    scalars = pl.BlockSpec(memory_space=pltpu.SMEM)

    def v(shape, kind=BF16):
        return pltpu.VMEM(shape, kind)

    out_shape = [
        jax.ShapeDtypeStruct((2, rows, width), BF16),
        jax.ShapeDtypeStruct((2, rows, deep), BF16),
        jax.ShapeDtypeStruct((2, ZED, kz, width), BF16),
        jax.ShapeDtypeStruct((2, width), F32),
        jax.ShapeDtypeStruct((2, 2, width), F32),
        jax.ShapeDtypeStruct((2, rows, deep), BF16),
        jax.ShapeDtypeStruct((2, rows, deep), BF16),
    ]
    scratch = [
        v((PHASES, kz, cat)),
        v((PHASES, rows, cat)),
        v((RING, 5, part, hw)),
        v((2, rows, hw), F32),
        v((2, chunk, kz)),
        v((PRODUCTS, ZED, part, hw), F32),
        v((2, 2, part, hw)),
        v((2, 2, part, hw)),
        v((HELD, chunk, deep), F32),
        v((HELD, chunk, deep)),
        v((chunk, deep)),
        v((chunk, deep)),
        v((rows, tile)),
        v((tile, rows)),
        v((tile, cat)),
        v((2, tile, cat)),
        v((3, ZED, tile, xw)),
        v((4, ZED, tile, xw)),
        v((3, ZED, tile, xw), F32),
        v((3, ZED, tile, xw)),
        v((rows, lane), F32),
        v((PHASES, 4, 8, hw), F32),
        v((3, 8, width), F32),
        v((2, 8, width), F32),
        v((2, 8, lane), F32),
        v((5, 8, lane), F32),
        dma((RING, 2)), dma((RING, 2)), dma((RING, 8)), dma((RING, 4)),
        dma((12,)), dma((12,)),
        dma((2, 4)), dma((2, 4)), dma((2, 4)), dma((2, 4)),
        dma((4, 4)), dma((4, 4)), dma((4, 4)), dma((4, 4)), dma((4, 4)), dma((4, 4)), dma((4,)),
        dma((2, 2)), dma((2,)), dma((2,)), dma((HELD,)), dma((12,)), dma((1,)), dma((1,)),
        dma((1,)), dma((1,)), dma((2,)), dma((3, 4)), dma((4, 4)), dma((3, 4)), dma((12, 4)),
        dma((3,)), dma((3,)),
        dma((12, 4)), dma((12, 4)), dma((12, 4)), dma((12, 4)), dma((8,)), dma((8,)),
    ]
    flops = 3 * 2 * 2 * rows * kz * cat * 2
    return pl.pallas_call(
        functools.partial(fused_kernel, rows, deep, width, chunk),
        out_shape=out_shape,
        in_specs=[anywhere] * 3 + [inside] * 4 + [scalars],
        out_specs=[anywhere] * 3 + [inside] * 2 + [anywhere] * 2,
        scratch_shapes=scratch,
        compiler_params=pltpu.CompilerParams(
            collective_id=0, has_side_effects=True, vmem_limit_bytes=64 * 1024 * 1024
        ),
        cost_estimate=pl.CostEstimate(
            flops=flops, bytes_accessed=200_000_000, transcendentals=2 * rows * width * 2
        ),
        name="cross_stitch_step",
    )(feat, wts, cot, bias, stitch, counts, mask, flags)


def finish_kernel(
    block, low, mixed, gfeat, gbias, gstitch,
    out, mixed_out, gfeat_out, gbias_out, gstitch_out,
    taken, given, held_mixed, held_gfeat, in_sem, out_sem, pass_sem,
):
    n_block = low.shape[0] // block
    fetched = (
        pltpu.make_async_copy(mixed, held_mixed, pass_sem.at[0]),
        pltpu.make_async_copy(gfeat, held_gfeat, pass_sem.at[1]),
    )
    passed = (
        pltpu.make_async_copy(held_mixed, mixed_out, pass_sem.at[2]),
        pltpu.make_async_copy(held_gfeat, gfeat_out, pass_sem.at[3]),
    )

    def take(i):
        return pltpu.make_async_copy(
            low.at[pl.ds(i * block, block)], taken.at[i % WIDEN_SLOTS], in_sem.at[i % WIDEN_SLOTS]
        )

    def give(i):
        return pltpu.make_async_copy(
            given.at[i % WIDEN_SLOTS], out.at[pl.ds(i * block, block)], out_sem.at[i % WIDEN_SLOTS]
        )

    for i in range(min(WIDEN_SLOTS, n_block)):
        take(i).start()
    for copy in fetched:
        copy.start()
    gbias_out[...] = gbias[...]
    gstitch_out[...] = gstitch[...]
    for i in range(n_block):
        slot = i % WIDEN_SLOTS
        take(i).wait()
        if i >= WIDEN_SLOTS:
            give(i - WIDEN_SLOTS).wait()
        given[slot] = wide(taken[slot])
        give(i).start()
        if i + WIDEN_SLOTS < n_block:
            take(i + WIDEN_SLOTS).start()
        if i == 2:
            for arrived, copy in zip(fetched, passed):
                arrived.wait()
                copy.start()
    for i in range(max(0, n_block - WIDEN_SLOTS), n_block):
        give(i).wait()
    for copy in passed:
        copy.wait()


def finish(low, mixed, gfeat, gbias, gstitch):
    tall, width = low.shape
    block = tall // WIDEN_BLOCKS
    anywhere = pl.BlockSpec(memory_space=pl.ANY)
    inside = pl.BlockSpec(memory_space=pltpu.VMEM)
    moved = sum(a.size * a.dtype.itemsize for a in (mixed, gfeat))
    return pl.pallas_call(
        functools.partial(finish_kernel, block),
        in_specs=[anywhere] * 3 + [inside] * 2,
        out_specs=[anywhere] * 3 + [inside] * 2,
        out_shape=[
            jax.ShapeDtypeStruct(a.shape, kind)
            for a, kind in ((low, F32), (mixed, BF16), (gfeat, BF16), (gbias, F32), (gstitch, F32))
        ],
        scratch_shapes=[
            pltpu.VMEM((WIDEN_SLOTS, block, width), BF16),
            pltpu.VMEM((WIDEN_SLOTS, block, width), F32),
            pltpu.VMEM(mixed.shape, BF16),
            pltpu.VMEM(gfeat.shape, BF16),
            pltpu.SemaphoreType.DMA((WIDEN_SLOTS,)),
            pltpu.SemaphoreType.DMA((WIDEN_SLOTS,)),
            pltpu.SemaphoreType.DMA((4,)),
        ],
        compiler_params=pltpu.CompilerParams(vmem_limit_bytes=60 * 1024 * 1024),
        cost_estimate=pl.CostEstimate(
            flops=tall * width, bytes_accessed=6 * tall * width + 2 * moved, transcendentals=0
        ),
        name="finish",
    )(low, mixed, gfeat, gbias, gstitch)


def fused_plan(mesh):
    def per_device(features, weights, bias, stitch, cotangent, crop_counts, row_mask, flags):
        rows, deep = features.shape[1:]
        width = weights.shape[2]
        mixed, gfeat, gwt, gbias, gstitch, _, _ = fused_call(
            features, weights, cotangent, bias, stitch,
            crop_counts.reshape(1, -1), row_mask.reshape(-1, min(128, rows // 6)), flags,
        )
        grad_weights, mixed, gfeat, gbias, gstitch = finish(
            gwt.reshape(-1, width), mixed, gfeat, gbias, gstitch
        )
        return mixed, gfeat, grad_weights.reshape(2, ZED * 2 * deep, width), gbias, gstitch

    return per_device


def plan_for(mesh):
    if mesh.shape["batch"] == 4 and mesh.shape["mp"] == 2 * ZED:
        return fused_plan(mesh)
    return generic_plan(mesh)


def solution(mesh):
    in_specs = (
        P(None, "batch", "mp"),
        P(None, None, "mp"),
        P(None, "mp"),
        P(None, None, "mp"),
        P(None, "batch", "mp"),
        P("batch"),
        P("batch"),
        P(),
    )
    out_specs = (
        P(None, "batch", "mp"),
        P(None, "batch", "mp"),
        P(None, None, "mp"),
        P(None, "mp"),
        P(None, None, "mp"),
    )
    return jax.shard_map(
        plan_for(mesh), mesh=mesh, in_specs=in_specs, out_specs=out_specs, check_vma=False
    )
```

```python
import collections
import functools

import jax
import jax.numpy as jnp
from jax import lax
from jax.experimental import pallas as pl
from jax.experimental.pallas import tpu as pltpu
from jax.sharding import PartitionSpec as P

FLAG_GROUPS = 8
OUTER = 4


def row_weights(counts, mask):
    ends = jnp.cumsum(counts)
    starts = ends - counts
    index = lax.broadcasted_iota(jnp.int32, (mask.shape[0], counts.shape[0]), 0)
    inside = (index >= starts[None, :]) & (index < ends[None, :])
    count_row = jnp.sum(jnp.where(inside, counts[None, :], 0), axis=1)
    live = (count_row > 0) & (mask == 1)
    return jnp.where(live, 1.0 / jnp.maximum(count_row, 1).astype(jnp.float32), 0.0)


def project_bias(task_bias, flags):
    local_width = task_bias.shape[2]
    channel = lax.axis_index("mp") * local_width + lax.broadcasted_iota(
        jnp.int32, (local_width, FLAG_GROUPS), 0
    )
    member = (
        channel % FLAG_GROUPS == lax.broadcasted_iota(jnp.int32, (local_width, FLAG_GROUPS), 1)
    ).astype(jnp.float32)
    dots = jnp.dot(task_bias[0] * task_bias[1], member, precision=lax.Precision.HIGHEST)
    norms = jnp.einsum(
        "stc,cg->stg", task_bias * task_bias, member, precision=lax.Precision.HIGHEST
    )
    dots, norms = lax.psum((dots, norms), "mp")
    flag = flags.astype(jnp.float32)
    coef_first = jnp.dot(
        flag[0] * dots / (norms[1] + 1e-06), member.T, precision=lax.Precision.HIGHEST
    )
    coef_second = jnp.dot(
        flag[1] * dots / (norms[0] + 1e-06), member.T, precision=lax.Precision.HIGHEST
    )
    first = task_bias[0] - coef_first * task_bias[1]
    second = task_bias[1] - coef_second * task_bias[0]
    return first + second


def generic_plan(mesh):
    n_mp = mesh.shape["mp"]
    n_batch = mesh.shape["batch"]
    inner = n_mp // OUTER
    inner_groups = [[o * inner + i for i in range(inner)] for o in range(OUTER)]
    outer_groups = [[o * inner + i for o in range(OUTER)] for i in range(inner)]

    def per_device(features, weights, bias, stitch, cotangent, crop_counts, row_mask, flags):
        rows = features.shape[1]
        width = weights.shape[2]
        depth = features.shape[2] * inner
        held = lax.all_gather(
            features, "mp", axis=2, tiled=True, axis_index_groups=inner_groups
        )
        split = weights.reshape(2, OUTER, depth, width)
        block = lax.all_to_all(
            split, "mp", split_axis=1, concat_axis=1, axis_index_groups=outer_groups
        )
        block = block.reshape(2, OUTER, depth, width)
        part = jnp.einsum("trk,tokc->otrc", held, block, preferred_element_type=jnp.float32)
        linear = lax.psum_scatter(
            part.astype(jnp.bfloat16),
            "mp",
            scatter_dimension=0,
            axis_index_groups=outer_groups,
        ).astype(jnp.float32)
        pre = linear + bias[:, None, :]
        hidden, gelu_back = jax.vjp(lambda v: jax.nn.gelu(v, approximate=False), pre)
        mixed = stitch[:, 0, None, :] * hidden[0][None] + stitch[:, 1, None, :] * hidden[1][None]
        scale_rows = row_weights(crop_counts, row_mask)
        grad_out = cotangent.astype(jnp.float32) * scale_rows[None, :, None]
        first_task = gelu_back(stitch[0][:, None, :] * grad_out[0][None])[0]
        second_task = gelu_back(stitch[1][:, None, :] * grad_out[1][None])[0]
        task_bias = jnp.stack([jnp.sum(first_task, axis=1), jnp.sum(second_task, axis=1)])
        grad_linear = (first_task + second_task).astype(jnp.bfloat16)
        grad_stitch = jnp.sum(grad_out[:, None] * hidden[None], axis=2)
        every = lax.all_gather(grad_linear, "mp", axis_index_groups=outer_groups)
        grad_part = jnp.einsum(
            "otrc,tokc->trk", every, block, preferred_element_type=jnp.float32
        )
        grad_part = grad_part.astype(jnp.bfloat16).reshape(2, rows, inner, depth // inner)
        grad_features = lax.psum_scatter(
            grad_part.transpose(2, 0, 1, 3),
            "mp",
            scatter_dimension=0,
            axis_index_groups=inner_groups,
        )
        weight_part = jnp.einsum(
            "trk,otrc->otkc", held, every, preferred_element_type=jnp.float32
        )
        weight_part = weight_part.astype(jnp.bfloat16).reshape(
            OUTER, 2, n_batch, depth // n_batch, width
        )
        share = lax.psum_scatter(
            weight_part.transpose(2, 0, 1, 3, 4), "batch", scatter_dimension=0
        )
        share = lax.all_to_all(
            share, "mp", split_axis=0, concat_axis=0, axis_index_groups=outer_groups
        )
        share = share.reshape(OUTER, 2, depth // n_batch, width)
        whole = lax.all_gather(share, "batch")
        grad_weights = whole.transpose(2, 1, 0, 3, 4).reshape(2, OUTER * depth, width)
        task_bias, grad_stitch = lax.psum((task_bias, grad_stitch), "batch")
        grad_bias = project_bias(task_bias, flags)
        return (
            mixed.astype(jnp.bfloat16),
            grad_features.astype(jnp.bfloat16),
            grad_weights.astype(jnp.float32),
            grad_bias,
            grad_stitch,
        )

    return per_device


MESH = pl.DeviceIdType.MESH
BF16 = jnp.bfloat16
F32 = jnp.float32
ZED = 4
HALVES = 2
PHASES = 4
RING = 10
BAND = 32
SUB = 2
PRODUCTS = 8
SUM_LAG = 2
GATHER_LAG = 1
HELD = 3
WIDEN_BLOCKS = 12
WIDEN_SLOTS = 4

DX_TIMES = (22, 24, 26, 28, 30, 32, 46, 48, 50, 52, 55, 61)
DX_BEGINS = (25, 27, 29, 31, 33, 35, 49, 52, 58, 62, 64, 66)
DX_ENDS = (26, 28, 30, 32, 34, 36, 50, 53, 61, 63, 65, 74)
ONES = (21, 23, 29, 33, 37, 41, 45, 47, 49, 57, 58, 59)
TWOS = (23, 27, 31, 35, 39, 43, 46, 48, 50, 58, 59, 60)
THREES = (24, 30, 34, 38, 42, 46, 48, 52, 55, 60, 61, 64)
FOURS = (29, 33, 37, 41, 45, 47, 51, 54, 57, 63, 66, 67)
FIVES = (31, 34, 38, 43, 47, 51, 56, 61, 62, 66, 68, 71)
SIXES = (34, 39, 43, 50, 51, 52, 60, 62, 64, 69, 72, 76)
W_STRIPS = {2: (9, 11, 12, 13, 14, 15), 3: (20, 21, 22, 23, 24, 25)}
W_ACROSS = {1: (4, 6, 7), 2: (19, 20, 21), 3: (29, 29, 32)}
W_CORES = {1: (8, 9, 10), 2: (20, 21, 22), 3: (33, 34, 35)}


Part = collections.namedtuple("Part", ("u", "p", "i", "t", "h", "slot", "prod", "buf"))
Tile = collections.namedtuple("Tile", ("g", "p", "t", "h", "j", "buf", "trio", "quad"))


def half(value):
    return value.astype(BF16)


def wide(value):
    return value.astype(F32)


def fused_kernel(
    rows, deep, width, chunk,
    feat, wts, cot, bias, stitch, counts, mask, flags,
    mixed, gfeat, gwt, gbias, gstitch, xn, dxn,
    wv, gl, rs, h0, xc, pf, cc, mx, own, dsend, dfetch, dout,
    xsrc, xt, cstage, cland, xstage, xland, kept, zstage,
    scale, stat, sums, sums_land, prods, prods_land,
    rs_send, rs_recv, ag_send, ag_recv, xs_send, xs_recv,
    wz_send, wz_recv, wx_send, wx_recv, wc_send, wc_recv, wl,
    xf, cf, mxs, dx_send, dx_recv, df, dod,
    tile_in, c_send, c_recv, x_send, x_recv, z_send, z_recv, zl, zx_send,
    ax_send, ax_recv, ac_send, ac_recv, t_send, t_recv,
):
    batch, mp = lax.axis_index("batch"), lax.axis_index("mp")
    z, y = mp // 2, mp % 2
    x, c = batch // 2, batch % 2
    up = {"mp": mp + 2}
    down = {"mp": mp - 2}
    across_y = {"mp": 2 * z + 1 - y}
    across_x = {"batch": 2 * (1 - x) + c}
    across_c = {"batch": 2 * x + 1 - c}

    def at_z(other):
        return {"mp": 2 * other + y}

    others = (3 - z, (z + 2) % 4, z + 1 - 2 * (z % 2))

    n_chunk = rows // chunk
    total = PHASES * n_chunk
    part = chunk // SUB
    n_part = rows // part
    parts = PHASES * n_part
    images = counts.shape[1]
    hw = width // HALVES
    kz = 2 * deep
    quarter = deep // 2
    tile = deep // 3
    strip = quarter // 6
    xw = hw // 2

    def mult(value, unit):
        return pl.multiple_of(value, unit)

    def remote(src, dst, send, recv, device):
        return pltpu.make_async_remote_copy(
            src_ref=src, dst_ref=dst, send_sem=send, recv_sem=recv,
            device_id=device, device_id_type=MESH,
        )

    def cols(b):
        return pl.ds(mult(b * hw, hw), hw)

    def chunk_rows(i):
        return pl.ds(mult(i * chunk, chunk), chunk)

    def part_rows(i):
        return pl.ds(mult(i * part, part), part)

    def tower(p):
        t = jnp.where(p >= HALVES, 1, 0)
        return t, p - HALVES * t

    def x_copy(t, i):
        e = t * n_chunk + i
        return remote(
            feat.at[t, chunk_rows(i)], xn.at[t, chunk_rows(i)],
            xs_send.at[e], xs_recv.at[e], across_y,
        )

    def x_fetch(t, i, buf):
        return (
            pltpu.make_async_copy(
                feat.at[t, chunk_rows(i)],
                xc.at[buf, :, pl.ds(mult(deep * y, deep), deep)], xf.at[buf, 0],
            ),
            pltpu.make_async_copy(
                xn.at[t, chunk_rows(i)],
                xc.at[buf, :, pl.ds(mult(deep * (1 - y), deep), deep)], xf.at[buf, 1],
            ),
        )

    def cot_fetch(h, i, buf):
        return pltpu.make_async_copy(
            cot.at[:, part_rows(i), cols(h)], cc.at[buf], cf.at[buf]
        )

    def w_own(p):
        t, h = tower(p)
        return pltpu.make_async_copy(
            wts.at[t, pl.ds(mult(kz * z, kz), kz), cols(h)], wv.at[p, :, cols(z)], wl.at[p],
        )

    def w_rows():
        return pl.ds(mult(deep * c + quarter * x, quarter), quarter)

    def w_z(p, to):
        t, h = tower(p)
        return remote(
            wts.at[
                t, pl.ds(mult(kz * to + deep * c + quarter * x, quarter), quarter), cols(h)
            ],
            wv.at[p, w_rows(), cols(z)],
            wz_send.at[p, to], wz_recv.at[p, z], at_z(to),
        )

    def w_z_strip(p, to, r):
        t, h = tower(p)
        at = deep * c + quarter * x + strip * r
        return remote(
            wts.at[t, pl.ds(mult(kz * to + at, strip), strip), cols(h)],
            wv.at[p, pl.ds(mult(at, strip), strip), cols(z)],
            wz_send.at[p, to], wz_recv.at[p, z], at_z(to),
        )

    def w_z_in(p, frm):
        here = wv.at[p, w_rows(), cols(frm)]
        return remote(here, here, wz_send.at[p, frm], wz_recv.at[p, frm], at_z(frm))

    def w_x(p, b):
        here = wv.at[p, w_rows(), cols(b)]
        return remote(here, here, wx_send.at[p, b], wx_recv.at[p, b], across_x)

    def w_x_in(p, b):
        here = wv.at[
            p, pl.ds(mult(deep * c + quarter * (1 - x), quarter), quarter), cols(b)
        ]
        return remote(here, here, wx_send.at[p, b], wx_recv.at[p, b], across_x)

    def w_c(p, b):
        here = wv.at[p, pl.ds(mult(deep * c, deep), deep), cols(b)]
        return remote(here, here, wc_send.at[p, b], wc_recv.at[p, b], across_c)

    def w_c_in(p, b):
        here = wv.at[p, pl.ds(mult(deep * (1 - c), deep), deep), cols(b)]
        return remote(here, here, wc_send.at[p, b], wc_recv.at[p, b], across_c)

    def rs_up(slot, zz):
        run = rs.at[slot, zz + 2 : ZED + 1]
        return remote(run, run, rs_send.at[slot, 0], rs_recv.at[slot, 0], up)

    def rs_down(slot, zz):
        run = rs.at[slot, 0:zz]
        return remote(run, run, rs_send.at[slot, 1], rs_recv.at[slot, 1], down)

    def rs_from_below(slot, zz):
        run = rs.at[slot, zz + 1 : ZED + 1]
        return remote(run, run, rs_send.at[slot, 0], rs_recv.at[slot, 0], down)

    def rs_from_above(slot, zz):
        run = rs.at[slot, 0 : zz + 1]
        return remote(run, run, rs_send.at[slot, 1], rs_recv.at[slot, 1], up)

    def at_place(first, last, do):
        for zz in range(first, last + 1):
            @pl.when(z == zz)
            def _(zz=zz):
                do(zz)

    def ag(at, b, going, device):
        here = gl.at[at.p, part_rows(at.i), cols(b)]
        return remote(
            here, here, ag_send.at[at.slot, going * ZED + b], ag_recv.at[at.slot, b], device
        )

    def dx_copy(t, i, buf):
        return remote(
            dsend.at[buf], dxn.at[t, chunk_rows(i)],
            dx_send.at[buf], dx_recv.at[t * n_chunk + i], across_y,
        )

    def dx_fetch(t, i):
        return pltpu.make_async_copy(dxn.at[t, chunk_rows(i)], dfetch, df.at[0])

    def dx_out(t, i):
        return pltpu.make_async_copy(dout, gfeat.at[t, chunk_rows(i)], dod.at[0])

    def mixed_out(h, i, buf):
        return pltpu.make_async_copy(
            mx.at[buf], mixed.at[:, part_rows(i), cols(h)], mxs.at[buf]
        )

    def tile_fetch(t, j, hk, start):
        lanes = pl.ds(mult(tile * j, tile), tile)
        near = pltpu.make_async_copy(feat.at[t, :, lanes], xsrc, tile_in.at[0])
        if not start:
            near.wait()
            return

        @pl.when(hk == y)
        def _():
            near.start()

        @pl.when(hk != y)
        def _():
            pltpu.make_async_copy(xn.at[t, :, lanes], xsrc, tile_in.at[0]).start()

    def core_copy(g):
        return remote(cstage, cland.at[g.buf], c_send.at[0], c_recv.at[g.buf], across_c)

    def across_copy(g, b):
        return remote(
            xstage.at[g.trio, b], xland.at[g.quad, b],
            x_send.at[g.trio, b], x_recv.at[g.quad, b], across_x,
        )

    def piece(g, source, core, lanes, n_lanes):
        return gwt.at[
            g.t, source,
            pl.ds(mult(deep * core + tile * g.j, tile), tile),
            pl.ds(mult(hw * g.h + lanes, xw), n_lanes),
        ]

    def z_copy(g, to):
        return remote(
            zstage.at[g.trio, to], piece(g, z, c, xw * x, xw),
            z_send.at[g.trio, to], z_recv.at[g.g, z], at_z(to),
        )

    def z_in(g, frm):
        here = piece(g, frm, c, xw * x, xw)
        return remote(here, here, z_send.at[g.trio, frm], z_recv.at[g.g, frm], at_z(frm))

    def z_own(g):
        return pltpu.make_async_copy(
            zstage.at[g.trio, z], piece(g, z, c, xw * x, xw), zl.at[g.trio]
        )

    def ax_own(g):
        return remote(
            zstage.at[g.trio, z], piece(g, z, c, xw * x, xw),
            zx_send.at[g.trio], ax_recv.at[g.g, z], across_x,
        )

    def ax_copy(g, b):
        here = piece(g, b, c, xw * x, xw)
        return remote(here, here, ax_send.at[g.g, b], ax_recv.at[g.g, b], across_x)

    def ax_in(g, b):
        here = piece(g, b, c, xw * (1 - x), xw)
        return remote(here, here, ax_send.at[g.g, b], ax_recv.at[g.g, b], across_x)

    def ac_copy(g, b):
        here = piece(g, b, c, 0, hw)
        return remote(here, here, ac_send.at[g.g, b], ac_recv.at[g.g, b], across_c)

    def ac_in(g, b):
        here = piece(g, b, 1 - c, 0, hw)
        return remote(here, here, ac_send.at[g.g, b], ac_recv.at[g.g, b], across_c)

    def sum_copy(stage, device):
        return remote(
            sums.at[stage], sums_land.at[stage], t_send.at[stage], t_recv.at[stage], device
        )

    def prod_y():
        return remote(prods.at[0], prods_land.at[ZED], t_send.at[2], t_recv.at[2], across_y)

    def prod_z(to):
        return remote(
            prods.at[1], prods_land.at[z], t_send.at[3 + to], t_recv.at[3 + z], at_z(to)
        )

    def prod_z_in(frm):
        here = prods_land.at[frm]
        return remote(here, here, t_send.at[3 + frm], t_recv.at[3 + frm], at_z(frm))

    barrier = pltpu.get_barrier_semaphore()
    for device in [at_z(o) for o in others] + [across_y, across_x, across_c]:
        pl.semaphore_signal(barrier, inc=1, device_id=device, device_id_type=MESH)
    pl.semaphore_wait(barrier, 6)

    for to in others:
        w_z(0, to).start()
    x_copy(0, 0).start()
    x_copy(0, 1).start()
    w_own(0).start()
    cot_fetch(0, 0, 0).start()

    image_row = lax.broadcasted_iota(jnp.int32, (images, images), 0)
    image_col = lax.broadcasted_iota(jnp.int32, (images, images), 1)
    crops = counts[...].astype(F32)
    ends = jnp.dot(
        jnp.broadcast_to(crops, (8, images)), (image_row <= image_col).astype(F32),
        precision=lax.Precision.HIGHEST, preferred_element_type=F32,
    )[0:1]
    starts = ends - crops
    block = mask.shape[1]
    lane = scale.shape[1]

    for r in range(rows // block):
        index = (
            lax.broadcasted_iota(jnp.int32, (block, images), 0) + r * block
        ).astype(F32)
        inside = (index >= starts) & (index < ends)
        count_row = jnp.sum(jnp.where(inside, crops, 0.0), axis=1, keepdims=True)
        diagonal = lax.broadcasted_iota(jnp.int32, (block, block), 0) == (
            lax.broadcasted_iota(jnp.int32, (block, block), 1)
        )
        usable = jnp.sum(
            jnp.where(diagonal, mask[r : r + 1, :].astype(F32), 0.0),
            axis=1, keepdims=True,
        )
        live = (count_row > 0.0) & (usable == 1.0)
        share = jnp.where(live, 1.0 / jnp.maximum(count_row, 1.0), 0.0)
        scale[r * block : (r + 1) * block, :] = jnp.broadcast_to(share, (block, lane))

    for frm in others:
        w_z_in(0, frm).wait_recv()
        w_x(0, frm).start()
    for to in others:
        w_z(1, to).start()
    w_own(1).start()
    for frm in others:
        w_x_in(0, frm).wait_recv()
        w_c(0, frm).start()
    x_copy(0, 0).wait_recv()
    for copy in x_fetch(0, 0, 0):
        copy.start()

    def final(at, later):
        p, i, slot, t, h, buf = at.p, at.i, at.slot, at.t, at.h, at.buf
        cot_fetch(h, i, buf).wait()

        @pl.when(at.u >= 2 * n_part + 2)
        def _():
            mixed_out(h, i, buf).wait()

        @pl.when(i == 0)
        def _():
            stat[p] = jnp.zeros(stat.shape[1:], F32)

        lanes = cols(h)
        shift = bias[pl.ds(t, 1), lanes]
        st = [stitch[s, pl.ds(t, 1), lanes] for s in range(2)]
        band = min(BAND, part)

        def step(r, carry):
            here = part_rows_of(r, band)
            there = pl.ds(mult(i * part + r * band, band), band)
            value = pf[at.prod, z, here, :]
            below = wide(rs[slot, z + 1, here, :])
            above = wide(rs[slot, z, here, :])
            value = value + jnp.where(z > 0, below, 0.0) + jnp.where(z < ZED - 1, above, 0.0)
            pre = value + shift
            phi = 0.5 * (1.0 + lax.erf(pre * 0.7071067811865476))
            hidden = pre * phi
            slope = phi + pre * (jnp.exp(-0.5 * pre * pre) * 0.3989422804014327)
            weight = scale[there, 0:1]
            first = wide(cc[buf, 0, here, :]) * weight
            second = wide(cc[buf, 1, here, :]) * weight
            back0 = st[0] * first * slope
            back1 = st[1] * second * slope
            gl[p, there, cols(z)] = half(back0 + back1)

            def fold(v):
                return jnp.sum(v.reshape(band // 8, 8, hw), axis=0)

            stat[p, 0] += fold(back0)
            stat[p, 1] += fold(back1)
            stat[p, 2] += fold(first * hidden)
            stat[p, 3] += fold(second * hidden)

            @pl.when(t == 0)
            def _():
                h0[h, there, :] = hidden

            @pl.when(t == 1)
            def _():
                before = h0[h, there, :]
                for s in range(2):
                    mx[buf, s, here, :] = half(
                        stitch[s, 0:1, lanes] * before + st[s] * hidden
                    )

            return carry

        lax.fori_loop(0, part // band, step, 0)

        @pl.when(z < ZED - 1)
        def _():
            ag(at, z, 0, up).start()

        @pl.when(z > 0)
        def _():
            ag(at, z, 1, down).start()

        @pl.when(t == 1)
        def _():
            mixed_out(h, i, buf).start()

        @pl.when(at.u + 1 < parts)
        def _():
            cot_fetch(later.h, later.i, later.buf).start()

    def part_rows_of(r, band):
        return pl.ds(mult(r * band, band), band)

    def forward_ag(at, far):
        @pl.when((at.u >= 0) & (at.u < parts))
        def _():
            @pl.when(z - far >= 0)
            def _():
                ag(at, z - far, 0, up).wait_recv()

                @pl.when(z < ZED - 1)
                def _():
                    ag(at, z - far, 0, up).start()

            @pl.when(z + far < ZED)
            def _():
                ag(at, z + far, 1, down).wait_recv()

                @pl.when(z > 0)
                def _():
                    ag(at, z + far, 1, down).start()

    def dx_part(t, i, hk):
        there = chunk_rows(i)
        krows = pl.ds(mult(deep * hk, deep), deep)
        acc = None
        for h in range(HALVES):
            term = lax.dot_general(
                gl[2 * t + h, there, :], wv[2 * t + h, krows, :],
                (((1,), (1,)), ((), ())), preferred_element_type=F32,
            )
            acc = term if acc is None else acc + term
        return acc

    def dx_step(t, i, buf):
        @pl.when((i >= HELD) | (t > 0))
        def _():
            dx_copy(t, i, buf).wait_send()

        dsend[buf] = half(dx_part(t, i, 1 - y))
        dx_copy(t, i, buf).start()
        own[buf] = dx_part(t, i, y)

    def dx_begin(t, i, buf):
        dx_copy(t, i, buf).wait_recv()
        dx_fetch(t, i).start()

    def dx_final(t, i, buf):
        @pl.when((i >= 1) | (t > 0))
        def _():
            dx_out(t, i).wait()

        dx_fetch(t, i).wait()

        def step(j, inner):
            lanes = pl.ds(mult(tile * j, tile), tile)
            dout[:, lanes] = half(own[buf, :, lanes] + wide(dfetch[:, lanes]))
            return inner

        lax.fori_loop(0, 3, step, 0)
        dx_out(t, i).start()

    def listed(u, times, do):
        e, hit = 0, False
        for index, time in enumerate(times):
            same = u == time
            e = jnp.where(same, index, e)
            hit = hit | same

        @pl.when(hit)
        def _():
            do(e)

    def chunk_of(do):
        def run(e):
            t = jnp.where(e >= n_chunk, 1, 0)
            do(t, e - n_chunk * t, lax.rem(e, HELD))

        return run

    def turn():
        lanes_at_once = min(128, tile)

        def step(q, carry):
            lanes = pl.ds(mult(q * lanes_at_once, lanes_at_once), lanes_at_once)
            xt[lanes, :] = xsrc[:, lanes].T
            return carry

        lax.fori_loop(0, tile // lanes_at_once, step, 0)

    def tile_dot(g):
        return jnp.dot(xt[...], gl[g.p], preferred_element_type=F32)

    def stage_one(g):
        tile_fetch(g.t, g.j, 1 - c, False)
        turn()
        tile_fetch(g.t, g.j, c, True)
        cstage[...] = half(tile_dot(g))
        core_copy(g).start()

    def stage_two(g):
        tile_fetch(g.t, g.j, c, False)
        turn()

        @pl.when(g.j < 2)
        def _():
            tile_fetch(g.t, g.j + 1, 1 - c, True)

        core_copy(g).wait()
        product = tile_dot(g)
        for b in range(ZED):
            block = product[:, b * hw : (b + 1) * hw] + wide(
                cland[g.buf, :, b * hw : (b + 1) * hw]
            )
            left, right = block[:, :xw], block[:, xw:]
            kept[g.trio, b] = jnp.where(x == 0, left, right)
            xstage[g.trio, b] = half(jnp.where(x == 0, right, left))

        def send(q, carry):
            across_copy(g, lax.rem(z + 3 + 3 * q, ZED)).start()
            return carry

        lax.fori_loop(0, ZED, send, 0)

    def stage_three(g):
        @pl.when(g.g >= 3)
        def _():
            for to in others:
                z_copy(g, to).wait_send()
            ax_own(g).wait_send()

        def add(b):
            across_copy(g, b).wait()
            zstage[g.trio, b] = half(kept[g.trio, b] + wide(xland[g.quad, b]))

        def step(q, carry):
            b = lax.rem(z + 3 + 3 * q, ZED)
            add(b)
            z_copy(g, b).start()
            return carry

        lax.fori_loop(0, ZED - 1, step, 0)
        add(z)
        z_own(g).start()
        ax_own(g).start()

    def stage_four(g):
        def step(q, carry):
            b = lax.rem(z + 1 + q, ZED)
            z_in(g, b).wait_recv()
            ax_copy(g, b).start()
            return carry

        lax.fori_loop(0, ZED - 1, step, 0)
        z_own(g).wait()

    def stage_five(g):
        def step(q, carry):
            b = lax.rem(z + q, ZED)
            ax_in(g, b).wait_recv()
            ac_copy(g, b).start()
            return carry

        lax.fori_loop(0, ZED, step, 0)

    def stage_six(g):
        def step(b, carry):
            ac_in(g, b).wait_recv()
            return carry

        lax.fori_loop(0, ZED, step, 0)

    def tile_of(g):
        p = lax.div(g, 3)
        t, h = tower(p)
        return Tile(
            g=g, p=p, t=t, h=h, j=g - 3 * p,
            buf=lax.rem(g, 2), trio=g - 3 * p, quad=lax.rem(g, 4),
        )

    def tile_in_hand(do):
        return lambda g: do(tile_of(g))

    def body(u, carry):
        p0 = lax.div(u, n_part)
        i0 = u - p0 * n_part
        slot0, prod0 = lax.rem(u, RING), lax.rem(u, PRODUCTS)
        buf0 = lax.rem(u, 2)

        def before(lag):
            if isinstance(lag, int):
                whole, left = divmod(lag, n_part)
            else:
                whole, left = 0, lag
            under = i0 < left
            p = p0 - whole - jnp.where(under, 1, 0)
            i = i0 - left + jnp.where(under, n_part, 0)
            in_ring = lag % RING if isinstance(lag, int) else lag
            in_prods = lag % PRODUCTS if isinstance(lag, int) else lag
            slot = slot0 - in_ring + jnp.where(slot0 < in_ring, RING, 0)
            prod = prod0 - in_prods + jnp.where(prod0 < in_prods, PRODUCTS, 0)
            t, h = tower(p)
            return Part(u=u - lag, p=p, i=i, t=t, h=h, slot=slot, prod=prod, buf=lax.rem(i, 2))

        retired = max(5, 3 * SUM_LAG)

        @pl.when((u >= retired) & (u < parts + retired))
        def _():
            slot = before(retired).slot
            at_place(0, ZED - 2, lambda zz: rs_up(slot, zz).wait_send())
            at_place(1, ZED - 1, lambda zz: rs_down(slot, zz).wait_send())

        @pl.when((u >= RING) & (u < parts + RING))
        def _():
            at = before(RING)

            def step(b, inner):
                @pl.when((z < ZED - 1) & (b <= z))
                def _():
                    ag(at, b, 0, up).wait_send()

                @pl.when((z > 0) & (b >= z))
                def _():
                    ag(at, b, 1, down).wait_send()

                return inner

            lax.fori_loop(0, ZED, step, 0)

        ck = lax.div(i0, SUB)
        fresh = ck * SUB == i0
        t0, h0_ = tower(p0)
        xbuf = lax.rem(ck, 2)

        @pl.when((u < parts) & fresh)
        def _():
            @pl.when(i0 == 0)
            def _():
                w_own(p0).wait()
                for frm in others:
                    w_c_in(p0, frm).wait_recv()

            for copy in x_fetch(t0, ck, xbuf):
                copy.wait()

            product = jnp.dot(xc[xbuf], wv[p0], preferred_element_type=F32)
            for b in range(ZED):
                for s in range(SUB):
                    pf[prod0 + s, b] = product[
                        s * part : (s + 1) * part, b * hw : (b + 1) * hw
                    ]

        going_up = before(SUM_LAG * z)

        @pl.when((going_up.u >= 0) & (going_up.u < parts))
        def _():
            slot, prod = going_up.slot, going_up.prod
            at_place(1, ZED - 1, lambda zz: rs_from_below(slot, zz).wait_recv())

            @pl.when(z == 0)
            def _():
                for b in range(1, ZED):
                    rs[slot, b + 1] = half(pf[prod, b])

            @pl.when(z > 0)
            def _():
                def step(b, inner):
                    rs[slot, b + 1] = half(wide(rs[slot, b + 1]) + pf[prod, b])
                    return inner

                lax.fori_loop(z + 1, ZED, step, 0)

            at_place(0, ZED - 2, lambda zz: rs_up(slot, zz).start())

        going_down = before(SUM_LAG * (ZED - 1 - z))

        @pl.when((going_down.u >= 0) & (going_down.u < parts))
        def _():
            slot, prod = going_down.slot, going_down.prod
            at_place(0, ZED - 2, lambda zz: rs_from_above(slot, zz).wait_recv())

            @pl.when(z == ZED - 1)
            def _():
                for b in range(ZED - 1):
                    rs[slot, b] = half(pf[prod, b])

            @pl.when(z < ZED - 1)
            def _():
                def step(b, inner):
                    rs[slot, b] = half(wide(rs[slot, b]) + pf[prod, b])
                    return inner

                lax.fori_loop(0, z, step, 0)

            at_place(1, ZED - 1, lambda zz: rs_down(slot, zz).start())

        @pl.when(fresh & (u + 2 * SUB < 2 * n_part))
        def _():
            k = p0 * n_chunk + ck + 2
            over = jnp.where(k >= n_chunk, 1, 0)
            x_copy(over, k - over * n_chunk).start()

        @pl.when(fresh & (u + SUB < parts))
        def _():
            wrap = jnp.where(ck + 1 == n_chunk, 1, 0)
            i = ck + 1 - wrap * n_chunk
            t, h = tower(p0 + wrap)

            @pl.when(h == 0)
            def _():
                x_copy(t, i).wait_recv()

            for copy in x_fetch(t, i, lax.rem(i, 2)):
                copy.start()

        summed = 3 * SUM_LAG

        @pl.when((u >= summed) & (u < parts + summed))
        def _():
            final(before(summed), before(summed - 1))

        for far in range(1, ZED):
            forward_ag(before(summed + far * GATHER_LAG), far)

        listed(u, DX_BEGINS, chunk_of(dx_begin))
        listed(u, DX_ENDS, chunk_of(dx_final))
        listed(u, DX_TIMES, chunk_of(dx_step))

        listed(u, THREES, tile_in_hand(stage_three))
        listed(u, TWOS, tile_in_hand(stage_two))
        listed(u, ONES, tile_in_hand(stage_one))
        listed(u, FOURS, tile_in_hand(stage_four))
        listed(u, FIVES, tile_in_hand(stage_five))
        listed(u, SIXES, tile_in_hand(stage_six))

        def first_fetch(p):
            tile_fetch(lax.div(p, HALVES), 0, 1 - c, True)

        listed(u, [time - 1 for time in ONES[::3]], first_fetch)

        for p, times in W_STRIPS.items():
            def send_strip(r, p=p):
                for to in others:
                    w_z_strip(p, to, r).start()

                @pl.when(r == 0)
                def _():
                    w_own(p).start()

            listed(u, times, send_strip)

        for p, times in W_ACROSS.items():
            for q, time in enumerate(times):
                @pl.when(u == time)
                def _(p=p, q=q):
                    w_z_in(p, others[q]).wait_recv()
                    w_x(p, others[q]).start()

        for p, times in W_CORES.items():
            for q, time in enumerate(times):
                @pl.when(u == time)
                def _(p=p, q=q):
                    w_x_in(p, others[q]).wait_recv()
                    w_c(p, others[q]).start()

        @pl.when(u == parts + summed + 0)
        def _():
            for p in range(PHASES):
                t, h = p // HALVES, p % HALVES
                for s in range(2):
                    for what in range(2):
                        sums[0, pl.ds(4 * what + 2 * s + t, 1), h * hw : (h + 1) * hw] = jnp.sum(
                            stat[p, 2 * what + s], axis=0, keepdims=True
                        )
            sum_copy(0, across_c).start()

        @pl.when(u == parts + summed + 1)
        def _():
            sum_copy(0, across_c).wait()
            sums[1] = sums[0] + sums_land[0]
            sum_copy(1, across_x).start()

        @pl.when(u == parts + summed + 2)
        def _():
            sum_copy(1, across_x).wait()
            both = sums[1] + sums_land[1]
            sums[2] = both
            member = (
                lax.broadcasted_iota(jnp.int32, (width, lane), 0) % FLAG_GROUPS
                == lax.broadcasted_iota(jnp.int32, (width, lane), 1) % FLAG_GROUPS
            ).astype(F32)
            bias_rows = both[0:4]
            inner = both[0:2] * both[2:4]
            stack = jnp.concatenate([inner, bias_rows * bias_rows, inner], axis=0)
            prods[0] = jnp.dot(
                stack, member, precision=lax.Precision.HIGHEST, preferred_element_type=F32
            )
            prod_y().start()

        @pl.when(u == parts + summed + 3)
        def _():
            prod_y().wait()
            prods[1] = prods[0] + prods_land[ZED]
            for to in others:
                prod_z(to).start()

        @pl.when(u == parts + summed + 4)
        def _():
            for frm in others:
                prod_z_in(frm).wait_recv()
            prods_land[z] = prods[1]
            whole = prods_land[0] + prods_land[1] + prods_land[2] + prods_land[3]
            both = sums[2]
            group = lax.broadcasted_iota(jnp.int32, (1, lane), 1) % FLAG_GROUPS

            def over(row):
                return jnp.concatenate([row] * (width // lane), axis=1)

            def flag_row(s, t):
                row = jnp.zeros((1, lane), F32)
                for g in range(FLAG_GROUPS):
                    row = jnp.where(group == g, flags[s, t, g].astype(F32), row)
                return row

            for t in range(2):
                task0, task1 = both[t : t + 1], both[2 + t : 3 + t]
                dots = whole[t : t + 1]
                coef0 = over(flag_row(0, t) * dots / (whole[4 + t : 5 + t] + 1e-06))
                coef1 = over(flag_row(1, t) * dots / (whole[2 + t : 3 + t] + 1e-06))
                gbias[t : t + 1] = (task0 - coef0 * task1) + (task1 - coef1 * task0)
            for s in range(2):
                gstitch[s] = both[4 + 2 * s : 6 + 2 * s]

        return carry

    lax.fori_loop(0, max(SIXES + DX_ENDS) + 1, body, 0)

    last = 3 * PHASES - 1

    for g in (last - 2, last - 1, last):
        for to in others:
            z_copy(tile_of(g), to).wait_send()
        ax_own(tile_of(g)).wait_send()
    for i in range(n_chunk - HELD, n_chunk):
        dx_copy(1, i, (n_chunk + i) % HELD).wait_send()
    for i in (n_part - 2, n_part - 1):
        mixed_out(1, i, i % 2).wait()
    dx_out(1, n_chunk - 1).wait()

    def drain_tiles(g, carry):
        at = tile_of(g)
        for b in others:
            ax_copy(at, b).wait_send()
        for b in range(ZED):
            ac_copy(at, b).wait_send()
        return carry

    lax.fori_loop(0, last + 1, drain_tiles, 0)

    def drain_x(i, carry):
        x_copy(0, i).wait_send()
        x_copy(1, i).wait_send()
        return carry

    lax.fori_loop(0, n_chunk, drain_x, 0)

    def drain_w(p, carry):
        for to in others:
            w_z(p, to).wait_send()
            w_x(p, to).wait_send()
            w_c(p, to).wait_send()
        return carry

    lax.fori_loop(0, PHASES, drain_w, 0)
    for to in others:
        prod_z(to).wait_send()


def fused_call(feat, wts, cot, bias, stitch, counts, mask, flags):
    rows, deep, width = feat.shape[1], feat.shape[2], wts.shape[2]
    chunk = rows // 6
    part = chunk // SUB
    hw, kz, tile = width // 2, 2 * deep, deep // 3
    cat, xw = 4 * hw, width // 4
    lane = min(128, width)
    dma = pltpu.SemaphoreType.DMA
    anywhere = pl.BlockSpec(memory_space=pl.ANY)
    inside = pl.BlockSpec(memory_space=pltpu.VMEM)
    scalars = pl.BlockSpec(memory_space=pltpu.SMEM)

    def v(shape, kind=BF16):
        return pltpu.VMEM(shape, kind)

    out_shape = [
        jax.ShapeDtypeStruct((2, rows, width), BF16),
        jax.ShapeDtypeStruct((2, rows, deep), BF16),
        jax.ShapeDtypeStruct((2, ZED, kz, width), BF16),
        jax.ShapeDtypeStruct((2, width), F32),
        jax.ShapeDtypeStruct((2, 2, width), F32),
        jax.ShapeDtypeStruct((2, rows, deep), BF16),
        jax.ShapeDtypeStruct((2, rows, deep), BF16),
    ]
    scratch = [
        v((PHASES, kz, cat)),
        v((PHASES, rows, cat)),
        v((RING, 5, part, hw)),
        v((2, rows, hw), F32),
        v((2, chunk, kz)),
        v((PRODUCTS, ZED, part, hw), F32),
        v((2, 2, part, hw)),
        v((2, 2, part, hw)),
        v((HELD, chunk, deep), F32),
        v((HELD, chunk, deep)),
        v((chunk, deep)),
        v((chunk, deep)),
        v((rows, tile)),
        v((tile, rows)),
        v((tile, cat)),
        v((2, tile, cat)),
        v((3, ZED, tile, xw)),
        v((4, ZED, tile, xw)),
        v((3, ZED, tile, xw), F32),
        v((3, ZED, tile, xw)),
        v((rows, lane), F32),
        v((PHASES, 4, 8, hw), F32),
        v((3, 8, width), F32),
        v((2, 8, width), F32),
        v((2, 8, lane), F32),
        v((5, 8, lane), F32),
        dma((RING, 2)), dma((RING, 2)), dma((RING, 8)), dma((RING, 4)),
        dma((12,)), dma((12,)),
        dma((4, 4)), dma((4, 4)), dma((4, 4)), dma((4, 4)), dma((4, 4)), dma((4, 4)), dma((4,)),
        dma((2, 2)), dma((2,)), dma((2,)), dma((HELD,)), dma((12,)), dma((1,)), dma((1,)),
        dma((1,)), dma((1,)), dma((2,)), dma((3, 4)), dma((4, 4)), dma((3, 4)), dma((12, 4)),
        dma((3,)), dma((3,)),
        dma((12, 4)), dma((12, 4)), dma((12, 4)), dma((12, 4)), dma((8,)), dma((8,)),
    ]
    flops = 3 * 2 * 2 * rows * kz * cat * 2
    return pl.pallas_call(
        functools.partial(fused_kernel, rows, deep, width, chunk),
        out_shape=out_shape,
        in_specs=[anywhere] * 3 + [inside] * 4 + [scalars],
        out_specs=[anywhere] * 3 + [inside] * 2 + [anywhere] * 2,
        scratch_shapes=scratch,
        compiler_params=pltpu.CompilerParams(
            collective_id=0, has_side_effects=True, vmem_limit_bytes=64 * 1024 * 1024
        ),
        cost_estimate=pl.CostEstimate(
            flops=flops, bytes_accessed=200_000_000, transcendentals=2 * rows * width * 2
        ),
        name="cross_stitch_step",
    )(feat, wts, cot, bias, stitch, counts, mask, flags)


def finish_kernel(
    block, low, mixed, gfeat, gbias, gstitch,
    out, mixed_out, gfeat_out, gbias_out, gstitch_out,
    taken, given, held_mixed, held_gfeat, in_sem, out_sem, pass_sem,
):
    n_block = low.shape[0] // block
    fetched = (
        pltpu.make_async_copy(mixed, held_mixed, pass_sem.at[0]),
        pltpu.make_async_copy(gfeat, held_gfeat, pass_sem.at[1]),
    )
    passed = (
        pltpu.make_async_copy(held_mixed, mixed_out, pass_sem.at[2]),
        pltpu.make_async_copy(held_gfeat, gfeat_out, pass_sem.at[3]),
    )

    def take(i):
        return pltpu.make_async_copy(
            low.at[pl.ds(i * block, block)], taken.at[i % WIDEN_SLOTS], in_sem.at[i % WIDEN_SLOTS]
        )

    def give(i):
        return pltpu.make_async_copy(
            given.at[i % WIDEN_SLOTS], out.at[pl.ds(i * block, block)], out_sem.at[i % WIDEN_SLOTS]
        )

    for i in range(min(WIDEN_SLOTS, n_block)):
        take(i).start()
    for copy in fetched:
        copy.start()
    gbias_out[...] = gbias[...]
    gstitch_out[...] = gstitch[...]
    for i in range(n_block):
        slot = i % WIDEN_SLOTS
        take(i).wait()
        if i >= WIDEN_SLOTS:
            give(i - WIDEN_SLOTS).wait()
        given[slot] = wide(taken[slot])
        give(i).start()
        if i + WIDEN_SLOTS < n_block:
            take(i + WIDEN_SLOTS).start()
        if i == 2:
            for arrived, copy in zip(fetched, passed):
                arrived.wait()
                copy.start()
    for i in range(max(0, n_block - WIDEN_SLOTS), n_block):
        give(i).wait()
    for copy in passed:
        copy.wait()


def finish(low, mixed, gfeat, gbias, gstitch):
    tall, width = low.shape
    block = tall // WIDEN_BLOCKS
    anywhere = pl.BlockSpec(memory_space=pl.ANY)
    inside = pl.BlockSpec(memory_space=pltpu.VMEM)
    moved = sum(a.size * a.dtype.itemsize for a in (mixed, gfeat))
    return pl.pallas_call(
        functools.partial(finish_kernel, block),
        in_specs=[anywhere] * 3 + [inside] * 2,
        out_specs=[anywhere] * 3 + [inside] * 2,
        out_shape=[
            jax.ShapeDtypeStruct(a.shape, kind)
            for a, kind in ((low, F32), (mixed, BF16), (gfeat, BF16), (gbias, F32), (gstitch, F32))
        ],
        scratch_shapes=[
            pltpu.VMEM((WIDEN_SLOTS, block, width), BF16),
            pltpu.VMEM((WIDEN_SLOTS, block, width), F32),
            pltpu.VMEM(mixed.shape, BF16),
            pltpu.VMEM(gfeat.shape, BF16),
            pltpu.SemaphoreType.DMA((WIDEN_SLOTS,)),
            pltpu.SemaphoreType.DMA((WIDEN_SLOTS,)),
            pltpu.SemaphoreType.DMA((4,)),
        ],
        compiler_params=pltpu.CompilerParams(vmem_limit_bytes=60 * 1024 * 1024),
        cost_estimate=pl.CostEstimate(
            flops=tall * width, bytes_accessed=6 * tall * width + 2 * moved, transcendentals=0
        ),
        name="finish",
    )(low, mixed, gfeat, gbias, gstitch)


def fused_plan(mesh):
    def per_device(features, weights, bias, stitch, cotangent, crop_counts, row_mask, flags):
        rows, deep = features.shape[1:]
        width = weights.shape[2]
        mixed, gfeat, gwt, gbias, gstitch, _, _ = fused_call(
            features, weights, cotangent, bias, stitch,
            crop_counts.reshape(1, -1), row_mask.reshape(-1, min(128, rows // 6)), flags,
        )
        grad_weights, mixed, gfeat, gbias, gstitch = finish(
            gwt.reshape(-1, width), mixed, gfeat, gbias, gstitch
        )
        return mixed, gfeat, grad_weights.reshape(2, ZED * 2 * deep, width), gbias, gstitch

    return per_device


def plan_for(mesh):
    if mesh.shape["batch"] == 4 and mesh.shape["mp"] == 2 * ZED:
        return fused_plan(mesh)
    return generic_plan(mesh)


def solution(mesh):
    in_specs = (
        P(None, "batch", "mp"),
        P(None, None, "mp"),
        P(None, "mp"),
        P(None, None, "mp"),
        P(None, "batch", "mp"),
        P("batch"),
        P("batch"),
        P(),
    )
    out_specs = (
        P(None, "batch", "mp"),
        P(None, "batch", "mp"),
        P(None, None, "mp"),
        P(None, "mp"),
        P(None, None, "mp"),
    )
    return jax.shard_map(
        plan_for(mesh), mesh=mesh, in_specs=in_specs, out_specs=out_specs, check_vma=False
    )
```

```python
import collections
import functools

import jax
import jax.numpy as jnp
from jax import lax
from jax.experimental import pallas as pl
from jax.experimental.pallas import tpu as pltpu
from jax.sharding import PartitionSpec as P

FLAG_GROUPS = 8
OUTER = 4


def row_weights(counts, mask):
    ends = jnp.cumsum(counts)
    starts = ends - counts
    index = lax.broadcasted_iota(jnp.int32, (mask.shape[0], counts.shape[0]), 0)
    inside = (index >= starts[None, :]) & (index < ends[None, :])
    count_row = jnp.sum(jnp.where(inside, counts[None, :], 0), axis=1)
    live = (count_row > 0) & (mask == 1)
    return jnp.where(live, 1.0 / jnp.maximum(count_row, 1).astype(jnp.float32), 0.0)


def project_bias(task_bias, flags):
    local_width = task_bias.shape[2]
    channel = lax.axis_index("mp") * local_width + lax.broadcasted_iota(
        jnp.int32, (local_width, FLAG_GROUPS), 0
    )
    member = (
        channel % FLAG_GROUPS == lax.broadcasted_iota(jnp.int32, (local_width, FLAG_GROUPS), 1)
    ).astype(jnp.float32)
    dots = jnp.dot(task_bias[0] * task_bias[1], member, precision=lax.Precision.HIGHEST)
    norms = jnp.einsum(
        "stc,cg->stg", task_bias * task_bias, member, precision=lax.Precision.HIGHEST
    )
    dots, norms = lax.psum((dots, norms), "mp")
    flag = flags.astype(jnp.float32)
    coef_first = jnp.dot(
        flag[0] * dots / (norms[1] + 1e-06), member.T, precision=lax.Precision.HIGHEST
    )
    coef_second = jnp.dot(
        flag[1] * dots / (norms[0] + 1e-06), member.T, precision=lax.Precision.HIGHEST
    )
    first = task_bias[0] - coef_first * task_bias[1]
    second = task_bias[1] - coef_second * task_bias[0]
    return first + second


def generic_plan(mesh):
    n_mp = mesh.shape["mp"]
    n_batch = mesh.shape["batch"]
    inner = n_mp // OUTER
    inner_groups = [[o * inner + i for i in range(inner)] for o in range(OUTER)]
    outer_groups = [[o * inner + i for o in range(OUTER)] for i in range(inner)]

    def per_device(features, weights, bias, stitch, cotangent, crop_counts, row_mask, flags):
        rows = features.shape[1]
        width = weights.shape[2]
        depth = features.shape[2] * inner
        held = lax.all_gather(
            features, "mp", axis=2, tiled=True, axis_index_groups=inner_groups
        )
        split = weights.reshape(2, OUTER, depth, width)
        block = lax.all_to_all(
            split, "mp", split_axis=1, concat_axis=1, axis_index_groups=outer_groups
        )
        block = block.reshape(2, OUTER, depth, width)
        part = jnp.einsum("trk,tokc->otrc", held, block, preferred_element_type=jnp.float32)
        linear = lax.psum_scatter(
            part.astype(jnp.bfloat16),
            "mp",
            scatter_dimension=0,
            axis_index_groups=outer_groups,
        ).astype(jnp.float32)
        pre = linear + bias[:, None, :]
        hidden, gelu_back = jax.vjp(lambda v: jax.nn.gelu(v, approximate=False), pre)
        mixed = stitch[:, 0, None, :] * hidden[0][None] + stitch[:, 1, None, :] * hidden[1][None]
        scale_rows = row_weights(crop_counts, row_mask)
        grad_out = cotangent.astype(jnp.float32) * scale_rows[None, :, None]
        first_task = gelu_back(stitch[0][:, None, :] * grad_out[0][None])[0]
        second_task = gelu_back(stitch[1][:, None, :] * grad_out[1][None])[0]
        task_bias = jnp.stack([jnp.sum(first_task, axis=1), jnp.sum(second_task, axis=1)])
        grad_linear = (first_task + second_task).astype(jnp.bfloat16)
        grad_stitch = jnp.sum(grad_out[:, None] * hidden[None], axis=2)
        every = lax.all_gather(grad_linear, "mp", axis_index_groups=outer_groups)
        grad_part = jnp.einsum(
            "otrc,tokc->trk", every, block, preferred_element_type=jnp.float32
        )
        grad_part = grad_part.astype(jnp.bfloat16).reshape(2, rows, inner, depth // inner)
        grad_features = lax.psum_scatter(
            grad_part.transpose(2, 0, 1, 3),
            "mp",
            scatter_dimension=0,
            axis_index_groups=inner_groups,
        )
        weight_part = jnp.einsum(
            "trk,otrc->otkc", held, every, preferred_element_type=jnp.float32
        )
        weight_part = weight_part.astype(jnp.bfloat16).reshape(
            OUTER, 2, n_batch, depth // n_batch, width
        )
        share = lax.psum_scatter(
            weight_part.transpose(2, 0, 1, 3, 4), "batch", scatter_dimension=0
        )
        share = lax.all_to_all(
            share, "mp", split_axis=0, concat_axis=0, axis_index_groups=outer_groups
        )
        share = share.reshape(OUTER, 2, depth // n_batch, width)
        whole = lax.all_gather(share, "batch")
        grad_weights = whole.transpose(2, 1, 0, 3, 4).reshape(2, OUTER * depth, width)
        task_bias, grad_stitch = lax.psum((task_bias, grad_stitch), "batch")
        grad_bias = project_bias(task_bias, flags)
        return (
            mixed.astype(jnp.bfloat16),
            grad_features.astype(jnp.bfloat16),
            grad_weights.astype(jnp.float32),
            grad_bias,
            grad_stitch,
        )

    return per_device


MESH = pl.DeviceIdType.MESH
BF16 = jnp.bfloat16
F32 = jnp.float32
ZED = 4
HALVES = 2
PHASES = 4
RING = 12
BAND = 32
SUB = 4
PRODUCTS = 12
SUM_LAG = 2
GATHER_LAG = 2
HELD = 4
WIDEN_BLOCKS = 12
WIDEN_SLOTS = 4

DX_TIMES = (42, 44, 49, 52, 56, 72, 89, 93, 96, 103, 109, 114)
DX_BEGINS = (48, 51, 54, 59, 64, 77, 91, 99, 105, 113, 118, 140)
DX_ENDS = (49, 52, 58, 63, 69, 78, 93, 100, 111, 117, 125, 146)
ONES = (38, 44, 49, 61, 72, 78, 85, 90, 96, 108, 113, 121)
TWOS = (40, 46, 56, 64, 73, 82, 90, 92, 99, 112, 117, 133)
THREES = (42, 47, 64, 71, 80, 90, 93, 99, 105, 121, 127, 146)
FOURS = (49, 58, 72, 80, 84, 93, 97, 102, 109, 127, 145, 151)
FIVES = (55, 73, 74, 83, 90, 95, 102, 106, 138, 143, 157, 162)
SIXES = (57, 79, 93, 94, 107, 119, 124, 137, 148, 155, 161, 167)
W_STRIPS = {2: (5, 8, 10, 11, 15, 19), 3: (36, 47, 49, 52, 56, 58)}
W_ACROSS = {1: (2, 4, 8), 2: (23, 30, 34), 3: (60, 61, 62)}
W_CORES = {1: (9, 10, 21), 2: (32, 46, 46), 3: (65, 65, 67)}


Part = collections.namedtuple("Part", ("u", "p", "i", "t", "h", "slot", "prod", "buf"))
Tile = collections.namedtuple("Tile", ("g", "p", "t", "h", "j", "buf", "trio", "quad"))


def half(value):
    return value.astype(BF16)


def wide(value):
    return value.astype(F32)


def fused_kernel(
    rows, deep, width, chunk,
    feat, wts, cot, bias, stitch, counts, mask, flags,
    mixed, gfeat, gwt, gbias, gstitch, xn, dxn,
    wv, gl, rs, h0, xc, pf, cc, mx, own, dsend, dfetch, dout,
    xsrc, xt, cstage, cland, xstage, xland, kept, zstage,
    scale, stat, sums, sums_land, prods, prods_land,
    rs_send, rs_recv, ag_send, ag_recv, xs_send, xs_recv,
    wz_send, wz_recv, wx_send, wx_recv, wc_send, wc_recv, wl,
    xf, cf, mxs, dx_send, dx_recv, df, dod,
    tile_in, c_send, c_recv, x_send, x_recv, z_send, z_recv, zl, zx_send,
    ax_send, ax_recv, ac_send, ac_recv, t_send, t_recv,
):
    batch, mp = lax.axis_index("batch"), lax.axis_index("mp")
    z, y = mp // 2, mp % 2
    x, c = batch // 2, batch % 2
    up = {"mp": mp + 2}
    down = {"mp": mp - 2}
    across_y = {"mp": 2 * z + 1 - y}
    across_x = {"batch": 2 * (1 - x) + c}
    across_c = {"batch": 2 * x + 1 - c}

    def at_z(other):
        return {"mp": 2 * other + y}

    others = (3 - z, (z + 2) % 4, z + 1 - 2 * (z % 2))

    n_chunk = rows // chunk
    total = PHASES * n_chunk
    part = chunk // SUB
    n_part = rows // part
    parts = PHASES * n_part
    images = counts.shape[1]
    hw = width // HALVES
    kz = 2 * deep
    quarter = deep // 2
    tile = deep // 3
    strip = quarter // 6
    xw = hw // 2

    def mult(value, unit):
        return pl.multiple_of(value, unit)

    def remote(src, dst, send, recv, device):
        return pltpu.make_async_remote_copy(
            src_ref=src, dst_ref=dst, send_sem=send, recv_sem=recv,
            device_id=device, device_id_type=MESH,
        )

    def cols(b):
        return pl.ds(mult(b * hw, hw), hw)

    def chunk_rows(i):
        return pl.ds(mult(i * chunk, chunk), chunk)

    def part_rows(i):
        return pl.ds(mult(i * part, part), part)

    def tower(p):
        t = jnp.where(p >= HALVES, 1, 0)
        return t, p - HALVES * t

    def x_copy(t, i):
        e = t * n_chunk + i
        return remote(
            feat.at[t, chunk_rows(i)], xn.at[t, chunk_rows(i)],
            xs_send.at[e], xs_recv.at[e], across_y,
        )

    def x_fetch(t, i, buf):
        return (
            pltpu.make_async_copy(
                feat.at[t, chunk_rows(i)],
                xc.at[buf, :, pl.ds(mult(deep * y, deep), deep)], xf.at[buf, 0],
            ),
            pltpu.make_async_copy(
                xn.at[t, chunk_rows(i)],
                xc.at[buf, :, pl.ds(mult(deep * (1 - y), deep), deep)], xf.at[buf, 1],
            ),
        )

    def cot_fetch(h, i, buf):
        return pltpu.make_async_copy(
            cot.at[:, part_rows(i), cols(h)], cc.at[buf], cf.at[buf]
        )

    def w_own(p):
        t, h = tower(p)
        return pltpu.make_async_copy(
            wts.at[t, pl.ds(mult(kz * z, kz), kz), cols(h)], wv.at[p, :, cols(z)], wl.at[p],
        )

    def w_rows():
        return pl.ds(mult(deep * c + quarter * x, quarter), quarter)

    def w_z(p, to):
        t, h = tower(p)
        return remote(
            wts.at[
                t, pl.ds(mult(kz * to + deep * c + quarter * x, quarter), quarter), cols(h)
            ],
            wv.at[p, w_rows(), cols(z)],
            wz_send.at[p, to], wz_recv.at[p, z], at_z(to),
        )

    def w_z_strip(p, to, r):
        t, h = tower(p)
        at = deep * c + quarter * x + strip * r
        return remote(
            wts.at[t, pl.ds(mult(kz * to + at, strip), strip), cols(h)],
            wv.at[p, pl.ds(mult(at, strip), strip), cols(z)],
            wz_send.at[p, to], wz_recv.at[p, z], at_z(to),
        )

    def w_z_in(p, frm):
        here = wv.at[p, w_rows(), cols(frm)]
        return remote(here, here, wz_send.at[p, frm], wz_recv.at[p, frm], at_z(frm))

    def w_x(p, b):
        here = wv.at[p, w_rows(), cols(b)]
        return remote(here, here, wx_send.at[p, b], wx_recv.at[p, b], across_x)

    def w_x_in(p, b):
        here = wv.at[
            p, pl.ds(mult(deep * c + quarter * (1 - x), quarter), quarter), cols(b)
        ]
        return remote(here, here, wx_send.at[p, b], wx_recv.at[p, b], across_x)

    def w_c(p, b):
        here = wv.at[p, pl.ds(mult(deep * c, deep), deep), cols(b)]
        return remote(here, here, wc_send.at[p, b], wc_recv.at[p, b], across_c)

    def w_c_in(p, b):
        here = wv.at[p, pl.ds(mult(deep * (1 - c), deep), deep), cols(b)]
        return remote(here, here, wc_send.at[p, b], wc_recv.at[p, b], across_c)

    def rs_up(slot, zz):
        run = rs.at[slot, zz + 2 : ZED + 1]
        return remote(run, run, rs_send.at[slot, 0], rs_recv.at[slot, 0], up)

    def rs_down(slot, zz):
        run = rs.at[slot, 0:zz]
        return remote(run, run, rs_send.at[slot, 1], rs_recv.at[slot, 1], down)

    def rs_from_below(slot, zz):
        run = rs.at[slot, zz + 1 : ZED + 1]
        return remote(run, run, rs_send.at[slot, 0], rs_recv.at[slot, 0], down)

    def rs_from_above(slot, zz):
        run = rs.at[slot, 0 : zz + 1]
        return remote(run, run, rs_send.at[slot, 1], rs_recv.at[slot, 1], up)

    def at_place(first, last, do):
        for zz in range(first, last + 1):
            @pl.when(z == zz)
            def _(zz=zz):
                do(zz)

    def ag(at, b, going, device):
        here = gl.at[at.p, part_rows(at.i), cols(b)]
        return remote(
            here, here, ag_send.at[at.slot, going * ZED + b], ag_recv.at[at.slot, b], device
        )

    def dx_copy(t, i, buf):
        return remote(
            dsend.at[buf], dxn.at[t, chunk_rows(i)],
            dx_send.at[buf], dx_recv.at[t * n_chunk + i], across_y,
        )

    def dx_fetch(t, i):
        return pltpu.make_async_copy(dxn.at[t, chunk_rows(i)], dfetch, df.at[0])

    def dx_out(t, i):
        return pltpu.make_async_copy(dout, gfeat.at[t, chunk_rows(i)], dod.at[0])

    def mixed_out(h, i, buf):
        return pltpu.make_async_copy(
            mx.at[buf], mixed.at[:, part_rows(i), cols(h)], mxs.at[buf]
        )

    def tile_fetch(t, j, hk, start):
        lanes = pl.ds(mult(tile * j, tile), tile)
        near = pltpu.make_async_copy(feat.at[t, :, lanes], xsrc, tile_in.at[0])
        if not start:
            near.wait()
            return

        @pl.when(hk == y)
        def _():
            near.start()

        @pl.when(hk != y)
        def _():
            pltpu.make_async_copy(xn.at[t, :, lanes], xsrc, tile_in.at[0]).start()

    def core_copy(g):
        return remote(cstage, cland.at[g.buf], c_send.at[0], c_recv.at[g.buf], across_c)

    def across_copy(g, b):
        return remote(
            xstage.at[g.trio, b], xland.at[g.quad, b],
            x_send.at[g.trio, b], x_recv.at[g.quad, b], across_x,
        )

    def piece(g, source, core, lanes, n_lanes):
        return gwt.at[
            g.t, source,
            pl.ds(mult(deep * core + tile * g.j, tile), tile),
            pl.ds(mult(hw * g.h + lanes, xw), n_lanes),
        ]

    def z_copy(g, to):
        return remote(
            zstage.at[g.trio, to], piece(g, z, c, xw * x, xw),
            z_send.at[g.trio, to], z_recv.at[g.g, z], at_z(to),
        )

    def z_in(g, frm):
        here = piece(g, frm, c, xw * x, xw)
        return remote(here, here, z_send.at[g.trio, frm], z_recv.at[g.g, frm], at_z(frm))

    def z_own(g):
        return pltpu.make_async_copy(
            zstage.at[g.trio, z], piece(g, z, c, xw * x, xw), zl.at[g.trio]
        )

    def ax_own(g):
        return remote(
            zstage.at[g.trio, z], piece(g, z, c, xw * x, xw),
            zx_send.at[g.trio], ax_recv.at[g.g, z], across_x,
        )

    def ax_copy(g, b):
        here = piece(g, b, c, xw * x, xw)
        return remote(here, here, ax_send.at[g.g, b], ax_recv.at[g.g, b], across_x)

    def ax_in(g, b):
        here = piece(g, b, c, xw * (1 - x), xw)
        return remote(here, here, ax_send.at[g.g, b], ax_recv.at[g.g, b], across_x)

    def ac_copy(g, b):
        here = piece(g, b, c, 0, hw)
        return remote(here, here, ac_send.at[g.g, b], ac_recv.at[g.g, b], across_c)

    def ac_in(g, b):
        here = piece(g, b, 1 - c, 0, hw)
        return remote(here, here, ac_send.at[g.g, b], ac_recv.at[g.g, b], across_c)

    def sum_copy(stage, device):
        return remote(
            sums.at[stage], sums_land.at[stage], t_send.at[stage], t_recv.at[stage], device
        )

    def prod_y():
        return remote(prods.at[0], prods_land.at[ZED], t_send.at[2], t_recv.at[2], across_y)

    def prod_z(to):
        return remote(
            prods.at[1], prods_land.at[z], t_send.at[3 + to], t_recv.at[3 + z], at_z(to)
        )

    def prod_z_in(frm):
        here = prods_land.at[frm]
        return remote(here, here, t_send.at[3 + frm], t_recv.at[3 + frm], at_z(frm))

    barrier = pltpu.get_barrier_semaphore()
    for device in [at_z(o) for o in others] + [across_y, across_x, across_c]:
        pl.semaphore_signal(barrier, inc=1, device_id=device, device_id_type=MESH)
    pl.semaphore_wait(barrier, 6)

    for to in others:
        w_z(0, to).start()
    x_copy(0, 0).start()
    x_copy(0, 1).start()
    w_own(0).start()
    cot_fetch(0, 0, 0).start()

    image_row = lax.broadcasted_iota(jnp.int32, (images, images), 0)
    image_col = lax.broadcasted_iota(jnp.int32, (images, images), 1)
    crops = counts[...].astype(F32)
    ends = jnp.dot(
        jnp.broadcast_to(crops, (8, images)), (image_row <= image_col).astype(F32),
        precision=lax.Precision.HIGHEST, preferred_element_type=F32,
    )[0:1]
    starts = ends - crops
    block = mask.shape[1]
    lane = scale.shape[1]

    for r in range(rows // block):
        index = (
            lax.broadcasted_iota(jnp.int32, (block, images), 0) + r * block
        ).astype(F32)
        inside = (index >= starts) & (index < ends)
        count_row = jnp.sum(jnp.where(inside, crops, 0.0), axis=1, keepdims=True)
        diagonal = lax.broadcasted_iota(jnp.int32, (block, block), 0) == (
            lax.broadcasted_iota(jnp.int32, (block, block), 1)
        )
        usable = jnp.sum(
            jnp.where(diagonal, mask[r : r + 1, :].astype(F32), 0.0),
            axis=1, keepdims=True,
        )
        live = (count_row > 0.0) & (usable == 1.0)
        share = jnp.where(live, 1.0 / jnp.maximum(count_row, 1.0), 0.0)
        scale[r * block : (r + 1) * block, :] = jnp.broadcast_to(share, (block, lane))

    for frm in others:
        w_z_in(0, frm).wait_recv()
        w_x(0, frm).start()
    for to in others:
        w_z(1, to).start()
    w_own(1).start()
    for frm in others:
        w_x_in(0, frm).wait_recv()
        w_c(0, frm).start()
    x_copy(0, 0).wait_recv()
    for copy in x_fetch(0, 0, 0):
        copy.start()

    def final(at, later):
        p, i, slot, t, h, buf = at.p, at.i, at.slot, at.t, at.h, at.buf
        cot_fetch(h, i, buf).wait()

        @pl.when(at.u >= 2 * n_part + 2)
        def _():
            mixed_out(h, i, buf).wait()

        @pl.when(i == 0)
        def _():
            stat[p] = jnp.zeros(stat.shape[1:], F32)

        lanes = cols(h)
        shift = bias[pl.ds(t, 1), lanes]
        st = [stitch[s, pl.ds(t, 1), lanes] for s in range(2)]
        band = min(BAND, part)

        def step(r, carry):
            here = part_rows_of(r, band)
            there = pl.ds(mult(i * part + r * band, band), band)
            value = pf[at.prod, z, here, :]
            below = wide(rs[slot, z + 1, here, :])
            above = wide(rs[slot, z, here, :])
            value = value + jnp.where(z > 0, below, 0.0) + jnp.where(z < ZED - 1, above, 0.0)
            pre = value + shift
            phi = 0.5 * (1.0 + lax.erf(pre * 0.7071067811865476))
            hidden = pre * phi
            slope = phi + pre * (jnp.exp(-0.5 * pre * pre) * 0.3989422804014327)
            weight = scale[there, 0:1]
            first = wide(cc[buf, 0, here, :]) * weight
            second = wide(cc[buf, 1, here, :]) * weight
            back0 = st[0] * first * slope
            back1 = st[1] * second * slope
            gl[p, there, cols(z)] = half(back0 + back1)

            def fold(v):
                return jnp.sum(v.reshape(band // 8, 8, hw), axis=0)

            stat[p, 0] += fold(back0)
            stat[p, 1] += fold(back1)
            stat[p, 2] += fold(first * hidden)
            stat[p, 3] += fold(second * hidden)

            @pl.when(t == 0)
            def _():
                h0[h, there, :] = hidden

            @pl.when(t == 1)
            def _():
                before = h0[h, there, :]
                for s in range(2):
                    mx[buf, s, here, :] = half(
                        stitch[s, 0:1, lanes] * before + st[s] * hidden
                    )

            return carry

        lax.fori_loop(0, part // band, step, 0)

        @pl.when(z < ZED - 1)
        def _():
            ag(at, z, 0, up).start()

        @pl.when(z > 0)
        def _():
            ag(at, z, 1, down).start()

        @pl.when(t == 1)
        def _():
            mixed_out(h, i, buf).start()

        @pl.when(at.u + 1 < parts)
        def _():
            cot_fetch(later.h, later.i, later.buf).start()

    def part_rows_of(r, band):
        return pl.ds(mult(r * band, band), band)

    def forward_ag(at, far):
        @pl.when((at.u >= 0) & (at.u < parts))
        def _():
            @pl.when(z - far >= 0)
            def _():
                ag(at, z - far, 0, up).wait_recv()

                @pl.when(z < ZED - 1)
                def _():
                    ag(at, z - far, 0, up).start()

            @pl.when(z + far < ZED)
            def _():
                ag(at, z + far, 1, down).wait_recv()

                @pl.when(z > 0)
                def _():
                    ag(at, z + far, 1, down).start()

    def dx_part(t, i, hk):
        there = chunk_rows(i)
        krows = pl.ds(mult(deep * hk, deep), deep)
        acc = None
        for h in range(HALVES):
            term = lax.dot_general(
                gl[2 * t + h, there, :], wv[2 * t + h, krows, :],
                (((1,), (1,)), ((), ())), preferred_element_type=F32,
            )
            acc = term if acc is None else acc + term
        return acc

    def dx_step(t, i, buf):
        @pl.when((i >= HELD) | (t > 0))
        def _():
            dx_copy(t, i, buf).wait_send()

        dsend[buf] = half(dx_part(t, i, 1 - y))
        dx_copy(t, i, buf).start()
        own[buf] = dx_part(t, i, y)

    def dx_begin(t, i, buf):
        dx_copy(t, i, buf).wait_recv()
        dx_fetch(t, i).start()

    def dx_final(t, i, buf):
        @pl.when((i >= 1) | (t > 0))
        def _():
            dx_out(t, i).wait()

        dx_fetch(t, i).wait()

        def step(j, inner):
            lanes = pl.ds(mult(tile * j, tile), tile)
            dout[:, lanes] = half(own[buf, :, lanes] + wide(dfetch[:, lanes]))
            return inner

        lax.fori_loop(0, 3, step, 0)
        dx_out(t, i).start()

    def listed(u, times, do):
        e, hit = 0, False
        for index, time in enumerate(times):
            same = u == time
            e = jnp.where(same, index, e)
            hit = hit | same

        @pl.when(hit)
        def _():
            do(e)

    def chunk_of(do):
        def run(e):
            t = jnp.where(e >= n_chunk, 1, 0)
            do(t, e - n_chunk * t, lax.rem(e, HELD))

        return run

    def turn():
        lanes_at_once = min(128, tile)

        def step(q, carry):
            lanes = pl.ds(mult(q * lanes_at_once, lanes_at_once), lanes_at_once)
            xt[lanes, :] = xsrc[:, lanes].T
            return carry

        lax.fori_loop(0, tile // lanes_at_once, step, 0)

    def tile_dot(g):
        return jnp.dot(xt[...], gl[g.p], preferred_element_type=F32)

    def stage_one(g):
        tile_fetch(g.t, g.j, 1 - c, False)
        turn()
        tile_fetch(g.t, g.j, c, True)
        cstage[...] = half(tile_dot(g))
        core_copy(g).start()

    def stage_two(g):
        tile_fetch(g.t, g.j, c, False)
        turn()

        @pl.when(g.j < 2)
        def _():
            tile_fetch(g.t, g.j + 1, 1 - c, True)

        core_copy(g).wait()
        product = tile_dot(g)
        for b in range(ZED):
            block = product[:, b * hw : (b + 1) * hw] + wide(
                cland[g.buf, :, b * hw : (b + 1) * hw]
            )
            left, right = block[:, :xw], block[:, xw:]
            kept[g.trio, b] = jnp.where(x == 0, left, right)
            xstage[g.trio, b] = half(jnp.where(x == 0, right, left))

        def send(q, carry):
            across_copy(g, lax.rem(z + 3 + 3 * q, ZED)).start()
            return carry

        lax.fori_loop(0, ZED, send, 0)

    def stage_three(g):
        @pl.when(g.g >= 3)
        def _():
            for to in others:
                z_copy(g, to).wait_send()
            ax_own(g).wait_send()

        def add(b):
            across_copy(g, b).wait()
            zstage[g.trio, b] = half(kept[g.trio, b] + wide(xland[g.quad, b]))

        def step(q, carry):
            b = lax.rem(z + 3 + 3 * q, ZED)
            add(b)
            z_copy(g, b).start()
            return carry

        lax.fori_loop(0, ZED - 1, step, 0)
        add(z)
        z_own(g).start()
        ax_own(g).start()

    def stage_four(g):
        def step(q, carry):
            b = lax.rem(z + 1 + q, ZED)
            z_in(g, b).wait_recv()
            ax_copy(g, b).start()
            return carry

        lax.fori_loop(0, ZED - 1, step, 0)
        z_own(g).wait()

    def stage_five(g):
        def step(q, carry):
            b = lax.rem(z + q, ZED)
            ax_in(g, b).wait_recv()
            ac_copy(g, b).start()
            return carry

        lax.fori_loop(0, ZED, step, 0)

    def stage_six(g):
        def step(b, carry):
            ac_in(g, b).wait_recv()
            return carry

        lax.fori_loop(0, ZED, step, 0)

    def tile_of(g):
        p = lax.div(g, 3)
        t, h = tower(p)
        return Tile(
            g=g, p=p, t=t, h=h, j=g - 3 * p,
            buf=lax.rem(g, 2), trio=g - 3 * p, quad=lax.rem(g, 4),
        )

    def tile_in_hand(do):
        return lambda g: do(tile_of(g))

    def body(u, carry):
        p0 = lax.div(u, n_part)
        i0 = u - p0 * n_part
        slot0, prod0 = lax.rem(u, RING), lax.rem(u, PRODUCTS)
        buf0 = lax.rem(u, 2)

        def before(lag):
            if isinstance(lag, int):
                whole, left = divmod(lag, n_part)
            else:
                whole, left = 0, lag
            under = i0 < left
            p = p0 - whole - jnp.where(under, 1, 0)
            i = i0 - left + jnp.where(under, n_part, 0)
            in_ring = lag % RING if isinstance(lag, int) else lag
            in_prods = lag % PRODUCTS if isinstance(lag, int) else lag
            slot = slot0 - in_ring + jnp.where(slot0 < in_ring, RING, 0)
            prod = prod0 - in_prods + jnp.where(prod0 < in_prods, PRODUCTS, 0)
            t, h = tower(p)
            return Part(u=u - lag, p=p, i=i, t=t, h=h, slot=slot, prod=prod, buf=lax.rem(i, 2))

        retired = max(5, 3 * SUM_LAG)

        @pl.when((u >= retired) & (u < parts + retired))
        def _():
            slot = before(retired).slot
            at_place(0, ZED - 2, lambda zz: rs_up(slot, zz).wait_send())
            at_place(1, ZED - 1, lambda zz: rs_down(slot, zz).wait_send())

        @pl.when((u >= RING) & (u < parts + RING))
        def _():
            at = before(RING)

            def step(b, inner):
                @pl.when((z < ZED - 1) & (b <= z))
                def _():
                    ag(at, b, 0, up).wait_send()

                @pl.when((z > 0) & (b >= z))
                def _():
                    ag(at, b, 1, down).wait_send()

                return inner

            lax.fori_loop(0, ZED, step, 0)

        ck = lax.div(i0, SUB)
        fresh = ck * SUB == i0
        t0, h0_ = tower(p0)
        xbuf = lax.rem(ck, 2)

        @pl.when((u < parts) & fresh)
        def _():
            @pl.when(i0 == 0)
            def _():
                w_own(p0).wait()
                for frm in others:
                    w_c_in(p0, frm).wait_recv()

            for copy in x_fetch(t0, ck, xbuf):
                copy.wait()

            product = jnp.dot(xc[xbuf], wv[p0], preferred_element_type=F32)
            for b in range(ZED):
                for s in range(SUB):
                    pf[prod0 + s, b] = product[
                        s * part : (s + 1) * part, b * hw : (b + 1) * hw
                    ]

        going_up = before(SUM_LAG * z)

        @pl.when((going_up.u >= 0) & (going_up.u < parts))
        def _():
            slot, prod = going_up.slot, going_up.prod
            at_place(1, ZED - 1, lambda zz: rs_from_below(slot, zz).wait_recv())

            @pl.when(z == 0)
            def _():
                for b in range(1, ZED):
                    rs[slot, b + 1] = half(pf[prod, b])

            @pl.when(z > 0)
            def _():
                def step(b, inner):
                    rs[slot, b + 1] = half(wide(rs[slot, b + 1]) + pf[prod, b])
                    return inner

                lax.fori_loop(z + 1, ZED, step, 0)

            at_place(0, ZED - 2, lambda zz: rs_up(slot, zz).start())

        going_down = before(SUM_LAG * (ZED - 1 - z))

        @pl.when((going_down.u >= 0) & (going_down.u < parts))
        def _():
            slot, prod = going_down.slot, going_down.prod
            at_place(0, ZED - 2, lambda zz: rs_from_above(slot, zz).wait_recv())

            @pl.when(z == ZED - 1)
            def _():
                for b in range(ZED - 1):
                    rs[slot, b] = half(pf[prod, b])

            @pl.when(z < ZED - 1)
            def _():
                def step(b, inner):
                    rs[slot, b] = half(wide(rs[slot, b]) + pf[prod, b])
                    return inner

                lax.fori_loop(0, z, step, 0)

            at_place(1, ZED - 1, lambda zz: rs_down(slot, zz).start())

        @pl.when(fresh & (u + 2 * SUB < 2 * n_part))
        def _():
            k = p0 * n_chunk + ck + 2
            over = jnp.where(k >= n_chunk, 1, 0)
            x_copy(over, k - over * n_chunk).start()

        @pl.when(fresh & (u + SUB < parts))
        def _():
            wrap = jnp.where(ck + 1 == n_chunk, 1, 0)
            i = ck + 1 - wrap * n_chunk
            t, h = tower(p0 + wrap)

            @pl.when(h == 0)
            def _():
                x_copy(t, i).wait_recv()

            for copy in x_fetch(t, i, lax.rem(i, 2)):
                copy.start()

        summed = 3 * SUM_LAG

        @pl.when((u >= summed) & (u < parts + summed))
        def _():
            final(before(summed), before(summed - 1))

        for far in range(1, ZED):
            forward_ag(before(summed + far * GATHER_LAG), far)

        listed(u, DX_BEGINS, chunk_of(dx_begin))
        listed(u, DX_ENDS, chunk_of(dx_final))
        listed(u, DX_TIMES, chunk_of(dx_step))

        listed(u, THREES, tile_in_hand(stage_three))
        listed(u, TWOS, tile_in_hand(stage_two))
        listed(u, ONES, tile_in_hand(stage_one))
        listed(u, FOURS, tile_in_hand(stage_four))
        listed(u, FIVES, tile_in_hand(stage_five))
        listed(u, SIXES, tile_in_hand(stage_six))

        def first_fetch(p):
            tile_fetch(lax.div(p, HALVES), 0, 1 - c, True)

        listed(u, [time - 1 for time in ONES[::3]], first_fetch)

        for p, times in W_STRIPS.items():
            def send_strip(r, p=p):
                for to in others:
                    w_z_strip(p, to, r).start()

                @pl.when(r == 0)
                def _():
                    w_own(p).start()

            listed(u, times, send_strip)

        for p, times in W_ACROSS.items():
            for q, time in enumerate(times):
                @pl.when(u == time)
                def _(p=p, q=q):
                    w_z_in(p, others[q]).wait_recv()
                    w_x(p, others[q]).start()

        for p, times in W_CORES.items():
            for q, time in enumerate(times):
                @pl.when(u == time)
                def _(p=p, q=q):
                    w_x_in(p, others[q]).wait_recv()
                    w_c(p, others[q]).start()

        @pl.when(u == parts + summed + 0)
        def _():
            for p in range(PHASES):
                t, h = p // HALVES, p % HALVES
                for s in range(2):
                    for what in range(2):
                        sums[0, pl.ds(4 * what + 2 * s + t, 1), h * hw : (h + 1) * hw] = jnp.sum(
                            stat[p, 2 * what + s], axis=0, keepdims=True
                        )
            sum_copy(0, across_c).start()

        @pl.when(u == parts + summed + 1)
        def _():
            sum_copy(0, across_c).wait()
            sums[1] = sums[0] + sums_land[0]
            sum_copy(1, across_x).start()

        @pl.when(u == parts + summed + 2)
        def _():
            sum_copy(1, across_x).wait()
            both = sums[1] + sums_land[1]
            sums[2] = both
            member = (
                lax.broadcasted_iota(jnp.int32, (width, lane), 0) % FLAG_GROUPS
                == lax.broadcasted_iota(jnp.int32, (width, lane), 1) % FLAG_GROUPS
            ).astype(F32)
            bias_rows = both[0:4]
            inner = both[0:2] * both[2:4]
            stack = jnp.concatenate([inner, bias_rows * bias_rows, inner], axis=0)
            prods[0] = jnp.dot(
                stack, member, precision=lax.Precision.HIGHEST, preferred_element_type=F32
            )
            prod_y().start()

        @pl.when(u == parts + summed + 3)
        def _():
            prod_y().wait()
            prods[1] = prods[0] + prods_land[ZED]
            for to in others:
                prod_z(to).start()

        @pl.when(u == parts + summed + 4)
        def _():
            for frm in others:
                prod_z_in(frm).wait_recv()
            prods_land[z] = prods[1]
            whole = prods_land[0] + prods_land[1] + prods_land[2] + prods_land[3]
            both = sums[2]
            group = lax.broadcasted_iota(jnp.int32, (1, lane), 1) % FLAG_GROUPS

            def over(row):
                return jnp.concatenate([row] * (width // lane), axis=1)

            def flag_row(s, t):
                row = jnp.zeros((1, lane), F32)
                for g in range(FLAG_GROUPS):
                    row = jnp.where(group == g, flags[s, t, g].astype(F32), row)
                return row

            for t in range(2):
                task0, task1 = both[t : t + 1], both[2 + t : 3 + t]
                dots = whole[t : t + 1]
                coef0 = over(flag_row(0, t) * dots / (whole[4 + t : 5 + t] + 1e-06))
                coef1 = over(flag_row(1, t) * dots / (whole[2 + t : 3 + t] + 1e-06))
                gbias[t : t + 1] = (task0 - coef0 * task1) + (task1 - coef1 * task0)
            for s in range(2):
                gstitch[s] = both[4 + 2 * s : 6 + 2 * s]

        return carry

    lax.fori_loop(0, max(SIXES + DX_ENDS) + 1, body, 0)

    last = 3 * PHASES - 1

    for g in (last - 2, last - 1, last):
        for to in others:
            z_copy(tile_of(g), to).wait_send()
        ax_own(tile_of(g)).wait_send()
    for i in range(n_chunk - HELD, n_chunk):
        dx_copy(1, i, (n_chunk + i) % HELD).wait_send()
    for i in (n_part - 2, n_part - 1):
        mixed_out(1, i, i % 2).wait()
    dx_out(1, n_chunk - 1).wait()

    def drain_tiles(g, carry):
        at = tile_of(g)
        for b in others:
            ax_copy(at, b).wait_send()
        for b in range(ZED):
            ac_copy(at, b).wait_send()
        return carry

    lax.fori_loop(0, last + 1, drain_tiles, 0)

    def drain_x(i, carry):
        x_copy(0, i).wait_send()
        x_copy(1, i).wait_send()
        return carry

    lax.fori_loop(0, n_chunk, drain_x, 0)

    def drain_w(p, carry):
        for to in others:
            w_z(p, to).wait_send()
            w_x(p, to).wait_send()
            w_c(p, to).wait_send()
        return carry

    lax.fori_loop(0, PHASES, drain_w, 0)
    for to in others:
        prod_z(to).wait_send()


def fused_call(feat, wts, cot, bias, stitch, counts, mask, flags):
    rows, deep, width = feat.shape[1], feat.shape[2], wts.shape[2]
    chunk = rows // 6
    part = chunk // SUB
    hw, kz, tile = width // 2, 2 * deep, deep // 3
    cat, xw = 4 * hw, width // 4
    lane = min(128, width)
    dma = pltpu.SemaphoreType.DMA
    anywhere = pl.BlockSpec(memory_space=pl.ANY)
    inside = pl.BlockSpec(memory_space=pltpu.VMEM)
    scalars = pl.BlockSpec(memory_space=pltpu.SMEM)

    def v(shape, kind=BF16):
        return pltpu.VMEM(shape, kind)

    out_shape = [
        jax.ShapeDtypeStruct((2, rows, width), BF16),
        jax.ShapeDtypeStruct((2, rows, deep), BF16),
        jax.ShapeDtypeStruct((2, ZED, kz, width), BF16),
        jax.ShapeDtypeStruct((2, width), F32),
        jax.ShapeDtypeStruct((2, 2, width), F32),
        jax.ShapeDtypeStruct((2, rows, deep), BF16),
        jax.ShapeDtypeStruct((2, rows, deep), BF16),
    ]
    scratch = [
        v((PHASES, kz, cat)),
        v((PHASES, rows, cat)),
        v((RING, 5, part, hw)),
        v((2, rows, hw), F32),
        v((2, chunk, kz)),
        v((PRODUCTS, ZED, part, hw), F32),
        v((2, 2, part, hw)),
        v((2, 2, part, hw)),
        v((HELD, chunk, deep), F32),
        v((HELD, chunk, deep)),
        v((chunk, deep)),
        v((chunk, deep)),
        v((rows, tile)),
        v((tile, rows)),
        v((tile, cat)),
        v((2, tile, cat)),
        v((3, ZED, tile, xw)),
        v((4, ZED, tile, xw)),
        v((3, ZED, tile, xw), F32),
        v((3, ZED, tile, xw)),
        v((rows, lane), F32),
        v((PHASES, 4, 8, hw), F32),
        v((3, 8, width), F32),
        v((2, 8, width), F32),
        v((2, 8, lane), F32),
        v((5, 8, lane), F32),
        dma((RING, 2)), dma((RING, 2)), dma((RING, 8)), dma((RING, 4)),
        dma((12,)), dma((12,)),
        dma((4, 4)), dma((4, 4)), dma((4, 4)), dma((4, 4)), dma((4, 4)), dma((4, 4)), dma((4,)),
        dma((2, 2)), dma((2,)), dma((2,)), dma((HELD,)), dma((12,)), dma((1,)), dma((1,)),
        dma((1,)), dma((1,)), dma((2,)), dma((3, 4)), dma((4, 4)), dma((3, 4)), dma((12, 4)),
        dma((3,)), dma((3,)),
        dma((12, 4)), dma((12, 4)), dma((12, 4)), dma((12, 4)), dma((8,)), dma((8,)),
    ]
    flops = 3 * 2 * 2 * rows * kz * cat * 2
    return pl.pallas_call(
        functools.partial(fused_kernel, rows, deep, width, chunk),
        out_shape=out_shape,
        in_specs=[anywhere] * 3 + [inside] * 4 + [scalars],
        out_specs=[anywhere] * 3 + [inside] * 2 + [anywhere] * 2,
        scratch_shapes=scratch,
        compiler_params=pltpu.CompilerParams(
            collective_id=0, has_side_effects=True, vmem_limit_bytes=64 * 1024 * 1024
        ),
        cost_estimate=pl.CostEstimate(
            flops=flops, bytes_accessed=200_000_000, transcendentals=2 * rows * width * 2
        ),
        name="cross_stitch_step",
    )(feat, wts, cot, bias, stitch, counts, mask, flags)


def finish_kernel(
    block, low, mixed, gfeat, gbias, gstitch,
    out, mixed_out, gfeat_out, gbias_out, gstitch_out,
    taken, given, held_mixed, held_gfeat, in_sem, out_sem, pass_sem,
):
    n_block = low.shape[0] // block
    fetched = (
        pltpu.make_async_copy(mixed, held_mixed, pass_sem.at[0]),
        pltpu.make_async_copy(gfeat, held_gfeat, pass_sem.at[1]),
    )
    passed = (
        pltpu.make_async_copy(held_mixed, mixed_out, pass_sem.at[2]),
        pltpu.make_async_copy(held_gfeat, gfeat_out, pass_sem.at[3]),
    )

    def take(i):
        return pltpu.make_async_copy(
            low.at[pl.ds(i * block, block)], taken.at[i % WIDEN_SLOTS], in_sem.at[i % WIDEN_SLOTS]
        )

    def give(i):
        return pltpu.make_async_copy(
            given.at[i % WIDEN_SLOTS], out.at[pl.ds(i * block, block)], out_sem.at[i % WIDEN_SLOTS]
        )

    for i in range(min(WIDEN_SLOTS, n_block)):
        take(i).start()
    for copy in fetched:
        copy.start()
    gbias_out[...] = gbias[...]
    gstitch_out[...] = gstitch[...]
    for i in range(n_block):
        slot = i % WIDEN_SLOTS
        take(i).wait()
        if i >= WIDEN_SLOTS:
            give(i - WIDEN_SLOTS).wait()
        given[slot] = wide(taken[slot])
        give(i).start()
        if i + WIDEN_SLOTS < n_block:
            take(i + WIDEN_SLOTS).start()
        if i == 2:
            for arrived, copy in zip(fetched, passed):
                arrived.wait()
                copy.start()
    for i in range(max(0, n_block - WIDEN_SLOTS), n_block):
        give(i).wait()
    for copy in passed:
        copy.wait()


def finish(low, mixed, gfeat, gbias, gstitch):
    tall, width = low.shape
    block = tall // WIDEN_BLOCKS
    anywhere = pl.BlockSpec(memory_space=pl.ANY)
    inside = pl.BlockSpec(memory_space=pltpu.VMEM)
    moved = sum(a.size * a.dtype.itemsize for a in (mixed, gfeat))
    return pl.pallas_call(
        functools.partial(finish_kernel, block),
        in_specs=[anywhere] * 3 + [inside] * 2,
        out_specs=[anywhere] * 3 + [inside] * 2,
        out_shape=[
            jax.ShapeDtypeStruct(a.shape, kind)
            for a, kind in ((low, F32), (mixed, BF16), (gfeat, BF16), (gbias, F32), (gstitch, F32))
        ],
        scratch_shapes=[
            pltpu.VMEM((WIDEN_SLOTS, block, width), BF16),
            pltpu.VMEM((WIDEN_SLOTS, block, width), F32),
            pltpu.VMEM(mixed.shape, BF16),
            pltpu.VMEM(gfeat.shape, BF16),
            pltpu.SemaphoreType.DMA((WIDEN_SLOTS,)),
            pltpu.SemaphoreType.DMA((WIDEN_SLOTS,)),
            pltpu.SemaphoreType.DMA((4,)),
        ],
        compiler_params=pltpu.CompilerParams(vmem_limit_bytes=60 * 1024 * 1024),
        cost_estimate=pl.CostEstimate(
            flops=tall * width, bytes_accessed=6 * tall * width + 2 * moved, transcendentals=0
        ),
        name="finish",
    )(low, mixed, gfeat, gbias, gstitch)


def fused_plan(mesh):
    def per_device(features, weights, bias, stitch, cotangent, crop_counts, row_mask, flags):
        rows, deep = features.shape[1:]
        width = weights.shape[2]
        mixed, gfeat, gwt, gbias, gstitch, _, _ = fused_call(
            features, weights, cotangent, bias, stitch,
            crop_counts.reshape(1, -1), row_mask.reshape(-1, min(128, rows // 6)), flags,
        )
        grad_weights, mixed, gfeat, gbias, gstitch = finish(
            gwt.reshape(-1, width), mixed, gfeat, gbias, gstitch
        )
        return mixed, gfeat, grad_weights.reshape(2, ZED * 2 * deep, width), gbias, gstitch

    return per_device


def plan_for(mesh):
    if mesh.shape["batch"] == 4 and mesh.shape["mp"] == 2 * ZED:
        return fused_plan(mesh)
    return generic_plan(mesh)


def solution(mesh):
    in_specs = (
        P(None, "batch", "mp"),
        P(None, None, "mp"),
        P(None, "mp"),
        P(None, None, "mp"),
        P(None, "batch", "mp"),
        P("batch"),
        P("batch"),
        P(),
    )
    out_specs = (
        P(None, "batch", "mp"),
        P(None, "batch", "mp"),
        P(None, None, "mp"),
        P(None, "mp"),
        P(None, None, "mp"),
    )
    return jax.shard_map(
        plan_for(mesh), mesh=mesh, in_specs=in_specs, out_specs=out_specs, check_vma=False
    )
```

```python
import collections
import functools

import jax
import jax.numpy as jnp
from jax import lax
from jax.experimental import pallas as pl
from jax.experimental.pallas import tpu as pltpu
from jax.sharding import PartitionSpec as P

FLAG_GROUPS = 8
OUTER = 4


def row_weights(counts, mask):
    ends = jnp.cumsum(counts)
    starts = ends - counts
    index = lax.broadcasted_iota(jnp.int32, (mask.shape[0], counts.shape[0]), 0)
    inside = (index >= starts[None, :]) & (index < ends[None, :])
    count_row = jnp.sum(jnp.where(inside, counts[None, :], 0), axis=1)
    live = (count_row > 0) & (mask == 1)
    return jnp.where(live, 1.0 / jnp.maximum(count_row, 1).astype(jnp.float32), 0.0)


def project_bias(task_bias, flags):
    local_width = task_bias.shape[2]
    channel = lax.axis_index("mp") * local_width + lax.broadcasted_iota(
        jnp.int32, (local_width, FLAG_GROUPS), 0
    )
    member = (
        channel % FLAG_GROUPS == lax.broadcasted_iota(jnp.int32, (local_width, FLAG_GROUPS), 1)
    ).astype(jnp.float32)
    dots = jnp.dot(task_bias[0] * task_bias[1], member, precision=lax.Precision.HIGHEST)
    norms = jnp.einsum(
        "stc,cg->stg", task_bias * task_bias, member, precision=lax.Precision.HIGHEST
    )
    dots, norms = lax.psum((dots, norms), "mp")
    flag = flags.astype(jnp.float32)
    coef_first = jnp.dot(
        flag[0] * dots / (norms[1] + 1e-06), member.T, precision=lax.Precision.HIGHEST
    )
    coef_second = jnp.dot(
        flag[1] * dots / (norms[0] + 1e-06), member.T, precision=lax.Precision.HIGHEST
    )
    first = task_bias[0] - coef_first * task_bias[1]
    second = task_bias[1] - coef_second * task_bias[0]
    return first + second


def generic_plan(mesh):
    n_mp = mesh.shape["mp"]
    n_batch = mesh.shape["batch"]
    inner = n_mp // OUTER
    inner_groups = [[o * inner + i for i in range(inner)] for o in range(OUTER)]
    outer_groups = [[o * inner + i for o in range(OUTER)] for i in range(inner)]

    def per_device(features, weights, bias, stitch, cotangent, crop_counts, row_mask, flags):
        rows = features.shape[1]
        width = weights.shape[2]
        depth = features.shape[2] * inner
        held = lax.all_gather(
            features, "mp", axis=2, tiled=True, axis_index_groups=inner_groups
        )
        split = weights.reshape(2, OUTER, depth, width)
        block = lax.all_to_all(
            split, "mp", split_axis=1, concat_axis=1, axis_index_groups=outer_groups
        )
        block = block.reshape(2, OUTER, depth, width)
        part = jnp.einsum("trk,tokc->otrc", held, block, preferred_element_type=jnp.float32)
        linear = lax.psum_scatter(
            part.astype(jnp.bfloat16),
            "mp",
            scatter_dimension=0,
            axis_index_groups=outer_groups,
        ).astype(jnp.float32)
        pre = linear + bias[:, None, :]
        hidden, gelu_back = jax.vjp(lambda v: jax.nn.gelu(v, approximate=False), pre)
        mixed = stitch[:, 0, None, :] * hidden[0][None] + stitch[:, 1, None, :] * hidden[1][None]
        scale_rows = row_weights(crop_counts, row_mask)
        grad_out = cotangent.astype(jnp.float32) * scale_rows[None, :, None]
        first_task = gelu_back(stitch[0][:, None, :] * grad_out[0][None])[0]
        second_task = gelu_back(stitch[1][:, None, :] * grad_out[1][None])[0]
        task_bias = jnp.stack([jnp.sum(first_task, axis=1), jnp.sum(second_task, axis=1)])
        grad_linear = (first_task + second_task).astype(jnp.bfloat16)
        grad_stitch = jnp.sum(grad_out[:, None] * hidden[None], axis=2)
        every = lax.all_gather(grad_linear, "mp", axis_index_groups=outer_groups)
        grad_part = jnp.einsum(
            "otrc,tokc->trk", every, block, preferred_element_type=jnp.float32
        )
        grad_part = grad_part.astype(jnp.bfloat16).reshape(2, rows, inner, depth // inner)
        grad_features = lax.psum_scatter(
            grad_part.transpose(2, 0, 1, 3),
            "mp",
            scatter_dimension=0,
            axis_index_groups=inner_groups,
        )
        weight_part = jnp.einsum(
            "trk,otrc->otkc", held, every, preferred_element_type=jnp.float32
        )
        weight_part = weight_part.astype(jnp.bfloat16).reshape(
            OUTER, 2, n_batch, depth // n_batch, width
        )
        share = lax.psum_scatter(
            weight_part.transpose(2, 0, 1, 3, 4), "batch", scatter_dimension=0
        )
        share = lax.all_to_all(
            share, "mp", split_axis=0, concat_axis=0, axis_index_groups=outer_groups
        )
        share = share.reshape(OUTER, 2, depth // n_batch, width)
        whole = lax.all_gather(share, "batch")
        grad_weights = whole.transpose(2, 1, 0, 3, 4).reshape(2, OUTER * depth, width)
        task_bias, grad_stitch = lax.psum((task_bias, grad_stitch), "batch")
        grad_bias = project_bias(task_bias, flags)
        return (
            mixed.astype(jnp.bfloat16),
            grad_features.astype(jnp.bfloat16),
            grad_weights.astype(jnp.float32),
            grad_bias,
            grad_stitch,
        )

    return per_device


MESH = pl.DeviceIdType.MESH
BF16 = jnp.bfloat16
F32 = jnp.float32
ZED = 4
HALVES = 2
PHASES = 4
RING = 8
BAND = 32
SUB = 2
PRODUCTS = 6
HELD = 4
WIDEN_BLOCKS = 12
WIDEN_SLOTS = 4

DX_TIMES = (20, 21, 23, 26, 27, 32, 45, 46, 49, 50, 72, 76)
DX_BEGINS = (22, 24, 26, 28, 30, 40, 49, 55, 59, 68, 80, 92)
DX_ENDS = (23, 25, 27, 29, 33, 45, 50, 57, 62, 69, 85, 94)
ONES = (19, 22, 25, 31, 33, 37, 42, 43, 47, 54, 62, 76)
TWOS = (22, 24, 27, 32, 36, 41, 43, 45, 48, 57, 73, 78)
THREES = (27, 32, 34, 35, 41, 42, 45, 52, 55, 69, 79, 91)
FOURS = (32, 34, 40, 41, 45, 47, 51, 63, 68, 76, 93, 97)
FIVES = (38, 46, 48, 54, 55, 59, 65, 69, 80, 89, 102, 107)
SIXES = (51, 57, 58, 61, 63, 70, 77, 95, 100, 102, 110, 113)
W_STRIPS = {2: (0, 2, 4, 7, 9, 11), 3: (19, 21, 22, 25, 26, 27)}
W_ACROSS = {1: (1, 1, 1), 2: (12, 12, 14), 3: (29, 30, 32)}
W_CORES = {1: (2, 2, 4), 2: (19, 19, 22), 3: (32, 35, 35)}


Part = collections.namedtuple("Part", ("u", "p", "i", "t", "h", "slot", "prod", "buf"))
Tile = collections.namedtuple("Tile", ("g", "p", "t", "h", "j", "buf", "trio", "quad"))


def half(value):
    return value.astype(BF16)


def wide(value):
    return value.astype(F32)


def fused_kernel(
    rows, deep, width, chunk,
    feat, wts, cot, bias, stitch, counts, mask, flags,
    mixed, gfeat, gwt, gbias, gstitch, xn, dxn,
    wv, gl, rs, h0, xc, pf, cc, mx, own, dsend, dfetch, dout,
    xsrc, xt, cstage, cland, xstage, xland, kept, zstage,
    scale, stat, sums, sums_land, prods, prods_land,
    rs_send, rs_recv, ag_send, ag_recv, xs_send, xs_recv,
    wz_send, wz_recv, wx_send, wx_recv, wc_send, wc_recv, wl,
    xf, cf, mxs, dx_send, dx_recv, df, dod,
    tile_in, c_send, c_recv, x_send, x_recv, z_send, z_recv, zl, zx_send,
    ax_send, ax_recv, ac_send, ac_recv, t_send, t_recv,
):
    batch, mp = lax.axis_index("batch"), lax.axis_index("mp")
    z, y = mp // 2, mp % 2
    x, c = batch // 2, batch % 2
    up = {"mp": mp + 2}
    down = {"mp": mp - 2}
    across_y = {"mp": 2 * z + 1 - y}
    across_x = {"batch": 2 * (1 - x) + c}
    across_c = {"batch": 2 * x + 1 - c}

    def at_z(other):
        return {"mp": 2 * other + y}

    others = (3 - z, (z + 2) % 4, z + 1 - 2 * (z % 2))

    n_chunk = rows // chunk
    total = PHASES * n_chunk
    part = chunk // SUB
    n_part = rows // part
    parts = PHASES * n_part
    images = counts.shape[1]
    hw = width // HALVES
    kz = 2 * deep
    quarter = deep // 2
    tile = deep // 3
    strip = quarter // 6
    xw = hw // 2

    def mult(value, unit):
        return pl.multiple_of(value, unit)

    def remote(src, dst, send, recv, device):
        return pltpu.make_async_remote_copy(
            src_ref=src, dst_ref=dst, send_sem=send, recv_sem=recv,
            device_id=device, device_id_type=MESH,
        )

    def cols(b):
        return pl.ds(mult(b * hw, hw), hw)

    def chunk_rows(i):
        return pl.ds(mult(i * chunk, chunk), chunk)

    def part_rows(i):
        return pl.ds(mult(i * part, part), part)

    def tower(p):
        t = jnp.where(p >= HALVES, 1, 0)
        return t, p - HALVES * t

    def x_copy(t, i):
        e = t * n_chunk + i
        return remote(
            feat.at[t, chunk_rows(i)], xn.at[t, chunk_rows(i)],
            xs_send.at[e], xs_recv.at[e], across_y,
        )

    def x_fetch(t, i, buf):
        return (
            pltpu.make_async_copy(
                feat.at[t, chunk_rows(i)],
                xc.at[buf, :, pl.ds(mult(deep * y, deep), deep)], xf.at[buf, 0],
            ),
            pltpu.make_async_copy(
                xn.at[t, chunk_rows(i)],
                xc.at[buf, :, pl.ds(mult(deep * (1 - y), deep), deep)], xf.at[buf, 1],
            ),
        )

    def cot_fetch(h, i, buf):
        return pltpu.make_async_copy(
            cot.at[:, part_rows(i), cols(h)], cc.at[buf], cf.at[buf]
        )

    def w_own(p):
        t, h = tower(p)
        return pltpu.make_async_copy(
            wts.at[t, pl.ds(mult(kz * z, kz), kz), cols(h)], wv.at[p, :, cols(z)], wl.at[p],
        )

    def w_rows():
        return pl.ds(mult(deep * c + quarter * x, quarter), quarter)

    def w_z(p, to):
        t, h = tower(p)
        return remote(
            wts.at[
                t, pl.ds(mult(kz * to + deep * c + quarter * x, quarter), quarter), cols(h)
            ],
            wv.at[p, w_rows(), cols(z)],
            wz_send.at[p, to], wz_recv.at[p, z], at_z(to),
        )

    def w_z_strip(p, to, r):
        t, h = tower(p)
        at = deep * c + quarter * x + strip * r
        return remote(
            wts.at[t, pl.ds(mult(kz * to + at, strip), strip), cols(h)],
            wv.at[p, pl.ds(mult(at, strip), strip), cols(z)],
            wz_send.at[p, to], wz_recv.at[p, z], at_z(to),
        )

    def w_z_in(p, frm):
        here = wv.at[p, w_rows(), cols(frm)]
        return remote(here, here, wz_send.at[p, frm], wz_recv.at[p, frm], at_z(frm))

    def w_x(p, b):
        here = wv.at[p, w_rows(), cols(b)]
        return remote(here, here, wx_send.at[p, b], wx_recv.at[p, b], across_x)

    def w_x_in(p, b):
        here = wv.at[
            p, pl.ds(mult(deep * c + quarter * (1 - x), quarter), quarter), cols(b)
        ]
        return remote(here, here, wx_send.at[p, b], wx_recv.at[p, b], across_x)

    def w_c(p, b):
        here = wv.at[p, pl.ds(mult(deep * c, deep), deep), cols(b)]
        return remote(here, here, wc_send.at[p, b], wc_recv.at[p, b], across_c)

    def w_c_in(p, b):
        here = wv.at[p, pl.ds(mult(deep * (1 - c), deep), deep), cols(b)]
        return remote(here, here, wc_send.at[p, b], wc_recv.at[p, b], across_c)

    def rs_up(slot, zz):
        run = rs.at[slot, zz + 2 : ZED + 1]
        return remote(run, run, rs_send.at[slot, 0], rs_recv.at[slot, 0], up)

    def rs_down(slot, zz):
        run = rs.at[slot, 0:zz]
        return remote(run, run, rs_send.at[slot, 1], rs_recv.at[slot, 1], down)

    def rs_from_below(slot, zz):
        run = rs.at[slot, zz + 1 : ZED + 1]
        return remote(run, run, rs_send.at[slot, 0], rs_recv.at[slot, 0], down)

    def rs_from_above(slot, zz):
        run = rs.at[slot, 0 : zz + 1]
        return remote(run, run, rs_send.at[slot, 1], rs_recv.at[slot, 1], up)

    def at_place(first, last, do):
        for zz in range(first, last + 1):
            @pl.when(z == zz)
            def _(zz=zz):
                do(zz)

    def ag(at, b, going, device):
        here = gl.at[at.p, part_rows(at.i), cols(b)]
        return remote(
            here, here, ag_send.at[at.slot, going * ZED + b], ag_recv.at[at.slot, b], device
        )

    def dx_copy(t, i, buf):
        return remote(
            dsend.at[buf], dxn.at[t, chunk_rows(i)],
            dx_send.at[buf], dx_recv.at[t * n_chunk + i], across_y,
        )

    def dx_fetch(t, i):
        return pltpu.make_async_copy(dxn.at[t, chunk_rows(i)], dfetch, df.at[0])

    def dx_out(t, i):
        return pltpu.make_async_copy(dout, gfeat.at[t, chunk_rows(i)], dod.at[0])

    def mixed_out(h, i, buf):
        return pltpu.make_async_copy(
            mx.at[buf], mixed.at[:, part_rows(i), cols(h)], mxs.at[buf]
        )

    def tile_fetch(t, j, hk, start):
        lanes = pl.ds(mult(tile * j, tile), tile)
        near = pltpu.make_async_copy(feat.at[t, :, lanes], xsrc, tile_in.at[0])
        if not start:
            near.wait()
            return

        @pl.when(hk == y)
        def _():
            near.start()

        @pl.when(hk != y)
        def _():
            pltpu.make_async_copy(xn.at[t, :, lanes], xsrc, tile_in.at[0]).start()

    def core_copy(g):
        return remote(cstage, cland.at[g.buf], c_send.at[0], c_recv.at[g.buf], across_c)

    def across_copy(g, b):
        return remote(
            xstage.at[g.trio, b], xland.at[g.quad, b],
            x_send.at[g.trio, b], x_recv.at[g.quad, b], across_x,
        )

    def piece(g, source, core, lanes, n_lanes):
        return gwt.at[
            g.t, source,
            pl.ds(mult(deep * core + tile * g.j, tile), tile),
            pl.ds(mult(hw * g.h + lanes, xw), n_lanes),
        ]

    def z_copy(g, to):
        return remote(
            zstage.at[g.trio, to], piece(g, z, c, xw * x, xw),
            z_send.at[g.trio, to], z_recv.at[g.g, z], at_z(to),
        )

    def z_in(g, frm):
        here = piece(g, frm, c, xw * x, xw)
        return remote(here, here, z_send.at[g.trio, frm], z_recv.at[g.g, frm], at_z(frm))

    def z_own(g):
        return pltpu.make_async_copy(
            zstage.at[g.trio, z], piece(g, z, c, xw * x, xw), zl.at[g.trio]
        )

    def ax_own(g):
        return remote(
            zstage.at[g.trio, z], piece(g, z, c, xw * x, xw),
            zx_send.at[g.trio], ax_recv.at[g.g, z], across_x,
        )

    def ax_copy(g, b):
        here = piece(g, b, c, xw * x, xw)
        return remote(here, here, ax_send.at[g.g, b], ax_recv.at[g.g, b], across_x)

    def ax_in(g, b):
        here = piece(g, b, c, xw * (1 - x), xw)
        return remote(here, here, ax_send.at[g.g, b], ax_recv.at[g.g, b], across_x)

    def ac_copy(g, b):
        here = piece(g, b, c, 0, hw)
        return remote(here, here, ac_send.at[g.g, b], ac_recv.at[g.g, b], across_c)

    def ac_in(g, b):
        here = piece(g, b, 1 - c, 0, hw)
        return remote(here, here, ac_send.at[g.g, b], ac_recv.at[g.g, b], across_c)

    def sum_copy(stage, device):
        return remote(
            sums.at[stage], sums_land.at[stage], t_send.at[stage], t_recv.at[stage], device
        )

    def prod_y():
        return remote(prods.at[0], prods_land.at[ZED], t_send.at[2], t_recv.at[2], across_y)

    def prod_z(to):
        return remote(
            prods.at[1], prods_land.at[z], t_send.at[3 + to], t_recv.at[3 + z], at_z(to)
        )

    def prod_z_in(frm):
        here = prods_land.at[frm]
        return remote(here, here, t_send.at[3 + frm], t_recv.at[3 + frm], at_z(frm))

    barrier = pltpu.get_barrier_semaphore()
    for device in [at_z(o) for o in others] + [across_y, across_x, across_c]:
        pl.semaphore_signal(barrier, inc=1, device_id=device, device_id_type=MESH)
    pl.semaphore_wait(barrier, 6)

    for to in others:
        w_z(0, to).start()
    x_copy(0, 0).start()
    x_copy(0, 1).start()
    w_own(0).start()
    cot_fetch(0, 0, 0).start()

    image_row = lax.broadcasted_iota(jnp.int32, (images, images), 0)
    image_col = lax.broadcasted_iota(jnp.int32, (images, images), 1)
    crops = counts[...].astype(F32)
    ends = jnp.dot(
        jnp.broadcast_to(crops, (8, images)), (image_row <= image_col).astype(F32),
        precision=lax.Precision.HIGHEST, preferred_element_type=F32,
    )[0:1]
    starts = ends - crops
    block = mask.shape[1]
    lane = scale.shape[1]

    for r in range(rows // block):
        index = (
            lax.broadcasted_iota(jnp.int32, (block, images), 0) + r * block
        ).astype(F32)
        inside = (index >= starts) & (index < ends)
        count_row = jnp.sum(jnp.where(inside, crops, 0.0), axis=1, keepdims=True)
        diagonal = lax.broadcasted_iota(jnp.int32, (block, block), 0) == (
            lax.broadcasted_iota(jnp.int32, (block, block), 1)
        )
        usable = jnp.sum(
            jnp.where(diagonal, mask[r : r + 1, :].astype(F32), 0.0),
            axis=1, keepdims=True,
        )
        live = (count_row > 0.0) & (usable == 1.0)
        share = jnp.where(live, 1.0 / jnp.maximum(count_row, 1.0), 0.0)
        scale[r * block : (r + 1) * block, :] = jnp.broadcast_to(share, (block, lane))

    for frm in others:
        w_z_in(0, frm).wait_recv()
        w_x(0, frm).start()
    for to in others:
        w_z(1, to).start()
    w_own(1).start()
    for frm in others:
        w_x_in(0, frm).wait_recv()
        w_c(0, frm).start()
    x_copy(0, 0).wait_recv()
    for copy in x_fetch(0, 0, 0):
        copy.start()

    def final(at, later):
        p, i, slot, t, h, buf = at.p, at.i, at.slot, at.t, at.h, at.buf
        cot_fetch(h, i, buf).wait()

        @pl.when(at.u >= 2 * n_part + 2)
        def _():
            mixed_out(h, i, buf).wait()

        @pl.when(i == 0)
        def _():
            stat[p] = jnp.zeros(stat.shape[1:], F32)

        lanes = cols(h)
        shift = bias[pl.ds(t, 1), lanes]
        st = [stitch[s, pl.ds(t, 1), lanes] for s in range(2)]
        band = min(BAND, part)

        def step(r, carry):
            here = part_rows_of(r, band)
            there = pl.ds(mult(i * part + r * band, band), band)
            value = pf[at.prod, z, here, :]
            below = wide(rs[slot, z + 1, here, :])
            above = wide(rs[slot, z, here, :])
            value = value + jnp.where(z > 0, below, 0.0) + jnp.where(z < ZED - 1, above, 0.0)
            pre = value + shift
            phi = 0.5 * (1.0 + lax.erf(pre * 0.7071067811865476))
            hidden = pre * phi
            slope = phi + pre * (jnp.exp(-0.5 * pre * pre) * 0.3989422804014327)
            weight = scale[there, 0:1]
            first = wide(cc[buf, 0, here, :]) * weight
            second = wide(cc[buf, 1, here, :]) * weight
            back0 = st[0] * first * slope
            back1 = st[1] * second * slope
            gl[p, there, cols(z)] = half(back0 + back1)

            def fold(v):
                return jnp.sum(v.reshape(band // 8, 8, hw), axis=0)

            stat[p, 0] += fold(back0)
            stat[p, 1] += fold(back1)
            stat[p, 2] += fold(first * hidden)
            stat[p, 3] += fold(second * hidden)

            @pl.when(t == 0)
            def _():
                h0[h, there, :] = hidden

            @pl.when(t == 1)
            def _():
                before = h0[h, there, :]
                for s in range(2):
                    mx[buf, s, here, :] = half(
                        stitch[s, 0:1, lanes] * before + st[s] * hidden
                    )

            return carry

        lax.fori_loop(0, part // band, step, 0)

        @pl.when(z < ZED - 1)
        def _():
            ag(at, z, 0, up).start()

        @pl.when(z > 0)
        def _():
            ag(at, z, 1, down).start()

        @pl.when(t == 1)
        def _():
            mixed_out(h, i, buf).start()

        @pl.when(at.u + 1 < parts)
        def _():
            cot_fetch(later.h, later.i, later.buf).start()

    def part_rows_of(r, band):
        return pl.ds(mult(r * band, band), band)

    def forward_ag(at, far):
        @pl.when((at.u >= 0) & (at.u < parts))
        def _():
            @pl.when(z - far >= 0)
            def _():
                ag(at, z - far, 0, up).wait_recv()

                @pl.when(z < ZED - 1)
                def _():
                    ag(at, z - far, 0, up).start()

            @pl.when(z + far < ZED)
            def _():
                ag(at, z + far, 1, down).wait_recv()

                @pl.when(z > 0)
                def _():
                    ag(at, z + far, 1, down).start()

    def dx_part(t, i, hk):
        there = chunk_rows(i)
        krows = pl.ds(mult(deep * hk, deep), deep)
        acc = None
        for h in range(HALVES):
            term = lax.dot_general(
                gl[2 * t + h, there, :], wv[2 * t + h, krows, :],
                (((1,), (1,)), ((), ())), preferred_element_type=F32,
            )
            acc = term if acc is None else acc + term
        return acc

    def dx_step(t, i, buf):
        @pl.when((i >= HELD) | (t > 0))
        def _():
            dx_copy(t, i, buf).wait_send()

        dsend[buf] = half(dx_part(t, i, 1 - y))
        dx_copy(t, i, buf).start()
        own[buf] = dx_part(t, i, y)

    def dx_begin(t, i, buf):
        dx_copy(t, i, buf).wait_recv()
        dx_fetch(t, i).start()

    def dx_final(t, i, buf):
        @pl.when((i >= 1) | (t > 0))
        def _():
            dx_out(t, i).wait()

        dx_fetch(t, i).wait()

        def step(j, inner):
            lanes = pl.ds(mult(tile * j, tile), tile)
            dout[:, lanes] = half(own[buf, :, lanes] + wide(dfetch[:, lanes]))
            return inner

        lax.fori_loop(0, 3, step, 0)
        dx_out(t, i).start()

    def listed(u, times, do):
        e, hit = 0, False
        for index, time in enumerate(times):
            same = u == time
            e = jnp.where(same, index, e)
            hit = hit | same

        @pl.when(hit)
        def _():
            do(e)

    def chunk_of(do):
        def run(e):
            t = jnp.where(e >= n_chunk, 1, 0)
            do(t, e - n_chunk * t, lax.rem(e, HELD))

        return run

    def turn():
        lanes_at_once = min(128, tile)

        def step(q, carry):
            lanes = pl.ds(mult(q * lanes_at_once, lanes_at_once), lanes_at_once)
            xt[lanes, :] = xsrc[:, lanes].T
            return carry

        lax.fori_loop(0, tile // lanes_at_once, step, 0)

    def tile_dot(g):
        return jnp.dot(xt[...], gl[g.p], preferred_element_type=F32)

    def stage_one(g):
        tile_fetch(g.t, g.j, 1 - c, False)
        turn()
        tile_fetch(g.t, g.j, c, True)
        cstage[...] = half(tile_dot(g))
        core_copy(g).start()

    def stage_two(g):
        tile_fetch(g.t, g.j, c, False)
        turn()

        @pl.when(g.j < 2)
        def _():
            tile_fetch(g.t, g.j + 1, 1 - c, True)

        core_copy(g).wait()
        product = tile_dot(g)
        for b in range(ZED):
            block = product[:, b * hw : (b + 1) * hw] + wide(
                cland[g.buf, :, b * hw : (b + 1) * hw]
            )
            left, right = block[:, :xw], block[:, xw:]
            kept[g.trio, b] = jnp.where(x == 0, left, right)
            xstage[g.trio, b] = half(jnp.where(x == 0, right, left))

        def send(q, carry):
            across_copy(g, lax.rem(z + 3 + 3 * q, ZED)).start()
            return carry

        lax.fori_loop(0, ZED, send, 0)

    def stage_three(g):
        @pl.when(g.g >= 3)
        def _():
            for to in others:
                z_copy(g, to).wait_send()
            ax_own(g).wait_send()

        def add(b):
            across_copy(g, b).wait()
            zstage[g.trio, b] = half(kept[g.trio, b] + wide(xland[g.quad, b]))

        def step(q, carry):
            b = lax.rem(z + 3 + 3 * q, ZED)
            add(b)
            z_copy(g, b).start()
            return carry

        lax.fori_loop(0, ZED - 1, step, 0)
        add(z)
        z_own(g).start()
        ax_own(g).start()

    def stage_four(g):
        def step(q, carry):
            b = lax.rem(z + 1 + q, ZED)
            z_in(g, b).wait_recv()
            ax_copy(g, b).start()
            return carry

        lax.fori_loop(0, ZED - 1, step, 0)
        z_own(g).wait()

    def stage_five(g):
        def step(q, carry):
            b = lax.rem(z + q, ZED)
            ax_in(g, b).wait_recv()
            ac_copy(g, b).start()
            return carry

        lax.fori_loop(0, ZED, step, 0)

    def stage_six(g):
        def step(b, carry):
            ac_in(g, b).wait_recv()
            return carry

        lax.fori_loop(0, ZED, step, 0)

    def tile_of(g):
        p = lax.div(g, 3)
        t, h = tower(p)
        return Tile(
            g=g, p=p, t=t, h=h, j=g - 3 * p,
            buf=lax.rem(g, 2), trio=g - 3 * p, quad=lax.rem(g, 4),
        )

    def tile_in_hand(do):
        return lambda g: do(tile_of(g))

    def body(u, carry):
        p0 = lax.div(u, n_part)
        i0 = u - p0 * n_part
        slot0, prod0 = lax.rem(u, RING), lax.rem(u, PRODUCTS)
        buf0 = lax.rem(u, 2)

        def before(lag):
            if isinstance(lag, int):
                whole, left = divmod(lag, n_part)
            else:
                whole, left = 0, lag
            under = i0 < left
            p = p0 - whole - jnp.where(under, 1, 0)
            i = i0 - left + jnp.where(under, n_part, 0)
            in_ring = lag % RING if isinstance(lag, int) else lag
            in_prods = lag % PRODUCTS if isinstance(lag, int) else lag
            slot = slot0 - in_ring + jnp.where(slot0 < in_ring, RING, 0)
            prod = prod0 - in_prods + jnp.where(prod0 < in_prods, PRODUCTS, 0)
            t, h = tower(p)
            return Part(u=u - lag, p=p, i=i, t=t, h=h, slot=slot, prod=prod, buf=lax.rem(i, 2))

        @pl.when((u >= 5) & (u < parts + 5))
        def _():
            slot = before(5).slot
            at_place(0, ZED - 2, lambda zz: rs_up(slot, zz).wait_send())
            at_place(1, ZED - 1, lambda zz: rs_down(slot, zz).wait_send())

        @pl.when((u >= 8) & (u < parts + 8))
        def _():
            at = before(8)

            def step(b, inner):
                @pl.when((z < ZED - 1) & (b <= z))
                def _():
                    ag(at, b, 0, up).wait_send()

                @pl.when((z > 0) & (b >= z))
                def _():
                    ag(at, b, 1, down).wait_send()

                return inner

            lax.fori_loop(0, ZED, step, 0)

        ck = lax.div(i0, SUB)
        fresh = ck * SUB == i0
        t0, h0_ = tower(p0)
        xbuf = lax.rem(ck, 2)

        @pl.when((u < parts) & fresh)
        def _():
            @pl.when(i0 == 0)
            def _():
                w_own(p0).wait()
                for frm in others:
                    w_c_in(p0, frm).wait_recv()

            for copy in x_fetch(t0, ck, xbuf):
                copy.wait()

            product = jnp.dot(xc[xbuf], wv[p0], preferred_element_type=F32)
            for b in range(ZED):
                for s in range(SUB):
                    pf[prod0 + s, b] = product[
                        s * part : (s + 1) * part, b * hw : (b + 1) * hw
                    ]

        going_up = before(z)

        @pl.when((going_up.u >= 0) & (going_up.u < parts))
        def _():
            slot, prod = going_up.slot, going_up.prod
            at_place(1, ZED - 1, lambda zz: rs_from_below(slot, zz).wait_recv())

            @pl.when(z == 0)
            def _():
                for b in range(1, ZED):
                    rs[slot, b + 1] = half(pf[prod, b])

            @pl.when(z > 0)
            def _():
                def step(b, inner):
                    rs[slot, b + 1] = half(wide(rs[slot, b + 1]) + pf[prod, b])
                    return inner

                lax.fori_loop(z + 1, ZED, step, 0)

            at_place(0, ZED - 2, lambda zz: rs_up(slot, zz).start())

        going_down = before(ZED - 1 - z)

        @pl.when((going_down.u >= 0) & (going_down.u < parts))
        def _():
            slot, prod = going_down.slot, going_down.prod
            at_place(0, ZED - 2, lambda zz: rs_from_above(slot, zz).wait_recv())

            @pl.when(z == ZED - 1)
            def _():
                for b in range(ZED - 1):
                    rs[slot, b] = half(pf[prod, b])

            @pl.when(z < ZED - 1)
            def _():
                def step(b, inner):
                    rs[slot, b] = half(wide(rs[slot, b]) + pf[prod, b])
                    return inner

                lax.fori_loop(0, z, step, 0)

            at_place(1, ZED - 1, lambda zz: rs_down(slot, zz).start())

        @pl.when(fresh & (u + 2 * SUB < 2 * n_part))
        def _():
            k = p0 * n_chunk + ck + 2
            over = jnp.where(k >= n_chunk, 1, 0)
            x_copy(over, k - over * n_chunk).start()

        @pl.when(fresh & (u + SUB < parts))
        def _():
            wrap = jnp.where(ck + 1 == n_chunk, 1, 0)
            i = ck + 1 - wrap * n_chunk
            t, h = tower(p0 + wrap)

            @pl.when(h == 0)
            def _():
                x_copy(t, i).wait_recv()

            for copy in x_fetch(t, i, lax.rem(i, 2)):
                copy.start()

        @pl.when((u >= 3) & (u < parts + 3))
        def _():
            final(before(3), before(2))

        forward_ag(before(4), 1)
        forward_ag(before(5), 2)
        forward_ag(before(6), 3)

        listed(u, DX_BEGINS, chunk_of(dx_begin))
        listed(u, DX_ENDS, chunk_of(dx_final))
        listed(u, DX_TIMES, chunk_of(dx_step))

        listed(u, THREES, tile_in_hand(stage_three))
        listed(u, TWOS, tile_in_hand(stage_two))
        listed(u, ONES, tile_in_hand(stage_one))
        listed(u, FOURS, tile_in_hand(stage_four))
        listed(u, FIVES, tile_in_hand(stage_five))
        listed(u, SIXES, tile_in_hand(stage_six))

        def first_fetch(p):
            tile_fetch(lax.div(p, HALVES), 0, 1 - c, True)

        listed(u, [time - 1 for time in ONES[::3]], first_fetch)

        for p, times in W_STRIPS.items():
            def send_strip(r, p=p):
                for to in others:
                    w_z_strip(p, to, r).start()

                @pl.when(r == 0)
                def _():
                    w_own(p).start()

            listed(u, times, send_strip)

        for p, times in W_ACROSS.items():
            for q, time in enumerate(times):
                @pl.when(u == time)
                def _(p=p, q=q):
                    w_z_in(p, others[q]).wait_recv()
                    w_x(p, others[q]).start()

        for p, times in W_CORES.items():
            for q, time in enumerate(times):
                @pl.when(u == time)
                def _(p=p, q=q):
                    w_x_in(p, others[q]).wait_recv()
                    w_c(p, others[q]).start()

        @pl.when(u == parts + 3)
        def _():
            for p in range(PHASES):
                t, h = p // HALVES, p % HALVES
                for s in range(2):
                    for what in range(2):
                        sums[0, pl.ds(4 * what + 2 * s + t, 1), h * hw : (h + 1) * hw] = jnp.sum(
                            stat[p, 2 * what + s], axis=0, keepdims=True
                        )
            sum_copy(0, across_c).start()

        @pl.when(u == parts + 4)
        def _():
            sum_copy(0, across_c).wait()
            sums[1] = sums[0] + sums_land[0]
            sum_copy(1, across_x).start()

        @pl.when(u == parts + 5)
        def _():
            sum_copy(1, across_x).wait()
            both = sums[1] + sums_land[1]
            sums[2] = both
            member = (
                lax.broadcasted_iota(jnp.int32, (width, lane), 0) % FLAG_GROUPS
                == lax.broadcasted_iota(jnp.int32, (width, lane), 1) % FLAG_GROUPS
            ).astype(F32)
            bias_rows = both[0:4]
            inner = both[0:2] * both[2:4]
            stack = jnp.concatenate([inner, bias_rows * bias_rows, inner], axis=0)
            prods[0] = jnp.dot(
                stack, member, precision=lax.Precision.HIGHEST, preferred_element_type=F32
            )
            prod_y().start()

        @pl.when(u == parts + 6)
        def _():
            prod_y().wait()
            prods[1] = prods[0] + prods_land[ZED]
            for to in others:
                prod_z(to).start()

        @pl.when(u == parts + 7)
        def _():
            for frm in others:
                prod_z_in(frm).wait_recv()
            prods_land[z] = prods[1]
            whole = prods_land[0] + prods_land[1] + prods_land[2] + prods_land[3]
            both = sums[2]
            group = lax.broadcasted_iota(jnp.int32, (1, lane), 1) % FLAG_GROUPS

            def over(row):
                return jnp.concatenate([row] * (width // lane), axis=1)

            def flag_row(s, t):
                row = jnp.zeros((1, lane), F32)
                for g in range(FLAG_GROUPS):
                    row = jnp.where(group == g, flags[s, t, g].astype(F32), row)
                return row

            for t in range(2):
                task0, task1 = both[t : t + 1], both[2 + t : 3 + t]
                dots = whole[t : t + 1]
                coef0 = over(flag_row(0, t) * dots / (whole[4 + t : 5 + t] + 1e-06))
                coef1 = over(flag_row(1, t) * dots / (whole[2 + t : 3 + t] + 1e-06))
                gbias[t : t + 1] = (task0 - coef0 * task1) + (task1 - coef1 * task0)
            for s in range(2):
                gstitch[s] = both[4 + 2 * s : 6 + 2 * s]

        return carry

    lax.fori_loop(0, max(SIXES + DX_ENDS) + 1, body, 0)

    last = 3 * PHASES - 1

    for g in (last - 2, last - 1, last):
        for to in others:
            z_copy(tile_of(g), to).wait_send()
        ax_own(tile_of(g)).wait_send()
    for i in range(n_chunk - HELD, n_chunk):
        dx_copy(1, i, (n_chunk + i) % HELD).wait_send()
    for i in (n_part - 2, n_part - 1):
        mixed_out(1, i, i % 2).wait()
    dx_out(1, n_chunk - 1).wait()

    def drain_tiles(g, carry):
        at = tile_of(g)
        for b in others:
            ax_copy(at, b).wait_send()
        for b in range(ZED):
            ac_copy(at, b).wait_send()
        return carry

    lax.fori_loop(0, last + 1, drain_tiles, 0)

    def drain_x(i, carry):
        x_copy(0, i).wait_send()
        x_copy(1, i).wait_send()
        return carry

    lax.fori_loop(0, n_chunk, drain_x, 0)

    def drain_w(p, carry):
        for to in others:
            w_z(p, to).wait_send()
            w_x(p, to).wait_send()
            w_c(p, to).wait_send()
        return carry

    lax.fori_loop(0, PHASES, drain_w, 0)
    for to in others:
        prod_z(to).wait_send()


def fused_call(feat, wts, cot, bias, stitch, counts, mask, flags):
    rows, deep, width = feat.shape[1], feat.shape[2], wts.shape[2]
    chunk = rows // 6
    part = chunk // SUB
    hw, kz, tile = width // 2, 2 * deep, deep // 3
    cat, xw = 4 * hw, width // 4
    lane = min(128, width)
    dma = pltpu.SemaphoreType.DMA
    anywhere = pl.BlockSpec(memory_space=pl.ANY)
    inside = pl.BlockSpec(memory_space=pltpu.VMEM)
    scalars = pl.BlockSpec(memory_space=pltpu.SMEM)

    def v(shape, kind=BF16):
        return pltpu.VMEM(shape, kind)

    out_shape = [
        jax.ShapeDtypeStruct((2, rows, width), BF16),
        jax.ShapeDtypeStruct((2, rows, deep), BF16),
        jax.ShapeDtypeStruct((2, ZED, kz, width), BF16),
        jax.ShapeDtypeStruct((2, width), F32),
        jax.ShapeDtypeStruct((2, 2, width), F32),
        jax.ShapeDtypeStruct((2, rows, deep), BF16),
        jax.ShapeDtypeStruct((2, rows, deep), BF16),
    ]
    scratch = [
        v((PHASES, kz, cat)),
        v((PHASES, rows, cat)),
        v((RING, 5, part, hw)),
        v((2, rows, hw), F32),
        v((2, chunk, kz)),
        v((PRODUCTS, ZED, part, hw), F32),
        v((2, 2, part, hw)),
        v((2, 2, part, hw)),
        v((HELD, chunk, deep), F32),
        v((HELD, chunk, deep)),
        v((chunk, deep)),
        v((chunk, deep)),
        v((rows, tile)),
        v((tile, rows)),
        v((tile, cat)),
        v((2, tile, cat)),
        v((3, ZED, tile, xw)),
        v((4, ZED, tile, xw)),
        v((3, ZED, tile, xw), F32),
        v((3, ZED, tile, xw)),
        v((rows, lane), F32),
        v((PHASES, 4, 8, hw), F32),
        v((3, 8, width), F32),
        v((2, 8, width), F32),
        v((2, 8, lane), F32),
        v((5, 8, lane), F32),
        dma((RING, 2)), dma((RING, 2)), dma((RING, 8)), dma((RING, 4)),
        dma((12,)), dma((12,)),
        dma((4, 4)), dma((4, 4)), dma((4, 4)), dma((4, 4)), dma((4, 4)), dma((4, 4)), dma((4,)),
        dma((2, 2)), dma((2,)), dma((2,)), dma((HELD,)), dma((12,)), dma((1,)), dma((1,)),
        dma((1,)), dma((1,)), dma((2,)), dma((3, 4)), dma((4, 4)), dma((3, 4)), dma((12, 4)),
        dma((3,)), dma((3,)),
        dma((12, 4)), dma((12, 4)), dma((12, 4)), dma((12, 4)), dma((8,)), dma((8,)),
    ]
    flops = 3 * 2 * 2 * rows * kz * cat * 2
    return pl.pallas_call(
        functools.partial(fused_kernel, rows, deep, width, chunk),
        out_shape=out_shape,
        in_specs=[anywhere] * 3 + [inside] * 4 + [scalars],
        out_specs=[anywhere] * 3 + [inside] * 2 + [anywhere] * 2,
        scratch_shapes=scratch,
        compiler_params=pltpu.CompilerParams(
            collective_id=0, has_side_effects=True, vmem_limit_bytes=64 * 1024 * 1024
        ),
        cost_estimate=pl.CostEstimate(
            flops=flops, bytes_accessed=200_000_000, transcendentals=2 * rows * width * 2
        ),
        name="cross_stitch_step",
    )(feat, wts, cot, bias, stitch, counts, mask, flags)


def finish_kernel(
    block, low, mixed, gfeat, gbias, gstitch,
    out, mixed_out, gfeat_out, gbias_out, gstitch_out,
    taken, given, held_mixed, held_gfeat, in_sem, out_sem, pass_sem,
):
    n_block = low.shape[0] // block
    fetched = (
        pltpu.make_async_copy(mixed, held_mixed, pass_sem.at[0]),
        pltpu.make_async_copy(gfeat, held_gfeat, pass_sem.at[1]),
    )
    passed = (
        pltpu.make_async_copy(held_mixed, mixed_out, pass_sem.at[2]),
        pltpu.make_async_copy(held_gfeat, gfeat_out, pass_sem.at[3]),
    )

    def take(i):
        return pltpu.make_async_copy(
            low.at[pl.ds(i * block, block)], taken.at[i % WIDEN_SLOTS], in_sem.at[i % WIDEN_SLOTS]
        )

    def give(i):
        return pltpu.make_async_copy(
            given.at[i % WIDEN_SLOTS], out.at[pl.ds(i * block, block)], out_sem.at[i % WIDEN_SLOTS]
        )

    for i in range(min(WIDEN_SLOTS, n_block)):
        take(i).start()
    for copy in fetched:
        copy.start()
    gbias_out[...] = gbias[...]
    gstitch_out[...] = gstitch[...]
    for i in range(n_block):
        slot = i % WIDEN_SLOTS
        take(i).wait()
        if i >= WIDEN_SLOTS:
            give(i - WIDEN_SLOTS).wait()
        given[slot] = wide(taken[slot])
        give(i).start()
        if i + WIDEN_SLOTS < n_block:
            take(i + WIDEN_SLOTS).start()
        if i == 2:
            for arrived, copy in zip(fetched, passed):
                arrived.wait()
                copy.start()
    for i in range(max(0, n_block - WIDEN_SLOTS), n_block):
        give(i).wait()
    for copy in passed:
        copy.wait()


def finish(low, mixed, gfeat, gbias, gstitch):
    tall, width = low.shape
    block = tall // WIDEN_BLOCKS
    anywhere = pl.BlockSpec(memory_space=pl.ANY)
    inside = pl.BlockSpec(memory_space=pltpu.VMEM)
    moved = sum(a.size * a.dtype.itemsize for a in (mixed, gfeat))
    return pl.pallas_call(
        functools.partial(finish_kernel, block),
        in_specs=[anywhere] * 3 + [inside] * 2,
        out_specs=[anywhere] * 3 + [inside] * 2,
        out_shape=[
            jax.ShapeDtypeStruct(a.shape, kind)
            for a, kind in ((low, F32), (mixed, BF16), (gfeat, BF16), (gbias, F32), (gstitch, F32))
        ],
        scratch_shapes=[
            pltpu.VMEM((WIDEN_SLOTS, block, width), BF16),
            pltpu.VMEM((WIDEN_SLOTS, block, width), F32),
            pltpu.VMEM(mixed.shape, BF16),
            pltpu.VMEM(gfeat.shape, BF16),
            pltpu.SemaphoreType.DMA((WIDEN_SLOTS,)),
            pltpu.SemaphoreType.DMA((WIDEN_SLOTS,)),
            pltpu.SemaphoreType.DMA((4,)),
        ],
        compiler_params=pltpu.CompilerParams(vmem_limit_bytes=60 * 1024 * 1024),
        cost_estimate=pl.CostEstimate(
            flops=tall * width, bytes_accessed=6 * tall * width + 2 * moved, transcendentals=0
        ),
        name="finish",
    )(low, mixed, gfeat, gbias, gstitch)


def fused_plan(mesh):
    def per_device(features, weights, bias, stitch, cotangent, crop_counts, row_mask, flags):
        rows, deep = features.shape[1:]
        width = weights.shape[2]
        mixed, gfeat, gwt, gbias, gstitch, _, _ = fused_call(
            features, weights, cotangent, bias, stitch,
            crop_counts.reshape(1, -1), row_mask.reshape(-1, min(128, rows // 6)), flags,
        )
        grad_weights, mixed, gfeat, gbias, gstitch = finish(
            gwt.reshape(-1, width), mixed, gfeat, gbias, gstitch
        )
        return mixed, gfeat, grad_weights.reshape(2, ZED * 2 * deep, width), gbias, gstitch

    return per_device


def plan_for(mesh):
    if mesh.shape["batch"] == 4 and mesh.shape["mp"] == 2 * ZED:
        return fused_plan(mesh)
    return generic_plan(mesh)


def solution(mesh):
    in_specs = (
        P(None, "batch", "mp"),
        P(None, None, "mp"),
        P(None, "mp"),
        P(None, None, "mp"),
        P(None, "batch", "mp"),
        P("batch"),
        P("batch"),
        P(),
    )
    out_specs = (
        P(None, "batch", "mp"),
        P(None, "batch", "mp"),
        P(None, None, "mp"),
        P(None, "mp"),
        P(None, None, "mp"),
    )
    return jax.shard_map(
        plan_for(mesh), mesh=mesh, in_specs=in_specs, out_specs=out_specs, check_vma=False
    )
```

```python
import collections
import functools

import jax
import jax.numpy as jnp
from jax import lax
from jax.experimental import pallas as pl
from jax.experimental.pallas import tpu as pltpu
from jax.sharding import PartitionSpec as P

FLAG_GROUPS = 8
OUTER = 4


def row_weights(counts, mask):
    ends = jnp.cumsum(counts)
    starts = ends - counts
    index = lax.broadcasted_iota(jnp.int32, (mask.shape[0], counts.shape[0]), 0)
    inside = (index >= starts[None, :]) & (index < ends[None, :])
    count_row = jnp.sum(jnp.where(inside, counts[None, :], 0), axis=1)
    live = (count_row > 0) & (mask == 1)
    return jnp.where(live, 1.0 / jnp.maximum(count_row, 1).astype(jnp.float32), 0.0)


def project_bias(task_bias, flags):
    local_width = task_bias.shape[2]
    channel = lax.axis_index("mp") * local_width + lax.broadcasted_iota(
        jnp.int32, (local_width, FLAG_GROUPS), 0
    )
    member = (
        channel % FLAG_GROUPS == lax.broadcasted_iota(jnp.int32, (local_width, FLAG_GROUPS), 1)
    ).astype(jnp.float32)
    dots = jnp.dot(task_bias[0] * task_bias[1], member, precision=lax.Precision.HIGHEST)
    norms = jnp.einsum(
        "stc,cg->stg", task_bias * task_bias, member, precision=lax.Precision.HIGHEST
    )
    dots, norms = lax.psum((dots, norms), "mp")
    flag = flags.astype(jnp.float32)
    coef_first = jnp.dot(
        flag[0] * dots / (norms[1] + 1e-06), member.T, precision=lax.Precision.HIGHEST
    )
    coef_second = jnp.dot(
        flag[1] * dots / (norms[0] + 1e-06), member.T, precision=lax.Precision.HIGHEST
    )
    first = task_bias[0] - coef_first * task_bias[1]
    second = task_bias[1] - coef_second * task_bias[0]
    return first + second


def generic_plan(mesh):
    n_mp = mesh.shape["mp"]
    n_batch = mesh.shape["batch"]
    inner = n_mp // OUTER
    inner_groups = [[o * inner + i for i in range(inner)] for o in range(OUTER)]
    outer_groups = [[o * inner + i for o in range(OUTER)] for i in range(inner)]

    def per_device(features, weights, bias, stitch, cotangent, crop_counts, row_mask, flags):
        rows = features.shape[1]
        width = weights.shape[2]
        depth = features.shape[2] * inner
        held = lax.all_gather(
            features, "mp", axis=2, tiled=True, axis_index_groups=inner_groups
        )
        split = weights.reshape(2, OUTER, depth, width)
        block = lax.all_to_all(
            split, "mp", split_axis=1, concat_axis=1, axis_index_groups=outer_groups
        )
        block = block.reshape(2, OUTER, depth, width)
        part = jnp.einsum("trk,tokc->otrc", held, block, preferred_element_type=jnp.float32)
        linear = lax.psum_scatter(
            part.astype(jnp.bfloat16),
            "mp",
            scatter_dimension=0,
            axis_index_groups=outer_groups,
        ).astype(jnp.float32)
        pre = linear + bias[:, None, :]
        hidden, gelu_back = jax.vjp(lambda v: jax.nn.gelu(v, approximate=False), pre)
        mixed = stitch[:, 0, None, :] * hidden[0][None] + stitch[:, 1, None, :] * hidden[1][None]
        scale_rows = row_weights(crop_counts, row_mask)
        grad_out = cotangent.astype(jnp.float32) * scale_rows[None, :, None]
        first_task = gelu_back(stitch[0][:, None, :] * grad_out[0][None])[0]
        second_task = gelu_back(stitch[1][:, None, :] * grad_out[1][None])[0]
        task_bias = jnp.stack([jnp.sum(first_task, axis=1), jnp.sum(second_task, axis=1)])
        grad_linear = (first_task + second_task).astype(jnp.bfloat16)
        grad_stitch = jnp.sum(grad_out[:, None] * hidden[None], axis=2)
        every = lax.all_gather(grad_linear, "mp", axis_index_groups=outer_groups)
        grad_part = jnp.einsum(
            "otrc,tokc->trk", every, block, preferred_element_type=jnp.float32
        )
        grad_part = grad_part.astype(jnp.bfloat16).reshape(2, rows, inner, depth // inner)
        grad_features = lax.psum_scatter(
            grad_part.transpose(2, 0, 1, 3),
            "mp",
            scatter_dimension=0,
            axis_index_groups=inner_groups,
        )
        weight_part = jnp.einsum(
            "trk,otrc->otkc", held, every, preferred_element_type=jnp.float32
        )
        weight_part = weight_part.astype(jnp.bfloat16).reshape(
            OUTER, 2, n_batch, depth // n_batch, width
        )
        share = lax.psum_scatter(
            weight_part.transpose(2, 0, 1, 3, 4), "batch", scatter_dimension=0
        )
        share = lax.all_to_all(
            share, "mp", split_axis=0, concat_axis=0, axis_index_groups=outer_groups
        )
        share = share.reshape(OUTER, 2, depth // n_batch, width)
        whole = lax.all_gather(share, "batch")
        grad_weights = whole.transpose(2, 1, 0, 3, 4).reshape(2, OUTER * depth, width)
        task_bias, grad_stitch = lax.psum((task_bias, grad_stitch), "batch")
        grad_bias = project_bias(task_bias, flags)
        return (
            mixed.astype(jnp.bfloat16),
            grad_features.astype(jnp.bfloat16),
            grad_weights.astype(jnp.float32),
            grad_bias,
            grad_stitch,
        )

    return per_device


MESH = pl.DeviceIdType.MESH
BF16 = jnp.bfloat16
F32 = jnp.float32
ZED = 4
HALVES = 2
PHASES = 4
RING = 8
BAND = 32
SUB = 2
PRODUCTS = 6
HELD = 4
WIDEN_BLOCKS = 12
WIDEN_SLOTS = 4

DX_TIMES = (20, 21, 23, 25, 28, 42, 43, 46, 48, 60, 66, 85)
DX_BEGINS = (22, 24, 26, 34, 40, 45, 50, 61, 64, 71, 78, 89)
DX_ENDS = (23, 25, 29, 35, 41, 47, 51, 62, 68, 75, 79, 95)
ONES = (19, 24, 25, 30, 36, 40, 43, 45, 47, 54, 62, 73)
TWOS = (24, 25, 28, 34, 40, 42, 44, 47, 50, 58, 70, 77)
THREES = (25, 28, 35, 40, 42, 46, 49, 57, 65, 67, 86, 91)
FOURS = (26, 31, 38, 44, 45, 47, 51, 63, 81, 88, 89, 106)
FIVES = (32, 38, 42, 49, 57, 59, 66, 69, 88, 97, 110, 112)
SIXES = (52, 53, 55, 62, 70, 79, 85, 86, 95, 108, 114, 115)
W_STRIPS = {2: (5, 6, 7, 8, 9, 10), 3: (16, 17, 21, 23, 24, 28)}
W_ACROSS = {1: (1, 1, 2), 2: (11, 17, 18), 3: (29, 30, 32)}
W_CORES = {1: (2, 4, 8), 2: (13, 20, 22), 3: (33, 34, 35)}


Part = collections.namedtuple("Part", ("u", "p", "i", "t", "h", "slot", "prod", "buf"))
Tile = collections.namedtuple("Tile", ("g", "p", "t", "h", "j", "buf", "trio", "quad"))


def half(value):
    return value.astype(BF16)


def wide(value):
    return value.astype(F32)


def fused_kernel(
    rows, deep, width, chunk,
    feat, wts, cot, bias, stitch, counts, mask, flags,
    mixed, gfeat, gwt, gbias, gstitch, xn, dxn,
    wv, gl, rs, h0, xc, pf, cc, mx, own, dsend, dfetch, dout,
    xsrc, xt, cstage, cland, xstage, xland, kept, zstage,
    scale, stat, sums, sums_land, prods, prods_land,
    rs_send, rs_recv, ag_send, ag_recv, xs_send, xs_recv,
    wz_send, wz_recv, wx_send, wx_recv, wc_send, wc_recv, wl,
    xf, cf, mxs, dx_send, dx_recv, df, dod,
    tile_in, c_send, c_recv, x_send, x_recv, z_send, z_recv, zl, zx_send,
    ax_send, ax_recv, ac_send, ac_recv, t_send, t_recv,
):
    batch, mp = lax.axis_index("batch"), lax.axis_index("mp")
    z, y = mp // 2, mp % 2
    x, c = batch // 2, batch % 2
    up = {"mp": mp + 2}
    down = {"mp": mp - 2}
    across_y = {"mp": 2 * z + 1 - y}
    across_x = {"batch": 2 * (1 - x) + c}
    across_c = {"batch": 2 * x + 1 - c}

    def at_z(other):
        return {"mp": 2 * other + y}

    others = (3 - z, (z + 2) % 4, z + 1 - 2 * (z % 2))

    n_chunk = rows // chunk
    total = PHASES * n_chunk
    part = chunk // SUB
    n_part = rows // part
    parts = PHASES * n_part
    images = counts.shape[1]
    hw = width // HALVES
    kz = 2 * deep
    quarter = deep // 2
    tile = deep // 3
    strip = quarter // 6
    xw = hw // 2

    def mult(value, unit):
        return pl.multiple_of(value, unit)

    def remote(src, dst, send, recv, device):
        return pltpu.make_async_remote_copy(
            src_ref=src, dst_ref=dst, send_sem=send, recv_sem=recv,
            device_id=device, device_id_type=MESH,
        )

    def cols(b):
        return pl.ds(mult(b * hw, hw), hw)

    def chunk_rows(i):
        return pl.ds(mult(i * chunk, chunk), chunk)

    def part_rows(i):
        return pl.ds(mult(i * part, part), part)

    def tower(p):
        t = jnp.where(p >= HALVES, 1, 0)
        return t, p - HALVES * t

    def x_copy(t, i):
        e = t * n_chunk + i
        return remote(
            feat.at[t, chunk_rows(i)], xn.at[t, chunk_rows(i)],
            xs_send.at[e], xs_recv.at[e], across_y,
        )

    def x_fetch(t, i, buf):
        return (
            pltpu.make_async_copy(
                feat.at[t, chunk_rows(i)],
                xc.at[buf, :, pl.ds(mult(deep * y, deep), deep)], xf.at[buf, 0],
            ),
            pltpu.make_async_copy(
                xn.at[t, chunk_rows(i)],
                xc.at[buf, :, pl.ds(mult(deep * (1 - y), deep), deep)], xf.at[buf, 1],
            ),
        )

    def cot_fetch(h, i, buf):
        return pltpu.make_async_copy(
            cot.at[:, part_rows(i), cols(h)], cc.at[buf], cf.at[buf]
        )

    def w_own(p):
        t, h = tower(p)
        return pltpu.make_async_copy(
            wts.at[t, pl.ds(mult(kz * z, kz), kz), cols(h)], wv.at[p, :, cols(z)], wl.at[p],
        )

    def w_rows():
        return pl.ds(mult(deep * c + quarter * x, quarter), quarter)

    def w_z(p, to):
        t, h = tower(p)
        return remote(
            wts.at[
                t, pl.ds(mult(kz * to + deep * c + quarter * x, quarter), quarter), cols(h)
            ],
            wv.at[p, w_rows(), cols(z)],
            wz_send.at[p, to], wz_recv.at[p, z], at_z(to),
        )

    def w_z_strip(p, to, r):
        t, h = tower(p)
        at = deep * c + quarter * x + strip * r
        return remote(
            wts.at[t, pl.ds(mult(kz * to + at, strip), strip), cols(h)],
            wv.at[p, pl.ds(mult(at, strip), strip), cols(z)],
            wz_send.at[p, to], wz_recv.at[p, z], at_z(to),
        )

    def w_z_in(p, frm):
        here = wv.at[p, w_rows(), cols(frm)]
        return remote(here, here, wz_send.at[p, frm], wz_recv.at[p, frm], at_z(frm))

    def w_x(p, b):
        here = wv.at[p, w_rows(), cols(b)]
        return remote(here, here, wx_send.at[p, b], wx_recv.at[p, b], across_x)

    def w_x_in(p, b):
        here = wv.at[
            p, pl.ds(mult(deep * c + quarter * (1 - x), quarter), quarter), cols(b)
        ]
        return remote(here, here, wx_send.at[p, b], wx_recv.at[p, b], across_x)

    def w_c(p, b):
        here = wv.at[p, pl.ds(mult(deep * c, deep), deep), cols(b)]
        return remote(here, here, wc_send.at[p, b], wc_recv.at[p, b], across_c)

    def w_c_in(p, b):
        here = wv.at[p, pl.ds(mult(deep * (1 - c), deep), deep), cols(b)]
        return remote(here, here, wc_send.at[p, b], wc_recv.at[p, b], across_c)

    def rs_up(slot, zz):
        run = rs.at[slot, zz + 2 : ZED + 1]
        return remote(run, run, rs_send.at[slot, 0], rs_recv.at[slot, 0], up)

    def rs_down(slot, zz):
        run = rs.at[slot, 0:zz]
        return remote(run, run, rs_send.at[slot, 1], rs_recv.at[slot, 1], down)

    def rs_from_below(slot, zz):
        run = rs.at[slot, zz + 1 : ZED + 1]
        return remote(run, run, rs_send.at[slot, 0], rs_recv.at[slot, 0], down)

    def rs_from_above(slot, zz):
        run = rs.at[slot, 0 : zz + 1]
        return remote(run, run, rs_send.at[slot, 1], rs_recv.at[slot, 1], up)

    def at_place(first, last, do):
        for zz in range(first, last + 1):
            @pl.when(z == zz)
            def _(zz=zz):
                do(zz)

    def ag(at, b, going, device):
        here = gl.at[at.p, part_rows(at.i), cols(b)]
        return remote(
            here, here, ag_send.at[at.slot, going * ZED + b], ag_recv.at[at.slot, b], device
        )

    def dx_copy(t, i, buf):
        return remote(
            dsend.at[buf], dxn.at[t, chunk_rows(i)],
            dx_send.at[buf], dx_recv.at[t * n_chunk + i], across_y,
        )

    def dx_fetch(t, i):
        return pltpu.make_async_copy(dxn.at[t, chunk_rows(i)], dfetch, df.at[0])

    def dx_out(t, i):
        return pltpu.make_async_copy(dout, gfeat.at[t, chunk_rows(i)], dod.at[0])

    def mixed_out(h, i, buf):
        return pltpu.make_async_copy(
            mx.at[buf], mixed.at[:, part_rows(i), cols(h)], mxs.at[buf]
        )

    def tile_fetch(t, j, hk, start):
        lanes = pl.ds(mult(tile * j, tile), tile)
        near = pltpu.make_async_copy(feat.at[t, :, lanes], xsrc, tile_in.at[0])
        if not start:
            near.wait()
            return

        @pl.when(hk == y)
        def _():
            near.start()

        @pl.when(hk != y)
        def _():
            pltpu.make_async_copy(xn.at[t, :, lanes], xsrc, tile_in.at[0]).start()

    def core_copy(g):
        return remote(cstage, cland.at[g.buf], c_send.at[0], c_recv.at[g.buf], across_c)

    def across_copy(g, b):
        return remote(
            xstage.at[g.trio, b], xland.at[g.quad, b],
            x_send.at[g.trio, b], x_recv.at[g.quad, b], across_x,
        )

    def piece(g, source, core, lanes, n_lanes):
        return gwt.at[
            g.t, source,
            pl.ds(mult(deep * core + tile * g.j, tile), tile),
            pl.ds(mult(hw * g.h + lanes, xw), n_lanes),
        ]

    def z_copy(g, to):
        return remote(
            zstage.at[g.trio, to], piece(g, z, c, xw * x, xw),
            z_send.at[g.trio, to], z_recv.at[g.g, z], at_z(to),
        )

    def z_in(g, frm):
        here = piece(g, frm, c, xw * x, xw)
        return remote(here, here, z_send.at[g.trio, frm], z_recv.at[g.g, frm], at_z(frm))

    def z_own(g):
        return pltpu.make_async_copy(
            zstage.at[g.trio, z], piece(g, z, c, xw * x, xw), zl.at[g.trio]
        )

    def ax_own(g):
        return remote(
            zstage.at[g.trio, z], piece(g, z, c, xw * x, xw),
            zx_send.at[g.trio], ax_recv.at[g.g, z], across_x,
        )

    def ax_copy(g, b):
        here = piece(g, b, c, xw * x, xw)
        return remote(here, here, ax_send.at[g.g, b], ax_recv.at[g.g, b], across_x)

    def ax_in(g, b):
        here = piece(g, b, c, xw * (1 - x), xw)
        return remote(here, here, ax_send.at[g.g, b], ax_recv.at[g.g, b], across_x)

    def ac_copy(g, b):
        here = piece(g, b, c, 0, hw)
        return remote(here, here, ac_send.at[g.g, b], ac_recv.at[g.g, b], across_c)

    def ac_in(g, b):
        here = piece(g, b, 1 - c, 0, hw)
        return remote(here, here, ac_send.at[g.g, b], ac_recv.at[g.g, b], across_c)

    def sum_copy(stage, device):
        return remote(
            sums.at[stage], sums_land.at[stage], t_send.at[stage], t_recv.at[stage], device
        )

    def prod_y():
        return remote(prods.at[0], prods_land.at[ZED], t_send.at[2], t_recv.at[2], across_y)

    def prod_z(to):
        return remote(
            prods.at[1], prods_land.at[z], t_send.at[3 + to], t_recv.at[3 + z], at_z(to)
        )

    def prod_z_in(frm):
        here = prods_land.at[frm]
        return remote(here, here, t_send.at[3 + frm], t_recv.at[3 + frm], at_z(frm))

    barrier = pltpu.get_barrier_semaphore()
    for device in [at_z(o) for o in others] + [across_y, across_x, across_c]:
        pl.semaphore_signal(barrier, inc=1, device_id=device, device_id_type=MESH)
    pl.semaphore_wait(barrier, 6)

    for to in others:
        w_z(0, to).start()
    x_copy(0, 0).start()
    x_copy(0, 1).start()
    w_own(0).start()
    cot_fetch(0, 0, 0).start()

    image_row = lax.broadcasted_iota(jnp.int32, (images, images), 0)
    image_col = lax.broadcasted_iota(jnp.int32, (images, images), 1)
    crops = counts[...].astype(F32)
    ends = jnp.dot(
        jnp.broadcast_to(crops, (8, images)), (image_row <= image_col).astype(F32),
        precision=lax.Precision.HIGHEST, preferred_element_type=F32,
    )[0:1]
    starts = ends - crops
    block = mask.shape[1]
    lane = scale.shape[1]

    for r in range(rows // block):
        index = (
            lax.broadcasted_iota(jnp.int32, (block, images), 0) + r * block
        ).astype(F32)
        inside = (index >= starts) & (index < ends)
        count_row = jnp.sum(jnp.where(inside, crops, 0.0), axis=1, keepdims=True)
        diagonal = lax.broadcasted_iota(jnp.int32, (block, block), 0) == (
            lax.broadcasted_iota(jnp.int32, (block, block), 1)
        )
        usable = jnp.sum(
            jnp.where(diagonal, mask[r : r + 1, :].astype(F32), 0.0),
            axis=1, keepdims=True,
        )
        live = (count_row > 0.0) & (usable == 1.0)
        share = jnp.where(live, 1.0 / jnp.maximum(count_row, 1.0), 0.0)
        scale[r * block : (r + 1) * block, :] = jnp.broadcast_to(share, (block, lane))

    for frm in others:
        w_z_in(0, frm).wait_recv()
        w_x(0, frm).start()
    for to in others:
        w_z(1, to).start()
    w_own(1).start()
    for frm in others:
        w_x_in(0, frm).wait_recv()
        w_c(0, frm).start()
    x_copy(0, 0).wait_recv()
    for copy in x_fetch(0, 0, 0):
        copy.start()

    def final(at, later):
        p, i, slot, t, h, buf = at.p, at.i, at.slot, at.t, at.h, at.buf
        cot_fetch(h, i, buf).wait()

        @pl.when(at.u >= 2 * n_part + 2)
        def _():
            mixed_out(h, i, buf).wait()

        @pl.when(i == 0)
        def _():
            stat[p] = jnp.zeros(stat.shape[1:], F32)

        lanes = cols(h)
        shift = bias[pl.ds(t, 1), lanes]
        st = [stitch[s, pl.ds(t, 1), lanes] for s in range(2)]
        band = min(BAND, part)

        def step(r, carry):
            here = part_rows_of(r, band)
            there = pl.ds(mult(i * part + r * band, band), band)
            value = pf[at.prod, z, here, :]
            below = wide(rs[slot, z + 1, here, :])
            above = wide(rs[slot, z, here, :])
            value = value + jnp.where(z > 0, below, 0.0) + jnp.where(z < ZED - 1, above, 0.0)
            pre = value + shift
            phi = 0.5 * (1.0 + lax.erf(pre * 0.7071067811865476))
            hidden = pre * phi
            slope = phi + pre * (jnp.exp(-0.5 * pre * pre) * 0.3989422804014327)
            weight = scale[there, 0:1]
            first = wide(cc[buf, 0, here, :]) * weight
            second = wide(cc[buf, 1, here, :]) * weight
            back0 = st[0] * first * slope
            back1 = st[1] * second * slope
            gl[p, there, cols(z)] = half(back0 + back1)

            def fold(v):
                return jnp.sum(v.reshape(band // 8, 8, hw), axis=0)

            stat[p, 0] += fold(back0)
            stat[p, 1] += fold(back1)
            stat[p, 2] += fold(first * hidden)
            stat[p, 3] += fold(second * hidden)

            @pl.when(t == 0)
            def _():
                h0[h, there, :] = hidden

            @pl.when(t == 1)
            def _():
                before = h0[h, there, :]
                for s in range(2):
                    mx[buf, s, here, :] = half(
                        stitch[s, 0:1, lanes] * before + st[s] * hidden
                    )

            return carry

        lax.fori_loop(0, part // band, step, 0)

        @pl.when(z < ZED - 1)
        def _():
            ag(at, z, 0, up).start()

        @pl.when(z > 0)
        def _():
            ag(at, z, 1, down).start()

        @pl.when(t == 1)
        def _():
            mixed_out(h, i, buf).start()

        @pl.when(at.u + 1 < parts)
        def _():
            cot_fetch(later.h, later.i, later.buf).start()

    def part_rows_of(r, band):
        return pl.ds(mult(r * band, band), band)

    def forward_ag(at, far):
        @pl.when((at.u >= 0) & (at.u < parts))
        def _():
            @pl.when(z - far >= 0)
            def _():
                ag(at, z - far, 0, up).wait_recv()

                @pl.when(z < ZED - 1)
                def _():
                    ag(at, z - far, 0, up).start()

            @pl.when(z + far < ZED)
            def _():
                ag(at, z + far, 1, down).wait_recv()

                @pl.when(z > 0)
                def _():
                    ag(at, z + far, 1, down).start()

    def dx_part(t, i, hk):
        there = chunk_rows(i)
        krows = pl.ds(mult(deep * hk, deep), deep)
        acc = None
        for h in range(HALVES):
            term = lax.dot_general(
                gl[2 * t + h, there, :], wv[2 * t + h, krows, :],
                (((1,), (1,)), ((), ())), preferred_element_type=F32,
            )
            acc = term if acc is None else acc + term
        return acc

    def dx_step(t, i, buf):
        @pl.when((i >= HELD) | (t > 0))
        def _():
            dx_copy(t, i, buf).wait_send()

        dsend[buf] = half(dx_part(t, i, 1 - y))
        dx_copy(t, i, buf).start()
        own[buf] = dx_part(t, i, y)

    def dx_begin(t, i, buf):
        dx_copy(t, i, buf).wait_recv()
        dx_fetch(t, i).start()

    def dx_final(t, i, buf):
        @pl.when((i >= 1) | (t > 0))
        def _():
            dx_out(t, i).wait()

        dx_fetch(t, i).wait()

        def step(j, inner):
            lanes = pl.ds(mult(tile * j, tile), tile)
            dout[:, lanes] = half(own[buf, :, lanes] + wide(dfetch[:, lanes]))
            return inner

        lax.fori_loop(0, 3, step, 0)
        dx_out(t, i).start()

    def listed(u, times, do):
        e, hit = 0, False
        for index, time in enumerate(times):
            same = u == time
            e = jnp.where(same, index, e)
            hit = hit | same

        @pl.when(hit)
        def _():
            do(e)

    def chunk_of(do):
        def run(e):
            t = jnp.where(e >= n_chunk, 1, 0)
            do(t, e - n_chunk * t, lax.rem(e, HELD))

        return run

    def turn():
        lanes_at_once = min(128, tile)

        def step(q, carry):
            lanes = pl.ds(mult(q * lanes_at_once, lanes_at_once), lanes_at_once)
            xt[lanes, :] = xsrc[:, lanes].T
            return carry

        lax.fori_loop(0, tile // lanes_at_once, step, 0)

    def tile_dot(g):
        return jnp.dot(xt[...], gl[g.p], preferred_element_type=F32)

    def stage_one(g):
        tile_fetch(g.t, g.j, 1 - c, False)
        turn()
        tile_fetch(g.t, g.j, c, True)
        cstage[...] = half(tile_dot(g))
        core_copy(g).start()

    def stage_two(g):
        tile_fetch(g.t, g.j, c, False)
        turn()

        @pl.when(g.j < 2)
        def _():
            tile_fetch(g.t, g.j + 1, 1 - c, True)

        core_copy(g).wait()
        product = tile_dot(g)
        for b in range(ZED):
            block = product[:, b * hw : (b + 1) * hw] + wide(
                cland[g.buf, :, b * hw : (b + 1) * hw]
            )
            left, right = block[:, :xw], block[:, xw:]
            kept[g.trio, b] = jnp.where(x == 0, left, right)
            xstage[g.trio, b] = half(jnp.where(x == 0, right, left))

        def send(q, carry):
            across_copy(g, lax.rem(z + 3 + 3 * q, ZED)).start()
            return carry

        lax.fori_loop(0, ZED, send, 0)

    def stage_three(g):
        @pl.when(g.g >= 3)
        def _():
            for to in others:
                z_copy(g, to).wait_send()
            ax_own(g).wait_send()

        def add(b):
            across_copy(g, b).wait()
            zstage[g.trio, b] = half(kept[g.trio, b] + wide(xland[g.quad, b]))

        def step(q, carry):
            b = lax.rem(z + 3 + 3 * q, ZED)
            add(b)
            z_copy(g, b).start()
            return carry

        lax.fori_loop(0, ZED - 1, step, 0)
        add(z)
        z_own(g).start()
        ax_own(g).start()

    def stage_four(g):
        def step(q, carry):
            b = lax.rem(z + 1 + q, ZED)
            z_in(g, b).wait_recv()
            ax_copy(g, b).start()
            return carry

        lax.fori_loop(0, ZED - 1, step, 0)
        z_own(g).wait()

    def stage_five(g):
        def step(q, carry):
            b = lax.rem(z + q, ZED)
            ax_in(g, b).wait_recv()
            ac_copy(g, b).start()
            return carry

        lax.fori_loop(0, ZED, step, 0)

    def stage_six(g):
        def step(b, carry):
            ac_in(g, b).wait_recv()
            return carry

        lax.fori_loop(0, ZED, step, 0)

    def tile_of(g):
        p = lax.div(g, 3)
        t, h = tower(p)
        return Tile(
            g=g, p=p, t=t, h=h, j=g - 3 * p,
            buf=lax.rem(g, 2), trio=g - 3 * p, quad=lax.rem(g, 4),
        )

    def tile_in_hand(do):
        return lambda g: do(tile_of(g))

    def body(u, carry):
        p0 = lax.div(u, n_part)
        i0 = u - p0 * n_part
        slot0, prod0 = lax.rem(u, RING), lax.rem(u, PRODUCTS)
        buf0 = lax.rem(u, 2)

        def before(lag):
            if isinstance(lag, int):
                whole, left = divmod(lag, n_part)
            else:
                whole, left = 0, lag
            under = i0 < left
            p = p0 - whole - jnp.where(under, 1, 0)
            i = i0 - left + jnp.where(under, n_part, 0)
            in_ring = lag % RING if isinstance(lag, int) else lag
            in_prods = lag % PRODUCTS if isinstance(lag, int) else lag
            slot = slot0 - in_ring + jnp.where(slot0 < in_ring, RING, 0)
            prod = prod0 - in_prods + jnp.where(prod0 < in_prods, PRODUCTS, 0)
            t, h = tower(p)
            return Part(u=u - lag, p=p, i=i, t=t, h=h, slot=slot, prod=prod, buf=lax.rem(i, 2))

        @pl.when((u >= 5) & (u < parts + 5))
        def _():
            slot = before(5).slot
            at_place(0, ZED - 2, lambda zz: rs_up(slot, zz).wait_send())
            at_place(1, ZED - 1, lambda zz: rs_down(slot, zz).wait_send())

        @pl.when((u >= 8) & (u < parts + 8))
        def _():
            at = before(8)

            def step(b, inner):
                @pl.when((z < ZED - 1) & (b <= z))
                def _():
                    ag(at, b, 0, up).wait_send()

                @pl.when((z > 0) & (b >= z))
                def _():
                    ag(at, b, 1, down).wait_send()

                return inner

            lax.fori_loop(0, ZED, step, 0)

        ck = lax.div(i0, SUB)
        fresh = ck * SUB == i0
        t0, h0_ = tower(p0)
        xbuf = lax.rem(ck, 2)

        @pl.when((u < parts) & fresh)
        def _():
            @pl.when(i0 == 0)
            def _():
                w_own(p0).wait()
                for frm in others:
                    w_c_in(p0, frm).wait_recv()

            for copy in x_fetch(t0, ck, xbuf):
                copy.wait()

            product = jnp.dot(xc[xbuf], wv[p0], preferred_element_type=F32)
            for b in range(ZED):
                for s in range(SUB):
                    pf[prod0 + s, b] = product[
                        s * part : (s + 1) * part, b * hw : (b + 1) * hw
                    ]

        going_up = before(z)

        @pl.when((going_up.u >= 0) & (going_up.u < parts))
        def _():
            slot, prod = going_up.slot, going_up.prod
            at_place(1, ZED - 1, lambda zz: rs_from_below(slot, zz).wait_recv())

            @pl.when(z == 0)
            def _():
                for b in range(1, ZED):
                    rs[slot, b + 1] = half(pf[prod, b])

            @pl.when(z > 0)
            def _():
                def step(b, inner):
                    rs[slot, b + 1] = half(wide(rs[slot, b + 1]) + pf[prod, b])
                    return inner

                lax.fori_loop(z + 1, ZED, step, 0)

            at_place(0, ZED - 2, lambda zz: rs_up(slot, zz).start())

        going_down = before(ZED - 1 - z)

        @pl.when((going_down.u >= 0) & (going_down.u < parts))
        def _():
            slot, prod = going_down.slot, going_down.prod
            at_place(0, ZED - 2, lambda zz: rs_from_above(slot, zz).wait_recv())

            @pl.when(z == ZED - 1)
            def _():
                for b in range(ZED - 1):
                    rs[slot, b] = half(pf[prod, b])

            @pl.when(z < ZED - 1)
            def _():
                def step(b, inner):
                    rs[slot, b] = half(wide(rs[slot, b]) + pf[prod, b])
                    return inner

                lax.fori_loop(0, z, step, 0)

            at_place(1, ZED - 1, lambda zz: rs_down(slot, zz).start())

        @pl.when(fresh & (u + 2 * SUB < 2 * n_part))
        def _():
            k = p0 * n_chunk + ck + 2
            over = jnp.where(k >= n_chunk, 1, 0)
            x_copy(over, k - over * n_chunk).start()

        @pl.when(fresh & (u + SUB < parts))
        def _():
            wrap = jnp.where(ck + 1 == n_chunk, 1, 0)
            i = ck + 1 - wrap * n_chunk
            t, h = tower(p0 + wrap)

            @pl.when(h == 0)
            def _():
                x_copy(t, i).wait_recv()

            for copy in x_fetch(t, i, lax.rem(i, 2)):
                copy.start()

        @pl.when((u >= 3) & (u < parts + 3))
        def _():
            final(before(3), before(2))

        forward_ag(before(4), 1)
        forward_ag(before(5), 2)
        forward_ag(before(6), 3)

        listed(u, DX_BEGINS, chunk_of(dx_begin))
        listed(u, DX_ENDS, chunk_of(dx_final))
        listed(u, DX_TIMES, chunk_of(dx_step))

        listed(u, THREES, tile_in_hand(stage_three))
        listed(u, TWOS, tile_in_hand(stage_two))
        listed(u, ONES, tile_in_hand(stage_one))
        listed(u, FOURS, tile_in_hand(stage_four))
        listed(u, FIVES, tile_in_hand(stage_five))
        listed(u, SIXES, tile_in_hand(stage_six))

        def first_fetch(p):
            tile_fetch(lax.div(p, HALVES), 0, 1 - c, True)

        listed(u, [time - 1 for time in ONES[::3]], first_fetch)

        for p, times in W_STRIPS.items():
            def send_strip(r, p=p):
                for to in others:
                    w_z_strip(p, to, r).start()

                @pl.when(r == 0)
                def _():
                    w_own(p).start()

            listed(u, times, send_strip)

        for p, times in W_ACROSS.items():
            for q, time in enumerate(times):
                @pl.when(u == time)
                def _(p=p, q=q):
                    w_z_in(p, others[q]).wait_recv()
                    w_x(p, others[q]).start()

        for p, times in W_CORES.items():
            for q, time in enumerate(times):
                @pl.when(u == time)
                def _(p=p, q=q):
                    w_x_in(p, others[q]).wait_recv()
                    w_c(p, others[q]).start()

        @pl.when(u == parts + 3)
        def _():
            for p in range(PHASES):
                t, h = p // HALVES, p % HALVES
                for s in range(2):
                    for what in range(2):
                        sums[0, pl.ds(4 * what + 2 * s + t, 1), h * hw : (h + 1) * hw] = jnp.sum(
                            stat[p, 2 * what + s], axis=0, keepdims=True
                        )
            sum_copy(0, across_c).start()

        @pl.when(u == parts + 4)
        def _():
            sum_copy(0, across_c).wait()
            sums[1] = sums[0] + sums_land[0]
            sum_copy(1, across_x).start()

        @pl.when(u == parts + 5)
        def _():
            sum_copy(1, across_x).wait()
            both = sums[1] + sums_land[1]
            sums[2] = both
            member = (
                lax.broadcasted_iota(jnp.int32, (width, lane), 0) % FLAG_GROUPS
                == lax.broadcasted_iota(jnp.int32, (width, lane), 1) % FLAG_GROUPS
            ).astype(F32)
            bias_rows = both[0:4]
            inner = both[0:2] * both[2:4]
            stack = jnp.concatenate([inner, bias_rows * bias_rows, inner], axis=0)
            prods[0] = jnp.dot(
                stack, member, precision=lax.Precision.HIGHEST, preferred_element_type=F32
            )
            prod_y().start()

        @pl.when(u == parts + 6)
        def _():
            prod_y().wait()
            prods[1] = prods[0] + prods_land[ZED]
            for to in others:
                prod_z(to).start()

        @pl.when(u == parts + 7)
        def _():
            for frm in others:
                prod_z_in(frm).wait_recv()
            prods_land[z] = prods[1]
            whole = prods_land[0] + prods_land[1] + prods_land[2] + prods_land[3]
            both = sums[2]
            group = lax.broadcasted_iota(jnp.int32, (1, lane), 1) % FLAG_GROUPS

            def over(row):
                return jnp.concatenate([row] * (width // lane), axis=1)

            def flag_row(s, t):
                row = jnp.zeros((1, lane), F32)
                for g in range(FLAG_GROUPS):
                    row = jnp.where(group == g, flags[s, t, g].astype(F32), row)
                return row

            for t in range(2):
                task0, task1 = both[t : t + 1], both[2 + t : 3 + t]
                dots = whole[t : t + 1]
                coef0 = over(flag_row(0, t) * dots / (whole[4 + t : 5 + t] + 1e-06))
                coef1 = over(flag_row(1, t) * dots / (whole[2 + t : 3 + t] + 1e-06))
                gbias[t : t + 1] = (task0 - coef0 * task1) + (task1 - coef1 * task0)
            for s in range(2):
                gstitch[s] = both[4 + 2 * s : 6 + 2 * s]

        return carry

    lax.fori_loop(0, max(SIXES + DX_ENDS) + 1, body, 0)

    last = 3 * PHASES - 1

    for g in (last - 2, last - 1, last):
        for to in others:
            z_copy(tile_of(g), to).wait_send()
        ax_own(tile_of(g)).wait_send()
    for i in range(n_chunk - HELD, n_chunk):
        dx_copy(1, i, (n_chunk + i) % HELD).wait_send()
    for i in (n_part - 2, n_part - 1):
        mixed_out(1, i, i % 2).wait()
    dx_out(1, n_chunk - 1).wait()

    def drain_tiles(g, carry):
        at = tile_of(g)
        for b in others:
            ax_copy(at, b).wait_send()
        for b in range(ZED):
            ac_copy(at, b).wait_send()
        return carry

    lax.fori_loop(0, last + 1, drain_tiles, 0)

    def drain_x(i, carry):
        x_copy(0, i).wait_send()
        x_copy(1, i).wait_send()
        return carry

    lax.fori_loop(0, n_chunk, drain_x, 0)

    def drain_w(p, carry):
        for to in others:
            w_z(p, to).wait_send()
            w_x(p, to).wait_send()
            w_c(p, to).wait_send()
        return carry

    lax.fori_loop(0, PHASES, drain_w, 0)
    for to in others:
        prod_z(to).wait_send()


def fused_call(feat, wts, cot, bias, stitch, counts, mask, flags):
    rows, deep, width = feat.shape[1], feat.shape[2], wts.shape[2]
    chunk = rows // 6
    part = chunk // SUB
    hw, kz, tile = width // 2, 2 * deep, deep // 3
    cat, xw = 4 * hw, width // 4
    lane = min(128, width)
    dma = pltpu.SemaphoreType.DMA
    anywhere = pl.BlockSpec(memory_space=pl.ANY)
    inside = pl.BlockSpec(memory_space=pltpu.VMEM)
    scalars = pl.BlockSpec(memory_space=pltpu.SMEM)

    def v(shape, kind=BF16):
        return pltpu.VMEM(shape, kind)

    out_shape = [
        jax.ShapeDtypeStruct((2, rows, width), BF16),
        jax.ShapeDtypeStruct((2, rows, deep), BF16),
        jax.ShapeDtypeStruct((2, ZED, kz, width), BF16),
        jax.ShapeDtypeStruct((2, width), F32),
        jax.ShapeDtypeStruct((2, 2, width), F32),
        jax.ShapeDtypeStruct((2, rows, deep), BF16),
        jax.ShapeDtypeStruct((2, rows, deep), BF16),
    ]
    scratch = [
        v((PHASES, kz, cat)),
        v((PHASES, rows, cat)),
        v((RING, 5, part, hw)),
        v((2, rows, hw), F32),
        v((2, chunk, kz)),
        v((PRODUCTS, ZED, part, hw), F32),
        v((2, 2, part, hw)),
        v((2, 2, part, hw)),
        v((HELD, chunk, deep), F32),
        v((HELD, chunk, deep)),
        v((chunk, deep)),
        v((chunk, deep)),
        v((rows, tile)),
        v((tile, rows)),
        v((tile, cat)),
        v((2, tile, cat)),
        v((3, ZED, tile, xw)),
        v((4, ZED, tile, xw)),
        v((3, ZED, tile, xw), F32),
        v((3, ZED, tile, xw)),
        v((rows, lane), F32),
        v((PHASES, 4, 8, hw), F32),
        v((3, 8, width), F32),
        v((2, 8, width), F32),
        v((2, 8, lane), F32),
        v((5, 8, lane), F32),
        dma((RING, 2)), dma((RING, 2)), dma((RING, 8)), dma((RING, 4)),
        dma((12,)), dma((12,)),
        dma((4, 4)), dma((4, 4)), dma((4, 4)), dma((4, 4)), dma((4, 4)), dma((4, 4)), dma((4,)),
        dma((2, 2)), dma((2,)), dma((2,)), dma((HELD,)), dma((12,)), dma((1,)), dma((1,)),
        dma((1,)), dma((1,)), dma((2,)), dma((3, 4)), dma((4, 4)), dma((3, 4)), dma((12, 4)),
        dma((3,)), dma((3,)),
        dma((12, 4)), dma((12, 4)), dma((12, 4)), dma((12, 4)), dma((8,)), dma((8,)),
    ]
    flops = 3 * 2 * 2 * rows * kz * cat * 2
    return pl.pallas_call(
        functools.partial(fused_kernel, rows, deep, width, chunk),
        out_shape=out_shape,
        in_specs=[anywhere] * 3 + [inside] * 4 + [scalars],
        out_specs=[anywhere] * 3 + [inside] * 2 + [anywhere] * 2,
        scratch_shapes=scratch,
        compiler_params=pltpu.CompilerParams(
            collective_id=0, has_side_effects=True, vmem_limit_bytes=64 * 1024 * 1024
        ),
        cost_estimate=pl.CostEstimate(
            flops=flops, bytes_accessed=200_000_000, transcendentals=2 * rows * width * 2
        ),
        name="cross_stitch_step",
    )(feat, wts, cot, bias, stitch, counts, mask, flags)


def finish_kernel(
    block, low, mixed, gfeat, gbias, gstitch,
    out, mixed_out, gfeat_out, gbias_out, gstitch_out,
    taken, given, held_mixed, held_gfeat, in_sem, out_sem, pass_sem,
):
    n_block = low.shape[0] // block
    fetched = (
        pltpu.make_async_copy(mixed, held_mixed, pass_sem.at[0]),
        pltpu.make_async_copy(gfeat, held_gfeat, pass_sem.at[1]),
    )
    passed = (
        pltpu.make_async_copy(held_mixed, mixed_out, pass_sem.at[2]),
        pltpu.make_async_copy(held_gfeat, gfeat_out, pass_sem.at[3]),
    )

    def take(i):
        return pltpu.make_async_copy(
            low.at[pl.ds(i * block, block)], taken.at[i % WIDEN_SLOTS], in_sem.at[i % WIDEN_SLOTS]
        )

    def give(i):
        return pltpu.make_async_copy(
            given.at[i % WIDEN_SLOTS], out.at[pl.ds(i * block, block)], out_sem.at[i % WIDEN_SLOTS]
        )

    for i in range(min(WIDEN_SLOTS, n_block)):
        take(i).start()
    for copy in fetched:
        copy.start()
    gbias_out[...] = gbias[...]
    gstitch_out[...] = gstitch[...]
    for i in range(n_block):
        slot = i % WIDEN_SLOTS
        take(i).wait()
        if i >= WIDEN_SLOTS:
            give(i - WIDEN_SLOTS).wait()
        given[slot] = wide(taken[slot])
        give(i).start()
        if i + WIDEN_SLOTS < n_block:
            take(i + WIDEN_SLOTS).start()
        if i == 2:
            for arrived, copy in zip(fetched, passed):
                arrived.wait()
                copy.start()
    for i in range(max(0, n_block - WIDEN_SLOTS), n_block):
        give(i).wait()
    for copy in passed:
        copy.wait()


def finish(low, mixed, gfeat, gbias, gstitch):
    tall, width = low.shape
    block = tall // WIDEN_BLOCKS
    anywhere = pl.BlockSpec(memory_space=pl.ANY)
    inside = pl.BlockSpec(memory_space=pltpu.VMEM)
    moved = sum(a.size * a.dtype.itemsize for a in (mixed, gfeat))
    return pl.pallas_call(
        functools.partial(finish_kernel, block),
        in_specs=[anywhere] * 3 + [inside] * 2,
        out_specs=[anywhere] * 3 + [inside] * 2,
        out_shape=[
            jax.ShapeDtypeStruct(a.shape, kind)
            for a, kind in ((low, F32), (mixed, BF16), (gfeat, BF16), (gbias, F32), (gstitch, F32))
        ],
        scratch_shapes=[
            pltpu.VMEM((WIDEN_SLOTS, block, width), BF16),
            pltpu.VMEM((WIDEN_SLOTS, block, width), F32),
            pltpu.VMEM(mixed.shape, BF16),
            pltpu.VMEM(gfeat.shape, BF16),
            pltpu.SemaphoreType.DMA((WIDEN_SLOTS,)),
            pltpu.SemaphoreType.DMA((WIDEN_SLOTS,)),
            pltpu.SemaphoreType.DMA((4,)),
        ],
        compiler_params=pltpu.CompilerParams(vmem_limit_bytes=60 * 1024 * 1024),
        cost_estimate=pl.CostEstimate(
            flops=tall * width, bytes_accessed=6 * tall * width + 2 * moved, transcendentals=0
        ),
        name="finish",
    )(low, mixed, gfeat, gbias, gstitch)


def fused_plan(mesh):
    def per_device(features, weights, bias, stitch, cotangent, crop_counts, row_mask, flags):
        rows, deep = features.shape[1:]
        width = weights.shape[2]
        mixed, gfeat, gwt, gbias, gstitch, _, _ = fused_call(
            features, weights, cotangent, bias, stitch,
            crop_counts.reshape(1, -1), row_mask.reshape(-1, min(128, rows // 6)), flags,
        )
        grad_weights, mixed, gfeat, gbias, gstitch = finish(
            gwt.reshape(-1, width), mixed, gfeat, gbias, gstitch
        )
        return mixed, gfeat, grad_weights.reshape(2, ZED * 2 * deep, width), gbias, gstitch

    return per_device


def plan_for(mesh):
    if mesh.shape["batch"] == 4 and mesh.shape["mp"] == 2 * ZED:
        return fused_plan(mesh)
    return generic_plan(mesh)


def solution(mesh):
    in_specs = (
        P(None, "batch", "mp"),
        P(None, None, "mp"),
        P(None, "mp"),
        P(None, None, "mp"),
        P(None, "batch", "mp"),
        P("batch"),
        P("batch"),
        P(),
    )
    out_specs = (
        P(None, "batch", "mp"),
        P(None, "batch", "mp"),
        P(None, None, "mp"),
        P(None, "mp"),
        P(None, None, "mp"),
    )
    return jax.shard_map(
        plan_for(mesh), mesh=mesh, in_specs=in_specs, out_specs=out_specs, check_vma=False
    )
```

```python
import collections
import functools

import jax
import jax.numpy as jnp
from jax import lax
from jax.experimental import pallas as pl
from jax.experimental.pallas import tpu as pltpu
from jax.sharding import PartitionSpec as P

FLAG_GROUPS = 8
OUTER = 4


def row_weights(counts, mask):
    ends = jnp.cumsum(counts)
    starts = ends - counts
    index = lax.broadcasted_iota(jnp.int32, (mask.shape[0], counts.shape[0]), 0)
    inside = (index >= starts[None, :]) & (index < ends[None, :])
    count_row = jnp.sum(jnp.where(inside, counts[None, :], 0), axis=1)
    live = (count_row > 0) & (mask == 1)
    return jnp.where(live, 1.0 / jnp.maximum(count_row, 1).astype(jnp.float32), 0.0)


def project_bias(task_bias, flags):
    local_width = task_bias.shape[2]
    channel = lax.axis_index("mp") * local_width + lax.broadcasted_iota(
        jnp.int32, (local_width, FLAG_GROUPS), 0
    )
    member = (
        channel % FLAG_GROUPS == lax.broadcasted_iota(jnp.int32, (local_width, FLAG_GROUPS), 1)
    ).astype(jnp.float32)
    dots = jnp.dot(task_bias[0] * task_bias[1], member, precision=lax.Precision.HIGHEST)
    norms = jnp.einsum(
        "stc,cg->stg", task_bias * task_bias, member, precision=lax.Precision.HIGHEST
    )
    dots, norms = lax.psum((dots, norms), "mp")
    flag = flags.astype(jnp.float32)
    coef_first = jnp.dot(
        flag[0] * dots / (norms[1] + 1e-06), member.T, precision=lax.Precision.HIGHEST
    )
    coef_second = jnp.dot(
        flag[1] * dots / (norms[0] + 1e-06), member.T, precision=lax.Precision.HIGHEST
    )
    first = task_bias[0] - coef_first * task_bias[1]
    second = task_bias[1] - coef_second * task_bias[0]
    return first + second


def generic_plan(mesh):
    n_mp = mesh.shape["mp"]
    n_batch = mesh.shape["batch"]
    inner = n_mp // OUTER
    inner_groups = [[o * inner + i for i in range(inner)] for o in range(OUTER)]
    outer_groups = [[o * inner + i for o in range(OUTER)] for i in range(inner)]

    def per_device(features, weights, bias, stitch, cotangent, crop_counts, row_mask, flags):
        rows = features.shape[1]
        width = weights.shape[2]
        depth = features.shape[2] * inner
        held = lax.all_gather(
            features, "mp", axis=2, tiled=True, axis_index_groups=inner_groups
        )
        split = weights.reshape(2, OUTER, depth, width)
        block = lax.all_to_all(
            split, "mp", split_axis=1, concat_axis=1, axis_index_groups=outer_groups
        )
        block = block.reshape(2, OUTER, depth, width)
        part = jnp.einsum("trk,tokc->otrc", held, block, preferred_element_type=jnp.float32)
        linear = lax.psum_scatter(
            part.astype(jnp.bfloat16),
            "mp",
            scatter_dimension=0,
            axis_index_groups=outer_groups,
        ).astype(jnp.float32)
        pre = linear + bias[:, None, :]
        hidden, gelu_back = jax.vjp(lambda v: jax.nn.gelu(v, approximate=False), pre)
        mixed = stitch[:, 0, None, :] * hidden[0][None] + stitch[:, 1, None, :] * hidden[1][None]
        scale_rows = row_weights(crop_counts, row_mask)
        grad_out = cotangent.astype(jnp.float32) * scale_rows[None, :, None]
        first_task = gelu_back(stitch[0][:, None, :] * grad_out[0][None])[0]
        second_task = gelu_back(stitch[1][:, None, :] * grad_out[1][None])[0]
        task_bias = jnp.stack([jnp.sum(first_task, axis=1), jnp.sum(second_task, axis=1)])
        grad_linear = (first_task + second_task).astype(jnp.bfloat16)
        grad_stitch = jnp.sum(grad_out[:, None] * hidden[None], axis=2)
        every = lax.all_gather(grad_linear, "mp", axis_index_groups=outer_groups)
        grad_part = jnp.einsum(
            "otrc,tokc->trk", every, block, preferred_element_type=jnp.float32
        )
        grad_part = grad_part.astype(jnp.bfloat16).reshape(2, rows, inner, depth // inner)
        grad_features = lax.psum_scatter(
            grad_part.transpose(2, 0, 1, 3),
            "mp",
            scatter_dimension=0,
            axis_index_groups=inner_groups,
        )
        weight_part = jnp.einsum(
            "trk,otrc->otkc", held, every, preferred_element_type=jnp.float32
        )
        weight_part = weight_part.astype(jnp.bfloat16).reshape(
            OUTER, 2, n_batch, depth // n_batch, width
        )
        share = lax.psum_scatter(
            weight_part.transpose(2, 0, 1, 3, 4), "batch", scatter_dimension=0
        )
        share = lax.all_to_all(
            share, "mp", split_axis=0, concat_axis=0, axis_index_groups=outer_groups
        )
        share = share.reshape(OUTER, 2, depth // n_batch, width)
        whole = lax.all_gather(share, "batch")
        grad_weights = whole.transpose(2, 1, 0, 3, 4).reshape(2, OUTER * depth, width)
        task_bias, grad_stitch = lax.psum((task_bias, grad_stitch), "batch")
        grad_bias = project_bias(task_bias, flags)
        return (
            mixed.astype(jnp.bfloat16),
            grad_features.astype(jnp.bfloat16),
            grad_weights.astype(jnp.float32),
            grad_bias,
            grad_stitch,
        )

    return per_device


MESH = pl.DeviceIdType.MESH
BF16 = jnp.bfloat16
F32 = jnp.float32
ZED = 4
HALVES = 2
PHASES = 4
RING = 8
BAND = 32
SUB = 2
PRODUCTS = 6
HELD = 4
WIDEN_BLOCKS = 12
WIDEN_SLOTS = 4

DX_TIMES = (20, 21, 23, 25, 27, 29, 43, 45, 48, 50, 58, 64)
DX_BEGINS = (22, 24, 26, 28, 30, 34, 44, 48, 57, 60, 68, 76)
DX_ENDS = (23, 25, 27, 29, 31, 43, 45, 50, 59, 62, 71, 81)
ONES = (19, 23, 26, 30, 33, 40, 43, 45, 46, 54, 56, 57)
TWOS = (22, 26, 27, 32, 36, 42, 44, 46, 49, 55, 57, 61)
THREES = (23, 28, 33, 35, 42, 43, 45, 52, 55, 58, 59, 70)
FOURS = (25, 30, 35, 37, 44, 47, 50, 54, 60, 67, 68, 73)
FIVES = (33, 36, 44, 45, 51, 59, 62, 67, 74, 76, 82, 85)
SIXES = (35, 43, 47, 57, 64, 70, 75, 82, 84, 86, 87, 90)
W_STRIPS = {2: (5, 7, 8, 11, 12, 13), 3: (19, 21, 23, 25, 26, 27)}
W_ACROSS = {1: (0, 0, 2), 2: (16, 21, 22), 3: (29, 29, 34)}
W_CORES = {1: (1, 6, 7), 2: (21, 23, 23), 3: (33, 33, 35)}


Part = collections.namedtuple("Part", ("u", "p", "i", "t", "h", "slot", "prod", "buf"))
Tile = collections.namedtuple("Tile", ("g", "p", "t", "h", "j", "buf", "trio", "quad"))


def half(value):
    return value.astype(BF16)


def wide(value):
    return value.astype(F32)


def fused_kernel(
    rows, deep, width, chunk,
    feat, wts, cot, bias, stitch, counts, mask, flags,
    mixed, gfeat, gwt, gbias, gstitch, xn, dxn,
    wv, gl, rs, h0, xc, pf, cc, mx, own, dsend, dfetch, dout,
    xsrc, xt, cstage, cland, xstage, xland, kept, zstage,
    scale, stat, sums, sums_land, prods, prods_land,
    rs_send, rs_recv, ag_send, ag_recv, xs_send, xs_recv,
    wz_send, wz_recv, wx_send, wx_recv, wc_send, wc_recv, wl,
    xf, cf, mxs, dx_send, dx_recv, df, dod,
    tile_in, c_send, c_recv, x_send, x_recv, z_send, z_recv, zl, zx_send,
    ax_send, ax_recv, ac_send, ac_recv, t_send, t_recv,
):
    batch, mp = lax.axis_index("batch"), lax.axis_index("mp")
    z, y = mp // 2, mp % 2
    x, c = batch // 2, batch % 2
    up = {"mp": mp + 2}
    down = {"mp": mp - 2}
    across_y = {"mp": 2 * z + 1 - y}
    across_x = {"batch": 2 * (1 - x) + c}
    across_c = {"batch": 2 * x + 1 - c}

    def at_z(other):
        return {"mp": 2 * other + y}

    others = (3 - z, (z + 2) % 4, z + 1 - 2 * (z % 2))

    n_chunk = rows // chunk
    total = PHASES * n_chunk
    part = chunk // SUB
    n_part = rows // part
    parts = PHASES * n_part
    images = counts.shape[1]
    hw = width // HALVES
    kz = 2 * deep
    quarter = deep // 2
    tile = deep // 3
    strip = quarter // 6
    xw = hw // 2

    def mult(value, unit):
        return pl.multiple_of(value, unit)

    def remote(src, dst, send, recv, device):
        return pltpu.make_async_remote_copy(
            src_ref=src, dst_ref=dst, send_sem=send, recv_sem=recv,
            device_id=device, device_id_type=MESH,
        )

    def cols(b):
        return pl.ds(mult(b * hw, hw), hw)

    def chunk_rows(i):
        return pl.ds(mult(i * chunk, chunk), chunk)

    def part_rows(i):
        return pl.ds(mult(i * part, part), part)

    def tower(p):
        t = jnp.where(p >= HALVES, 1, 0)
        return t, p - HALVES * t

    def x_copy(t, i):
        e = t * n_chunk + i
        return remote(
            feat.at[t, chunk_rows(i)], xn.at[t, chunk_rows(i)],
            xs_send.at[e], xs_recv.at[e], across_y,
        )

    def x_fetch(t, i, buf):
        return (
            pltpu.make_async_copy(
                feat.at[t, chunk_rows(i)],
                xc.at[buf, :, pl.ds(mult(deep * y, deep), deep)], xf.at[buf, 0],
            ),
            pltpu.make_async_copy(
                xn.at[t, chunk_rows(i)],
                xc.at[buf, :, pl.ds(mult(deep * (1 - y), deep), deep)], xf.at[buf, 1],
            ),
        )

    def cot_fetch(h, i, buf):
        return pltpu.make_async_copy(
            cot.at[:, part_rows(i), cols(h)], cc.at[buf], cf.at[buf]
        )

    def w_own(p):
        t, h = tower(p)
        return pltpu.make_async_copy(
            wts.at[t, pl.ds(mult(kz * z, kz), kz), cols(h)], wv.at[p, :, cols(z)], wl.at[p],
        )

    def w_rows():
        return pl.ds(mult(deep * c + quarter * x, quarter), quarter)

    def w_z(p, to):
        t, h = tower(p)
        return remote(
            wts.at[
                t, pl.ds(mult(kz * to + deep * c + quarter * x, quarter), quarter), cols(h)
            ],
            wv.at[p, w_rows(), cols(z)],
            wz_send.at[p, to], wz_recv.at[p, z], at_z(to),
        )

    def w_z_strip(p, to, r):
        t, h = tower(p)
        at = deep * c + quarter * x + strip * r
        return remote(
            wts.at[t, pl.ds(mult(kz * to + at, strip), strip), cols(h)],
            wv.at[p, pl.ds(mult(at, strip), strip), cols(z)],
            wz_send.at[p, to], wz_recv.at[p, z], at_z(to),
        )

    def w_z_in(p, frm):
        here = wv.at[p, w_rows(), cols(frm)]
        return remote(here, here, wz_send.at[p, frm], wz_recv.at[p, frm], at_z(frm))

    def w_x(p, b):
        here = wv.at[p, w_rows(), cols(b)]
        return remote(here, here, wx_send.at[p, b], wx_recv.at[p, b], across_x)

    def w_x_in(p, b):
        here = wv.at[
            p, pl.ds(mult(deep * c + quarter * (1 - x), quarter), quarter), cols(b)
        ]
        return remote(here, here, wx_send.at[p, b], wx_recv.at[p, b], across_x)

    def w_c(p, b):
        here = wv.at[p, pl.ds(mult(deep * c, deep), deep), cols(b)]
        return remote(here, here, wc_send.at[p, b], wc_recv.at[p, b], across_c)

    def w_c_in(p, b):
        here = wv.at[p, pl.ds(mult(deep * (1 - c), deep), deep), cols(b)]
        return remote(here, here, wc_send.at[p, b], wc_recv.at[p, b], across_c)

    def rs_up(slot, zz):
        run = rs.at[slot, zz + 2 : ZED + 1]
        return remote(run, run, rs_send.at[slot, 0], rs_recv.at[slot, 0], up)

    def rs_down(slot, zz):
        run = rs.at[slot, 0:zz]
        return remote(run, run, rs_send.at[slot, 1], rs_recv.at[slot, 1], down)

    def rs_from_below(slot, zz):
        run = rs.at[slot, zz + 1 : ZED + 1]
        return remote(run, run, rs_send.at[slot, 0], rs_recv.at[slot, 0], down)

    def rs_from_above(slot, zz):
        run = rs.at[slot, 0 : zz + 1]
        return remote(run, run, rs_send.at[slot, 1], rs_recv.at[slot, 1], up)

    def at_place(first, last, do):
        for zz in range(first, last + 1):
            @pl.when(z == zz)
            def _(zz=zz):
                do(zz)

    def ag(at, b, going, device):
        here = gl.at[at.p, part_rows(at.i), cols(b)]
        return remote(
            here, here, ag_send.at[at.slot, going * ZED + b], ag_recv.at[at.slot, b], device
        )

    def dx_copy(t, i, buf):
        return remote(
            dsend.at[buf], dxn.at[t, chunk_rows(i)],
            dx_send.at[buf], dx_recv.at[t * n_chunk + i], across_y,
        )

    def dx_fetch(t, i):
        return pltpu.make_async_copy(dxn.at[t, chunk_rows(i)], dfetch, df.at[0])

    def dx_out(t, i):
        return pltpu.make_async_copy(dout, gfeat.at[t, chunk_rows(i)], dod.at[0])

    def mixed_out(h, i, buf):
        return pltpu.make_async_copy(
            mx.at[buf], mixed.at[:, part_rows(i), cols(h)], mxs.at[buf]
        )

    def tile_fetch(t, j, hk, start):
        lanes = pl.ds(mult(tile * j, tile), tile)
        near = pltpu.make_async_copy(feat.at[t, :, lanes], xsrc, tile_in.at[0])
        if not start:
            near.wait()
            return

        @pl.when(hk == y)
        def _():
            near.start()

        @pl.when(hk != y)
        def _():
            pltpu.make_async_copy(xn.at[t, :, lanes], xsrc, tile_in.at[0]).start()

    def core_copy(g):
        return remote(cstage, cland.at[g.buf], c_send.at[0], c_recv.at[g.buf], across_c)

    def across_copy(g, b):
        return remote(
            xstage.at[g.trio, b], xland.at[g.quad, b],
            x_send.at[g.trio, b], x_recv.at[g.quad, b], across_x,
        )

    def piece(g, source, core, lanes, n_lanes):
        return gwt.at[
            g.t, source,
            pl.ds(mult(deep * core + tile * g.j, tile), tile),
            pl.ds(mult(hw * g.h + lanes, xw), n_lanes),
        ]

    def z_copy(g, to):
        return remote(
            zstage.at[g.trio, to], piece(g, z, c, xw * x, xw),
            z_send.at[g.trio, to], z_recv.at[g.g, z], at_z(to),
        )

    def z_in(g, frm):
        here = piece(g, frm, c, xw * x, xw)
        return remote(here, here, z_send.at[g.trio, frm], z_recv.at[g.g, frm], at_z(frm))

    def z_own(g):
        return pltpu.make_async_copy(
            zstage.at[g.trio, z], piece(g, z, c, xw * x, xw), zl.at[g.trio]
        )

    def ax_own(g):
        return remote(
            zstage.at[g.trio, z], piece(g, z, c, xw * x, xw),
            zx_send.at[g.trio], ax_recv.at[g.g, z], across_x,
        )

    def ax_copy(g, b):
        here = piece(g, b, c, xw * x, xw)
        return remote(here, here, ax_send.at[g.g, b], ax_recv.at[g.g, b], across_x)

    def ax_in(g, b):
        here = piece(g, b, c, xw * (1 - x), xw)
        return remote(here, here, ax_send.at[g.g, b], ax_recv.at[g.g, b], across_x)

    def ac_copy(g, b):
        here = piece(g, b, c, 0, hw)
        return remote(here, here, ac_send.at[g.g, b], ac_recv.at[g.g, b], across_c)

    def ac_in(g, b):
        here = piece(g, b, 1 - c, 0, hw)
        return remote(here, here, ac_send.at[g.g, b], ac_recv.at[g.g, b], across_c)

    def sum_copy(stage, device):
        return remote(
            sums.at[stage], sums_land.at[stage], t_send.at[stage], t_recv.at[stage], device
        )

    def prod_y():
        return remote(prods.at[0], prods_land.at[ZED], t_send.at[2], t_recv.at[2], across_y)

    def prod_z(to):
        return remote(
            prods.at[1], prods_land.at[z], t_send.at[3 + to], t_recv.at[3 + z], at_z(to)
        )

    def prod_z_in(frm):
        here = prods_land.at[frm]
        return remote(here, here, t_send.at[3 + frm], t_recv.at[3 + frm], at_z(frm))

    barrier = pltpu.get_barrier_semaphore()
    for device in [at_z(o) for o in others] + [across_y, across_x, across_c]:
        pl.semaphore_signal(barrier, inc=1, device_id=device, device_id_type=MESH)
    pl.semaphore_wait(barrier, 6)

    for to in others:
        w_z(0, to).start()
    x_copy(0, 0).start()
    x_copy(0, 1).start()
    w_own(0).start()
    cot_fetch(0, 0, 0).start()

    image_row = lax.broadcasted_iota(jnp.int32, (images, images), 0)
    image_col = lax.broadcasted_iota(jnp.int32, (images, images), 1)
    crops = counts[...].astype(F32)
    ends = jnp.dot(
        jnp.broadcast_to(crops, (8, images)), (image_row <= image_col).astype(F32),
        precision=lax.Precision.HIGHEST, preferred_element_type=F32,
    )[0:1]
    starts = ends - crops
    block = mask.shape[1]
    lane = scale.shape[1]

    for r in range(rows // block):
        index = (
            lax.broadcasted_iota(jnp.int32, (block, images), 0) + r * block
        ).astype(F32)
        inside = (index >= starts) & (index < ends)
        count_row = jnp.sum(jnp.where(inside, crops, 0.0), axis=1, keepdims=True)
        diagonal = lax.broadcasted_iota(jnp.int32, (block, block), 0) == (
            lax.broadcasted_iota(jnp.int32, (block, block), 1)
        )
        usable = jnp.sum(
            jnp.where(diagonal, mask[r : r + 1, :].astype(F32), 0.0),
            axis=1, keepdims=True,
        )
        live = (count_row > 0.0) & (usable == 1.0)
        share = jnp.where(live, 1.0 / jnp.maximum(count_row, 1.0), 0.0)
        scale[r * block : (r + 1) * block, :] = jnp.broadcast_to(share, (block, lane))

    for frm in others:
        w_z_in(0, frm).wait_recv()
        w_x(0, frm).start()
    for to in others:
        w_z(1, to).start()
    w_own(1).start()
    for frm in others:
        w_x_in(0, frm).wait_recv()
        w_c(0, frm).start()
    x_copy(0, 0).wait_recv()
    for copy in x_fetch(0, 0, 0):
        copy.start()

    def final(at, later):
        p, i, slot, t, h, buf = at.p, at.i, at.slot, at.t, at.h, at.buf
        cot_fetch(h, i, buf).wait()

        @pl.when(at.u >= 2 * n_part + 2)
        def _():
            mixed_out(h, i, buf).wait()

        @pl.when(i == 0)
        def _():
            stat[p] = jnp.zeros(stat.shape[1:], F32)

        lanes = cols(h)
        shift = bias[pl.ds(t, 1), lanes]
        st = [stitch[s, pl.ds(t, 1), lanes] for s in range(2)]
        band = min(BAND, part)

        def step(r, carry):
            here = part_rows_of(r, band)
            there = pl.ds(mult(i * part + r * band, band), band)
            value = pf[at.prod, z, here, :]
            below = wide(rs[slot, z + 1, here, :])
            above = wide(rs[slot, z, here, :])
            value = value + jnp.where(z > 0, below, 0.0) + jnp.where(z < ZED - 1, above, 0.0)
            pre = value + shift
            phi = 0.5 * (1.0 + lax.erf(pre * 0.7071067811865476))
            hidden = pre * phi
            slope = phi + pre * (jnp.exp(-0.5 * pre * pre) * 0.3989422804014327)
            weight = scale[there, 0:1]
            first = wide(cc[buf, 0, here, :]) * weight
            second = wide(cc[buf, 1, here, :]) * weight
            back0 = st[0] * first * slope
            back1 = st[1] * second * slope
            gl[p, there, cols(z)] = half(back0 + back1)

            def fold(v):
                return jnp.sum(v.reshape(band // 8, 8, hw), axis=0)

            stat[p, 0] += fold(back0)
            stat[p, 1] += fold(back1)
            stat[p, 2] += fold(first * hidden)
            stat[p, 3] += fold(second * hidden)

            @pl.when(t == 0)
            def _():
                h0[h, there, :] = hidden

            @pl.when(t == 1)
            def _():
                before = h0[h, there, :]
                for s in range(2):
                    mx[buf, s, here, :] = half(
                        stitch[s, 0:1, lanes] * before + st[s] * hidden
                    )

            return carry

        lax.fori_loop(0, part // band, step, 0)

        @pl.when(z < ZED - 1)
        def _():
            ag(at, z, 0, up).start()

        @pl.when(z > 0)
        def _():
            ag(at, z, 1, down).start()

        @pl.when(t == 1)
        def _():
            mixed_out(h, i, buf).start()

        @pl.when(at.u + 1 < parts)
        def _():
            cot_fetch(later.h, later.i, later.buf).start()

    def part_rows_of(r, band):
        return pl.ds(mult(r * band, band), band)

    def forward_ag(at, far):
        @pl.when((at.u >= 0) & (at.u < parts))
        def _():
            @pl.when(z - far >= 0)
            def _():
                ag(at, z - far, 0, up).wait_recv()

                @pl.when(z < ZED - 1)
                def _():
                    ag(at, z - far, 0, up).start()

            @pl.when(z + far < ZED)
            def _():
                ag(at, z + far, 1, down).wait_recv()

                @pl.when(z > 0)
                def _():
                    ag(at, z + far, 1, down).start()

    def dx_part(t, i, hk):
        there = chunk_rows(i)
        krows = pl.ds(mult(deep * hk, deep), deep)
        acc = None
        for h in range(HALVES):
            term = lax.dot_general(
                gl[2 * t + h, there, :], wv[2 * t + h, krows, :],
                (((1,), (1,)), ((), ())), preferred_element_type=F32,
            )
            acc = term if acc is None else acc + term
        return acc

    def dx_step(t, i, buf):
        @pl.when((i >= HELD) | (t > 0))
        def _():
            dx_copy(t, i, buf).wait_send()

        dsend[buf] = half(dx_part(t, i, 1 - y))
        dx_copy(t, i, buf).start()
        own[buf] = dx_part(t, i, y)

    def dx_begin(t, i, buf):
        dx_copy(t, i, buf).wait_recv()
        dx_fetch(t, i).start()

    def dx_final(t, i, buf):
        @pl.when((i >= 1) | (t > 0))
        def _():
            dx_out(t, i).wait()

        dx_fetch(t, i).wait()

        def step(j, inner):
            lanes = pl.ds(mult(tile * j, tile), tile)
            dout[:, lanes] = half(own[buf, :, lanes] + wide(dfetch[:, lanes]))
            return inner

        lax.fori_loop(0, 3, step, 0)
        dx_out(t, i).start()

    def listed(u, times, do):
        e, hit = 0, False
        for index, time in enumerate(times):
            same = u == time
            e = jnp.where(same, index, e)
            hit = hit | same

        @pl.when(hit)
        def _():
            do(e)

    def chunk_of(do):
        def run(e):
            t = jnp.where(e >= n_chunk, 1, 0)
            do(t, e - n_chunk * t, lax.rem(e, HELD))

        return run

    def turn():
        lanes_at_once = min(128, tile)

        def step(q, carry):
            lanes = pl.ds(mult(q * lanes_at_once, lanes_at_once), lanes_at_once)
            xt[lanes, :] = xsrc[:, lanes].T
            return carry

        lax.fori_loop(0, tile // lanes_at_once, step, 0)

    def tile_dot(g):
        return jnp.dot(xt[...], gl[g.p], preferred_element_type=F32)

    def stage_one(g):
        tile_fetch(g.t, g.j, 1 - c, False)
        turn()
        tile_fetch(g.t, g.j, c, True)
        cstage[...] = half(tile_dot(g))
        core_copy(g).start()

    def stage_two(g):
        tile_fetch(g.t, g.j, c, False)
        turn()

        @pl.when(g.j < 2)
        def _():
            tile_fetch(g.t, g.j + 1, 1 - c, True)

        core_copy(g).wait()
        product = tile_dot(g)
        for b in range(ZED):
            block = product[:, b * hw : (b + 1) * hw] + wide(
                cland[g.buf, :, b * hw : (b + 1) * hw]
            )
            left, right = block[:, :xw], block[:, xw:]
            kept[g.trio, b] = jnp.where(x == 0, left, right)
            xstage[g.trio, b] = half(jnp.where(x == 0, right, left))

        def send(q, carry):
            across_copy(g, lax.rem(z + 3 + 3 * q, ZED)).start()
            return carry

        lax.fori_loop(0, ZED, send, 0)

    def stage_three(g):
        @pl.when(g.g >= 3)
        def _():
            for to in others:
                z_copy(g, to).wait_send()
            ax_own(g).wait_send()

        def add(b):
            across_copy(g, b).wait()
            zstage[g.trio, b] = half(kept[g.trio, b] + wide(xland[g.quad, b]))

        def step(q, carry):
            b = lax.rem(z + 3 + 3 * q, ZED)
            add(b)
            z_copy(g, b).start()
            return carry

        lax.fori_loop(0, ZED - 1, step, 0)
        add(z)
        z_own(g).start()
        ax_own(g).start()

    def stage_four(g):
        def step(q, carry):
            b = lax.rem(z + 1 + q, ZED)
            z_in(g, b).wait_recv()
            ax_copy(g, b).start()
            return carry

        lax.fori_loop(0, ZED - 1, step, 0)
        z_own(g).wait()

    def stage_five(g):
        def step(q, carry):
            b = lax.rem(z + q, ZED)
            ax_in(g, b).wait_recv()
            ac_copy(g, b).start()
            return carry

        lax.fori_loop(0, ZED, step, 0)

    def stage_six(g):
        def step(b, carry):
            ac_in(g, b).wait_recv()
            return carry

        lax.fori_loop(0, ZED, step, 0)

    def tile_of(g):
        p = lax.div(g, 3)
        t, h = tower(p)
        return Tile(
            g=g, p=p, t=t, h=h, j=g - 3 * p,
            buf=lax.rem(g, 2), trio=g - 3 * p, quad=lax.rem(g, 4),
        )

    def tile_in_hand(do):
        return lambda g: do(tile_of(g))

    def body(u, carry):
        p0 = lax.div(u, n_part)
        i0 = u - p0 * n_part
        slot0, prod0 = lax.rem(u, RING), lax.rem(u, PRODUCTS)
        buf0 = lax.rem(u, 2)

        def before(lag):
            if isinstance(lag, int):
                whole, left = divmod(lag, n_part)
            else:
                whole, left = 0, lag
            under = i0 < left
            p = p0 - whole - jnp.where(under, 1, 0)
            i = i0 - left + jnp.where(under, n_part, 0)
            in_ring = lag % RING if isinstance(lag, int) else lag
            in_prods = lag % PRODUCTS if isinstance(lag, int) else lag
            slot = slot0 - in_ring + jnp.where(slot0 < in_ring, RING, 0)
            prod = prod0 - in_prods + jnp.where(prod0 < in_prods, PRODUCTS, 0)
            t, h = tower(p)
            return Part(u=u - lag, p=p, i=i, t=t, h=h, slot=slot, prod=prod, buf=lax.rem(i, 2))

        @pl.when((u >= 5) & (u < parts + 5))
        def _():
            slot = before(5).slot
            at_place(0, ZED - 2, lambda zz: rs_up(slot, zz).wait_send())
            at_place(1, ZED - 1, lambda zz: rs_down(slot, zz).wait_send())

        @pl.when((u >= 8) & (u < parts + 8))
        def _():
            at = before(8)

            def step(b, inner):
                @pl.when((z < ZED - 1) & (b <= z))
                def _():
                    ag(at, b, 0, up).wait_send()

                @pl.when((z > 0) & (b >= z))
                def _():
                    ag(at, b, 1, down).wait_send()

                return inner

            lax.fori_loop(0, ZED, step, 0)

        ck = lax.div(i0, SUB)
        fresh = ck * SUB == i0
        t0, h0_ = tower(p0)
        xbuf = lax.rem(ck, 2)

        @pl.when((u < parts) & fresh)
        def _():
            @pl.when(i0 == 0)
            def _():
                w_own(p0).wait()
                for frm in others:
                    w_c_in(p0, frm).wait_recv()

            for copy in x_fetch(t0, ck, xbuf):
                copy.wait()

            product = jnp.dot(xc[xbuf], wv[p0], preferred_element_type=F32)
            for b in range(ZED):
                for s in range(SUB):
                    pf[prod0 + s, b] = product[
                        s * part : (s + 1) * part, b * hw : (b + 1) * hw
                    ]

        going_up = before(z)

        @pl.when((going_up.u >= 0) & (going_up.u < parts))
        def _():
            slot, prod = going_up.slot, going_up.prod
            at_place(1, ZED - 1, lambda zz: rs_from_below(slot, zz).wait_recv())

            @pl.when(z == 0)
            def _():
                for b in range(1, ZED):
                    rs[slot, b + 1] = half(pf[prod, b])

            @pl.when(z > 0)
            def _():
                def step(b, inner):
                    rs[slot, b + 1] = half(wide(rs[slot, b + 1]) + pf[prod, b])
                    return inner

                lax.fori_loop(z + 1, ZED, step, 0)

            at_place(0, ZED - 2, lambda zz: rs_up(slot, zz).start())

        going_down = before(ZED - 1 - z)

        @pl.when((going_down.u >= 0) & (going_down.u < parts))
        def _():
            slot, prod = going_down.slot, going_down.prod
            at_place(0, ZED - 2, lambda zz: rs_from_above(slot, zz).wait_recv())

            @pl.when(z == ZED - 1)
            def _():
                for b in range(ZED - 1):
                    rs[slot, b] = half(pf[prod, b])

            @pl.when(z < ZED - 1)
            def _():
                def step(b, inner):
                    rs[slot, b] = half(wide(rs[slot, b]) + pf[prod, b])
                    return inner

                lax.fori_loop(0, z, step, 0)

            at_place(1, ZED - 1, lambda zz: rs_down(slot, zz).start())

        @pl.when(fresh & (u + 2 * SUB < 2 * n_part))
        def _():
            k = p0 * n_chunk + ck + 2
            over = jnp.where(k >= n_chunk, 1, 0)
            x_copy(over, k - over * n_chunk).start()

        @pl.when(fresh & (u + SUB < parts))
        def _():
            wrap = jnp.where(ck + 1 == n_chunk, 1, 0)
            i = ck + 1 - wrap * n_chunk
            t, h = tower(p0 + wrap)

            @pl.when(h == 0)
            def _():
                x_copy(t, i).wait_recv()

            for copy in x_fetch(t, i, lax.rem(i, 2)):
                copy.start()

        @pl.when((u >= 3) & (u < parts + 3))
        def _():
            final(before(3), before(2))

        forward_ag(before(4), 1)
        forward_ag(before(5), 2)
        forward_ag(before(6), 3)

        listed(u, DX_BEGINS, chunk_of(dx_begin))
        listed(u, DX_ENDS, chunk_of(dx_final))
        listed(u, DX_TIMES, chunk_of(dx_step))

        listed(u, THREES, tile_in_hand(stage_three))
        listed(u, TWOS, tile_in_hand(stage_two))
        listed(u, ONES, tile_in_hand(stage_one))
        listed(u, FOURS, tile_in_hand(stage_four))
        listed(u, FIVES, tile_in_hand(stage_five))
        listed(u, SIXES, tile_in_hand(stage_six))

        def first_fetch(p):
            tile_fetch(lax.div(p, HALVES), 0, 1 - c, True)

        listed(u, [time - 1 for time in ONES[::3]], first_fetch)

        for p, times in W_STRIPS.items():
            def send_strip(r, p=p):
                for to in others:
                    w_z_strip(p, to, r).start()

                @pl.when(r == 0)
                def _():
                    w_own(p).start()

            listed(u, times, send_strip)

        for p, times in W_ACROSS.items():
            for q, time in enumerate(times):
                @pl.when(u == time)
                def _(p=p, q=q):
                    w_z_in(p, others[q]).wait_recv()
                    w_x(p, others[q]).start()

        for p, times in W_CORES.items():
            for q, time in enumerate(times):
                @pl.when(u == time)
                def _(p=p, q=q):
                    w_x_in(p, others[q]).wait_recv()
                    w_c(p, others[q]).start()

        @pl.when(u == parts + 3)
        def _():
            for p in range(PHASES):
                t, h = p // HALVES, p % HALVES
                for s in range(2):
                    for what in range(2):
                        sums[0, pl.ds(4 * what + 2 * s + t, 1), h * hw : (h + 1) * hw] = jnp.sum(
                            stat[p, 2 * what + s], axis=0, keepdims=True
                        )
            sum_copy(0, across_c).start()

        @pl.when(u == parts + 4)
        def _():
            sum_copy(0, across_c).wait()
            sums[1] = sums[0] + sums_land[0]
            sum_copy(1, across_x).start()

        @pl.when(u == parts + 5)
        def _():
            sum_copy(1, across_x).wait()
            both = sums[1] + sums_land[1]
            sums[2] = both
            member = (
                lax.broadcasted_iota(jnp.int32, (width, lane), 0) % FLAG_GROUPS
                == lax.broadcasted_iota(jnp.int32, (width, lane), 1) % FLAG_GROUPS
            ).astype(F32)
            bias_rows = both[0:4]
            inner = both[0:2] * both[2:4]
            stack = jnp.concatenate([inner, bias_rows * bias_rows, inner], axis=0)
            prods[0] = jnp.dot(
                stack, member, precision=lax.Precision.HIGHEST, preferred_element_type=F32
            )
            prod_y().start()

        @pl.when(u == parts + 6)
        def _():
            prod_y().wait()
            prods[1] = prods[0] + prods_land[ZED]
            for to in others:
                prod_z(to).start()

        @pl.when(u == parts + 7)
        def _():
            for frm in others:
                prod_z_in(frm).wait_recv()
            prods_land[z] = prods[1]
            whole = prods_land[0] + prods_land[1] + prods_land[2] + prods_land[3]
            both = sums[2]
            group = lax.broadcasted_iota(jnp.int32, (1, lane), 1) % FLAG_GROUPS

            def over(row):
                return jnp.concatenate([row] * (width // lane), axis=1)

            def flag_row(s, t):
                row = jnp.zeros((1, lane), F32)
                for g in range(FLAG_GROUPS):
                    row = jnp.where(group == g, flags[s, t, g].astype(F32), row)
                return row

            for t in range(2):
                task0, task1 = both[t : t + 1], both[2 + t : 3 + t]
                dots = whole[t : t + 1]
                coef0 = over(flag_row(0, t) * dots / (whole[4 + t : 5 + t] + 1e-06))
                coef1 = over(flag_row(1, t) * dots / (whole[2 + t : 3 + t] + 1e-06))
                gbias[t : t + 1] = (task0 - coef0 * task1) + (task1 - coef1 * task0)
            for s in range(2):
                gstitch[s] = both[4 + 2 * s : 6 + 2 * s]

        return carry

    lax.fori_loop(0, max(SIXES + DX_ENDS) + 1, body, 0)

    last = 3 * PHASES - 1

    for g in (last - 2, last - 1, last):
        for to in others:
            z_copy(tile_of(g), to).wait_send()
        ax_own(tile_of(g)).wait_send()
    for i in range(n_chunk - HELD, n_chunk):
        dx_copy(1, i, (n_chunk + i) % HELD).wait_send()
    for i in (n_part - 2, n_part - 1):
        mixed_out(1, i, i % 2).wait()
    dx_out(1, n_chunk - 1).wait()

    def drain_tiles(g, carry):
        at = tile_of(g)
        for b in others:
            ax_copy(at, b).wait_send()
        for b in range(ZED):
            ac_copy(at, b).wait_send()
        return carry

    lax.fori_loop(0, last + 1, drain_tiles, 0)

    def drain_x(i, carry):
        x_copy(0, i).wait_send()
        x_copy(1, i).wait_send()
        return carry

    lax.fori_loop(0, n_chunk, drain_x, 0)

    def drain_w(p, carry):
        for to in others:
            w_z(p, to).wait_send()
            w_x(p, to).wait_send()
            w_c(p, to).wait_send()
        return carry

    lax.fori_loop(0, PHASES, drain_w, 0)
    for to in others:
        prod_z(to).wait_send()


def fused_call(feat, wts, cot, bias, stitch, counts, mask, flags):
    rows, deep, width = feat.shape[1], feat.shape[2], wts.shape[2]
    chunk = rows // 6
    part = chunk // SUB
    hw, kz, tile = width // 2, 2 * deep, deep // 3
    cat, xw = 4 * hw, width // 4
    lane = min(128, width)
    dma = pltpu.SemaphoreType.DMA
    anywhere = pl.BlockSpec(memory_space=pl.ANY)
    inside = pl.BlockSpec(memory_space=pltpu.VMEM)
    scalars = pl.BlockSpec(memory_space=pltpu.SMEM)

    def v(shape, kind=BF16):
        return pltpu.VMEM(shape, kind)

    out_shape = [
        jax.ShapeDtypeStruct((2, rows, width), BF16),
        jax.ShapeDtypeStruct((2, rows, deep), BF16),
        jax.ShapeDtypeStruct((2, ZED, kz, width), BF16),
        jax.ShapeDtypeStruct((2, width), F32),
        jax.ShapeDtypeStruct((2, 2, width), F32),
        jax.ShapeDtypeStruct((2, rows, deep), BF16),
        jax.ShapeDtypeStruct((2, rows, deep), BF16),
    ]
    scratch = [
        v((PHASES, kz, cat)),
        v((PHASES, rows, cat)),
        v((RING, 5, part, hw)),
        v((2, rows, hw), F32),
        v((2, chunk, kz)),
        v((PRODUCTS, ZED, part, hw), F32),
        v((2, 2, part, hw)),
        v((2, 2, part, hw)),
        v((HELD, chunk, deep), F32),
        v((HELD, chunk, deep)),
        v((chunk, deep)),
        v((chunk, deep)),
        v((rows, tile)),
        v((tile, rows)),
        v((tile, cat)),
        v((2, tile, cat)),
        v((3, ZED, tile, xw)),
        v((4, ZED, tile, xw)),
        v((3, ZED, tile, xw), F32),
        v((3, ZED, tile, xw)),
        v((rows, lane), F32),
        v((PHASES, 4, 8, hw), F32),
        v((3, 8, width), F32),
        v((2, 8, width), F32),
        v((2, 8, lane), F32),
        v((5, 8, lane), F32),
        dma((RING, 2)), dma((RING, 2)), dma((RING, 8)), dma((RING, 4)),
        dma((12,)), dma((12,)),
        dma((4, 4)), dma((4, 4)), dma((4, 4)), dma((4, 4)), dma((4, 4)), dma((4, 4)), dma((4,)),
        dma((2, 2)), dma((2,)), dma((2,)), dma((HELD,)), dma((12,)), dma((1,)), dma((1,)),
        dma((1,)), dma((1,)), dma((2,)), dma((3, 4)), dma((4, 4)), dma((3, 4)), dma((12, 4)),
        dma((3,)), dma((3,)),
        dma((12, 4)), dma((12, 4)), dma((12, 4)), dma((12, 4)), dma((8,)), dma((8,)),
    ]
    flops = 3 * 2 * 2 * rows * kz * cat * 2
    return pl.pallas_call(
        functools.partial(fused_kernel, rows, deep, width, chunk),
        out_shape=out_shape,
        in_specs=[anywhere] * 3 + [inside] * 4 + [scalars],
        out_specs=[anywhere] * 3 + [inside] * 2 + [anywhere] * 2,
        scratch_shapes=scratch,
        compiler_params=pltpu.CompilerParams(
            collective_id=0, has_side_effects=True, vmem_limit_bytes=64 * 1024 * 1024
        ),
        cost_estimate=pl.CostEstimate(
            flops=flops, bytes_accessed=200_000_000, transcendentals=2 * rows * width * 2
        ),
        name="cross_stitch_step",
    )(feat, wts, cot, bias, stitch, counts, mask, flags)


def finish_kernel(
    block, low, mixed, gfeat, gbias, gstitch,
    out, mixed_out, gfeat_out, gbias_out, gstitch_out,
    taken, given, held_mixed, held_gfeat, in_sem, out_sem, pass_sem,
):
    n_block = low.shape[0] // block
    fetched = (
        pltpu.make_async_copy(mixed, held_mixed, pass_sem.at[0]),
        pltpu.make_async_copy(gfeat, held_gfeat, pass_sem.at[1]),
    )
    passed = (
        pltpu.make_async_copy(held_mixed, mixed_out, pass_sem.at[2]),
        pltpu.make_async_copy(held_gfeat, gfeat_out, pass_sem.at[3]),
    )

    def take(i):
        return pltpu.make_async_copy(
            low.at[pl.ds(i * block, block)], taken.at[i % WIDEN_SLOTS], in_sem.at[i % WIDEN_SLOTS]
        )

    def give(i):
        return pltpu.make_async_copy(
            given.at[i % WIDEN_SLOTS], out.at[pl.ds(i * block, block)], out_sem.at[i % WIDEN_SLOTS]
        )

    for i in range(min(WIDEN_SLOTS, n_block)):
        take(i).start()
    for copy in fetched:
        copy.start()
    gbias_out[...] = gbias[...]
    gstitch_out[...] = gstitch[...]
    for i in range(n_block):
        slot = i % WIDEN_SLOTS
        take(i).wait()
        if i >= WIDEN_SLOTS:
            give(i - WIDEN_SLOTS).wait()
        given[slot] = wide(taken[slot])
        give(i).start()
        if i + WIDEN_SLOTS < n_block:
            take(i + WIDEN_SLOTS).start()
        if i == 2:
            for arrived, copy in zip(fetched, passed):
                arrived.wait()
                copy.start()
    for i in range(max(0, n_block - WIDEN_SLOTS), n_block):
        give(i).wait()
    for copy in passed:
        copy.wait()


def finish(low, mixed, gfeat, gbias, gstitch):
    tall, width = low.shape
    block = tall // WIDEN_BLOCKS
    anywhere = pl.BlockSpec(memory_space=pl.ANY)
    inside = pl.BlockSpec(memory_space=pltpu.VMEM)
    moved = sum(a.size * a.dtype.itemsize for a in (mixed, gfeat))
    return pl.pallas_call(
        functools.partial(finish_kernel, block),
        in_specs=[anywhere] * 3 + [inside] * 2,
        out_specs=[anywhere] * 3 + [inside] * 2,
        out_shape=[
            jax.ShapeDtypeStruct(a.shape, kind)
            for a, kind in ((low, F32), (mixed, BF16), (gfeat, BF16), (gbias, F32), (gstitch, F32))
        ],
        scratch_shapes=[
            pltpu.VMEM((WIDEN_SLOTS, block, width), BF16),
            pltpu.VMEM((WIDEN_SLOTS, block, width), F32),
            pltpu.VMEM(mixed.shape, BF16),
            pltpu.VMEM(gfeat.shape, BF16),
            pltpu.SemaphoreType.DMA((WIDEN_SLOTS,)),
            pltpu.SemaphoreType.DMA((WIDEN_SLOTS,)),
            pltpu.SemaphoreType.DMA((4,)),
        ],
        compiler_params=pltpu.CompilerParams(vmem_limit_bytes=60 * 1024 * 1024),
        cost_estimate=pl.CostEstimate(
            flops=tall * width, bytes_accessed=6 * tall * width + 2 * moved, transcendentals=0
        ),
        name="finish",
    )(low, mixed, gfeat, gbias, gstitch)


def fused_plan(mesh):
    def per_device(features, weights, bias, stitch, cotangent, crop_counts, row_mask, flags):
        rows, deep = features.shape[1:]
        width = weights.shape[2]
        mixed, gfeat, gwt, gbias, gstitch, _, _ = fused_call(
            features, weights, cotangent, bias, stitch,
            crop_counts.reshape(1, -1), row_mask.reshape(-1, min(128, rows // 6)), flags,
        )
        grad_weights, mixed, gfeat, gbias, gstitch = finish(
            gwt.reshape(-1, width), mixed, gfeat, gbias, gstitch
        )
        return mixed, gfeat, grad_weights.reshape(2, ZED * 2 * deep, width), gbias, gstitch

    return per_device


def plan_for(mesh):
    if mesh.shape["batch"] == 4 and mesh.shape["mp"] == 2 * ZED:
        return fused_plan(mesh)
    return generic_plan(mesh)


def solution(mesh):
    in_specs = (
        P(None, "batch", "mp"),
        P(None, None, "mp"),
        P(None, "mp"),
        P(None, None, "mp"),
        P(None, "batch", "mp"),
        P("batch"),
        P("batch"),
        P(),
    )
    out_specs = (
        P(None, "batch", "mp"),
        P(None, "batch", "mp"),
        P(None, None, "mp"),
        P(None, "mp"),
        P(None, None, "mp"),
    )
    return jax.shard_map(
        plan_for(mesh), mesh=mesh, in_specs=in_specs, out_specs=out_specs, check_vma=False
    )
```
